32 devices in a mesh: page: 16 (over z, y, core), blk: 2 (over x).
Axes of the slice: x: 2, y: 2, z: 4, core: 2. Of those that a mesh axis runs over, the one named last changes fastest.
Arguments:
- tokens: bfloat16 [16, 720, 768], P('page', 'blk'), may hold values from -6 to 6
- patch_count: int32 [16], P('page'), may hold values from 49 to 196, as said below
- reading_rank: int32 [16, 720], P('page'), may hold values from 0 to 719, as said below
- boxes: int32 [2, 16, 720], P(None, 'page'), may hold values from 0 to 255
- text_kernel: float32 [9, 768], replicated, may hold values from -2 to 2
- patch_kernel: float32 [9, 768], replicated, may hold values from -2 to 2
- qkv_weight: bfloat16 [768, 2304], replicated, may hold values from -0.21875 to 0.21875
- rank_table: bfloat16 [12, 32], replicated, may hold values from -3 to 3
- box_tables: bfloat16 [2, 12, 64], replicated, may hold values from -3 to 3
- out_weight: bfloat16 [768, 768], replicated, may hold values from -0.4375 to 0.4375
- norm_gains: float32 [2, 768], replicated, may hold values from 0.5 to 1.5
- norm_shifts: float32 [2, 768], replicated, may hold values from -2 to 2
- up_weight: bfloat16 [768, 3072], replicated, may hold values from -0.21875 to 0.21875
- up_bias: float32 [3072], replicated, may hold values from -3 to 3
- down_weight: bfloat16 [3072, 768], replicated, may hold values from -0.15625 to 0.15625
- down_bias: float32 [768], replicated, may hold values from -3 to 3
- cotangent: bfloat16 [16, 720, 768], P('page', 'blk'), may hold values from -6 to 6
Outputs:
- layer_output: bfloat16 [16, 720, 768], P('page', 'blk')
- token_grad: float32 [16, 720, 768], P('page', 'blk')
- text_kernel_grad: float32 [9, 768], P(None, ('page', 'blk'))
- patch_kernel_grad: float32 [9, 768], P(None, ('page', 'blk'))
- qkv_weight_grad: float32 [768, 2304], P(('page', 'blk'))
- rank_table_grad: float32 [12, 32], replicated
- box_tables_grad: float32 [2, 12, 64], replicated
- out_weight_grad: float32 [768, 768], P(('page', 'blk'))
- norm_gains_grad: float32 [2, 768], P(None, ('page', 'blk'))
- norm_shifts_grad: float32 [2, 768], P(None, ('page', 'blk'))
- up_weight_grad: float32 [768, 3072], P(('page', 'blk'))
- up_bias_grad: float32 [3072], P(('page', 'blk'))
- down_weight_grad: float32 [3072, 768], P(('page', 'blk'))
- down_bias_grad: float32 [768], P(('page', 'blk'))
The draws below stay inside these ranges and needn't reach their ends.
Inputs may be any that keep to these rules, and one draw needn't show every extreme that they name: `patch_count`: each page image has 49 or 196 patches; both counts occur in every draw. `reading_rank`: for each page, the first 512 entries are a permutation of 0 to 511 made of runs of 16 consecutive slots holding consecutive values in order, the runs permuted; patch slot s holds 512 + s.
All inputs are finite; a program needn't handle non-finite values.
Results may differ from the reference program's by a relative error of at most 0.015.
The reference program's roundings to bfloat16 on the way count: a program that leaves them out, or rounds other values in their place, can miss the bound.
Values may be sent and summed in bfloat16 or wider, within the bound.
No kernel may reach another device: no remote copies, remote signals or barrier semaphores. Data moves between devices by JAX's collectives and lax.ppermute only.
A program may use at most 256 MiB of HBM per device.

```python
import jax
import jax.numpy as jnp
from jax import lax

TEXT = 512
PATCH = 208
GRID_LO = 7
GRID_HI = 14
RUN = 16
D = 768
HEADS = 12
HEAD_DIM = 64
FF = 3072
NB1 = 32
NB2 = 64
SEQ = 720
PAGES = 16


def draw_patch_count(key, part):
    key = jax.random.fold_in(key, 11)
    choose_key, order_key = jax.random.split(key)
    larger = jax.random.randint(choose_key, (PAGES,), 0, 2)
    order = jax.random.permutation(order_key, PAGES)
    larger = larger.at[order[0]].set(1).at[order[1]].set(0)
    return jnp.where(larger == 1, GRID_HI * GRID_HI, GRID_LO * GRID_LO).astype(jnp.int32)


def draw_reading_rank(key, part):
    key = jax.random.fold_in(key, 23)
    runs = TEXT // RUN
    page_keys = jax.random.split(key, PAGES)

    def run_order(single_key):
        return jax.random.permutation(single_key, runs)
    orders = jax.vmap(run_order)(page_keys).astype(jnp.int32)
    within = jnp.arange(TEXT, dtype=jnp.int32)
    text_rank = orders[:, within // RUN] * RUN + within % RUN
    patch_rank = jnp.broadcast_to(TEXT + jnp.arange(PATCH, dtype=jnp.int32), (PAGES, PATCH))
    return jnp.concatenate([text_rank, patch_rank], axis=1).astype(jnp.int32)


def place_ends(values, rng, low, top_value):
    longest = values.shape.index(max(values.shape))
    spots = []
    for shift in (0, 1):
        where = [jax.random.randint(jax.random.fold_in(rng, axis), (), 0, length) for axis, length in enumerate(values.shape)]
        where[longest] = (where[longest] + shift) % values.shape[longest]
        spots.append(tuple(where))
    return values.at[spots[0]].set(low).at[spots[1]].set(top_value)


def spiked(entries, own_key, source, target, parts, factor):
    owner, partner = [(jnp.arange(entries.shape[position]) // (entries.shape[position] // parts)).reshape([-1 if axis == position else 1 for axis in range(entries.ndim)]) for position in (source, target)]
    chosen = jax.random.permutation(own_key, parts)[partner]
    strong = (owner == chosen) | (owner == (partner + parts // 2) % parts)
    return jnp.where(strong, factor * entries, entries)


def block_levels(stream_key, extent, cuts, least, high):
    def one(position, blocks):
        heights = jax.random.uniform(jax.random.fold_in(jax.random.fold_in(stream_key, 6), position), (blocks,), jnp.float32, least / len(cuts), high / len(cuts))
        return jnp.repeat(jnp.exp(heights), extent[position] // blocks).reshape((-1,) + (1,) * (len(extent) - position - 1))

    factor_of = one(*cuts[0])
    for cut in cuts[1:]:
        factor_of = factor_of * one(*cut)
    return factor_of


def bell_draw(stream_key, extent, deviation, most, pieces=(), kind=jnp.bfloat16):
    factor_of = block_levels(stream_key, extent, pieces, -0.22, 0.18) if pieces else 1.0
    entries = jax.random.normal(stream_key, extent, jnp.float32) * deviation * factor_of
    return jnp.minimum(jnp.maximum(entries, -most), most).astype(kind)


def noise_with(stream_key, shape, scale, most, pieces, heavy, kind=jnp.bfloat16):
    array = scale * jax.random.normal(stream_key, shape, jnp.float32)
    if pieces:
        array = array * block_levels(stream_key, shape, pieces, -0.22, 0.18)
    return jnp.clip(spiked(array, jax.random.fold_in(stream_key, 3), *heavy), -most, most).astype(kind)


def setup_inputs(seed: int = 0) -> dict:
    key_of = jax.random.split(jax.random.key(seed), 18)
    tokens = bell_draw(key_of[0], (PAGES, SEQ, D), 1.0, 6.0, ((0, 16), (1, 2)))
    patch_count = draw_patch_count(jax.random.fold_in(key_of[17], 71), 0)
    reading_rank = draw_reading_rank(jax.random.fold_in(key_of[17], 71), 0)
    boxes = place_ends(jax.random.randint(key_of[3], (2, PAGES, SEQ), 0, 256), jax.random.fold_in(key_of[3], 1), 0, 255).astype(jnp.int32)
    text_kernel = bell_draw(key_of[4], (9, D), 9 ** -0.5, 2.0, (), jnp.float32)
    patch_kernel = bell_draw(key_of[5], (9, D), 9 ** -0.5, 2.0, (), jnp.float32)
    qkv_weight = bell_draw(key_of[6], (D, 3 * D), D ** -0.5, 0.21875)
    rank_table = bell_draw(key_of[7], (HEADS, NB1), 0.5, 3.0)
    box_tables = bell_draw(key_of[8], (2, HEADS, NB2), 0.5, 3.0)
    out_weight = bell_draw(key_of[9], (D, D), (D // 4) ** -0.5, 0.4375)
    norm_gains = jnp.clip(1.0 + 0.1 * jax.random.normal(key_of[10], (2, D), jnp.float32), 0.5, 1.5)
    norm_shifts = bell_draw(key_of[11], (2, D), 0.3, 2.0, (), jnp.float32)
    up_weight = bell_draw(key_of[12], (D, FF), D ** -0.5, 0.21875)
    up_bias = bell_draw(key_of[13], (FF,), 0.5, 3.0, (), jnp.float32)
    down_weight = bell_draw(key_of[14], (FF, D), (FF // 2) ** -0.5, 0.15625)
    down_bias = bell_draw(key_of[15], (D,), 0.5, 3.0, (), jnp.float32)
    cotangent = noise_with(key_of[16], (PAGES, SEQ, D), 1.0, 6.0, ((0, 16), (1, 2)), (0, 2, 16, 2.0))
    return {"tokens": tokens, "patch_count": patch_count, "reading_rank": reading_rank, "boxes": boxes, "text_kernel": text_kernel, "patch_kernel": patch_kernel, "qkv_weight": qkv_weight, "rank_table": rank_table, "box_tables": box_tables, "out_weight": out_weight, "norm_gains": norm_gains, "norm_shifts": norm_shifts, "up_weight": up_weight, "up_bias": up_bias, "down_weight": down_weight, "down_bias": down_bias, "cotangent": cotangent}


@jax.custom_vjp
def low(v):
    return lax.optimization_barrier(v.astype(jnp.bfloat16)).astype(jnp.float32)

@jax.custom_vjp
def low_back(v):
    return v

def low_keep(v):
    return (low(v), None)

def low_pass(kept, grad):
    return (grad,)

def back_keep(v):
    return (v, None)

def back_low(kept, grad):
    return (low(grad),)
low.defvjp(low_keep, low_pass)
low_back.defvjp(back_keep, back_low)
rank_marks = (1, 2, 3, 4, 5, 6, 7, 8, 12, 16, 23, 32, 46, 64, 91)
box_marks = tuple(range(1, 17)) + (19, 23, 27, 32, 39, 46, 54, 64, 77, 91, 108, 128, 153, 182, 216)
neg_fill = -1000000000.0
norm_eps = 1e-05
root_half = 0.7071067811865476
highest = lax.Precision.HIGHEST

def bucket(delta, marks, half):
    spread = jnp.abs(delta)
    counted = jnp.zeros(delta.shape, jnp.int32)
    for mark in marks:
        counted = counted + (spread >= mark).astype(jnp.int32)
    return counted + half * (delta > 0).astype(jnp.int32)

def gelu(values):
    return 0.5 * values * (1.0 + lax.erf(values * root_half))

def layer_norm(values, gain, shift):
    center = values - lax.optimization_barrier(jnp.mean(values, axis=-1, keepdims=True))
    inverse = lax.rsqrt(lax.optimization_barrier(jnp.mean(center * center, axis=-1, keepdims=True)) + norm_eps)
    return center * inverse * gain + shift

def positions(tokens_f, text_kernel, patch_kernel, grid):
    text_part = tokens_f[:TEXT]
    padded = jnp.pad(text_part, ((3, 3), (0, 0)))
    text_term = jnp.zeros_like(text_part)
    number = 0
    for reach in (1, 2, 3):
        for side in (-1, 0, 1):
            offset = reach * side
            text_term = text_term + padded[3 + offset:3 + offset + TEXT] * text_kernel[number]
            number += 1
    patches = tokens_f[TEXT:]
    slots = jnp.arange(PATCH, dtype=jnp.int32)
    row_of = slots // grid
    column = slots % grid
    alive = slots < grid * grid
    patch_term = jnp.zeros_like(patches)
    number = 0
    for down in (-1, 0, 1):
        for across in (-1, 0, 1):
            valid = alive & (row_of + down >= 0) & (row_of + down < grid) & (column + across >= 0) & (column + across < grid)
            source = jnp.clip(slots + down * grid + across, 0, PATCH - 1)
            patch_term = patch_term + jnp.where(valid[:, None], patches[source], 0.0) * patch_kernel[number]
            number += 1
    return tokens_f + jnp.concatenate([text_term, patch_term], axis=0)

def layer(tokens_f, params, count, ranks, box_x, box_y):
    text_kernel, patch_kernel, qkv_weight, rank_table, box_tables, out_weight, norm_gains, norm_shifts, up_weight, up_bias, down_weight, down_bias = params
    seq_len = tokens_f.shape[0]
    width = HEADS * HEAD_DIM
    grid = jnp.where(count == GRID_HI * GRID_HI, GRID_HI, GRID_LO).astype(jnp.int32)
    places = jnp.arange(seq_len, dtype=jnp.int32)
    row_live = places < TEXT + count
    mixed = positions(tokens_f, text_kernel, patch_kernel, grid)
    packed = low_back(low(jnp.dot(low(mixed), qkv_weight, precision=highest)))
    queries = packed[:, :width].reshape(seq_len, HEADS, HEAD_DIM)
    keys = packed[:, width:2 * width].reshape(seq_len, HEADS, HEAD_DIM)
    values = packed[:, 2 * width:].reshape(seq_len, HEADS, HEAD_DIM)
    dotted = jnp.einsum('qhd,khd->hqk', queries, keys, precision=highest) * HEAD_DIM ** (-0.5)
    rank_ids = bucket(ranks[None, :] - ranks[:, None], rank_marks, NB1 // 2)
    xbox_ids = bucket(box_x[None, :] - box_x[:, None], box_marks, NB2 // 2)
    ybox_ids = bucket(box_y[None, :] - box_y[:, None], box_marks, NB2 // 2)
    biased = dotted + jnp.take(rank_table, rank_ids, axis=1)
    biased = biased + jnp.take(box_tables[0], xbox_ids, axis=1) + jnp.take(box_tables[1], ybox_ids, axis=1)
    scores = low_back(jnp.where(row_live[None, None, :], biased, neg_fill))
    powered = jnp.exp(scores - lax.optimization_barrier(jnp.max(scores, axis=-1, keepdims=True)))
    shares = powered / lax.optimization_barrier(jnp.sum(powered, axis=-1, keepdims=True))
    context = jnp.einsum('hqk,khd->qhd', low(shares), values, precision=highest).reshape(seq_len, width)
    context = low_back(low(context))
    resid_one = mixed + low_back(jnp.dot(context, out_weight, precision=highest))
    hidden_one = layer_norm(resid_one, norm_gains[0], norm_shifts[0])
    pre_act = low_back(jnp.dot(low(hidden_one), up_weight, precision=highest) + up_bias)
    resid_two = hidden_one + low_back(jnp.dot(low(gelu(pre_act)), down_weight, precision=highest)) + down_bias
    result = layer_norm(resid_two, norm_gains[1], norm_shifts[1])
    return result * row_live[:, None].astype(jnp.float32)

def reference(tokens, patch_count, reading_rank, boxes, text_kernel, patch_kernel, qkv_weight, rank_table, box_tables, out_weight, norm_gains, norm_shifts, up_weight, up_bias, down_weight, down_bias, cotangent):
    params = tuple((argument.astype(jnp.float32) for argument in (text_kernel, patch_kernel, qkv_weight, rank_table, box_tables, out_weight, norm_gains, norm_shifts, up_weight, up_bias, down_weight, down_bias)))

    def one_page(totals, page):
        page_tokens, count, ranks, box_x, box_y, page_cot = page

        def forward(tokens_f, weights):
            return layer(tokens_f, weights, count, ranks, box_x, box_y)
        result, pullback = jax.vjp(forward, page_tokens.astype(jnp.float32), params)
        page_grad, weight_grads = pullback(page_cot.astype(jnp.float32))
        return (jax.tree.map(jnp.add, totals, weight_grads), (result.astype(jnp.bfloat16), page_grad))
    zeros = jax.tree.map(jnp.zeros_like, params)
    totals, (layer_output, token_grad) = lax.scan(one_page, zeros, (tokens, patch_count, reading_rank, boxes[0], boxes[1], cotangent))
    return (layer_output, token_grad, totals[0], totals[1], totals[2], totals[3], totals[4], totals[5], totals[6], totals[7], totals[8], totals[9], totals[10], totals[11])
```

```python
import functools

import jax
import jax.numpy as jnp
import numpy as np
from jax import lax
from jax.experimental import pallas as pl
from jax.experimental.pallas import tpu as pltpu
from jax.sharding import PartitionSpec as P

TEXT = 512
GRID_LO = 7
GRID_HI = 14
RUN = 16
HEADS = 12
HEAD_DIM = 64
NB1 = 32
NB2 = 64
SPAN = 256
RANK_LANES = 1536
RANK_MID = RANK_LANES // 2
ROWS = 128
F32 = jnp.float32
BF16 = jnp.bfloat16
MIB = 1 << 20

rank_marks = (1, 2, 3, 4, 5, 6, 7, 8, 12, 16, 23, 32, 46, 64, 91)
box_marks = tuple(range(1, 17)) + (19, 23, 27, 32, 39, 46, 54, 64, 77, 91, 108, 128, 153, 182, 216)
neg_fill = -1000000000.0
norm_eps = 1e-05
root_half = 0.7071067811865476
inv_root_tau = 0.3989422804014327
tap_list = ((1, -1), (1, 0), (1, 1), (2, -1), (2, 0), (2, 1), (3, -1), (3, 0), (3, 1))
cell_list = ((-1, -1), (-1, 0), (-1, 1), (0, -1), (0, 0), (0, 1), (1, -1), (1, 0), (1, 1))


def bucket_rows(deltas, marks, bins):
    spread = np.abs(deltas)
    ids = np.sum(spread[:, None] >= np.asarray(marks)[None, :], axis=1) + (bins // 2) * (deltas > 0)
    return (ids[:, None] == np.arange(bins)[None, :]).astype(np.float32)


def gelu(values):
    return 0.5 * values * (1.0 + lax.erf(values * root_half))


def gelu_slope(values):
    return (
        0.5 * (1.0 + lax.erf(values * root_half))
        + values * jnp.exp(-0.5 * values * values) * inv_root_tau
    )


def layer_norm(values, gain, shift):
    center = values - jnp.mean(values, axis=-1, keepdims=True)
    inverse = lax.rsqrt(jnp.mean(center * center, axis=-1, keepdims=True) + norm_eps)
    normed = center * inverse
    return (normed * gain + shift, normed, inverse)


def norm_back(upstream, normed, inverse, gain):
    scaled = upstream * gain
    return inverse * (
        scaled
        - jnp.mean(scaled, axis=-1, keepdims=True)
        - normed * jnp.mean(scaled * normed, axis=-1, keepdims=True)
    )


def dot_nn(left, right):
    return lax.dot_general(left, right, (((1,), (0,)), ((), ())), preferred_element_type=F32)


def dot_nt(left, right):
    return lax.dot_general(left, right, (((1,), (1,)), ((), ())), preferred_element_type=F32)


def dot_tn(left, right):
    return lax.dot_general(left, right, (((0,), (0,)), ((), ())), preferred_element_type=F32)


def row_chunks(total, size):
    return [(start, min(size, total - start)) for start in range(0, total, size)]


def vmem():
    return pl.BlockSpec(memory_space=pltpu.VMEM)


def smem():
    return pl.BlockSpec(memory_space=pltpu.SMEM)


def params(mib):
    return pltpu.CompilerParams(vmem_limit_bytes=mib * MIB)


def onehot_kernel(rank_ref, box_ref, xy_ref, xyt_ref):
    seq = rank_ref.shape[1]
    for start, size in row_chunks(seq, 240):
        spot = lax.broadcasted_iota(jnp.int32, (size, seq), 0) + start
        order = (spot == rank_ref[...]).astype(F32).astype(BF16)
        for half in range(2):
            level = lax.broadcasted_iota(jnp.int32, (SPAN, seq), 0)
            marks = (level == box_ref[half : half + 1, :]).astype(F32).astype(BF16)
            xy_ref[start : start + size, half * SPAN : (half + 1) * SPAN] = dot_nt(
                order, marks
            ).astype(BF16)
    row = lax.broadcasted_iota(jnp.int32, (SPAN, SPAN), 0)
    col = lax.broadcasted_iota(jnp.int32, (SPAN, SPAN), 1)
    flip = (row + col == SPAN - 1).astype(F32).astype(BF16)
    for half in range(2):
        part = slice(half * SPAN, (half + 1) * SPAN)
        xyt_ref[part, :] = dot_nt(flip, xy_ref[:, part]).astype(BF16)


def onehots(ranks, boxes):
    seq = ranks.shape[0]
    return pl.pallas_call(
        onehot_kernel,
        out_shape=(
            jax.ShapeDtypeStruct((seq, 2 * SPAN), BF16),
            jax.ShapeDtypeStruct((2 * SPAN, seq), BF16),
        ),
        in_specs=[vmem(), vmem()],
        out_specs=(vmem(), vmem()),
        compiler_params=params(32),
        cost_estimate=pl.CostEstimate(
            flops=4 * seq * seq * SPAN, bytes_accessed=4 * seq * 2 * SPAN, transcendentals=0
        ),
        name="onehots",
    )(ranks[None, :], boxes)


def place_slots(own_ref, other_ref, side, text, patch, patch_pad):
    local = own_ref.shape[0]
    head = TEXT - local
    groups = text.shape[0]

    def place(low_ref, high_ref):
        for lane in range(groups):
            cols = slice(128 * lane, 128 * lane + 128)
            text[lane, 8 : 8 + local, :] = low_ref[:, cols].astype(F32)
            high = high_ref[:, cols].astype(F32)
            text[lane, 8 + local : 8 + TEXT, :] = high[:head]
            patch[lane, patch_pad : patch_pad + local - head, :] = high[head:]

    pl.when(side == 0)(lambda: place(own_ref, other_ref))
    pl.when(side != 0)(lambda: place(other_ref, own_ref))


def clear_pads(text, patch, patch_pad):
    groups, rows = patch.shape[0], patch.shape[1]
    for lane in range(groups):
        text[lane, 0:8, :] = jnp.zeros((8, 128), F32)
        text[lane, 8 + TEXT : 16 + TEXT, :] = jnp.zeros((8, 128), F32)
        patch[lane, 0:patch_pad, :] = jnp.zeros((patch_pad, 128), F32)
        patch[lane, rows - patch_pad : rows, :] = jnp.zeros((patch_pad, 128), F32)


def cell_masks(grid, rows):
    slot = lax.broadcasted_iota(jnp.int32, (rows, 128), 0)
    row_of = jnp.zeros((rows, 128), jnp.int32)
    for line in range(1, grid):
        row_of = row_of + (slot >= line * grid).astype(jnp.int32)
    column = slot - row_of * grid
    alive = slot < grid * grid
    masks = []
    for down, across in cell_list:
        masks.append(
            alive
            & (row_of + down >= 0)
            & (row_of + down < grid)
            & (column + across >= 0)
            & (column + across < grid)
        )
    return masks


def store_masks(masks, fine, rows):
    for grid, chosen in ((GRID_HI, fine != 0), (GRID_LO, fine == 0)):

        def fill(grid=grid):
            for number, mask in enumerate(cell_masks(grid, rows)):
                masks[number] = mask.astype(F32)

        pl.when(chosen)(fill)


def mix_lane(text, patch, masks, out, lane, text_kernel, patch_kernel, fine, patch_pad, flip):
    cols = pl.ds(pl.multiple_of(lane * 128, 128), 128)
    taps = {}
    for number, (reach, side) in enumerate(tap_list):
        offset = -reach * side if flip else reach * side
        value = text_kernel[number : number + 1, cols]
        taps[offset] = taps[offset] + value if offset in taps else value
    for start, size in row_chunks(TEXT, ROWS):
        total = text[lane, pl.ds(8 + start, size), :] * (1.0 + taps[0])
        for offset, value in taps.items():
            if offset:
                total = total + text[lane, pl.ds(8 + start + offset, size), :] * value
        out[lane, pl.ds(start, size), :] = total
    rows = masks.shape[1]
    for grid, chosen in ((GRID_HI, fine != 0), (GRID_LO, fine == 0)):

        def cells(grid=grid):
            for start, size in row_chunks(rows, 104):
                total = patch[lane, pl.ds(patch_pad + start, size), :]
                for number, (down, across) in enumerate(cell_list):
                    tap = len(cell_list) - 1 - number if flip else number
                    moved = patch[lane, pl.ds(patch_pad + start + down * grid + across, size), :]
                    total = total + (
                        moved * masks[number, pl.ds(start, size), :]
                    ) * patch_kernel[tap : tap + 1, cols]
                out[lane, pl.ds(TEXT + start, size), :] = total

        pl.when(chosen)(cells)


def sort_rows(ranks_ref, source, target, seq, cast):
    for run in range(TEXT // RUN):
        spot = pl.multiple_of(ranks_ref[run * RUN], RUN)
        target[pl.ds(spot, RUN), :] = source[run * RUN : (run + 1) * RUN, :].astype(cast)
    target[TEXT:seq, :] = source[TEXT:seq, :].astype(cast)


def unsort_rows(ranks_ref, source, target, seq):
    for run in range(TEXT // RUN):
        spot = pl.multiple_of(ranks_ref[run * RUN], RUN)
        target[run * RUN : (run + 1) * RUN, :] = source[pl.ds(spot, RUN), :]
    target[TEXT:seq, :] = source[TEXT:seq, :]


def mix_kernel(
    scalars, ranks_ref, own_ref, other_ref, text_kernel, patch_kernel, weight_ref,
    mixed_ref, low_ref, packed_ref, text, patch, masks, lanes, whole,
):
    side, fine = scalars[0], scalars[2]
    local, width = own_ref.shape
    seq = low_ref.shape[0]
    groups = width // 128
    pad = GRID_HI + 2
    place_slots(own_ref, other_ref, side, text, patch, pad)
    clear_pads(text, patch, pad)
    store_masks(masks, fine, seq - TEXT)

    def one_lane(lane, carry):
        mix_lane(text, patch, masks, lanes, lane, text_kernel, patch_kernel, fine, pad, False)
        return carry

    lax.fori_loop(0, groups, one_lane, 0)
    for lane in range(groups):
        whole[:, 128 * lane : 128 * lane + 128] = lanes[lane]
    mixed_ref[...] = whole[pl.ds(pl.multiple_of(side * local, 8), local), :]
    sort_rows(ranks_ref, whole, low_ref, seq, BF16)
    part = width // 2
    for block in range(3):
        cols = pl.ds(pl.multiple_of(block * width + side * part, 128), part)
        weight = weight_ref[:, cols]
        for start, size in row_chunks(seq, 240):
            value = dot_nn(low_ref[start : start + size, :], weight).astype(BF16)
            if block == 0:
                value = value * (HEAD_DIM**-0.5)
            packed_ref[start : start + size, block * part : (block + 1) * part] = value


def mix_and_project(scalars, ranks, own, other, text_kernel, patch_kernel, qkv_weight):
    local, width = own.shape
    seq = ranks.shape[0]
    groups = width // 128
    return pl.pallas_call(
        mix_kernel,
        out_shape=(
            jax.ShapeDtypeStruct((local, width), F32),
            jax.ShapeDtypeStruct((seq, width), BF16),
            jax.ShapeDtypeStruct((seq, 3 * width // 2), BF16),
        ),
        in_specs=[smem(), smem()] + [vmem()] * 5,
        out_specs=(vmem(),) * 3,
        scratch_shapes=[
            pltpu.VMEM((groups, TEXT + 16, 128), F32),
            pltpu.VMEM((groups, seq - TEXT + 2 * (GRID_HI + 2), 128), F32),
            pltpu.VMEM((9, seq - TEXT, 128), F32),
            pltpu.VMEM((groups, seq, 128), F32),
            pltpu.VMEM((seq, width), F32),
        ],
        compiler_params=params(40),
        cost_estimate=pl.CostEstimate(
            flops=2 * seq * width * 3 * width // 2, bytes_accessed=12 * MIB, transcendentals=0
        ),
        name="mix_and_project",
    )(scalars, ranks, own, other, text_kernel, patch_kernel, qkv_weight)


def head_lanes(shape, parity):
    return (lax.broadcasted_iota(jnp.int32, shape, 1) >= HEAD_DIM) == (parity != 0)


def skewed(vector, rows, lanes, shift):
    return pltpu.roll(jnp.broadcast_to(vector, (rows, lanes)), shift, 1, stride=1, stride_axis=0)


def attend_kernel(
    scalars, ranks_ref, queries, keys, values, xy_ref, vectors,
    shares_ref, own_ref, other_ref, left, right, rank_bias, gathered, slots,
):
    side, live = scalars[0], scalars[1]
    seq = queries.shape[0]
    local = own_ref.shape[0]
    head = pl.program_id(0)
    parity = lax.rem(head, 2)

    @pl.when(head == 0)
    def _():
        left[:, 128:] = xy_ref[...]

    left[:, :128] = queries[...]
    mine = head_lanes((seq, 128), parity)
    right[:, :128] = jnp.where(mine, keys[...], jnp.zeros((), BF16))
    for half in range(2):
        table = skewed(vectors[0, half + 1 : half + 2, : 2 * SPAN], SPAN, 2 * SPAN, SPAN + 1)
        table = table[:, :SPAN].astype(BF16)
        right[:, 128 + half * SPAN : 128 + (half + 1) * SPAN] = dot_nn(
            xy_ref[:, half * SPAN : (half + 1) * SPAN], table
        ).astype(BF16)
    rank_bias[...] = skewed(vectors[0, 0:1, :], ROWS, RANK_LANES, RANK_LANES - 128)
    top = (seq // ROWS) * ROWS
    for start, size in row_chunks(seq, ROWS):
        scores = dot_nt(left[start : start + size, :], right[...])
        scores = scores + rank_bias[:size, top - start : top - start + seq]
        alive = lax.broadcasted_iota(jnp.int32, (size, seq), 1) < live
        scores = jnp.where(alive, scores, neg_fill)
        powered = jnp.exp(scores - jnp.max(scores, axis=1, keepdims=True))
        shares = powered * (1.0 / jnp.sum(powered, axis=1, keepdims=True))
        low = shares.astype(BF16)
        shares_ref[0, start : start + size, :] = low
        context = dot_nn(low, values[...])
        gathered[start : start + size, :] = jnp.where(
            head_lanes((size, 128), parity), context, gathered[start : start + size, :]
        )

    @pl.when(parity == 1)
    def _():
        unsort_rows(ranks_ref, gathered, slots, seq)
        own_ref[...] = slots[pl.ds(pl.multiple_of(side * local, 8), local), :].astype(BF16)
        other_ref[...] = slots[pl.ds(pl.multiple_of((1 - side) * local, 8), local), :].astype(BF16)


def attend(scalars, ranks, packed, xy, vectors, local):
    seq = packed.shape[0]
    heads = vectors.shape[0]
    pairs = heads // 2
    width = heads * HEAD_DIM
    whole = pl.BlockSpec((seq, 2 * SPAN), lambda h: (0, 0))
    slot_spec = pl.BlockSpec((local, 128), lambda h: (0, h // 2))
    return pl.pallas_call(
        attend_kernel,
        grid=(heads,),
        out_shape=(
            jax.ShapeDtypeStruct((heads, seq, seq), BF16),
            jax.ShapeDtypeStruct((local, width), BF16),
            jax.ShapeDtypeStruct((local, width), BF16),
        ),
        in_specs=[
            smem(),
            smem(),
            pl.BlockSpec((seq, 128), lambda h: (0, h // 2)),
            pl.BlockSpec((seq, 128), lambda h: (0, pairs + h // 2)),
            pl.BlockSpec((seq, 128), lambda h: (0, 2 * pairs + h // 2)),
            whole,
            pl.BlockSpec((1, 8, RANK_LANES), lambda h: (h, 0, 0)),
        ],
        out_specs=(pl.BlockSpec((1, seq, seq), lambda h: (h, 0, 0)), slot_spec, slot_spec),
        scratch_shapes=[
            pltpu.VMEM((seq, 128 + 2 * SPAN), BF16),
            pltpu.VMEM((seq, 128 + 2 * SPAN), BF16),
            pltpu.VMEM((ROWS, RANK_LANES), F32),
            pltpu.VMEM((seq, 128), F32),
            pltpu.VMEM((seq, 128), F32),
        ],
        compiler_params=params(40),
        cost_estimate=pl.CostEstimate(
            flops=heads * 2 * seq * seq * 1024,
            bytes_accessed=heads * seq * seq * 2,
            transcendentals=heads * seq * seq,
        ),
        name="attend",
    )(scalars, ranks, packed, packed, packed, xy, vectors)


def attend_back_kernel(
    ranks_ref, own_ref, other_ref, side_ref, shares_ref, queries, keys, values, xy_ref, xyt_ref,
    dq_ref, dk_ref, dv_ref, sums_ref, right, score_grad, spread, rank_sum, slots, upstream,
):
    seq = queries.shape[0]
    local = own_ref.shape[0]
    side = side_ref[0]
    head = pl.program_id(0)
    parity = lax.rem(head, 2)
    scale = HEAD_DIM**-0.5

    @pl.when(head == 0)
    def _():
        right[:, 128:] = xy_ref[...]

    @pl.when(parity == 0)
    def _():
        slots[pl.ds(pl.multiple_of(side * local, 8), local), :] = own_ref[...].astype(F32)
        slots[pl.ds(pl.multiple_of((1 - side) * local, 8), local), :] = other_ref[...].astype(F32)
        sort_rows(ranks_ref, slots, upstream, seq, BF16)

    right[:, :128] = keys[...]
    mine = head_lanes((seq, 128), parity)
    own_values = jnp.where(mine, values[...], jnp.zeros((), BF16))
    rank_sum[...] = jnp.zeros(rank_sum.shape, F32)
    top = (seq // ROWS) * ROWS
    for start, size in row_chunks(seq, ROWS):
        rows = slice(start, start + size)
        share_grad = dot_nt(upstream[rows, :], own_values)
        shares = shares_ref[0, rows, :].astype(F32)
        weighted = shares * share_grad
        low = (weighted - shares * jnp.sum(weighted, axis=1, keepdims=True)).astype(BF16)
        score_grad[rows, :] = low
        lanes = slice(top - start, top - start + seq)
        rank_sum[:size, lanes] = rank_sum[:size, lanes] + low.astype(F32)
        product = dot_nn(low, right[...])
        spread[rows, :] = product[:, 128:].astype(BF16)
        dq_ref[rows, :] = jnp.where(
            head_lanes((size, 128), parity), (product[:, :128] * scale).astype(BF16), dq_ref[rows, :]
        )
    dk = dot_tn(score_grad[...], queries[...]).astype(BF16)
    dk_ref[...] = jnp.where(mine, dk, dk_ref[...])
    dv = dot_tn(shares_ref[0], upstream[...]).astype(BF16)
    dv_ref[...] = jnp.where(mine, dv, dv_ref[...])
    row = lax.broadcasted_iota(jnp.int32, (ROWS, ROWS), 0)
    col = lax.broadcasted_iota(jnp.int32, (ROWS, ROWS), 1)
    flip = (row + col == ROWS - 1).astype(F32)
    turned = lax.dot_general(
        flip, rank_sum[...], (((1,), (0,)), ((), ())),
        precision=lax.Precision.HIGHEST, preferred_element_type=F32,
    )
    turned = pltpu.roll(turned, 0, 1, stride=1, stride_axis=0)
    sums_ref[0, 0:1, :] = jnp.sum(turned, axis=0, keepdims=True)
    for half in range(2):
        part = slice(half * SPAN, (half + 1) * SPAN)
        table = dot_nn(xyt_ref[part, :], spread[:, part])
        table = jnp.concatenate([table, jnp.zeros((SPAN, SPAN), F32)], axis=1)
        table = pltpu.roll(table, 0, 1, stride=1, stride_axis=0)
        sums_ref[0, half + 1 : half + 2, : 2 * SPAN] = jnp.sum(table, axis=0, keepdims=True)


def attend_back(scalars, ranks, own, other, shares, packed, xy, xyt):
    heads, seq, _ = shares.shape
    local = own.shape[0]
    pairs = heads // 2
    width = heads * HEAD_DIM
    slot_spec = pl.BlockSpec((local, 128), lambda h: (0, h // 2))
    out_spec = pl.BlockSpec((seq, 128), lambda h: (0, h // 2))
    return pl.pallas_call(
        attend_back_kernel,
        grid=(heads,),
        out_shape=(jax.ShapeDtypeStruct((seq, width), BF16),) * 3
        + (jax.ShapeDtypeStruct((heads, 8, RANK_LANES), F32),),
        in_specs=[
            smem(),
            slot_spec,
            slot_spec,
            smem(),
            pl.BlockSpec((1, seq, seq), lambda h: (h, 0, 0)),
            pl.BlockSpec((seq, 128), lambda h: (0, h // 2)),
            pl.BlockSpec((seq, 128), lambda h: (0, pairs + h // 2)),
            pl.BlockSpec((seq, 128), lambda h: (0, 2 * pairs + h // 2)),
            pl.BlockSpec((seq, 2 * SPAN), lambda h: (0, 0)),
            pl.BlockSpec((2 * SPAN, seq), lambda h: (0, 0)),
        ],
        out_specs=(out_spec,) * 3 + (pl.BlockSpec((1, 8, RANK_LANES), lambda h: (h, 0, 0)),),
        scratch_shapes=[
            pltpu.VMEM((seq, 128 + 2 * SPAN), BF16),
            pltpu.VMEM((seq, seq), BF16),
            pltpu.VMEM((seq, 2 * SPAN), BF16),
            pltpu.VMEM((ROWS, RANK_LANES), F32),
            pltpu.VMEM((seq, 128), F32),
            pltpu.VMEM((seq, 128), BF16),
        ],
        compiler_params=params(40),
        cost_estimate=pl.CostEstimate(
            flops=heads * 2 * seq * seq * 1600,
            bytes_accessed=heads * seq * seq * 2,
            transcendentals=0,
        ),
        name="attend_back",
    )(ranks, own, other, scalars, shares, packed, packed, packed, xy, xyt)


def project_back_kernel(order_ref, low_ref, dq_ref, dk_ref, dv_ref, keep_ref, send_ref):
    turned = dot_nt(order_ref[...], low_ref[...]).astype(BF16)
    half, part = keep_ref.shape[0], dq_ref.shape[1]
    for block, ref in enumerate((dq_ref, dk_ref, dv_ref)):
        cols = slice(block * part, (block + 1) * part)
        send_ref[:, cols] = dot_nn(turned[half:], ref[...]).astype(BF16)
        keep_ref[:, cols] = dot_nn(turned[:half], ref[...]).astype(BF16)


def project_weight_grad(order, low, dq, dk, dv):
    seq, width = low.shape
    shape = jax.ShapeDtypeStruct((width // 2, 3 * dq.shape[1]), BF16)
    return pl.pallas_call(
        project_back_kernel,
        out_shape=(shape, shape),
        in_specs=[vmem()] * 5,
        out_specs=(vmem(), vmem()),
        compiler_params=params(40),
        cost_estimate=pl.CostEstimate(
            flops=2 * seq * width * 5 * width // 2, bytes_accessed=8 * MIB, transcendentals=0
        ),
        name="project_weight_grad",
    )(order, low, dq, dk, dv)


def up_kernel(order_ref, hidden_ref, context_ref, grad_ref, attend_ref, keep_ref, send_ref, turned):
    step = pl.program_id(0)
    half = keep_ref.shape[0]
    last = pl.num_programs(0) - 1

    @pl.when(step == 0)
    def _():
        turned[...] = dot_nt(order_ref[...], hidden_ref[...]).astype(BF16)

    @pl.when(step == last)
    def _():
        turned[...] = dot_nt(order_ref[...], context_ref[...]).astype(BF16)

    def fill(right):
        send_ref[...] = dot_nn(turned[half:, :], right).astype(BF16)
        keep_ref[...] = dot_nn(turned[:half, :], right).astype(BF16)

    pl.when(step < last)(lambda: fill(grad_ref[...]))
    pl.when(step == last)(lambda: fill(attend_ref[...]))


def up_weight_grad(order, hidden, context, pre_grad, attend_grad):
    local, width = hidden.shape
    steps = pre_grad.shape[1] // width
    whole = lambda shape: pl.BlockSpec(shape, lambda s: (0, 0))
    out_spec = pl.BlockSpec((width // 2, width), lambda s: (0, s))
    shape = jax.ShapeDtypeStruct((width // 2, (steps + 1) * width), BF16)
    return pl.pallas_call(
        up_kernel,
        grid=(steps + 1,),
        out_shape=(shape, shape),
        in_specs=[
            whole((width, width)),
            whole((local, width)),
            whole((local, width)),
            pl.BlockSpec((local, width), lambda s: (0, jnp.minimum(s, steps - 1))),
            whole((local, width)),
        ],
        out_specs=(out_spec, out_spec),
        scratch_shapes=[pltpu.VMEM((width, local), BF16)],
        compiler_params=params(40),
        cost_estimate=pl.CostEstimate(
            flops=2 * local * width * (steps + 3) * width, bytes_accessed=12 * MIB, transcendentals=0
        ),
        name="up_weight_grad",
    )(order, hidden, context, pre_grad, attend_grad)


def down_kernel(spots, act_ref, grad_ref, keep_ref, send_ref, *, piece):
    step = pl.program_id(0)
    width = act_ref.shape[1]
    half = keep_ref.shape[0]
    value = dot_tn(act_ref[...], grad_ref[...]).astype(BF16)
    for block in range(width // piece):
        spot = spots[step * (width // piece) + block]
        rows = value[block * piece : (block + 1) * piece, :]

        def keep(spot=spot, rows=rows):
            keep_ref[pl.ds(pl.multiple_of(spot, 16), piece), :] = rows

        def send(spot=spot, rows=rows):
            send_ref[pl.ds(pl.multiple_of(spot - half, 16), piece), :] = rows

        pl.when(spot < half)(keep)
        pl.when(spot >= half)(send)


def down_weight_grad(spots, act, grad, piece):
    local, deep = act.shape
    width = grad.shape[1]
    shape = jax.ShapeDtypeStruct((deep // 2, width), BF16)
    out_spec = pl.BlockSpec((deep // 2, width), lambda s: (0, 0))
    return pl.pallas_call(
        functools.partial(down_kernel, piece=piece),
        grid=(deep // width,),
        out_shape=(shape, shape),
        in_specs=[
            smem(),
            pl.BlockSpec((local, width), lambda s: (0, s)),
            pl.BlockSpec((local, width), lambda s: (0, 0)),
        ],
        out_specs=(out_spec, out_spec),
        compiler_params=params(40),
        cost_estimate=pl.CostEstimate(
            flops=2 * local * width * deep, bytes_accessed=8 * MIB, transcendentals=0
        ),
        name="down_weight_grad",
    )(spots, act, grad)


def mixed_back_kernel(
    scalars, ranks_ref, dq_ref, dk_ref, dv_ref, weight_ref, resid_ref, own_ref, other_ref,
    grad_ref, send_ref, taps_ref, cells_ref, sorted_grad, whole, text, patch, masks, edge,
):
    side, fine = scalars[0], scalars[2]
    local, width = own_ref.shape
    seq, part = dq_ref.shape
    groups = width // 128
    pad = GRID_HI + 2
    for start, size in row_chunks(seq, 240):
        total = None
        for block, ref in enumerate((dq_ref, dk_ref, dv_ref)):
            cols = pl.ds(pl.multiple_of(block * width + side * part, 128), part)
            product = dot_nt(ref[start : start + size, :], weight_ref[:, cols])
            total = product if total is None else total + product
        sorted_grad[start : start + size, :] = total
    unsort_rows(ranks_ref, sorted_grad, whole, seq)
    mine = pl.ds(pl.multiple_of(side * local, 8), local)
    theirs = pl.ds(pl.multiple_of((1 - side) * local, 8), local)
    whole[mine, :] = whole[mine, :] + resid_ref[...]
    inner = pl.ds(pl.multiple_of(local - 8 + side * 8, 8), 8)
    outer = pl.ds(pl.multiple_of(local - side * 8, 8), 8)
    edge[0:local, :] = whole[theirs, :]
    edge[local : local + 8, :] = whole[inner, :]
    send_ref[...] = edge[...].astype(BF16)
    grad_ref[0:local, :] = whole[mine, :]
    grad_ref[local : local + 8, :] = whole[outer, :]
    place_slots(own_ref, other_ref, side, text, patch, pad)
    clear_pads(text, patch, pad)
    store_masks(masks, fine, seq - TEXT)
    taps_ref[...] = jnp.zeros(taps_ref.shape, F32)
    cells_ref[...] = jnp.zeros(cells_ref.shape, F32)
    for lane in range(groups):
        cols = slice(lane * 128, lane * 128 + 128)
        for offset in range(-3, 4):
            total = None
            for start, size in row_chunks(TEXT, ROWS):
                value = jnp.sum(
                    whole[start : start + size, cols]
                    * text[lane, pl.ds(8 + start + offset, size), :],
                    axis=0, keepdims=True,
                )
                total = value if total is None else total + value
            for number, (reach, direction) in enumerate(tap_list):
                if reach * direction == offset:
                    taps_ref[number : number + 1, cols] = total
    for grid, chosen in ((GRID_HI, fine != 0), (GRID_LO, fine == 0)):

        def cells(grid=grid):
            for lane in range(groups):
                cols = slice(lane * 128, lane * 128 + 128)
                for number, (down, across) in enumerate(cell_list):
                    moved = patch[lane, pl.ds(pad + down * grid + across, seq - TEXT), :]
                    cells_ref[number : number + 1, cols] = jnp.sum(
                        whole[TEXT:seq, cols] * (moved * masks[number]), axis=0, keepdims=True
                    )

        pl.when(chosen)(cells)


def mixed_back(scalars, ranks, dq, dk, dv, qkv_weight, resid_grad, own, other):
    local, width = own.shape
    seq = ranks.shape[0]
    groups = width // 128
    return pl.pallas_call(
        mixed_back_kernel,
        out_shape=(
            jax.ShapeDtypeStruct((local + 8, width), F32),
            jax.ShapeDtypeStruct((local + 8, width), BF16),
            jax.ShapeDtypeStruct((16, width), F32),
            jax.ShapeDtypeStruct((16, width), F32),
        ),
        in_specs=[smem(), smem()] + [vmem()] * 7,
        out_specs=(vmem(),) * 4,
        scratch_shapes=[
            pltpu.VMEM((seq, width), F32),
            pltpu.VMEM((seq, width), F32),
            pltpu.VMEM((groups, TEXT + 16, 128), F32),
            pltpu.VMEM((groups, seq - TEXT + 2 * (GRID_HI + 2), 128), F32),
            pltpu.VMEM((9, seq - TEXT, 128), F32),
            pltpu.VMEM((local + 8, width), F32),
        ],
        compiler_params=params(40),
        cost_estimate=pl.CostEstimate(
            flops=2 * seq * width * 3 * width // 2, bytes_accessed=12 * MIB, transcendentals=0
        ),
        name="mixed_back",
    )(scalars, ranks, dq, dk, dv, qkv_weight, resid_grad, own, other)


def token_kernel(
    scalars, grad_ref, received_ref, text_kernel, patch_kernel, out_ref, text, patch, masks, lanes
):
    side, fine = scalars[0], scalars[2]
    local, width = out_ref.shape
    groups = width // 128
    pad = GRID_HI + 2
    rows = masks.shape[1]
    head = TEXT - local
    clear_pads(text, patch, pad)
    store_masks(masks, fine, rows)

    def load(low):
        for lane in range(groups):
            cols = slice(lane * 128, lane * 128 + 128)
            total = grad_ref[:, cols] + received_ref[:, cols].astype(F32)
            if low:
                text[lane, 8 : 8 + local + 8, :] = total
                text[lane, 16 + local : 8 + TEXT, :] = jnp.zeros((head - 8, 128), F32)
                patch[lane, pad : pad + rows, :] = jnp.zeros((rows, 128), F32)
            else:
                text[lane, 8 : local, :] = jnp.zeros((local - 8, 128), F32)
                text[lane, local : local + 8, :] = total[local:]
                text[lane, 8 + local : 8 + TEXT, :] = total[:head]
                patch[lane, pad : pad + rows, :] = total[head:local]

    pl.when(side == 0)(lambda: load(True))
    pl.when(side != 0)(lambda: load(False))

    def one_lane(lane, carry):
        mix_lane(text, patch, masks, lanes, lane, text_kernel, patch_kernel, fine, pad, True)
        return carry

    lax.fori_loop(0, groups, one_lane, 0)
    mine = pl.ds(pl.multiple_of(side * local, 8), local)
    for lane in range(groups):
        out_ref[:, lane * 128 : lane * 128 + 128] = lanes[lane, mine, :]


def token_back(scalars, grad, received, text_kernel, patch_kernel, seq):
    local, width = grad.shape[0] - 8, grad.shape[1]
    groups = width // 128
    return pl.pallas_call(
        token_kernel,
        out_shape=jax.ShapeDtypeStruct((local, width), F32),
        in_specs=[smem()] + [vmem()] * 4,
        out_specs=vmem(),
        scratch_shapes=[
            pltpu.VMEM((groups, TEXT + 16, 128), F32),
            pltpu.VMEM((groups, seq - TEXT + 2 * (GRID_HI + 2), 128), F32),
            pltpu.VMEM((9, seq - TEXT, 128), F32),
            pltpu.VMEM((groups, seq, 128), F32),
        ],
        compiler_params=params(32),
        cost_estimate=pl.CostEstimate(
            flops=40 * local * width, bytes_accessed=4 * MIB, transcendentals=0
        ),
        name="token_back",
    )(scalars, grad, received, text_kernel, patch_kernel)


def swap(value, stage):
    axis, bit = stage
    count = lax.axis_size(axis)
    return lax.ppermute(value, axis, [(i, i ^ bit) for i in range(count)])


def stage_flag(stage):
    axis, bit = stage
    return (lax.axis_index(axis) & bit) // bit


def block_bit(block, stage, blk_count):
    axis, bit = stage
    shift = bit * blk_count if axis == "page" else bit
    return (block // shift) & 1


def spot_of(block, stages, blk_count):
    spot = jnp.zeros_like(block)
    for stage in stages:
        spot = spot * 2 + (block_bit(block, stage, blk_count) ^ stage_flag(stage))
    return spot


def order_matrix(width, stages, blk_count):
    count = lax.axis_size("page") * blk_count
    piece = width // count
    place = jnp.arange(width, dtype=jnp.int32)
    spot, inside = place // piece, place % piece
    block = jnp.zeros_like(spot)
    for depth, stage in enumerate(stages):
        axis, bit = stage
        shift = bit * blk_count if axis == "page" else bit
        value = ((spot >> (len(stages) - 1 - depth)) & 1) ^ stage_flag(stage)
        block = block + value * shift
    column = block * piece + inside
    return (column[:, None] == jnp.arange(width, dtype=jnp.int32)[None, :]).astype(BF16)


def halve(keep, send, stages):
    total = keep.astype(F32) + swap(send, stages[0]).astype(F32)
    for stage in stages[1:]:
        half = total.shape[0] // 2
        received = swap(total[half:].astype(BF16), stage)
        total = total[:half] + received.astype(F32)
    return total


def halve_lanes(total, stages):
    for stage in stages:
        half = total.shape[1] // 2
        total = total[:, :half] + swap(total[:, half:], stage)
    return total


def per_device(
    tokens,
    patch_count,
    reading_rank,
    boxes,
    text_kernel,
    patch_kernel,
    qkv_weight,
    rank_table,
    box_tables,
    out_weight,
    norm_gains,
    norm_shifts,
    up_weight,
    up_bias,
    down_weight,
    down_bias,
    cotangent,
):
    side = lax.axis_index("blk")
    blk_count = lax.axis_size("blk")
    page_stages = [("page", 1 << n) for n in range(lax.axis_size("page").bit_length() - 1)]
    across = ("blk", 1)
    first_x = page_stages[:1] + [across] + page_stages[1:]
    then_x = page_stages[:2] + [across] + page_stages[2:]
    last_x = page_stages + [across]
    count = patch_count[0]
    ranks = reading_rank[0]
    own = tokens[0]
    local, width = own.shape
    deep = up_bias.shape[0]
    seq = ranks.shape[0]
    heads = HEADS // blk_count
    scalars = jnp.stack(
        [side, TEXT + count, (count == GRID_HI * GRID_HI).astype(jnp.int32), jnp.int32(0)]
    ).astype(jnp.int32)
    other = swap(own, across)

    xy, xyt = onehots(ranks, boxes[:, 0])
    box_spread = np.arange(2 * SPAN) - (SPAN - 1)
    box_rows = jnp.asarray(bucket_rows(box_spread, box_marks, NB2))
    box_turned = jnp.asarray(bucket_rows(-box_spread, box_marks, NB2))
    rank_rows = jnp.asarray(bucket_rows(np.arange(RANK_LANES) - (RANK_MID - 1), rank_marks, NB1))
    rank_shifted = jnp.asarray(bucket_rows(np.arange(RANK_LANES) - RANK_MID, rank_marks, NB1))
    own_rank = lax.dynamic_slice_in_dim(rank_table, side * heads, heads, 0)
    own_box = lax.dynamic_slice_in_dim(box_tables, side * heads, heads, 1)
    rank_vector = dot_nt(own_rank, rank_shifted.astype(BF16))
    box_vector = lax.dot_general(
        own_box, box_turned.astype(BF16), (((2,), (1,)), ((), ())), preferred_element_type=F32
    )
    box_vector = jnp.pad(jnp.swapaxes(box_vector, 0, 1), ((0, 0), (0, 5), (0, RANK_LANES - 2 * SPAN)))
    vectors = jnp.concatenate([rank_vector[:, None, :], box_vector], axis=1)

    mixed, mixed_low, packed = mix_and_project(
        scalars, ranks, own, other, text_kernel, patch_kernel, qkv_weight
    )
    shares, own_context, their_context = attend(scalars, ranks, packed, xy, vectors, local)
    received = swap(their_context, across)
    context = jnp.where(
        side == 0,
        jnp.concatenate([own_context, received], axis=1),
        jnp.concatenate([received, own_context], axis=1),
    )

    places = side * local + jnp.arange(local, dtype=jnp.int32)
    row_alive = (places < TEXT + count).astype(F32)
    resid_one = mixed + dot_nn(context, out_weight)
    hidden_one, normed_one, inv_one = layer_norm(resid_one, norm_gains[0], norm_shifts[0])
    hidden_low = hidden_one.astype(BF16)
    pre_act = dot_nn(hidden_low, up_weight) + up_bias
    act_low = gelu(pre_act).astype(BF16)
    resid_two = hidden_one + dot_nn(act_low, down_weight) + down_bias
    result, normed_two, inv_two = layer_norm(resid_two, norm_gains[1], norm_shifts[1])
    layer_output = (result * row_alive[:, None]).astype(BF16)
    out_grad = cotangent[0].astype(F32) * row_alive[:, None]
    gain_two = jnp.sum(out_grad * normed_two, axis=0)
    shift_two = jnp.sum(out_grad, axis=0)
    resid_two_grad = norm_back(out_grad, normed_two, inv_two, norm_gains[1])
    down_bias_grad = jnp.sum(resid_two_grad, axis=0)
    branch_grad = resid_two_grad.astype(BF16)
    pre_grad = (dot_nt(branch_grad, down_weight) * gelu_slope(pre_act)).astype(BF16)
    up_bias_grad = jnp.sum(pre_grad.astype(F32), axis=0)
    hidden_grad = resid_two_grad + dot_nt(pre_grad, up_weight)
    gain_one = jnp.sum(hidden_grad * normed_one, axis=0)
    shift_one = jnp.sum(hidden_grad, axis=0)
    resid_one_grad = norm_back(hidden_grad, normed_one, inv_one, norm_gains[0])
    attend_grad = resid_one_grad.astype(BF16)
    context_grad = dot_nt(attend_grad, out_weight).astype(BF16)
    part = width // blk_count
    own_part = lax.dynamic_slice_in_dim(context_grad, side * part, part, 1)
    their_part = lax.dynamic_slice_in_dim(context_grad, (1 - side) * part, part, 1)
    received_part = swap(their_part, across)

    order_up = order_matrix(width, first_x, blk_count)
    order_qkv = order_matrix(width, last_x, blk_count)
    devices = lax.axis_size("page") * blk_count
    piece = deep // devices
    blocks = jnp.arange(devices, dtype=jnp.int32)
    spots = spot_of(blocks, then_x, blk_count) * piece
    act_rows = act_low
    if piece % 16:
        place = jnp.arange(deep, dtype=jnp.int32)
        target = spots[place // piece] + place % piece
        act_rows = jnp.zeros_like(act_low).at[:, target].set(act_low, unique_indices=True)
        piece = width // 8
        spots = jnp.arange(deep // piece, dtype=jnp.int32) * piece
    down_sum = halve(*down_weight_grad(spots, act_rows, branch_grad, piece), then_x)
    up_sum = halve(
        *up_weight_grad(order_up, hidden_low, context, pre_grad, attend_grad), first_x
    )

    dq, dk, dv, sums = attend_back(scalars, ranks, own_part, received_part, shares, packed, xy, xyt)
    qkv_keep, qkv_send = project_weight_grad(order_qkv, mixed_low, dq, dk, dv)
    qkv_part = halve(qkv_keep, qkv_send, page_stages)
    grad, outgoing, taps, cells = mixed_back(
        scalars, ranks, dq, dk, dv, qkv_weight, resid_one_grad, own, other
    )
    incoming = swap(outgoing, across)
    token_grad = token_back(scalars, grad, incoming, text_kernel, patch_kernel, seq)
    half = qkv_part.shape[0] // 2
    qkv_low = qkv_part.astype(BF16)
    received_qkv = swap(qkv_low[half:], across).astype(F32)
    kept_qkv = qkv_part[:half]
    low_side = jnp.where(side == 0, kept_qkv, received_qkv)
    high_side = jnp.where(side == 0, received_qkv, kept_qkv)
    pieces = []
    for block in range(3):
        cols = slice(block * part, (block + 1) * part)
        pieces += [low_side[:, cols], high_side[:, cols]]
    qkv_weight_grad = jnp.concatenate(pieces, axis=1)

    small = jnp.concatenate(
        [
            taps[:9],
            cells[:9],
            jnp.stack([gain_one, gain_two, shift_one, shift_two, down_bias_grad]),
            up_bias_grad.reshape(width, deep // width).T,
        ],
        axis=0,
    )
    small = jnp.pad(small, ((0, -small.shape[0] % 8), (0, 0)))
    small = lax.dot_general(
        small, order_up.astype(F32), (((1,), (1,)), ((), ())),
        precision=lax.Precision.HIGHEST, preferred_element_type=F32,
    )
    small = halve_lanes(small, first_x)
    rank_part = jnp.dot(sums[:, 0], rank_rows, precision=lax.Precision.HIGHEST)
    box_part = lax.dot_general(
        sums[:, 1:3, : 2 * SPAN], box_rows, (((2,), (0,)), ((), ())), precision=lax.Precision.HIGHEST
    )
    tables = jnp.concatenate([rank_part, box_part[:, 0], box_part[:, 1]], axis=1)
    for stage in page_stages:
        tables = tables + swap(tables, stage)
    their_tables = swap(tables, across)
    tables = jnp.where(
        side == 0,
        jnp.concatenate([tables, their_tables], axis=0),
        jnp.concatenate([their_tables, tables], axis=0),
    )
    box_tables_grad = jnp.stack([tables[:, NB1 : NB1 + NB2], tables[:, NB1 + NB2 :]])
    return (
        layer_output[None],
        token_grad[None],
        small[:9],
        small[9:18],
        qkv_weight_grad,
        tables[:, :NB1],
        box_tables_grad,
        up_sum[:, deep:],
        small[18:20],
        small[20:22],
        up_sum[:, :deep],
        small[23 : 23 + deep // width].T.reshape(-1),
        down_sum,
        small[22],
    )


def solution(mesh):
    in_specs = (
        P("page", "blk", None),
        P("page"),
        P("page", None),
        P(None, "page", None),
        P(),
        P(),
        P(),
        P(),
        P(),
        P(),
        P(),
        P(),
        P(),
        P(),
        P(),
        P(),
        P("page", "blk", None),
    )
    out_specs = (
        P("page", "blk", None),
        P("page", "blk", None),
        P(None, ("page", "blk")),
        P(None, ("page", "blk")),
        P(("page", "blk"), None),
        P(),
        P(),
        P(("page", "blk"), None),
        P(None, ("page", "blk")),
        P(None, ("page", "blk")),
        P(("page", "blk"), None),
        P(("page", "blk")),
        P(("page", "blk"), None),
        P(("page", "blk")),
    )
    return jax.shard_map(
        per_device, mesh=mesh, in_specs=in_specs, out_specs=out_specs, check_vma=False
    )
```

```python
import functools

import jax
import jax.numpy as jnp
import numpy as np
from jax import lax
from jax.experimental import pallas as pl
from jax.experimental.pallas import tpu as pltpu
from jax.sharding import PartitionSpec as P

TEXT = 512
GRID_LO = 7
GRID_HI = 14
RUN = 16
HEADS = 12
HEAD_DIM = 64
NB1 = 32
NB2 = 64
SPAN = 256
RANK_LANES = 1536
RANK_MID = RANK_LANES // 2
ROWS = 128
F32 = jnp.float32
BF16 = jnp.bfloat16
MIB = 1 << 20

rank_marks = (1, 2, 3, 4, 5, 6, 7, 8, 12, 16, 23, 32, 46, 64, 91)
box_marks = tuple(range(1, 17)) + (19, 23, 27, 32, 39, 46, 54, 64, 77, 91, 108, 128, 153, 182, 216)
neg_fill = -1000000000.0
norm_eps = 1e-05
root_half = 0.7071067811865476
inv_root_tau = 0.3989422804014327
tap_list = ((1, -1), (1, 0), (1, 1), (2, -1), (2, 0), (2, 1), (3, -1), (3, 0), (3, 1))
cell_list = ((-1, -1), (-1, 0), (-1, 1), (0, -1), (0, 0), (0, 1), (1, -1), (1, 0), (1, 1))


def bucket_rows(deltas, marks, bins):
    spread = np.abs(deltas)
    ids = np.sum(spread[:, None] >= np.asarray(marks)[None, :], axis=1) + (bins // 2) * (deltas > 0)
    return (ids[:, None] == np.arange(bins)[None, :]).astype(np.float32)


def dot_nn(left, right):
    return lax.dot_general(left, right, (((1,), (0,)), ((), ())), preferred_element_type=F32)


def dot_nt(left, right):
    return lax.dot_general(left, right, (((1,), (1,)), ((), ())), preferred_element_type=F32)


def dot_tn(left, right):
    return lax.dot_general(left, right, (((0,), (0,)), ((), ())), preferred_element_type=F32)


def row_chunks(total, size):
    return [(start, min(size, total - start)) for start in range(0, total, size)]


def vmem():
    return pl.BlockSpec(memory_space=pltpu.VMEM)


def smem():
    return pl.BlockSpec(memory_space=pltpu.SMEM)


def anywhere():
    return pl.BlockSpec(memory_space=pl.ANY)


def fetch(sources, targets, semaphores):
    copies = []
    for number, (source, target) in enumerate(zip(sources, targets)):
        copies.append(pltpu.make_async_copy(source, target, semaphores.at[number]))
        copies[-1].start()
    return copies


def params(mib):
    return pltpu.CompilerParams(vmem_limit_bytes=mib * MIB)


def onehot_kernel(
    scalars, rank_ref, box_ref, rank_table, box_tables, rank_rows, box_rows, xy_ref, xyt_ref, vectors
):
    seq = rank_ref.shape[1]
    for start, size in row_chunks(seq, 240):
        spot = lax.broadcasted_iota(jnp.int32, (size, seq), 0) + start
        order = (spot == rank_ref[...]).astype(F32).astype(BF16)
        for half in range(2):
            level = lax.broadcasted_iota(jnp.int32, (SPAN, seq), 0)
            marks = (level == box_ref[half]).astype(F32).astype(BF16)
            xy_ref[start : start + size, half * SPAN : (half + 1) * SPAN] = dot_nt(
                order, marks
            ).astype(BF16)
    row = lax.broadcasted_iota(jnp.int32, (SPAN, SPAN), 0)
    col = lax.broadcasted_iota(jnp.int32, (SPAN, SPAN), 1)
    flip = (row + col == SPAN - 1).astype(F32).astype(BF16)
    for half in range(2):
        part = slice(half * SPAN, (half + 1) * SPAN)
        xyt_ref[part, :] = dot_nt(flip, xy_ref[:, part]).astype(BF16)
    heads = vectors.shape[0]
    tables = [(dot_nt(rank_table[...], rank_rows[...]), RANK_LANES)]
    tables += [(dot_nt(box_tables[half], box_rows[...]), 2 * SPAN) for half in range(2)]
    for place, (table, lanes) in enumerate(tables):
        own = jnp.where(scalars[0] == 0, table[:heads], table[table.shape[0] - heads :])
        for head in range(heads):
            vectors[head, place : place + 1, :lanes] = own[head : head + 1]


def onehots(scalars, ranks, boxes, rank_table, box_tables, heads):
    seq = ranks.shape[1]
    rank_rows = jnp.asarray(bucket_rows(np.arange(RANK_LANES) - RANK_MID, rank_marks, NB1), BF16)
    box_rows = jnp.asarray(bucket_rows(SPAN - 1 - np.arange(2 * SPAN), box_marks, NB2), BF16)
    return pl.pallas_call(
        onehot_kernel,
        out_shape=(
            jax.ShapeDtypeStruct((seq, 2 * SPAN), BF16),
            jax.ShapeDtypeStruct((2 * SPAN, seq), BF16),
            jax.ShapeDtypeStruct((heads, 8, RANK_LANES), F32),
        ),
        in_specs=[smem()] + [vmem()] * 6,
        out_specs=(vmem(),) * 3,
        compiler_params=params(12),
        cost_estimate=pl.CostEstimate(
            flops=4 * seq * seq * SPAN, bytes_accessed=4 * seq * 2 * SPAN, transcendentals=0
        ),
        name="onehots",
    )(scalars, ranks, boxes, rank_table, box_tables, rank_rows, box_rows)


def place_slots(own_ref, other_ref, side, text, patch, patch_pad):
    local = own_ref.shape[0]
    head = TEXT - local
    groups = text.shape[0]

    def place(low_ref, high_ref):
        for lane in range(groups):
            cols = slice(128 * lane, 128 * lane + 128)
            text[lane, 8 : 8 + local, :] = low_ref[:, cols].astype(F32)
            high = high_ref[:, cols].astype(F32)
            text[lane, 8 + local : 8 + TEXT, :] = high[:head]
            patch[lane, patch_pad : patch_pad + local - head, :] = high[head:]

    pl.when(side == 0)(lambda: place(own_ref, other_ref))
    pl.when(side != 0)(lambda: place(other_ref, own_ref))


def clear_pads(text, patch, patch_pad):
    groups, rows = patch.shape[0], patch.shape[1]
    for lane in range(groups):
        text[lane, 0:8, :] = jnp.zeros((8, 128), F32)
        text[lane, 8 + TEXT : 16 + TEXT, :] = jnp.zeros((8, 128), F32)
        patch[lane, 0:patch_pad, :] = jnp.zeros((patch_pad, 128), F32)
        patch[lane, rows - patch_pad : rows, :] = jnp.zeros((patch_pad, 128), F32)


def cell_masks(grid, rows):
    slot = lax.broadcasted_iota(jnp.int32, (rows, 128), 0)
    row_of = jnp.zeros((rows, 128), jnp.int32)
    for line in range(1, grid):
        row_of = row_of + (slot >= line * grid).astype(jnp.int32)
    column = slot - row_of * grid
    alive = slot < grid * grid
    masks = []
    for down, across in cell_list:
        masks.append(
            alive
            & (row_of + down >= 0)
            & (row_of + down < grid)
            & (column + across >= 0)
            & (column + across < grid)
        )
    return masks


def store_masks(masks, fine, rows):
    for grid, chosen in ((GRID_HI, fine != 0), (GRID_LO, fine == 0)):

        def fill(grid=grid):
            for number, mask in enumerate(cell_masks(grid, rows)):
                masks[number] = mask.astype(F32)

        pl.when(chosen)(fill)


def mix_lane(text, patch, masks, out, lane, text_kernel, patch_kernel, fine, patch_pad, flip):
    cols = pl.ds(pl.multiple_of(lane * 128, 128), 128)
    taps = {}
    for number, (reach, side) in enumerate(tap_list):
        offset = -reach * side if flip else reach * side
        value = text_kernel[number : number + 1, cols]
        taps[offset] = taps[offset] + value if offset in taps else value
    for start, size in row_chunks(TEXT, ROWS):
        total = text[lane, pl.ds(8 + start, size), :] * (1.0 + taps[0])
        for offset, value in taps.items():
            if offset:
                total = total + text[lane, pl.ds(8 + start + offset, size), :] * value
        out[lane, pl.ds(start, size), :] = total
    rows = masks.shape[1]
    for grid, chosen in ((GRID_HI, fine != 0), (GRID_LO, fine == 0)):

        def cells(grid=grid):
            for start, size in row_chunks(rows, 104):
                total = patch[lane, pl.ds(patch_pad + start, size), :]
                for number, (down, across) in enumerate(cell_list):
                    tap = len(cell_list) - 1 - number if flip else number
                    moved = patch[lane, pl.ds(patch_pad + start + down * grid + across, size), :]
                    total = total + (
                        moved * masks[number, pl.ds(start, size), :]
                    ) * patch_kernel[tap : tap + 1, cols]
                out[lane, pl.ds(TEXT + start, size), :] = total

        pl.when(chosen)(cells)


def sort_rows(ranks_ref, source, target, seq, cast):
    for run in range(TEXT // RUN):
        spot = pl.multiple_of(ranks_ref[0, run * RUN], RUN)
        target[pl.ds(spot, RUN), :] = source[run * RUN : (run + 1) * RUN, :].astype(cast)
    target[TEXT:seq, :] = source[TEXT:seq, :].astype(cast)


def unsort_rows(ranks_ref, source, target, seq):
    for run in range(TEXT // RUN):
        spot = pl.multiple_of(ranks_ref[0, run * RUN], RUN)
        target[run * RUN : (run + 1) * RUN, :] = source[pl.ds(spot, RUN), :]
    target[TEXT:seq, :] = source[TEXT:seq, :]


def mix_kernel(
    scalars, ranks_ref, own_ref, other_ref, text_kernel, patch_kernel, weight_ref,
    mixed_ref, low_ref, packed_ref, text, patch, masks, lanes, whole, weights, copies,
):
    side, fine = scalars[0], scalars[2]
    local, width = own_ref.shape
    seq = low_ref.shape[0]
    groups = width // 128
    pad = GRID_HI + 2
    part = width // 2
    fetches = fetch(
        [
            weight_ref.at[:, pl.ds(pl.multiple_of(block * width + side * part, 128), part)]
            for block in range(3)
        ],
        [weights.at[block] for block in range(3)],
        copies,
    )
    place_slots(own_ref, other_ref, side, text, patch, pad)
    clear_pads(text, patch, pad)
    store_masks(masks, fine, seq - TEXT)

    def one_lane(lane, carry):
        mix_lane(text, patch, masks, lanes, lane, text_kernel, patch_kernel, fine, pad, False)
        return carry

    lax.fori_loop(0, groups, one_lane, 0)
    for lane in range(groups):
        whole[:, 128 * lane : 128 * lane + 128] = lanes[lane]
    mixed_ref[...] = whole[pl.ds(pl.multiple_of(side * local, 8), local), :]
    sort_rows(ranks_ref, whole, low_ref, seq, BF16)
    for block in range(3):
        fetches[block].wait()
        for start, size in row_chunks(seq, 240):
            value = dot_nn(low_ref[start : start + size, :], weights[block]).astype(BF16)
            if block == 0:
                value = value * (HEAD_DIM**-0.5)
            packed_ref[start : start + size, block * part : (block + 1) * part] = value


def mix_and_project(scalars, ranks, own, other, text_kernel, patch_kernel, qkv_weight):
    local, width = own.shape
    seq = ranks.shape[1]
    groups = width // 128
    return pl.pallas_call(
        mix_kernel,
        out_shape=(
            jax.ShapeDtypeStruct((local, width), F32),
            jax.ShapeDtypeStruct((seq, width), BF16),
            jax.ShapeDtypeStruct((seq, 3 * width // 2), BF16),
        ),
        in_specs=[smem(), smem()] + [vmem()] * 4 + [anywhere()],
        out_specs=(vmem(),) * 3,
        scratch_shapes=[
            pltpu.VMEM((groups, TEXT + 16, 128), F32),
            pltpu.VMEM((groups, seq - TEXT + 2 * (GRID_HI + 2), 128), F32),
            pltpu.VMEM((9, seq - TEXT, 128), F32),
            pltpu.VMEM((groups, seq, 128), F32),
            pltpu.VMEM((seq, width), F32),
            pltpu.VMEM((3, width, width // 2), BF16),
            pltpu.SemaphoreType.DMA((3,)),
        ],
        compiler_params=params(16),
        cost_estimate=pl.CostEstimate(
            flops=2 * seq * width * 3 * width // 2, bytes_accessed=12 * MIB, transcendentals=0
        ),
        name="mix_and_project",
    )(scalars, ranks, own, other, text_kernel, patch_kernel, qkv_weight)


def head_lanes(shape, parity):
    return (lax.broadcasted_iota(jnp.int32, shape, 1) >= HEAD_DIM) == (parity != 0)


def skewed(vector, rows, lanes, shift):
    return pltpu.roll(jnp.broadcast_to(vector, (rows, lanes)), shift, 1, stride=1, stride_axis=0)


def attend_kernel(
    scalars, ranks_ref, queries, keys, values, xy_ref, vectors,
    shares_ref, own_ref, other_ref, left, right, rank_bias, gathered, slots, scores_ref,
):
    side, live = scalars[0], scalars[1]
    seq = queries.shape[0]
    local = own_ref.shape[0]
    head = pl.program_id(0)
    parity = lax.rem(head, 2)

    @pl.when(head == 0)
    def _():
        left[:, 128:] = xy_ref[...]

    left[:, :128] = queries[...]
    mine = head_lanes((seq, 128), parity)
    right[:, :128] = jnp.where(mine, keys[...], jnp.zeros((), BF16))
    for half in range(2):
        table = skewed(vectors[0, half + 1 : half + 2, : 2 * SPAN], SPAN, 2 * SPAN, SPAN + 1)
        table = table[:, :SPAN].astype(BF16)
        right[:, 128 + half * SPAN : 128 + (half + 1) * SPAN] = dot_nn(
            xy_ref[:, half * SPAN : (half + 1) * SPAN], table
        ).astype(BF16)
    rank_bias[...] = skewed(vectors[0, 0:1, :], ROWS, RANK_LANES, RANK_LANES - 128)
    top = (seq // ROWS) * ROWS
    alive = lax.broadcasted_iota(jnp.int32, (16, seq), 1) < live
    chunks = row_chunks(seq, 240)

    def product(start, size):
        scores_ref[start : start + size, :] = dot_nt(left[start : start + size, :], right[...])

    def soften(start, size):
        for first in range(start, start + size, 16):
            base = first // ROWS * ROWS
            scores = scores_ref[first : first + 16, :]
            scores = scores + rank_bias[first - base : first - base + 16, top - base : top - base + seq]
            scores = jnp.where(alive, scores, neg_fill)
            powered = jnp.exp(scores - jnp.max(scores, axis=1, keepdims=True))
            shares = powered * (1.0 / jnp.sum(powered, axis=1, keepdims=True))
            shares_ref[0, first : first + 16, :] = shares.astype(BF16)

    def apply(start, size):
        context = dot_nn(shares_ref[0, start : start + size, :], values[...])
        gathered[start : start + size, :] = jnp.where(
            head_lanes((size, 128), parity), context, gathered[start : start + size, :]
        )

    product(*chunks[0])
    for n in range(len(chunks)):
        if n + 1 < len(chunks):
            product(*chunks[n + 1])
        if n:
            apply(*chunks[n - 1])
        soften(*chunks[n])
    apply(*chunks[-1])

    @pl.when(parity == 1)
    def _():
        unsort_rows(ranks_ref, gathered, slots, seq)
        own_ref[...] = slots[pl.ds(pl.multiple_of(side * local, 8), local), :].astype(BF16)
        other_ref[...] = slots[pl.ds(pl.multiple_of((1 - side) * local, 8), local), :].astype(BF16)


def attend(scalars, ranks, packed, xy, vectors, local, first, count):
    seq = packed.shape[0]
    pairs = vectors.shape[0] // 2
    heads = 2 * count
    width = heads * HEAD_DIM
    whole = pl.BlockSpec((seq, 2 * SPAN), lambda h: (0, 0))
    slot_spec = pl.BlockSpec((local, 128), lambda h: (0, h // 2))
    return pl.pallas_call(
        attend_kernel,
        grid=(heads,),
        out_shape=(
            jax.ShapeDtypeStruct((heads, seq, seq), BF16),
            jax.ShapeDtypeStruct((local, width), BF16),
            jax.ShapeDtypeStruct((local, width), BF16),
        ),
        in_specs=[
            smem(),
            smem(),
            pl.BlockSpec((seq, 128), lambda h: (0, first + h // 2)),
            pl.BlockSpec((seq, 128), lambda h: (0, pairs + first + h // 2)),
            pl.BlockSpec((seq, 128), lambda h: (0, 2 * pairs + first + h // 2)),
            whole,
            pl.BlockSpec((1, 8, RANK_LANES), lambda h: (2 * first + h, 0, 0)),
        ],
        out_specs=(pl.BlockSpec((1, seq, seq), lambda h: (h, 0, 0)), slot_spec, slot_spec),
        scratch_shapes=[
            pltpu.VMEM((seq, 128 + 2 * SPAN), BF16),
            pltpu.VMEM((seq, 128 + 2 * SPAN), BF16),
            pltpu.VMEM((ROWS, RANK_LANES), F32),
            pltpu.VMEM((seq, 128), F32),
            pltpu.VMEM((seq, 128), F32),
            pltpu.VMEM((seq, seq), F32),
        ],
        compiler_params=params(13),
        cost_estimate=pl.CostEstimate(
            flops=heads * 2 * seq * seq * 1024, bytes_accessed=heads * seq * seq * 2,
            transcendentals=heads * seq * seq,
        ),
        name="attend",
    )(scalars, ranks, packed, packed, packed, xy, vectors)


def attend_back_kernel(
    ranks_ref, own_ref, other_ref, side_ref, shares_ref, queries, keys, values, xy_ref, xyt_ref,
    dq_ref, dk_ref, dv_ref, sums_ref, right, score_grad, spread, rank_sum, slots, upstream, share_grads,
):
    seq = queries.shape[0]
    local = own_ref.shape[0]
    side = side_ref[0]
    head = pl.program_id(0)
    parity = lax.rem(head, 2)
    scale = HEAD_DIM**-0.5

    @pl.when(head == 0)
    def _():
        right[:, 128:] = xy_ref[...]

    @pl.when(parity == 0)
    def _():
        slots[pl.ds(pl.multiple_of(side * local, 8), local), :] = own_ref[...].astype(F32)
        slots[pl.ds(pl.multiple_of((1 - side) * local, 8), local), :] = other_ref[...].astype(F32)
        sort_rows(ranks_ref, slots, upstream, seq, BF16)

    right[:, :128] = keys[...]
    mine = head_lanes((seq, 128), parity)
    own_values = jnp.where(mine, values[...], jnp.zeros((), BF16))
    rank_sum[...] = jnp.zeros(rank_sum.shape, F32)
    top = (seq // ROWS) * ROWS
    chunks = row_chunks(seq, 240)

    def product(start, size):
        share_grads[start : start + size, :] = dot_nt(upstream[start : start + size, :], own_values)

    def soften(start, size):
        for first in range(start, start + size, 16):
            base = first // ROWS * ROWS
            rows = slice(first, first + 16)
            shares = shares_ref[0, rows, :].astype(F32)
            weighted = shares * share_grads[rows, :]
            low = (weighted - shares * jnp.sum(weighted, axis=1, keepdims=True)).astype(BF16)
            score_grad[rows, :] = low
            place = (slice(first - base, first - base + 16), slice(top - base, top - base + seq))
            rank_sum[place] = rank_sum[place] + low.astype(F32)

    def apply(start, size):
        rows = slice(start, start + size)
        product = dot_nn(score_grad[rows, :], right[...])
        spread[rows, :] = product[:, 128:].astype(BF16)
        dq_ref[rows, :] = jnp.where(
            head_lanes((size, 128), parity), (product[:, :128] * scale).astype(BF16), dq_ref[rows, :]
        )

    product(*chunks[0])
    for n in range(len(chunks)):
        if n + 1 < len(chunks):
            product(*chunks[n + 1])
        if n:
            apply(*chunks[n - 1])
        soften(*chunks[n])
    apply(*chunks[-1])
    dk = dot_tn(score_grad[...], queries[...]).astype(BF16)
    dk_ref[...] = jnp.where(mine, dk, dk_ref[...])
    dv = dot_tn(shares_ref[0], upstream[...]).astype(BF16)
    dv_ref[...] = jnp.where(mine, dv, dv_ref[...])
    row = lax.broadcasted_iota(jnp.int32, (ROWS, ROWS), 0)
    col = lax.broadcasted_iota(jnp.int32, (ROWS, ROWS), 1)
    flip = (row + col == ROWS - 1).astype(F32).astype(BF16)
    high = rank_sum[...].astype(BF16)
    rest = (rank_sum[...] - high.astype(F32)).astype(BF16)
    turned = dot_nn(flip, high) + dot_nn(flip, rest)
    turned = pltpu.roll(turned, 0, 1, stride=1, stride_axis=0)
    sums_ref[0, 0:1, :] = jnp.sum(turned, axis=0, keepdims=True)
    for half in range(2):
        part = slice(half * SPAN, (half + 1) * SPAN)
        table = dot_nn(xyt_ref[part, :], spread[:, part])
        table = jnp.concatenate([table, jnp.zeros((SPAN, SPAN), F32)], axis=1)
        table = pltpu.roll(table, 0, 1, stride=1, stride_axis=0)
        sums_ref[0, half + 1 : half + 2, : 2 * SPAN] = jnp.sum(table, axis=0, keepdims=True)


def attend_back(scalars, ranks, own, other, shares, packed, xy, xyt, pair, place, so_far, marker):
    seq = packed.shape[0]
    local = own.shape[0]
    width = packed.shape[1] // 3
    pairs = width // 128
    slot_spec = pl.BlockSpec((local, 128), lambda h: (0, pair))
    out_spec = pl.BlockSpec((seq, 128), lambda h: (0, pair))
    so_far = tuple(so_far) if so_far else ()
    extra = so_far + ((marker,) if marker is not None else ())

    def body(*refs):
        ins, rest = refs[:10], refs[10 + len(extra) :]
        attend_back_kernel(*ins, *rest)

    return pl.pallas_call(
        body,
        grid=(2,),
        out_shape=(jax.ShapeDtypeStruct((seq, width), BF16),) * 3
        + (jax.ShapeDtypeStruct((2, 8, RANK_LANES), F32),),
        in_specs=[
            smem(),
            slot_spec,
            slot_spec,
            smem(),
            pl.BlockSpec((1, seq, seq), lambda h: (2 * place + h, 0, 0)),
            pl.BlockSpec((seq, 128), lambda h: (0, pair)),
            pl.BlockSpec((seq, 128), lambda h: (0, pairs + pair)),
            pl.BlockSpec((seq, 128), lambda h: (0, 2 * pairs + pair)),
            pl.BlockSpec((seq, 2 * SPAN), lambda h: (0, 0)),
            pl.BlockSpec((2 * SPAN, seq), lambda h: (0, 0)),
        ]
        + [anywhere()] * len(extra),
        out_specs=(out_spec,) * 3 + (pl.BlockSpec((1, 8, RANK_LANES), lambda h: (h, 0, 0)),),
        scratch_shapes=[
            pltpu.VMEM((seq, 128 + 2 * SPAN), BF16),
            pltpu.VMEM((seq, seq), BF16),
            pltpu.VMEM((seq, 2 * SPAN), BF16),
            pltpu.VMEM((ROWS, RANK_LANES), F32),
            pltpu.VMEM((seq, 128), F32),
            pltpu.VMEM((seq, 128), BF16),
            pltpu.VMEM((seq, seq), F32),
        ],
        input_output_aliases={10 + n: n for n in range(len(so_far))},
        compiler_params=params(15),
        cost_estimate=pl.CostEstimate(flops=1000, bytes_accessed=1000, transcendentals=0),
        name="attend_back",
    )(ranks, own, other, scalars, shares, packed, packed, packed, xy, xyt, *extra)


def fold_rows(value):
    total = value[0:8]
    for start in range(8, value.shape[0], 8):
        total = total + value[start : start + 8]
    return total


def row_mean(value):
    return jnp.sum(value, axis=1, keepdims=True) * (1.0 / value.shape[1])


def normalize(value):
    center = value - row_mean(value)
    inverse = lax.rsqrt(row_mean(center * center) + norm_eps)
    return center * inverse, inverse


def dense_kernel(
    scalars, mixed_ref, own_a, own_b, other_a, other_b, pack, cot_ref, out_hbm, up_hbm, down_hbm,
    result_ref, context_ref, hidden_ref, act_ref, branch_ref, pre_ref, attend_ref, resid_ref,
    own_grad, other_grad, sums_ref, blocks_ref,
    out_w, up_w, down_w, slope, product, stash, hidden, normed, scale, bias_sums_ref, copies,
):
    side, live = scalars[0], scalars[1]
    local, width = mixed_ref.shape
    deep = act_ref.shape[1]
    part = own_grad.shape[1]
    step = width // 2
    blocks = deep // step
    gains, shifts, down_bias = pack.at[0:2], pack.at[2:4], pack.at[4:5]
    fetches = [pltpu.make_async_copy(out_hbm, out_w, copies.at[0])]
    fetches += [
        pltpu.make_async_copy(
            up_hbm.at[:, n * width : (n + 1) * width], up_w.at[:, n * width : (n + 1) * width],
            copies.at[1 + n],
        )
        for n in range(deep // width)
    ]
    fetches.append(pltpu.make_async_copy(down_hbm, down_w, copies.at[1 + deep // width]))
    for fetch in fetches:
        fetch.start()
    wide = own_a.shape[1]
    for base, (first, second) in ((side * part, (own_a, own_b)), ((1 - side) * part, (other_a, other_b))):
        context_ref[:, pl.ds(pl.multiple_of(base, 128), wide)] = first[...]
        context_ref[:, pl.ds(pl.multiple_of(base + wide, 128), part - wide)] = second[...]
    chunks = row_chunks(local, 24)
    fetches[0].wait()
    product[...] = dot_nn(context_ref[...], out_w[...])
    for start, size in chunks:
        rows = slice(start, start + size)
        value, inverse = normalize(mixed_ref[rows, :] + product[rows, :])
        normed[rows, :] = value
        scale[rows, :] = jnp.broadcast_to(inverse, (size, 128))
        value = value * gains[0:1, :] + shifts[0:1, :]
        hidden[rows, :] = value
        hidden_ref[rows, :] = value.astype(BF16)

    def lift(block):
        if block % 2 == 0:
            fetches[1 + block // 2].wait()
        cols = slice(block * step, (block + 1) * step)
        stash[block % 2] = dot_nn(hidden_ref[...], up_w[:, cols])

    def bend(block):
        cols = slice(block * step, (block + 1) * step)
        half_cols = slice(block % 2 * step, (block % 2 + 1) * step)
        for start, size in chunks:
            rows = slice(start, start + size)
            value = stash[block % 2, rows, :] + pack[5 + block // 2 : 6 + block // 2, half_cols]
            half = 0.5 + 0.5 * lax.erf(value * root_half)
            act_ref[rows, cols] = (value * half).astype(BF16)
            slope[rows, cols] = half + value * jnp.exp(-0.5 * value * value) * inv_root_tau

    lift(0)
    for block in range(blocks):
        if block + 1 < blocks:
            lift(block + 1)
        bend(block)
    fetches[-1].wait()
    product[...] = dot_nn(act_ref[...], down_w[...])
    zero = jnp.zeros((8, width), F32)
    gain_sum, shift_sum, bias_sum = zero, zero, zero
    for start, size in chunks:
        rows = slice(start, start + size)
        value, inverse = normalize(hidden[rows, :] + product[rows, :] + down_bias[...])
        slot = lax.broadcasted_iota(jnp.int32, (size, width), 0) + (side * local + start)
        alive = (slot < live).astype(F32)
        result_ref[rows, :] = (alive * (value * gains[1:2, :] + shifts[1:2, :])).astype(BF16)
        upstream = cot_ref[rows, :].astype(F32) * alive
        gain_sum = gain_sum + fold_rows(upstream * value)
        shift_sum = shift_sum + fold_rows(upstream)
        scaled = upstream * gains[1:2, :]
        grad = inverse * (scaled - row_mean(scaled) - value * row_mean(scaled * value))
        bias_sum = bias_sum + fold_rows(grad)
        hidden[rows, :] = grad
        branch_ref[rows, :] = grad.astype(BF16)
    sums_ref[1:2, :] = jnp.sum(gain_sum, axis=0, keepdims=True)
    sums_ref[3:4, :] = jnp.sum(shift_sum, axis=0, keepdims=True)
    sums_ref[4:5, :] = jnp.sum(bias_sum, axis=0, keepdims=True)
    sums_ref[5:8, :] = jnp.zeros((3, width), F32)

    def lower(block):
        cols = slice(block * step, (block + 1) * step)
        stash[block % 2] = dot_nt(branch_ref[...], down_w[cols, :])

    def unbend(block):
        cols = slice(block * step, (block + 1) * step)
        total = jnp.zeros((8, step), F32)
        for start, size in chunks:
            rows = slice(start, start + size)
            value = (stash[block % 2, rows, :] * slope[rows, cols]).astype(BF16)
            pre_ref[rows, cols] = value
            total = total + fold_rows(value.astype(F32))
        bias_sums_ref[:, cols] = jnp.sum(total, axis=0, keepdims=True)

    lower(0)
    for block in range(blocks):
        if block + 1 < blocks:
            lower(block + 1)
        unbend(block)
    product[...] = dot_nt(pre_ref[...], up_w[...])
    piece = deep // blocks_ref.shape[0]
    blocks_ref[...] = jnp.zeros(blocks_ref.shape, F32)
    for block in range(blocks_ref.shape[0]):
        blocks_ref[block : block + 1, :piece] = bias_sums_ref[:, block * piece : (block + 1) * piece]
    gain_sum, shift_sum = zero, zero
    for start, size in chunks:
        rows = slice(start, start + size)
        upstream = hidden[rows, :] + product[rows, :]
        value = normed[rows, :]
        gain_sum = gain_sum + fold_rows(upstream * value)
        shift_sum = shift_sum + fold_rows(upstream)
        scaled = upstream * gains[0:1, :]
        inverse = jnp.concatenate([scale[rows, :]] * (width // 128), axis=1)
        grad = inverse * (scaled - row_mean(scaled) - value * row_mean(scaled * value))
        resid_ref[rows, :] = grad
        attend_ref[rows, :] = grad.astype(BF16)
    sums_ref[0:1, :] = jnp.sum(gain_sum, axis=0, keepdims=True)
    sums_ref[2:3, :] = jnp.sum(shift_sum, axis=0, keepdims=True)
    for base, ref in (((1 - side) * part, other_grad), (side * part, own_grad)):
        weight = out_w[pl.ds(pl.multiple_of(base, 128), part), :]
        ref[...] = dot_nt(attend_ref[...], weight).astype(BF16)


def dense(
    scalars, mixed, own_context, other_context, pack, cotangent, out_weight, up_weight, down_weight, devices,
):
    local, width = mixed.shape
    deep = up_weight.shape[1]
    part = width // 2
    low = lambda *shape: jax.ShapeDtypeStruct(shape, BF16)
    full = lambda *shape: jax.ShapeDtypeStruct(shape, F32)
    hbm = pl.BlockSpec(memory_space=pl.ANY)
    return pl.pallas_call(
        dense_kernel,
        out_shape=(
            low(local, width), low(local, width), low(local, width), low(local, deep),
            low(local, width), low(local, deep), low(local, width), full(local, width),
            low(local, part), low(local, part), full(8, width), full(devices, 128),
        ),
        in_specs=[smem()] + [vmem()] * 7 + [hbm] * 3,
        out_specs=(vmem(),) * 12,
        scratch_shapes=[
            pltpu.VMEM((width, width), BF16),
            pltpu.VMEM((width, deep), BF16),
            pltpu.VMEM((deep, width), BF16),
            pltpu.VMEM((local, deep), F32),
            pltpu.VMEM((local, width), F32),
            pltpu.VMEM((2, local, width // 2), F32),
            pltpu.VMEM((local, width), F32),
            pltpu.VMEM((local, width), F32),
            pltpu.VMEM((local, 128), F32),
            pltpu.VMEM((1, deep), F32),
            pltpu.SemaphoreType.DMA((2 + deep // width,)),
        ],
        compiler_params=params(23),
        cost_estimate=pl.CostEstimate(
            flops=2 * local * width * (4 * deep + 2 * width), bytes_accessed=20 * MIB,
            transcendentals=2 * local * deep,
        ),
        name="dense",
    )(
        scalars, mixed, *own_context, *other_context, pack, cotangent, out_weight, up_weight, down_weight,
    )


def project_back_kernel(
    order_hbm, low_hbm, dq_hbm, dk_hbm, dv_hbm, marker, keep_ref, send_ref, after_ref,
    order, low, grads, turned, copies,
):
    after_ref[...] = jnp.zeros(after_ref.shape, F32)
    half, part = keep_ref.shape[0], dq_hbm.shape[1]
    fetches = fetch(
        [order_hbm, low_hbm, dq_hbm, dk_hbm, dv_hbm],
        [order, low] + [grads.at[block] for block in range(3)],
        copies,
    )
    fetches[0].wait()
    fetches[1].wait()
    turned[...] = dot_nt(order[...], low[...]).astype(BF16)
    for block in range(3):
        fetches[2 + block].wait()
        cols = slice(block * part, (block + 1) * part)
        send_ref[:, cols] = dot_nn(turned[half:, :], grads[block]).astype(BF16)
        keep_ref[:, cols] = dot_nn(turned[:half, :], grads[block]).astype(BF16)


def project_weight_grad(order, low, dq, dk, dv, marker):
    seq, width = low.shape
    part = dq.shape[1]
    shape = jax.ShapeDtypeStruct((width // 2, 3 * part), BF16)
    return pl.pallas_call(
        project_back_kernel,
        out_shape=(shape, shape, jax.ShapeDtypeStruct((8, 128), F32)),
        in_specs=[anywhere()] * 6,
        out_specs=(vmem(), vmem(), vmem()),
        scratch_shapes=[
            pltpu.VMEM((width, width), BF16),
            pltpu.VMEM((seq, width), BF16),
            pltpu.VMEM((3, seq, part), BF16),
            pltpu.VMEM((width, seq), BF16),
            pltpu.SemaphoreType.DMA((5,)),
        ],
        compiler_params=params(14),
        cost_estimate=pl.CostEstimate(flops=1000, bytes_accessed=1000, transcendentals=0),
        name="project_weight_grad",
    )(order, low, dq, dk, dv, marker)


def deep_kernel(
    spots, act_ref, branch_ref, pre_ref, hidden_ref, context_ref, attend_ref, first_ref, second_ref,
    down_keep, down_send, out_keep, out_send, up_keep, up_send, turned, whole, *, piece, steps, split,
):
    width = branch_ref.shape[1]
    half = down_keep.shape[0]
    middle = width // 2

    def fill(keep_ref, send_ref, place, right):
        cols = slice(place * width, (place + 1) * width)
        send_ref[:, cols] = dot_nn(turned[middle:, :], right).astype(BF16)
        keep_ref[:, cols] = dot_nn(turned[:middle, :], right).astype(BF16)

    for step in range(steps):
        whole[...] = dot_tn(act_ref[:, step * width : (step + 1) * width], branch_ref[...]).astype(BF16)
        for block in range(width // piece):
            spot = spots[step * (width // piece) + block]
            rows = slice(block * piece, (block + 1) * piece)

            def keep(spot=spot, rows=rows):
                down_keep[pl.ds(pl.multiple_of(spot, 16), piece), :] = whole[rows, :]

            def send(spot=spot, rows=rows):
                down_send[pl.ds(pl.multiple_of(spot - half, 16), piece), :] = whole[rows, :]

            pl.when(spot < half)(keep)
            pl.when(spot >= half)(send)
    turned[...] = dot_nt(first_ref[...], hidden_ref[...]).astype(BF16)
    for step in range(split):
        fill(out_keep, out_send, step, pre_ref[:, step * width : (step + 1) * width])
    turned[...] = dot_nt(first_ref[...], context_ref[...]).astype(BF16)
    fill(out_keep, out_send, split, attend_ref[...])
    turned[...] = dot_nt(second_ref[...], hidden_ref[...]).astype(BF16)
    for step in range(split, steps):
        fill(up_keep, up_send, step - split, pre_ref[:, step * width : (step + 1) * width])


def deep_weight_grads(spots, act, branch, pre, hidden, context, attend, first, second, piece, split):
    local, deep = act.shape
    width = branch.shape[1]
    steps = deep // width
    tall = jax.ShapeDtypeStruct((deep // 2, width), BF16)
    low = lambda blocks: jax.ShapeDtypeStruct((width // 2, blocks * width), BF16)
    return pl.pallas_call(
        functools.partial(deep_kernel, piece=piece, steps=steps, split=split),
        out_shape=(tall, tall, low(split + 1), low(split + 1), low(steps - split), low(steps - split)),
        in_specs=[smem()] + [vmem()] * 8,
        out_specs=(vmem(),) * 6,
        scratch_shapes=[pltpu.VMEM((width, local), BF16), pltpu.VMEM((width, width), BF16)],
        compiler_params=params(16),
        cost_estimate=pl.CostEstimate(flops=1000, bytes_accessed=1000, transcendentals=0),
        name="deep_weight_grads",
    )(spots, act, branch, pre, hidden, context, attend, first, second)


def mixed_back_kernel(
    scalars, ranks_ref, dq_hbm, dk_hbm, dv_hbm, weight_hbm, resid_hbm, own_hbm, other_hbm,
    marker, grad_ref, send_ref, taps_ref, cells_ref, sorted_grad, whole, text, patch, masks, edge,
    grads, weights, resid_ref, own_ref, other_ref, copies,
):
    side, fine = scalars[0], scalars[2]
    local, width = own_ref.shape
    seq, part = dq_hbm.shape
    groups = width // 128
    pad = GRID_HI + 2
    fetches = fetch(
        [own_hbm, other_hbm, dq_hbm, dk_hbm, dv_hbm]
        + [
            weight_hbm.at[:, pl.ds(pl.multiple_of(block * width + side * part, 128), part)]
            for block in range(3)
        ]
        + [resid_hbm],
        [own_ref, other_ref]
        + [grads.at[block] for block in range(3)]
        + [weights.at[block] for block in range(3)]
        + [resid_ref],
        copies,
    )
    fetches[0].wait()
    fetches[1].wait()
    place_slots(own_ref, other_ref, side, text, patch, pad)
    clear_pads(text, patch, pad)
    store_masks(masks, fine, seq - TEXT)
    for copy in fetches[2:]:
        copy.wait()
    for start, size in row_chunks(seq, 240):
        total = None
        for block in range(3):
            product = dot_nt(grads[block, start : start + size, :], weights[block])
            total = product if total is None else total + product
        sorted_grad[start : start + size, :] = total
    unsort_rows(ranks_ref, sorted_grad, whole, seq)
    mine = pl.ds(pl.multiple_of(side * local, 8), local)
    theirs = pl.ds(pl.multiple_of((1 - side) * local, 8), local)
    whole[mine, :] = whole[mine, :] + resid_ref[...]
    inner = pl.ds(pl.multiple_of(local - 8 + side * 8, 8), 8)
    outer = pl.ds(pl.multiple_of(local - side * 8, 8), 8)
    edge[0:local, :] = whole[theirs, :]
    edge[local : local + 8, :] = whole[inner, :]
    send_ref[...] = edge[...].astype(BF16)
    grad_ref[0:local, :] = whole[mine, :]
    grad_ref[local : local + 8, :] = whole[outer, :]
    taps_ref[...] = jnp.zeros(taps_ref.shape, F32)
    cells_ref[...] = jnp.zeros(cells_ref.shape, F32)
    for lane in range(groups):
        cols = slice(lane * 128, lane * 128 + 128)
        for offset in range(-3, 4):
            total = None
            for start, size in row_chunks(TEXT, ROWS):
                value = jnp.sum(
                    whole[start : start + size, cols]
                    * text[lane, pl.ds(8 + start + offset, size), :],
                    axis=0, keepdims=True,
                )
                total = value if total is None else total + value
            for number, (reach, direction) in enumerate(tap_list):
                if reach * direction == offset:
                    taps_ref[number : number + 1, cols] = total
    for grid, chosen in ((GRID_HI, fine != 0), (GRID_LO, fine == 0)):

        def cells(grid=grid):
            for lane in range(groups):
                cols = slice(lane * 128, lane * 128 + 128)
                for number, (down, across) in enumerate(cell_list):
                    moved = patch[lane, pl.ds(pad + down * grid + across, seq - TEXT), :]
                    cells_ref[number : number + 1, cols] = jnp.sum(
                        whole[TEXT:seq, cols] * (moved * masks[number]), axis=0, keepdims=True
                    )

        pl.when(chosen)(cells)


def mixed_back(scalars, ranks, dq, dk, dv, qkv_weight, resid_grad, own, other, marker):
    local, width = own.shape
    seq, part = dq.shape
    groups = width // 128
    return pl.pallas_call(
        mixed_back_kernel,
        out_shape=(
            jax.ShapeDtypeStruct((local + 8, width), F32),
            jax.ShapeDtypeStruct((local + 8, width), BF16),
            jax.ShapeDtypeStruct((16, width), F32),
            jax.ShapeDtypeStruct((16, width), F32),
        ),
        in_specs=[smem(), smem()] + [anywhere()] * 8,
        out_specs=(vmem(),) * 4,
        scratch_shapes=[
            pltpu.VMEM((seq, width), F32),
            pltpu.VMEM((seq, width), F32),
            pltpu.VMEM((groups, TEXT + 16, 128), F32),
            pltpu.VMEM((groups, seq - TEXT + 2 * (GRID_HI + 2), 128), F32),
            pltpu.VMEM((9, seq - TEXT, 128), F32),
            pltpu.VMEM((local + 8, width), F32),
            pltpu.VMEM((3, seq, part), BF16),
            pltpu.VMEM((3, width, part), BF16),
            pltpu.VMEM((local, width), F32),
            pltpu.VMEM((local, width), BF16),
            pltpu.VMEM((local, width), BF16),
            pltpu.SemaphoreType.DMA((9,)),
        ],
        compiler_params=params(15),
        cost_estimate=pl.CostEstimate(flops=1000, bytes_accessed=1000, transcendentals=0),
        name="mixed_back",
    )(scalars, ranks, dq, dk, dv, qkv_weight, resid_grad, own, other, marker)


def token_kernel(
    scalars, grad_ref, received_ref, text_kernel, patch_kernel, marker, out_ref, after_ref,
    text, patch, masks, lanes,
):
    side, fine = scalars[0], scalars[2]
    local, width = out_ref.shape
    groups = width // 128
    pad = GRID_HI + 2
    after_ref[...] = jnp.zeros(after_ref.shape, F32)
    rows = masks.shape[1]
    head = TEXT - local
    clear_pads(text, patch, pad)
    store_masks(masks, fine, rows)

    def load(low):
        for lane in range(groups):
            cols = slice(lane * 128, lane * 128 + 128)
            total = grad_ref[:, cols] + received_ref[:, cols].astype(F32)
            if low:
                text[lane, 8 : 8 + local + 8, :] = total
                text[lane, 16 + local : 8 + TEXT, :] = jnp.zeros((head - 8, 128), F32)
                patch[lane, pad : pad + rows, :] = jnp.zeros((rows, 128), F32)
            else:
                text[lane, 8 : local, :] = jnp.zeros((local - 8, 128), F32)
                text[lane, local : local + 8, :] = total[local:]
                text[lane, 8 + local : 8 + TEXT, :] = total[:head]
                patch[lane, pad : pad + rows, :] = total[head:local]

    pl.when(side == 0)(lambda: load(True))
    pl.when(side != 0)(lambda: load(False))

    def one_lane(lane, carry):
        mix_lane(text, patch, masks, lanes, lane, text_kernel, patch_kernel, fine, pad, True)
        return carry

    lax.fori_loop(0, groups, one_lane, 0)
    mine = pl.ds(pl.multiple_of(side * local, 8), local)
    for lane in range(groups):
        out_ref[:, lane * 128 : lane * 128 + 128] = lanes[lane, mine, :]


def token_back(scalars, grad, received, text_kernel, patch_kernel, seq, marker):
    local, width = grad.shape[0] - 8, grad.shape[1]
    groups = width // 128
    return pl.pallas_call(
        token_kernel,
        out_shape=(jax.ShapeDtypeStruct((local, width), F32), jax.ShapeDtypeStruct((8, 128), F32)),
        in_specs=[smem()] + [vmem()] * 4 + [anywhere()],
        out_specs=(vmem(), vmem()),
        scratch_shapes=[
            pltpu.VMEM((groups, TEXT + 16, 128), F32),
            pltpu.VMEM((groups, seq - TEXT + 2 * (GRID_HI + 2), 128), F32),
            pltpu.VMEM((9, seq - TEXT, 128), F32),
            pltpu.VMEM((groups, seq, 128), F32),
        ],
        compiler_params=params(9),
        cost_estimate=pl.CostEstimate(flops=1000, bytes_accessed=1000, transcendentals=0),
        name="token_back",
    )(scalars, grad, received, text_kernel, patch_kernel, marker)


def finish_kernel(scalars, kept_ref, received_ref, grad_ref, *, part):
    side = scalars[0]
    for block in range(3):
        cols = slice(block * part, (block + 1) * part)
        mine = pl.ds(pl.multiple_of((2 * block + side) * part, 128), part)
        theirs = pl.ds(pl.multiple_of((2 * block + 1 - side) * part, 128), part)
        grad_ref[:, mine] = kept_ref[:, cols]
        grad_ref[:, theirs] = received_ref[:, cols].astype(F32)


def finish(scalars, kept, received, part):
    return pl.pallas_call(
        functools.partial(finish_kernel, part=part),
        out_shape=jax.ShapeDtypeStruct((kept.shape[0], 6 * part), F32),
        in_specs=[smem(), vmem(), vmem()],
        out_specs=vmem(),
        compiler_params=params(8),
        cost_estimate=pl.CostEstimate(flops=1000, bytes_accessed=1000, transcendentals=0),
        name="finish",
    )(scalars, kept, received)


def finish_little_kernel(
    scalars, kept_ref, received_ref, taps_ref, cells_ref, gains_ref, shifts_ref, down_ref, up_ref,
    rank_ref, box_ref, *, ratio, shared, heads,
):
    rows = taps_ref.shape[1]
    small = kept_ref[:rows, :] + received_ref[:rows, :]
    padded = jnp.concatenate([small, jnp.zeros((128 - rows, 128), F32)], axis=0)
    turned = padded.T
    taps_ref[...] = turned[0:9, :rows]
    cells_ref[...] = turned[16:25, :rows]
    gains_ref[...] = turned[32:34, :rows]
    shifts_ref[...] = turned[34:36, :rows]
    down_ref[...] = turned[36:37, :rows]
    row = lax.broadcasted_iota(jnp.int32, (rows, 128), 0)
    lane = lax.broadcasted_iota(jnp.int32, (rows, 128), 1)
    total = jnp.zeros((rows, 128), F32)
    for column in range(ratio):
        value = jnp.broadcast_to(small[:, 40 + column : 41 + column], (rows, 128))
        total = total + jnp.where(lane == row * ratio + column, value, 0.0)
    up_ref[...] = jnp.sum(total, axis=0, keepdims=True)[:, : rows * ratio]
    mine = kept_ref[kept_ref.shape[0] - shared :, :]
    theirs = received_ref[received_ref.shape[0] - shared :, :]
    first = jnp.where(scalars[0] == 0, mine, theirs)
    second = jnp.where(scalars[0] == 0, theirs, mine)
    for place, value in enumerate((first, second)):
        part = slice(place * heads, (place + 1) * heads)
        rank_ref[part, :] = value[:heads, :NB1]
        box_ref[0, part, :] = value[:heads, NB1 : NB1 + NB2]
        box_ref[1, part, :] = value[8 : 8 + heads, :NB2]


def finish_little(scalars, kept, received, ratio, shared, heads):
    rows = received.shape[0] - shared
    full = lambda *shape: jax.ShapeDtypeStruct(shape, F32)
    return pl.pallas_call(
        functools.partial(finish_little_kernel, ratio=ratio, shared=shared, heads=heads),
        out_shape=(
            full(9, rows), full(9, rows), full(2, rows), full(2, rows), full(1, rows),
            full(1, rows * ratio), full(2 * heads, NB1), full(2, 2 * heads, NB2),
        ),
        in_specs=[smem(), vmem(), vmem()],
        out_specs=(vmem(),) * 8,
        compiler_params=params(4),
        cost_estimate=pl.CostEstimate(flops=1000, bytes_accessed=1000, transcendentals=0),
        name="finish_little",
    )(scalars, kept, received)


def swap(value, stage):
    axis, bit = stage
    count = lax.axis_size(axis)
    return lax.ppermute(value, axis, [(i, i ^ bit) for i in range(count)])


def stage_flag(stage):
    axis, bit = stage
    return (lax.axis_index(axis) & bit) // bit


def block_bit(block, stage, blk_count):
    axis, bit = stage
    shift = bit * blk_count if axis == "page" else bit
    return (block // shift) & 1


def spot_of(block, stages, blk_count):
    spot = jnp.zeros_like(block)
    for stage in stages:
        spot = spot * 2 + (block_bit(block, stage, blk_count) ^ stage_flag(stage))
    return spot


def order_matrix(width, stages, blk_count):
    count = lax.axis_size("page") * blk_count
    piece = width // count
    place = jnp.arange(width, dtype=jnp.int32)
    spot, inside = place // piece, place % piece
    block = jnp.zeros_like(spot)
    for depth, stage in enumerate(stages):
        axis, bit = stage
        shift = bit * blk_count if axis == "page" else bit
        value = ((spot >> (len(stages) - 1 - depth)) & 1) ^ stage_flag(stage)
        block = block + value * shift
    column = block * piece + inside
    return (column[:, None] == jnp.arange(width, dtype=jnp.int32)[None, :]).astype(BF16)


def add_up(terms):
    total = terms[0].astype(F32)
    for term in terms[1:]:
        total = total + term.astype(F32)
    return total


def gate(values, marker):
    count = len(values)
    return pl.pallas_call(
        lambda *refs: None,
        out_shape=tuple(jax.ShapeDtypeStruct(value.shape, value.dtype) for value in values),
        in_specs=[anywhere()] * (count + 1),
        out_specs=(anywhere(),) * count,
        input_output_aliases={n: n for n in range(count)},
        compiler_params=params(1),
        cost_estimate=pl.CostEstimate(flops=0, bytes_accessed=0, transcendentals=0),
        name="gate",
    )(*values, marker)


def halve_kernel(kept_ref, received_ref, marker, next_ref, send_ref, after_ref):
    rows = next_ref.shape[0]
    size = rows if rows % 48 else 48
    for start in range(0, rows, size):
        for base, ref in ((rows, send_ref), (0, next_ref)):
            if base % 16 or size % 16:
                place = slice(base + start, base + start + size)
                value = kept_ref[...].astype(F32)[place] + received_ref[...].astype(F32)[place]
            else:
                place = slice(base + start, base + start + size)
                value = kept_ref[place, :].astype(F32) + received_ref[place, :].astype(F32)
            ref[start : start + size, :] = value.astype(ref.dtype)
    after_ref[...] = jnp.zeros(after_ref.shape, F32)


def halve(kept, received, marker):
    rows, width = received.shape[0] // 2, received.shape[1]
    if rows % 8:
        total = kept.astype(F32) + received.astype(F32)
        return total[:rows], total[rows:].astype(BF16), marker
    return pl.pallas_call(
        halve_kernel,
        out_shape=(
            jax.ShapeDtypeStruct((rows, width), F32),
            jax.ShapeDtypeStruct((rows, width), BF16),
            jax.ShapeDtypeStruct((8, 128), F32),
        ),
        in_specs=[vmem(), vmem(), anywhere()],
        out_specs=(vmem(),) * 3,
        compiler_params=params(8),
        cost_estimate=pl.CostEstimate(flops=1000, bytes_accessed=1000, transcendentals=0),
        name="halve",
    )(kept, received, marker)


class Chain:
    def __init__(self, keep, send, stages):
        self.kept, self.stages, self.done = keep, stages, 0
        self.received = swap(send, stages[0])

    def turn(self, marker):
        self.done += 1
        if self.done >= len(self.stages):
            return marker
        self.kept, send, marker = halve(self.kept, self.received, marker)
        self.received = swap(send, self.stages[self.done])
        return marker

    def total(self):
        return self.kept.astype(F32) + self.received.astype(F32)


def little_kernel(now_ref, received_ref, marker, next_ref, message_ref, after_ref, *, shared):
    rows = received_ref.shape[0] - shared
    half = message_ref.shape[0] - shared
    common = now_ref[2 * rows :, :] + received_ref[rows:, :]
    kept = now_ref[:rows, :] + received_ref[:rows, :]
    next_ref[:rows, :] = kept
    next_ref[rows:, :] = common
    message_ref[:half, :] = kept[half:]
    message_ref[half:, :] = common
    after_ref[...] = jnp.zeros(after_ref.shape, F32)


class Little:
    def __init__(self, now, shared, stages):
        self.now, self.shared, self.stages, self.done = now, shared, stages, 0
        rows = (now.shape[0] - shared) // 2
        self.received = swap(now[rows:], stages[0])

    def turn(self, marker):
        self.done += 1
        if self.done > len(self.stages):
            return marker
        rows = self.received.shape[0] - self.shared
        if self.done == len(self.stages):
            return marker
        half = rows // 2
        if half % 8:
            kept = self.now[:rows] + self.received[:rows]
            common = self.now[2 * rows :] + self.received[rows:]
            self.now = jnp.concatenate([kept, common], axis=0)
            message = self.now[half:]
        else:
            lanes = self.now.shape[1]
            self.now, message, marker = pl.pallas_call(
                functools.partial(little_kernel, shared=self.shared),
                out_shape=(
                    jax.ShapeDtypeStruct((rows + self.shared, lanes), F32),
                    jax.ShapeDtypeStruct((half + self.shared, lanes), F32),
                    jax.ShapeDtypeStruct((8, 128), F32),
                ),
                in_specs=[vmem(), vmem(), anywhere()],
                out_specs=(vmem(),) * 3,
                compiler_params=params(4),
                cost_estimate=pl.CostEstimate(flops=1000, bytes_accessed=1000, transcendentals=0),
                name="little",
            )(self.now, self.received, marker)
        self.received = swap(message, self.stages[self.done])
        return marker


def halves_of(value):
    high = value.astype(BF16)
    return high, (value - high.astype(F32)).astype(BF16)


def gather_kernel(
    order_hbm, owner_hbm, inside_hbm, fold_hbm, rank_hbm, box_hbm, taps_hbm, cells_hbm, dense_hbm,
    blocks_hbm, sums_a, sums_b, sums_c, marker, out_ref, after_ref,
    order, owner, inside, fold, rank, box, taps, cells, dense_sums, blocks, sums, copies,
):
    fetches = fetch(
        [order_hbm, owner_hbm, inside_hbm, fold_hbm, rank_hbm, box_hbm, taps_hbm, cells_hbm,
         dense_hbm, blocks_hbm, sums_a, sums_b, sums_c],
        [order, owner, inside, fold, rank, box, taps, cells, dense_sums, blocks]
        + [sums.at[pl.ds(2 * n, 2)] for n in range(3)],
        copies,
    )
    for copy in fetches:
        copy.wait()
    after_ref[...] = jnp.zeros(after_ref.shape, F32)
    width = order.shape[0]

    def exact(dot, left, right):
        return sum(dot(left, piece) for piece in halves_of(right))

    rows = jnp.concatenate([taps[...], cells[...], dense_sums[...]], axis=0)
    rows = jnp.concatenate([rows, jnp.zeros((128 - rows.shape[0], width), F32)], axis=0)
    spread = exact(dot_nn, owner[...], blocks[...]) * inside[...].astype(F32)
    bias = sum(dot_nn(piece, fold[...]) for piece in halves_of(spread))
    out_ref[:width, :] = exact(dot_nt, order[...], rows) + exact(dot_nn, order[...], bias)
    out_ref[width:, :] = jnp.zeros((16, 128), F32)
    heads = sums.shape[0]
    pad = lambda value: jnp.concatenate([value, jnp.zeros((8 - heads, value.shape[1]), F32)], axis=0)
    by_rank = pad(jnp.concatenate([sums[head, 0:1, :] for head in range(heads)], axis=0))
    table = sum(dot_nn(piece, rank[...]) for piece in halves_of(by_rank))
    out_ref[width : width + 8, 0:NB1] = table
    for half in range(2):
        by_box = pad(
            jnp.concatenate([sums[head, half + 1 : half + 2, : 2 * SPAN] for head in range(heads)], axis=0)
        )
        table = sum(dot_nn(piece, box[...]) for piece in halves_of(by_box))
        if half == 0:
            out_ref[width : width + 8, NB1 : NB1 + NB2] = table
        else:
            out_ref[width + 8 : width + 16, 0:NB2] = table


def gather_small(order, taps, cells, dense_sums, blocks, sums, deep, marker):
    width = order.shape[0]
    devices = blocks.shape[0]
    ratio = deep // width
    piece = width // devices
    rows, lanes = np.arange(width), np.arange(128)
    owner = jnp.asarray(rows[:, None] // piece == np.arange(devices)[None, :], BF16)
    inside = jnp.asarray(
        (lanes[None, :] // ratio == rows[:, None] % piece) & (lanes[None, :] < piece * ratio), BF16
    )
    fold = jnp.asarray(lanes[:, None] % ratio + 40 == lanes[None, :], BF16)
    rank = jnp.asarray(bucket_rows(np.arange(RANK_LANES) - (RANK_MID - 1), rank_marks, NB1), BF16)
    box = jnp.asarray(bucket_rows(np.arange(2 * SPAN) - (SPAN - 1), box_marks, NB2), BF16)
    operands = (order, owner, inside, fold, rank, box, taps, cells, dense_sums, blocks)
    return pl.pallas_call(
        gather_kernel,
        out_shape=(
            jax.ShapeDtypeStruct((width + 16, 128), F32), jax.ShapeDtypeStruct((8, 128), F32)
        ),
        in_specs=[anywhere()] * 14,
        out_specs=(vmem(), vmem()),
        scratch_shapes=[pltpu.VMEM(value.shape, value.dtype) for value in operands]
        + [pltpu.VMEM((2 * len(sums), 8, RANK_LANES), F32), pltpu.SemaphoreType.DMA((13,))],
        compiler_params=params(10),
        cost_estimate=pl.CostEstimate(flops=1000, bytes_accessed=1000, transcendentals=0),
        name="gather_small",
    )(*operands, *sums, marker)


def per_device(
    tokens,
    patch_count,
    reading_rank,
    boxes,
    text_kernel,
    patch_kernel,
    qkv_weight,
    rank_table,
    box_tables,
    out_weight,
    norm_gains,
    norm_shifts,
    up_weight,
    up_bias,
    down_weight,
    down_bias,
    cotangent,
):
    side = lax.axis_index("blk")
    blk_count = lax.axis_size("blk")
    page_stages = [("page", 1 << n) for n in range(lax.axis_size("page").bit_length() - 1)]
    across = ("blk", 1)
    out_stages = page_stages[:1] + [across] + page_stages[1:]
    up_stages = page_stages[:1] + page_stages[2:] + [across] + page_stages[1:2]
    down_stages = page_stages + [across]
    devices = lax.axis_size("page") * blk_count
    count = patch_count[0]
    ranks = reading_rank
    own = tokens[0]
    local, width = own.shape
    deep = up_bias.shape[0]
    seq = ranks.shape[1]
    heads = HEADS // blk_count
    scalars = jnp.stack(
        [side, TEXT + count, (count == GRID_HI * GRID_HI).astype(jnp.int32), jnp.int32(0)]
    ).astype(jnp.int32)
    other = swap(own, across)

    xy, xyt, vectors = onehots(scalars, ranks, boxes, rank_table, box_tables, heads)
    mixed, mixed_low, packed = mix_and_project(
        scalars, ranks, own, other, text_kernel, patch_kernel, qkv_weight
    )
    pack = jnp.concatenate([norm_gains, norm_shifts, down_bias[None], up_bias.reshape(-1, width)], axis=0)
    own_context, other_context, shares = [], [], []
    for first, pairs in ((0, 2), (2, 1)):
        share, mine, theirs = attend(scalars, ranks, packed, xy, vectors, local, first, pairs)
        shares += [(share, place) for place in range(pairs)]
        own_context.append(mine)
        other_context.append(swap(theirs, across))
    (
        layer_output, context, hidden_low, act_low, branch_grad, pre_grad, attend_grad,
        resid_one_grad, own_part, their_part, dense_sums, bias_blocks,
    ) = dense(
        scalars, mixed, own_context, other_context, pack, cotangent[0], out_weight, up_weight,
        down_weight, devices,
    )
    part = width // blk_count
    received_part = swap(their_part, across)

    order_out = order_matrix(width, out_stages, blk_count)
    order_up = order_matrix(width, up_stages, blk_count)
    order_qkv = order_matrix(width, down_stages, blk_count)
    piece = deep // devices
    blocks = jnp.arange(devices, dtype=jnp.int32)
    spots = spot_of(blocks, down_stages, blk_count) * piece
    act_rows = act_low
    if piece % 16:
        place = jnp.arange(deep, dtype=jnp.int32)
        target = spots[place // piece] + place % piece
        act_rows = jnp.zeros_like(act_low).at[:, target].set(act_low, unique_indices=True)
        piece = width // 8
        spots = jnp.arange(deep // piece, dtype=jnp.int32) * piece
    steps = deep // width
    split = steps // 2
    down_keep, down_send, out_keep, out_send, up_keep, up_send = deep_weight_grads(
        spots, act_rows, branch_grad, pre_grad, hidden_low, context, attend_grad,
        order_out, order_up, piece, split,
    )
    down_send, out_send, up_send = gate((down_send, out_send, up_send), received_part)
    down = Chain(down_keep, down_send, down_stages)
    out = Chain(out_keep, out_send, out_stages)
    up = Chain(up_keep, up_send, up_stages)

    grads, sums, marker = None, [], None
    for pair, (share, place) in enumerate(shares):
        if pair == 1:
            marker = sums[0]
            for chain in (up, out, down):
                marker = chain.turn(marker)
        *grads, pair_sums = attend_back(
            scalars, ranks, own_part, received_part, share, packed, xy, xyt, pair, place, grads,
            marker if pair == 1 else None,
        )
        sums.append(pair_sums)
    dq, dk, dv = grads
    marker = out.turn(up.turn(sums[-1]))
    qkv_keep, qkv_send, marker = project_weight_grad(order_qkv, mixed_low, dq, dk, dv, marker)
    qkv = Chain(qkv_keep, qkv_send, down_stages)
    grad, outgoing, taps, cells = mixed_back(
        scalars, ranks, dq, dk, dv, qkv_weight, resid_one_grad, own, other, marker
    )
    incoming = swap(outgoing, across)
    marker = taps
    for chain in (qkv, up, down):
        marker = chain.turn(marker)
    gathered, marker = gather_small(order_qkv, taps, cells, dense_sums, bias_blocks, sums, deep, marker)
    little = Little(gathered, 16, down_stages)
    marker = little.turn(marker)
    token_grad, marker = token_back(
        scalars, grad, incoming, text_kernel, patch_kernel, seq, marker
    )
    order = [up, qkv, little, out, down, up, little, qkv, out, little, down, qkv, little, out, down, qkv]
    for chain in order + [down, out, up, little, qkv] * (len(down_stages) + 1):
        marker = chain.turn(marker)
    qkv_weight_grad = finish(scalars, qkv.kept, qkv.received, part)
    taps, cells, gains, shifts, down_bias_grad, up_bias_grad, rank_grad, box_grad = finish_little(
        scalars, little.now, little.received, steps, 16, heads
    )
    out_sum, up_sum = out.total(), up.total()
    return (
        layer_output[None],
        token_grad[None],
        taps,
        cells,
        qkv_weight_grad,
        rank_grad,
        box_grad,
        out_sum[:, split * width :],
        gains,
        shifts,
        jnp.concatenate([out_sum[:, : split * width], up_sum], axis=1),
        up_bias_grad[0],
        down.total(),
        down_bias_grad[0],
    )


def solution(mesh):
    in_specs = (
        P("page", "blk", None),
        P("page"),
        P("page", None),
        P(None, "page", None),
        P(),
        P(),
        P(),
        P(),
        P(),
        P(),
        P(),
        P(),
        P(),
        P(),
        P(),
        P(),
        P("page", "blk", None),
    )
    out_specs = (
        P("page", "blk", None),
        P("page", "blk", None),
        P(None, ("page", "blk")),
        P(None, ("page", "blk")),
        P(("page", "blk"), None),
        P(),
        P(),
        P(("page", "blk"), None),
        P(None, ("page", "blk")),
        P(None, ("page", "blk")),
        P(("page", "blk"), None),
        P(("page", "blk")),
        P(("page", "blk"), None),
        P(("page", "blk")),
    )
    return jax.shard_map(
        per_device, mesh=mesh, in_specs=in_specs, out_specs=out_specs, check_vma=False
    )
```

```python
import functools

import jax
import jax.numpy as jnp
import numpy as np
from jax import lax
from jax.experimental import pallas as pl
from jax.experimental.pallas import tpu as pltpu
from jax.sharding import PartitionSpec as P

TEXT = 512
GRID_LO = 7
GRID_HI = 14
RUN = 16
HEADS = 12
HEAD_DIM = 64
NB1 = 32
NB2 = 64
SPAN = 256
RANK_LANES = 1536
RANK_MID = RANK_LANES // 2
ROWS = 128
F32 = jnp.float32
BF16 = jnp.bfloat16
MIB = 1 << 20
LONG = 10**11

rank_marks = (1, 2, 3, 4, 5, 6, 7, 8, 12, 16, 23, 32, 46, 64, 91)
box_marks = tuple(range(1, 17)) + (19, 23, 27, 32, 39, 46, 54, 64, 77, 91, 108, 128, 153, 182, 216)
neg_fill = -1000000000.0
norm_eps = 1e-05
root_half = 0.7071067811865476
inv_root_tau = 0.3989422804014327
tap_list = ((1, -1), (1, 0), (1, 1), (2, -1), (2, 0), (2, 1), (3, -1), (3, 0), (3, 1))
cell_list = ((-1, -1), (-1, 0), (-1, 1), (0, -1), (0, 0), (0, 1), (1, -1), (1, 0), (1, 1))


def bucket_rows(deltas, marks, bins):
    spread = np.abs(deltas)
    ids = np.sum(spread[:, None] >= np.asarray(marks)[None, :], axis=1) + (bins // 2) * (deltas > 0)
    return (ids[:, None] == np.arange(bins)[None, :]).astype(np.float32)


def dot_nn(left, right):
    return lax.dot_general(left, right, (((1,), (0,)), ((), ())), preferred_element_type=F32)


def dot_nt(left, right):
    return lax.dot_general(left, right, (((1,), (1,)), ((), ())), preferred_element_type=F32)


def dot_tn(left, right):
    return lax.dot_general(left, right, (((0,), (0,)), ((), ())), preferred_element_type=F32)


def row_chunks(total, size):
    return [(start, min(size, total - start)) for start in range(0, total, size)]


def vmem():
    return pl.BlockSpec(memory_space=pltpu.VMEM)


def smem():
    return pl.BlockSpec(memory_space=pltpu.SMEM)


def anywhere():
    return pl.BlockSpec(memory_space=pl.ANY)


def parameter():
    return pl.BlockSpec(memory_space=pltpu.HBM)


def fetch(sources, targets, semaphores):
    copies = []
    for number, (source, target) in enumerate(zip(sources, targets)):
        copies.append(pltpu.make_async_copy(source, target, semaphores.at[number]))
        copies[-1].start()
    return copies


def params(mib):
    return pltpu.CompilerParams(vmem_limit_bytes=mib * MIB)


def onehot_kernel(
    scalars, rank_ref, box_ref, rank_table, box_tables, rank_rows, box_rows, xy_ref, xyt_ref, vectors
):
    seq = rank_ref.shape[1]
    for start, size in row_chunks(seq, 240):
        spot = lax.broadcasted_iota(jnp.int32, (size, seq), 0) + start
        order = (spot == rank_ref[...]).astype(F32).astype(BF16)
        for half in range(2):
            level = lax.broadcasted_iota(jnp.int32, (SPAN, seq), 0)
            marks = (level == box_ref[half]).astype(F32).astype(BF16)
            xy_ref[start : start + size, half * SPAN : (half + 1) * SPAN] = dot_nt(
                order, marks
            ).astype(BF16)
    row = lax.broadcasted_iota(jnp.int32, (SPAN, SPAN), 0)
    col = lax.broadcasted_iota(jnp.int32, (SPAN, SPAN), 1)
    flip = (row + col == SPAN - 1).astype(F32).astype(BF16)
    for half in range(2):
        part = slice(half * SPAN, (half + 1) * SPAN)
        xyt_ref[part, :] = dot_nt(flip, xy_ref[:, part]).astype(BF16)
    heads = vectors.shape[0]
    tables = [(dot_nt(rank_table[...], rank_rows[...]), RANK_LANES)]
    tables += [(dot_nt(box_tables[half], box_rows[...]), 2 * SPAN) for half in range(2)]
    for place, (table, lanes) in enumerate(tables):
        own = jnp.where(scalars[0] == 0, table[:heads], table[table.shape[0] - heads :])
        for head in range(heads):
            vectors[head, place : place + 1, :lanes] = own[head : head + 1]


def onehots(scalars, ranks, boxes, rank_table, box_tables, heads):
    seq = ranks.shape[1]
    rank_rows = jnp.asarray(bucket_rows(np.arange(RANK_LANES) - RANK_MID, rank_marks, NB1), BF16)
    box_rows = jnp.asarray(bucket_rows(SPAN - 1 - np.arange(2 * SPAN), box_marks, NB2), BF16)
    return pl.pallas_call(
        onehot_kernel,
        out_shape=(
            jax.ShapeDtypeStruct((seq, 2 * SPAN), BF16),
            jax.ShapeDtypeStruct((2 * SPAN, seq), BF16),
            jax.ShapeDtypeStruct((heads, 8, RANK_LANES), F32),
        ),
        in_specs=[smem()] + [vmem()] * 6,
        out_specs=(vmem(),) * 3,
        compiler_params=params(12),
        cost_estimate=pl.CostEstimate(
            flops=4 * seq * seq * SPAN, bytes_accessed=4 * seq * 2 * SPAN, transcendentals=0
        ),
        name="onehots",
    )(scalars, ranks, boxes, rank_table, box_tables, rank_rows, box_rows)


def place_slots(own_ref, other_ref, side, text, patch, patch_pad):
    local = own_ref.shape[0]
    head = TEXT - local
    groups = text.shape[0]

    def place(low_ref, high_ref):
        for lane in range(groups):
            cols = slice(128 * lane, 128 * lane + 128)
            text[lane, 8 : 8 + local, :] = low_ref[:, cols].astype(F32)
            high = high_ref[:, cols].astype(F32)
            text[lane, 8 + local : 8 + TEXT, :] = high[:head]
            patch[lane, patch_pad : patch_pad + local - head, :] = high[head:]

    pl.when(side == 0)(lambda: place(own_ref, other_ref))
    pl.when(side != 0)(lambda: place(other_ref, own_ref))


def clear_pads(text, patch, patch_pad):
    groups, rows = patch.shape[0], patch.shape[1]
    for lane in range(groups):
        text[lane, 0:8, :] = jnp.zeros((8, 128), F32)
        text[lane, 8 + TEXT : 16 + TEXT, :] = jnp.zeros((8, 128), F32)
        patch[lane, 0:patch_pad, :] = jnp.zeros((patch_pad, 128), F32)
        patch[lane, rows - patch_pad : rows, :] = jnp.zeros((patch_pad, 128), F32)


def cell_masks(grid, rows):
    slot = lax.broadcasted_iota(jnp.int32, (rows, 128), 0)
    row_of = jnp.zeros((rows, 128), jnp.int32)
    for line in range(1, grid):
        row_of = row_of + (slot >= line * grid).astype(jnp.int32)
    column = slot - row_of * grid
    alive = slot < grid * grid
    masks = []
    for down, across in cell_list:
        masks.append(
            alive
            & (row_of + down >= 0)
            & (row_of + down < grid)
            & (column + across >= 0)
            & (column + across < grid)
        )
    return masks


def store_masks(masks, fine, rows):
    for grid, chosen in ((GRID_HI, fine != 0), (GRID_LO, fine == 0)):

        def fill(grid=grid):
            for number, mask in enumerate(cell_masks(grid, rows)):
                masks[number] = mask.astype(F32)

        pl.when(chosen)(fill)


def mix_lane(text, patch, masks, out, lane, text_kernel, patch_kernel, fine, patch_pad, flip):
    cols = pl.ds(pl.multiple_of(lane * 128, 128), 128)
    taps = {}
    for number, (reach, side) in enumerate(tap_list):
        offset = -reach * side if flip else reach * side
        value = text_kernel[number : number + 1, cols]
        taps[offset] = taps[offset] + value if offset in taps else value
    for start, size in row_chunks(TEXT, ROWS):
        total = text[lane, pl.ds(8 + start, size), :] * (1.0 + taps[0])
        for offset, value in taps.items():
            if offset:
                total = total + text[lane, pl.ds(8 + start + offset, size), :] * value
        out[lane, pl.ds(start, size), :] = total
    rows = masks.shape[1]
    for grid, chosen in ((GRID_HI, fine != 0), (GRID_LO, fine == 0)):

        def cells(grid=grid):
            for start, size in row_chunks(rows, 104):
                total = patch[lane, pl.ds(patch_pad + start, size), :]
                for number, (down, across) in enumerate(cell_list):
                    tap = len(cell_list) - 1 - number if flip else number
                    moved = patch[lane, pl.ds(patch_pad + start + down * grid + across, size), :]
                    total = total + (
                        moved * masks[number, pl.ds(start, size), :]
                    ) * patch_kernel[tap : tap + 1, cols]
                out[lane, pl.ds(TEXT + start, size), :] = total

        pl.when(chosen)(cells)


def sort_rows(ranks_ref, source, target, seq, cast):
    for run in range(TEXT // RUN):
        spot = pl.multiple_of(ranks_ref[0, run * RUN], RUN)
        target[pl.ds(spot, RUN), :] = source[run * RUN : (run + 1) * RUN, :].astype(cast)
    target[TEXT:seq, :] = source[TEXT:seq, :].astype(cast)


def unsort_rows(ranks_ref, source, target, seq):
    for run in range(TEXT // RUN):
        spot = pl.multiple_of(ranks_ref[0, run * RUN], RUN)
        target[run * RUN : (run + 1) * RUN, :] = source[pl.ds(spot, RUN), :]
    target[TEXT:seq, :] = source[TEXT:seq, :]


def mix_kernel(
    scalars, ranks_ref, own_ref, other_ref, text_kernel, patch_kernel, weight_ref,
    mixed_ref, low_ref, packed_ref, text, patch, masks, lanes, whole, weights, copies,
):
    side, fine = scalars[0], scalars[2]
    local, width = own_ref.shape
    seq = low_ref.shape[0]
    groups = width // 128
    pad = GRID_HI + 2
    part = width // 2
    fetches = fetch(
        [
            weight_ref.at[:, pl.ds(pl.multiple_of(block * width + side * part, 128), part)]
            for block in range(3)
        ],
        [weights.at[block] for block in range(3)],
        copies,
    )
    place_slots(own_ref, other_ref, side, text, patch, pad)
    clear_pads(text, patch, pad)
    store_masks(masks, fine, seq - TEXT)

    def one_lane(lane, carry):
        mix_lane(text, patch, masks, lanes, lane, text_kernel, patch_kernel, fine, pad, False)
        return carry

    lax.fori_loop(0, groups, one_lane, 0)
    for lane in range(groups):
        whole[:, 128 * lane : 128 * lane + 128] = lanes[lane]
    mixed_ref[...] = whole[pl.ds(pl.multiple_of(side * local, 8), local), :]
    sort_rows(ranks_ref, whole, low_ref, seq, BF16)
    for block in range(3):
        fetches[block].wait()
        for start, size in row_chunks(seq, 240):
            value = dot_nn(low_ref[start : start + size, :], weights[block]).astype(BF16)
            if block == 0:
                value = value * (HEAD_DIM**-0.5)
            packed_ref[start : start + size, block * part : (block + 1) * part] = value


def mix_and_project(scalars, ranks, own, other, text_kernel, patch_kernel, qkv_weight):
    local, width = own.shape
    seq = ranks.shape[1]
    groups = width // 128
    return pl.pallas_call(
        mix_kernel,
        out_shape=(
            jax.ShapeDtypeStruct((local, width), F32),
            jax.ShapeDtypeStruct((seq, width), BF16),
            jax.ShapeDtypeStruct((seq, 3 * width // 2), BF16),
        ),
        in_specs=[smem(), smem()] + [vmem()] * 4 + [parameter()],
        out_specs=(vmem(),) * 3,
        scratch_shapes=[
            pltpu.VMEM((groups, TEXT + 16, 128), F32),
            pltpu.VMEM((groups, seq - TEXT + 2 * (GRID_HI + 2), 128), F32),
            pltpu.VMEM((9, seq - TEXT, 128), F32),
            pltpu.VMEM((groups, seq, 128), F32),
            pltpu.VMEM((seq, width), F32),
            pltpu.VMEM((3, width, width // 2), BF16),
            pltpu.SemaphoreType.DMA((3,)),
        ],
        compiler_params=params(16),
        cost_estimate=pl.CostEstimate(
            flops=2 * seq * width * 3 * width // 2, bytes_accessed=12 * MIB, transcendentals=0
        ),
        name="mix_and_project",
    )(scalars, ranks, own, other, text_kernel, patch_kernel, qkv_weight)


def head_lanes(shape, parity):
    return (lax.broadcasted_iota(jnp.int32, shape, 1) >= HEAD_DIM) == (parity != 0)


def skewed(vector, rows, lanes, shift):
    return pltpu.roll(jnp.broadcast_to(vector, (rows, lanes)), shift, 1, stride=1, stride_axis=0)


def attend_kernel(
    scalars, ranks_ref, queries, keys, values, xy_ref, vectors,
    shares_ref, own_ref, other_ref, left, right, rank_bias, gathered, slots, scores_ref,
):
    side, live = scalars[0], scalars[1]
    seq = queries.shape[0]
    local = own_ref.shape[0]
    head = pl.program_id(0)
    parity = lax.rem(head, 2)

    @pl.when(head == 0)
    def _():
        left[:, 128:] = xy_ref[...]

    left[:, :128] = queries[...]
    mine = head_lanes((seq, 128), parity)
    right[:, :128] = jnp.where(mine, keys[...], jnp.zeros((), BF16))
    for half in range(2):
        table = skewed(vectors[0, half + 1 : half + 2, : 2 * SPAN], SPAN, 2 * SPAN, SPAN + 1)
        table = table[:, :SPAN].astype(BF16)
        right[:, 128 + half * SPAN : 128 + (half + 1) * SPAN] = dot_nn(
            xy_ref[:, half * SPAN : (half + 1) * SPAN], table
        ).astype(BF16)
    rank_bias[...] = skewed(vectors[0, 0:1, :], ROWS, RANK_LANES, RANK_LANES - 128)
    top = (seq // ROWS) * ROWS
    alive = lax.broadcasted_iota(jnp.int32, (16, seq), 1) < live
    chunks = row_chunks(seq, 240)

    def product(start, size):
        scores_ref[start : start + size, :] = dot_nt(left[start : start + size, :], right[...])

    def soften(start, size):
        for first in range(start, start + size, 16):
            base = first // ROWS * ROWS
            scores = scores_ref[first : first + 16, :]
            scores = scores + rank_bias[first - base : first - base + 16, top - base : top - base + seq]
            scores = jnp.where(alive, scores, neg_fill)
            powered = jnp.exp(scores - jnp.max(scores, axis=1, keepdims=True))
            shares = powered * (1.0 / jnp.sum(powered, axis=1, keepdims=True))
            shares_ref[0, first : first + 16, :] = shares.astype(BF16)

    def apply(start, size):
        context = dot_nn(shares_ref[0, start : start + size, :], values[...])
        gathered[start : start + size, :] = jnp.where(
            head_lanes((size, 128), parity), context, gathered[start : start + size, :]
        )

    product(*chunks[0])
    for n in range(len(chunks)):
        if n + 1 < len(chunks):
            product(*chunks[n + 1])
        if n:
            apply(*chunks[n - 1])
        soften(*chunks[n])
    apply(*chunks[-1])

    @pl.when(parity == 1)
    def _():
        unsort_rows(ranks_ref, gathered, slots, seq)
        own_ref[...] = slots[pl.ds(pl.multiple_of(side * local, 8), local), :].astype(BF16)
        other_ref[...] = slots[pl.ds(pl.multiple_of((1 - side) * local, 8), local), :].astype(BF16)


def attend(scalars, ranks, packed, xy, vectors, local, first, count):
    seq = packed.shape[0]
    pairs = vectors.shape[0] // 2
    heads = 2 * count
    width = heads * HEAD_DIM
    whole = pl.BlockSpec((seq, 2 * SPAN), lambda h: (0, 0))
    slot_spec = pl.BlockSpec((local, 128), lambda h: (0, h // 2))
    return pl.pallas_call(
        attend_kernel,
        grid=(heads,),
        out_shape=(
            jax.ShapeDtypeStruct((heads, seq, seq), BF16),
            jax.ShapeDtypeStruct((local, width), BF16),
            jax.ShapeDtypeStruct((local, width), BF16),
        ),
        in_specs=[
            smem(),
            smem(),
            pl.BlockSpec((seq, 128), lambda h: (0, first + h // 2)),
            pl.BlockSpec((seq, 128), lambda h: (0, pairs + first + h // 2)),
            pl.BlockSpec((seq, 128), lambda h: (0, 2 * pairs + first + h // 2)),
            whole,
            pl.BlockSpec((1, 8, RANK_LANES), lambda h: (2 * first + h, 0, 0)),
        ],
        out_specs=(pl.BlockSpec((1, seq, seq), lambda h: (h, 0, 0)), slot_spec, slot_spec),
        scratch_shapes=[
            pltpu.VMEM((seq, 128 + 2 * SPAN), BF16),
            pltpu.VMEM((seq, 128 + 2 * SPAN), BF16),
            pltpu.VMEM((ROWS, RANK_LANES), F32),
            pltpu.VMEM((seq, 128), F32),
            pltpu.VMEM((seq, 128), F32),
            pltpu.VMEM((seq, seq), F32),
        ],
        compiler_params=params(13),
        cost_estimate=pl.CostEstimate(
            flops=heads * 2 * seq * seq * 1024, bytes_accessed=heads * seq * seq * 2,
            transcendentals=heads * seq * seq,
        ),
        name="attend",
    )(scalars, ranks, packed, packed, packed, xy, vectors)


def attend_back_kernel(
    ranks_ref, own_ref, other_ref, side_ref, shares_ref, queries, keys, values, xy_ref, xyt_ref,
    dq_ref, dk_ref, dv_ref, sums_ref, right, score_grad, spread, rank_sum, slots, upstream, share_grads,
):
    seq = queries.shape[0]
    local = own_ref.shape[0]
    side = side_ref[0]
    head = pl.program_id(0)
    parity = lax.rem(head, 2)
    scale = HEAD_DIM**-0.5

    @pl.when(head == 0)
    def _():
        right[:, 128:] = xy_ref[...]

    @pl.when(parity == 0)
    def _():
        slots[pl.ds(pl.multiple_of(side * local, 8), local), :] = own_ref[...].astype(F32)
        slots[pl.ds(pl.multiple_of((1 - side) * local, 8), local), :] = other_ref[...].astype(F32)
        sort_rows(ranks_ref, slots, upstream, seq, BF16)

    right[:, :128] = keys[...]
    mine = head_lanes((seq, 128), parity)
    own_values = jnp.where(mine, values[...], jnp.zeros((), BF16))
    rank_sum[...] = jnp.zeros(rank_sum.shape, F32)
    top = (seq // ROWS) * ROWS
    chunks = row_chunks(seq, 240)

    def product(start, size):
        share_grads[start : start + size, :] = dot_nt(upstream[start : start + size, :], own_values)

    def soften(start, size):
        for first in range(start, start + size, 16):
            base = first // ROWS * ROWS
            rows = slice(first, first + 16)
            shares = shares_ref[0, rows, :].astype(F32)
            weighted = shares * share_grads[rows, :]
            low = (weighted - shares * jnp.sum(weighted, axis=1, keepdims=True)).astype(BF16)
            score_grad[rows, :] = low
            place = (slice(first - base, first - base + 16), slice(top - base, top - base + seq))
            rank_sum[place] = rank_sum[place] + low.astype(F32)

    def apply(start, size):
        rows = slice(start, start + size)
        product = dot_nn(score_grad[rows, :], right[...])
        spread[rows, :] = product[:, 128:].astype(BF16)
        dq_ref[rows, :] = jnp.where(
            head_lanes((size, 128), parity), (product[:, :128] * scale).astype(BF16), dq_ref[rows, :]
        )

    product(*chunks[0])
    for n in range(len(chunks)):
        if n + 1 < len(chunks):
            product(*chunks[n + 1])
        if n:
            apply(*chunks[n - 1])
        soften(*chunks[n])
    apply(*chunks[-1])
    dk = dot_tn(score_grad[...], queries[...]).astype(BF16)
    dk_ref[...] = jnp.where(mine, dk, dk_ref[...])
    dv = dot_tn(shares_ref[0], upstream[...]).astype(BF16)
    dv_ref[...] = jnp.where(mine, dv, dv_ref[...])
    row = lax.broadcasted_iota(jnp.int32, (ROWS, ROWS), 0)
    col = lax.broadcasted_iota(jnp.int32, (ROWS, ROWS), 1)
    flip = (row + col == ROWS - 1).astype(F32).astype(BF16)
    high = rank_sum[...].astype(BF16)
    rest = (rank_sum[...] - high.astype(F32)).astype(BF16)
    turned = dot_nn(flip, high) + dot_nn(flip, rest)
    turned = pltpu.roll(turned, 0, 1, stride=1, stride_axis=0)
    sums_ref[0, 0:1, :] = jnp.sum(turned, axis=0, keepdims=True)
    for half in range(2):
        part = slice(half * SPAN, (half + 1) * SPAN)
        table = dot_nn(xyt_ref[part, :], spread[:, part])
        table = jnp.concatenate([table, jnp.zeros((SPAN, SPAN), F32)], axis=1)
        table = pltpu.roll(table, 0, 1, stride=1, stride_axis=0)
        sums_ref[0, half + 1 : half + 2, : 2 * SPAN] = jnp.sum(table, axis=0, keepdims=True)


def attend_back(scalars, ranks, own, other, shares, packed, xy, xyt, pair, place, so_far, marker):
    seq = packed.shape[0]
    local = own.shape[0]
    width = packed.shape[1] // 3
    pairs = width // 128
    slot_spec = pl.BlockSpec((local, 128), lambda h: (0, pair))
    out_spec = pl.BlockSpec((seq, 128), lambda h: (0, pair))
    so_far = tuple(so_far) if so_far else ()
    extra = so_far + ((marker,) if marker is not None else ())

    def body(*refs):
        ins, rest = refs[:10], refs[10 + len(extra) :]
        attend_back_kernel(*ins, *rest)

    return pl.pallas_call(
        body,
        grid=(2,),
        out_shape=(jax.ShapeDtypeStruct((seq, width), BF16),) * 3
        + (jax.ShapeDtypeStruct((2, 8, RANK_LANES), F32),),
        in_specs=[
            smem(),
            slot_spec,
            slot_spec,
            smem(),
            pl.BlockSpec((1, seq, seq), lambda h: (2 * place + h, 0, 0)),
            pl.BlockSpec((seq, 128), lambda h: (0, pair)),
            pl.BlockSpec((seq, 128), lambda h: (0, pairs + pair)),
            pl.BlockSpec((seq, 128), lambda h: (0, 2 * pairs + pair)),
            pl.BlockSpec((seq, 2 * SPAN), lambda h: (0, 0)),
            pl.BlockSpec((2 * SPAN, seq), lambda h: (0, 0)),
        ]
        + [anywhere()] * len(extra),
        out_specs=(out_spec,) * 3 + (pl.BlockSpec((1, 8, RANK_LANES), lambda h: (h, 0, 0)),),
        scratch_shapes=[
            pltpu.VMEM((seq, 128 + 2 * SPAN), BF16),
            pltpu.VMEM((seq, seq), BF16),
            pltpu.VMEM((seq, 2 * SPAN), BF16),
            pltpu.VMEM((ROWS, RANK_LANES), F32),
            pltpu.VMEM((seq, 128), F32),
            pltpu.VMEM((seq, 128), BF16),
            pltpu.VMEM((seq, seq), F32),
        ],
        input_output_aliases={10 + n: n for n in range(len(so_far))},
        compiler_params=params(15),
        cost_estimate=pl.CostEstimate(
            flops=1000 if pair else LONG, bytes_accessed=1000, transcendentals=0
        ),
        name="attend_back",
    )(ranks, own, other, scalars, shares, packed, packed, packed, xy, xyt, *extra)


def fold_rows(value):
    total = value[0:8]
    for start in range(8, value.shape[0], 8):
        total = total + value[start : start + 8]
    return total


def row_mean(value):
    return jnp.sum(value, axis=1, keepdims=True) * (1.0 / value.shape[1])


def normalize(value):
    center = value - row_mean(value)
    inverse = lax.rsqrt(row_mean(center * center) + norm_eps)
    return center * inverse, inverse


def dense_kernel(
    scalars, mixed_ref, own_a, own_b, other_a, other_b, pack, cot_ref, out_hbm, up_hbm, down_hbm, marker,
    result_ref, context_ref, hidden_ref, act_ref, branch_ref, pre_ref, attend_ref, resid_ref,
    own_grad, other_grad, sums_ref, blocks_ref,
    out_w, up_w, down_w, slope, product, stash, hidden, normed, scale, bias_sums_ref, copies,
):
    side, live = scalars[0], scalars[1]
    local, width = mixed_ref.shape
    deep = act_ref.shape[1]
    part = own_grad.shape[1]
    step = width // 2
    blocks = deep // step
    gains, shifts, down_bias = pack.at[0:2], pack.at[2:4], pack.at[4:5]
    fetches = [pltpu.make_async_copy(out_hbm, out_w, copies.at[0])]
    fetches += [
        pltpu.make_async_copy(
            up_hbm.at[:, n * width : (n + 1) * width], up_w.at[:, n * width : (n + 1) * width],
            copies.at[1 + n],
        )
        for n in range(deep // width)
    ]
    fetches.append(pltpu.make_async_copy(down_hbm, down_w, copies.at[1 + deep // width]))
    for fetch in fetches:
        fetch.start()
    wide = own_a.shape[1]
    for base, (first, second) in ((side * part, (own_a, own_b)), ((1 - side) * part, (other_a, other_b))):
        context_ref[:, pl.ds(pl.multiple_of(base, 128), wide)] = first[...]
        context_ref[:, pl.ds(pl.multiple_of(base + wide, 128), part - wide)] = second[...]
    chunks = row_chunks(local, 24)
    fetches[0].wait()
    product[...] = dot_nn(context_ref[...], out_w[...])
    for start, size in chunks:
        rows = slice(start, start + size)
        value, inverse = normalize(mixed_ref[rows, :] + product[rows, :])
        normed[rows, :] = value
        scale[rows, :] = jnp.broadcast_to(inverse, (size, 128))
        value = value * gains[0:1, :] + shifts[0:1, :]
        hidden[rows, :] = value
        hidden_ref[rows, :] = value.astype(BF16)

    def lift(block):
        if block % 2 == 0:
            fetches[1 + block // 2].wait()
        cols = slice(block * step, (block + 1) * step)
        stash[block % 2] = dot_nn(hidden_ref[...], up_w[:, cols])

    def bend(block):
        cols = slice(block * step, (block + 1) * step)
        half_cols = slice(block % 2 * step, (block % 2 + 1) * step)
        for start, size in chunks:
            rows = slice(start, start + size)
            value = stash[block % 2, rows, :] + pack[5 + block // 2 : 6 + block // 2, half_cols]
            half = 0.5 + 0.5 * lax.erf(value * root_half)
            act_ref[rows, cols] = (value * half).astype(BF16)
            slope[rows, cols] = half + value * jnp.exp(-0.5 * value * value) * inv_root_tau

    lift(0)
    for block in range(blocks):
        if block + 1 < blocks:
            lift(block + 1)
        bend(block)
    fetches[-1].wait()
    product[...] = dot_nn(act_ref[...], down_w[...])
    zero = jnp.zeros((8, width), F32)
    gain_sum, shift_sum, bias_sum = zero, zero, zero
    for start, size in chunks:
        rows = slice(start, start + size)
        value, inverse = normalize(hidden[rows, :] + product[rows, :] + down_bias[...])
        slot = lax.broadcasted_iota(jnp.int32, (size, width), 0) + (side * local + start)
        alive = (slot < live).astype(F32)
        result_ref[rows, :] = (alive * (value * gains[1:2, :] + shifts[1:2, :])).astype(BF16)
        upstream = cot_ref[rows, :].astype(F32) * alive
        gain_sum = gain_sum + fold_rows(upstream * value)
        shift_sum = shift_sum + fold_rows(upstream)
        scaled = upstream * gains[1:2, :]
        grad = inverse * (scaled - row_mean(scaled) - value * row_mean(scaled * value))
        bias_sum = bias_sum + fold_rows(grad)
        hidden[rows, :] = grad
        branch_ref[rows, :] = grad.astype(BF16)
    sums_ref[1:2, :] = jnp.sum(gain_sum, axis=0, keepdims=True)
    sums_ref[3:4, :] = jnp.sum(shift_sum, axis=0, keepdims=True)
    sums_ref[4:5, :] = jnp.sum(bias_sum, axis=0, keepdims=True)
    sums_ref[5:8, :] = jnp.zeros((3, width), F32)

    def lower(block):
        cols = slice(block * step, (block + 1) * step)
        stash[block % 2] = dot_nt(branch_ref[...], down_w[cols, :])

    def unbend(block):
        cols = slice(block * step, (block + 1) * step)
        total = jnp.zeros((8, step), F32)
        for start, size in chunks:
            rows = slice(start, start + size)
            value = (stash[block % 2, rows, :] * slope[rows, cols]).astype(BF16)
            pre_ref[rows, cols] = value
            total = total + fold_rows(value.astype(F32))
        bias_sums_ref[:, cols] = jnp.sum(total, axis=0, keepdims=True)

    lower(0)
    for block in range(blocks):
        if block + 1 < blocks:
            lower(block + 1)
        unbend(block)
    product[...] = dot_nt(pre_ref[...], up_w[...])
    piece = deep // blocks_ref.shape[0]
    blocks_ref[...] = jnp.zeros(blocks_ref.shape, F32)
    for block in range(blocks_ref.shape[0]):
        blocks_ref[block : block + 1, :piece] = bias_sums_ref[:, block * piece : (block + 1) * piece]
    gain_sum, shift_sum = zero, zero
    for start, size in chunks:
        rows = slice(start, start + size)
        upstream = hidden[rows, :] + product[rows, :]
        value = normed[rows, :]
        gain_sum = gain_sum + fold_rows(upstream * value)
        shift_sum = shift_sum + fold_rows(upstream)
        scaled = upstream * gains[0:1, :]
        inverse = jnp.concatenate([scale[rows, :]] * (width // 128), axis=1)
        grad = inverse * (scaled - row_mean(scaled) - value * row_mean(scaled * value))
        resid_ref[rows, :] = grad
        attend_ref[rows, :] = grad.astype(BF16)
    sums_ref[0:1, :] = jnp.sum(gain_sum, axis=0, keepdims=True)
    sums_ref[2:3, :] = jnp.sum(shift_sum, axis=0, keepdims=True)
    for base, ref in (((1 - side) * part, other_grad), (side * part, own_grad)):
        weight = out_w[pl.ds(pl.multiple_of(base, 128), part), :]
        ref[...] = dot_nt(attend_ref[...], weight).astype(BF16)


def dense(
    scalars, mixed, own_context, other_context, pack, cotangent, out_weight, up_weight, down_weight, devices, marker,
):
    local, width = mixed.shape
    deep = up_weight.shape[1]
    part = width // 2
    low = lambda *shape: jax.ShapeDtypeStruct(shape, BF16)
    full = lambda *shape: jax.ShapeDtypeStruct(shape, F32)
    hbm = pl.BlockSpec(memory_space=pl.ANY)
    return pl.pallas_call(
        dense_kernel,
        out_shape=(
            low(local, width), low(local, width), low(local, width), low(local, deep),
            low(local, width), low(local, deep), low(local, width), full(local, width),
            low(local, part), low(local, part), full(8, width), full(devices, 128),
        ),
        in_specs=[smem()] + [vmem()] * 7 + [hbm] * 4,
        out_specs=(vmem(),) * 12,
        scratch_shapes=[
            pltpu.VMEM((width, width), BF16),
            pltpu.VMEM((width, deep), BF16),
            pltpu.VMEM((deep, width), BF16),
            pltpu.VMEM((local, deep), F32),
            pltpu.VMEM((local, width), F32),
            pltpu.VMEM((2, local, width // 2), F32),
            pltpu.VMEM((local, width), F32),
            pltpu.VMEM((local, width), F32),
            pltpu.VMEM((local, 128), F32),
            pltpu.VMEM((1, deep), F32),
            pltpu.SemaphoreType.DMA((2 + deep // width,)),
        ],
        compiler_params=params(23),
        cost_estimate=pl.CostEstimate(
            flops=2 * local * width * (4 * deep + 2 * width), bytes_accessed=20 * MIB,
            transcendentals=2 * local * deep,
        ),
        name="dense",
    )(
        scalars, mixed, *own_context, *other_context, pack, cotangent, out_weight, up_weight, down_weight,
        marker,
    )


def halves_of(value):
    high = value.astype(BF16)
    return high, (value - high.astype(F32)).astype(BF16)


def turn_kernel(order_ref, low_ref, marker, turned_ref, after_ref):
    turned_ref[...] = dot_nt(order_ref[...], low_ref[...]).astype(BF16)
    after_ref[...] = jnp.zeros(after_ref.shape, F32)


def turn_rows(order, low, marker):
    return pl.pallas_call(
        turn_kernel,
        out_shape=(
            jax.ShapeDtypeStruct((order.shape[0], low.shape[0]), BF16),
            jax.ShapeDtypeStruct((8, 128), F32),
        ),
        in_specs=[vmem(), vmem(), anywhere()],
        out_specs=(vmem(), vmem()),
        compiler_params=params(8),
        cost_estimate=pl.CostEstimate(flops=10**9, bytes_accessed=1000, transcendentals=0),
        name="turn_rows",
    )(order, low, marker)


def project_back_kernel(
    turned_hbm, dq_hbm, dk_hbm, dv_hbm, marker, keep_ref, send_ref, after_ref, turned, grads, copies
):
    half, part = keep_ref.shape[0], dq_hbm.shape[1]
    fetches = fetch(
        [turned_hbm, dq_hbm, dk_hbm, dv_hbm], [turned] + [grads.at[block] for block in range(3)], copies
    )
    after_ref[...] = jnp.zeros(after_ref.shape, F32)
    fetches[0].wait()
    for block in range(3):
        fetches[1 + block].wait()
        cols = slice(block * part, (block + 1) * part)
        send_ref[:, cols] = dot_nn(turned[half:, :], grads[block]).astype(BF16)
        keep_ref[:, cols] = dot_nn(turned[:half, :], grads[block]).astype(BF16)


def project_weight_grad(turned, dq, dk, dv, marker):
    width, seq = turned.shape
    part = dq.shape[1]
    shape = jax.ShapeDtypeStruct((width // 2, 3 * part), BF16)
    return pl.pallas_call(
        project_back_kernel,
        out_shape=(shape, shape, jax.ShapeDtypeStruct((8, 128), F32)),
        in_specs=[anywhere()] * 5,
        out_specs=(vmem(),) * 3,
        scratch_shapes=[
            pltpu.VMEM((width, seq), BF16),
            pltpu.VMEM((3, seq, part), BF16),
            pltpu.SemaphoreType.DMA((4,)),
        ],
        compiler_params=params(12),
        cost_estimate=pl.CostEstimate(flops=1000, bytes_accessed=1000, transcendentals=0),
        name="project_weight_grad",
    )(turned, dq, dk, dv, marker)


def fill_block(turned, keep_ref, send_ref, place, right):
    width = right.shape[1]
    middle = turned.shape[0] // 2
    cols = slice(place * width, (place + 1) * width)
    send_ref[:, cols] = dot_nn(turned[middle:, :], right).astype(BF16)
    keep_ref[:, cols] = dot_nn(turned[:middle, :], right).astype(BF16)


def down_kernel(spots, act_ref, branch_ref, keep_ref, send_ref, whole, *, piece):
    width = branch_ref.shape[1]
    half = keep_ref.shape[0]
    for step in range(act_ref.shape[1] // width):
        whole[...] = dot_tn(act_ref[:, step * width : (step + 1) * width], branch_ref[...]).astype(BF16)
        for block in range(width // piece):
            spot = spots[step * (width // piece) + block]
            rows = slice(block * piece, (block + 1) * piece)

            def keep(spot=spot, rows=rows):
                keep_ref[pl.ds(pl.multiple_of(spot, 16), piece), :] = whole[rows, :]

            def send(spot=spot, rows=rows):
                send_ref[pl.ds(pl.multiple_of(spot - half, 16), piece), :] = whole[rows, :]

            pl.when(spot < half)(keep)
            pl.when(spot >= half)(send)


def down_weight_grad(spots, act, branch, piece):
    deep, width = act.shape[1], branch.shape[1]
    tall = jax.ShapeDtypeStruct((deep // 2, width), BF16)
    return pl.pallas_call(
        functools.partial(down_kernel, piece=piece),
        out_shape=(tall, tall),
        in_specs=[smem()] + [vmem()] * 2,
        out_specs=(vmem(),) * 2,
        scratch_shapes=[pltpu.VMEM((width, width), BF16)],
        compiler_params=params(12),
        cost_estimate=pl.CostEstimate(flops=1000, bytes_accessed=1000, transcendentals=0),
        name="down_weight_grad",
    )(spots, act, branch)


def up_kernel(
    pre_ref, hidden_ref, context_ref, attend_ref, first_ref, second_ref, marker,
    out_keep, out_send, up_keep, up_send, turned, *, split,
):
    width = hidden_ref.shape[1]
    block = lambda step: pre_ref[:, step * width : (step + 1) * width]
    turned[...] = dot_nt(first_ref[...], hidden_ref[...]).astype(BF16)
    for step in range(split):
        fill_block(turned, out_keep, out_send, step, block(step))
    turned[...] = dot_nt(first_ref[...], context_ref[...]).astype(BF16)
    fill_block(turned, out_keep, out_send, split, attend_ref[...])
    turned[...] = dot_nt(second_ref[...], hidden_ref[...]).astype(BF16)
    for step in range(split, pre_ref.shape[1] // width):
        fill_block(turned, up_keep, up_send, step - split, block(step))


def up_weight_grads_of(pre, hidden, context, attend, first, second, split, marker):
    local, width = hidden.shape
    steps = pre.shape[1] // width
    low = lambda blocks: jax.ShapeDtypeStruct((width // 2, blocks * width), BF16)
    return pl.pallas_call(
        functools.partial(up_kernel, split=split),
        out_shape=(low(split + 1), low(split + 1), low(steps - split), low(steps - split)),
        in_specs=[vmem()] * 6 + [anywhere()],
        out_specs=(vmem(),) * 4,
        scratch_shapes=[pltpu.VMEM((width, local), BF16)],
        compiler_params=params(14),
        cost_estimate=pl.CostEstimate(flops=LONG, bytes_accessed=1000, transcendentals=0),
        name="up_weight_grad",
    )(pre, hidden, context, attend, first, second, marker)


def mixed_back_kernel(
    scalars, ranks_ref, dq_hbm, dk_hbm, dv_hbm, weight_hbm, resid_hbm, own_hbm, other_hbm,
    marker, grad_ref, send_ref, taps_ref, cells_ref, sorted_grad, whole, text, patch, masks, edge,
    grads, weights, resid_ref, own_ref, other_ref, copies,
):
    side, fine = scalars[0], scalars[2]
    local, width = own_ref.shape
    seq, part = dq_hbm.shape
    groups = width // 128
    pad = GRID_HI + 2
    fetches = fetch(
        [own_hbm, other_hbm, dq_hbm, dk_hbm, dv_hbm]
        + [
            weight_hbm.at[:, pl.ds(pl.multiple_of(block * width + side * part, 128), part)]
            for block in range(3)
        ]
        + [resid_hbm],
        [own_ref, other_ref]
        + [grads.at[block] for block in range(3)]
        + [weights.at[block] for block in range(3)]
        + [resid_ref],
        copies,
    )
    fetches[0].wait()
    fetches[1].wait()
    place_slots(own_ref, other_ref, side, text, patch, pad)
    clear_pads(text, patch, pad)
    store_masks(masks, fine, seq - TEXT)
    for copy in fetches[2:]:
        copy.wait()
    for start, size in row_chunks(seq, 240):
        total = None
        for block in range(3):
            product = dot_nt(grads[block, start : start + size, :], weights[block])
            total = product if total is None else total + product
        sorted_grad[start : start + size, :] = total
    unsort_rows(ranks_ref, sorted_grad, whole, seq)
    mine = pl.ds(pl.multiple_of(side * local, 8), local)
    theirs = pl.ds(pl.multiple_of((1 - side) * local, 8), local)
    whole[mine, :] = whole[mine, :] + resid_ref[...]
    inner = pl.ds(pl.multiple_of(local - 8 + side * 8, 8), 8)
    outer = pl.ds(pl.multiple_of(local - side * 8, 8), 8)
    edge[0:local, :] = whole[theirs, :]
    edge[local : local + 8, :] = whole[inner, :]
    send_ref[...] = edge[...].astype(BF16)
    grad_ref[0:local, :] = whole[mine, :]
    grad_ref[local : local + 8, :] = whole[outer, :]
    taps_ref[...] = jnp.zeros(taps_ref.shape, F32)
    cells_ref[...] = jnp.zeros(cells_ref.shape, F32)
    for lane in range(groups):
        cols = slice(lane * 128, lane * 128 + 128)
        for offset in range(-3, 4):
            total = None
            for start, size in row_chunks(TEXT, ROWS):
                value = jnp.sum(
                    whole[start : start + size, cols]
                    * text[lane, pl.ds(8 + start + offset, size), :],
                    axis=0, keepdims=True,
                )
                total = value if total is None else total + value
            for number, (reach, direction) in enumerate(tap_list):
                if reach * direction == offset:
                    taps_ref[number : number + 1, cols] = total
    for grid, chosen in ((GRID_HI, fine != 0), (GRID_LO, fine == 0)):

        def cells(grid=grid):
            for lane in range(groups):
                cols = slice(lane * 128, lane * 128 + 128)
                for number, (down, across) in enumerate(cell_list):
                    moved = patch[lane, pl.ds(pad + down * grid + across, seq - TEXT), :]
                    cells_ref[number : number + 1, cols] = jnp.sum(
                        whole[TEXT:seq, cols] * (moved * masks[number]), axis=0, keepdims=True
                    )

        pl.when(chosen)(cells)


def mixed_back(scalars, ranks, dq, dk, dv, qkv_weight, resid_grad, own, other, marker):
    local, width = own.shape
    seq, part = dq.shape
    groups = width // 128
    return pl.pallas_call(
        mixed_back_kernel,
        out_shape=(
            jax.ShapeDtypeStruct((local + 8, width), F32),
            jax.ShapeDtypeStruct((local + 8, width), BF16),
            jax.ShapeDtypeStruct((16, width), F32),
            jax.ShapeDtypeStruct((16, width), F32),
        ),
        in_specs=[smem(), smem()] + [anywhere()] * 3 + [parameter()] + [anywhere()] * 4,
        out_specs=(vmem(),) * 4,
        scratch_shapes=[
            pltpu.VMEM((seq, width), F32),
            pltpu.VMEM((seq, width), F32),
            pltpu.VMEM((groups, TEXT + 16, 128), F32),
            pltpu.VMEM((groups, seq - TEXT + 2 * (GRID_HI + 2), 128), F32),
            pltpu.VMEM((9, seq - TEXT, 128), F32),
            pltpu.VMEM((local + 8, width), F32),
            pltpu.VMEM((3, seq, part), BF16),
            pltpu.VMEM((3, width, part), BF16),
            pltpu.VMEM((local, width), F32),
            pltpu.VMEM((local, width), BF16),
            pltpu.VMEM((local, width), BF16),
            pltpu.SemaphoreType.DMA((9,)),
        ],
        compiler_params=params(15),
        cost_estimate=pl.CostEstimate(flops=1000, bytes_accessed=1000, transcendentals=0),
        name="mixed_back",
    )(scalars, ranks, dq, dk, dv, qkv_weight, resid_grad, own, other, marker)


def token_kernel(
    scalars, grad_ref, received_ref, text_kernel, patch_kernel, marker, out_ref, after_ref,
    text, patch, masks, lanes,
):
    side, fine = scalars[0], scalars[2]
    local, width = out_ref.shape
    groups = width // 128
    pad = GRID_HI + 2
    after_ref[...] = jnp.zeros(after_ref.shape, F32)
    rows = masks.shape[1]
    head = TEXT - local
    clear_pads(text, patch, pad)
    store_masks(masks, fine, rows)

    def load(low):
        for lane in range(groups):
            cols = slice(lane * 128, lane * 128 + 128)
            total = grad_ref[:, cols] + received_ref[:, cols].astype(F32)
            if low:
                text[lane, 8 : 8 + local + 8, :] = total
                text[lane, 16 + local : 8 + TEXT, :] = jnp.zeros((head - 8, 128), F32)
                patch[lane, pad : pad + rows, :] = jnp.zeros((rows, 128), F32)
            else:
                text[lane, 8 : local, :] = jnp.zeros((local - 8, 128), F32)
                text[lane, local : local + 8, :] = total[local:]
                text[lane, 8 + local : 8 + TEXT, :] = total[:head]
                patch[lane, pad : pad + rows, :] = total[head:local]

    pl.when(side == 0)(lambda: load(True))
    pl.when(side != 0)(lambda: load(False))

    def one_lane(lane, carry):
        mix_lane(text, patch, masks, lanes, lane, text_kernel, patch_kernel, fine, pad, True)
        return carry

    lax.fori_loop(0, groups, one_lane, 0)
    mine = pl.ds(pl.multiple_of(side * local, 8), local)
    for lane in range(groups):
        out_ref[:, lane * 128 : lane * 128 + 128] = lanes[lane, mine, :]


def token_back(scalars, grad, received, text_kernel, patch_kernel, seq, marker):
    local, width = grad.shape[0] - 8, grad.shape[1]
    groups = width // 128
    return pl.pallas_call(
        token_kernel,
        out_shape=(jax.ShapeDtypeStruct((local, width), F32), jax.ShapeDtypeStruct((8, 128), F32)),
        in_specs=[smem()] + [vmem()] * 4 + [anywhere()],
        out_specs=(vmem(), vmem()),
        scratch_shapes=[
            pltpu.VMEM((groups, TEXT + 16, 128), F32),
            pltpu.VMEM((groups, seq - TEXT + 2 * (GRID_HI + 2), 128), F32),
            pltpu.VMEM((9, seq - TEXT, 128), F32),
            pltpu.VMEM((groups, seq, 128), F32),
        ],
        compiler_params=params(9),
        cost_estimate=pl.CostEstimate(flops=1000, bytes_accessed=1000, transcendentals=0),
        name="token_back",
    )(scalars, grad, received, text_kernel, patch_kernel, marker)


def finish_kernel(scalars, kept_ref, received_ref, marker, grad_ref, after_ref):
    side = scalars[0]
    part = kept_ref.shape[1] // 3
    after_ref[...] = jnp.zeros(after_ref.shape, F32)
    for block in range(3):
        cols = slice(block * part, (block + 1) * part)
        mine = pl.ds(pl.multiple_of((2 * block + side) * part, 128), part)
        theirs = pl.ds(pl.multiple_of((2 * block + 1 - side) * part, 128), part)
        grad_ref[:, mine] = kept_ref[:, cols]
        grad_ref[:, theirs] = received_ref[:, cols].astype(F32)


def finish(scalars, kept, received, marker):
    return pl.pallas_call(
        finish_kernel,
        out_shape=(
            jax.ShapeDtypeStruct((kept.shape[0], 2 * kept.shape[1]), F32),
            jax.ShapeDtypeStruct((8, 128), F32),
        ),
        in_specs=[smem(), vmem(), vmem(), anywhere()],
        out_specs=(vmem(), vmem()),
        compiler_params=params(8),
        cost_estimate=pl.CostEstimate(flops=1000, bytes_accessed=1000, transcendentals=0),
        name="finish",
    )(scalars, kept, received, marker)


def finish_little_kernel(
    kept_ref, received_ref, marker, taps_ref, cells_ref, gains_ref, shifts_ref, down_ref, up_ref,
    rank_ref, box_ref, *, ratio, shared, heads,
):
    rows = taps_ref.shape[1]
    small = kept_ref[:rows, :] + received_ref[:rows, :]
    padded = jnp.concatenate([small, jnp.zeros((128 - rows, 128), F32)], axis=0)
    turned = padded.T
    taps_ref[...] = turned[0:9, :rows]
    cells_ref[...] = turned[16:25, :rows]
    gains_ref[...] = turned[32:34, :rows]
    shifts_ref[...] = turned[34:36, :rows]
    down_ref[...] = turned[36:37, :rows]
    row = lax.broadcasted_iota(jnp.int32, (rows, 128), 0)
    lane = lax.broadcasted_iota(jnp.int32, (rows, 128), 1)
    total = jnp.zeros((rows, 128), F32)
    for column in range(ratio):
        value = jnp.broadcast_to(small[:, 40 + column : 41 + column], (rows, 128))
        total = total + jnp.where(lane == row * ratio + column, value, 0.0)
    up_ref[...] = jnp.sum(total, axis=0, keepdims=True)[:, : rows * ratio]
    tables = kept_ref[kept_ref.shape[0] - shared :, :] + received_ref[received_ref.shape[0] - shared :, :]
    for head in range(2 * heads):
        row = head // heads * 16 + head % heads
        rank_ref[head : head + 1, :] = tables[row : row + 1, :NB1]
        box_ref[head, 0:1, :] = tables[row : row + 1, NB1 : NB1 + NB2]
        box_ref[head, 1:2, :] = tables[row + 8 : row + 9, :NB2]


def finish_little(kept, received, ratio, shared, heads, marker):
    rows = received.shape[0] - shared
    full = lambda *shape: jax.ShapeDtypeStruct(shape, F32)
    return pl.pallas_call(
        functools.partial(finish_little_kernel, ratio=ratio, shared=shared, heads=heads),
        out_shape=(
            full(9, rows), full(9, rows), full(2, rows), full(2, rows), full(1, rows),
            full(1, rows * ratio), full(2 * heads, NB1), full(2 * heads, 2, NB2),
        ),
        in_specs=[vmem(), vmem(), anywhere()],
        out_specs=(vmem(),) * 8,
        compiler_params=params(4),
        cost_estimate=pl.CostEstimate(flops=1000, bytes_accessed=1000, transcendentals=0),
        name="finish_little",
    )(kept, received, marker)


def swap(value, stage):
    axis, bit = stage
    count = lax.axis_size(axis)
    return lax.ppermute(value, axis, [(i, i ^ bit) for i in range(count)])


def stage_flag(stage):
    axis, bit = stage
    return (lax.axis_index(axis) & bit) // bit


def block_bit(block, stage, blk_count):
    axis, bit = stage
    shift = bit * blk_count if axis == "page" else bit
    return (block // shift) & 1


def spot_of(block, stages, blk_count):
    spot = jnp.zeros_like(block)
    for stage in stages:
        spot = spot * 2 + (block_bit(block, stage, blk_count) ^ stage_flag(stage))
    return spot


def order_matrix(width, stages, blk_count):
    count = lax.axis_size("page") * blk_count
    piece = width // count
    place = jnp.arange(width, dtype=jnp.int32)
    spot, inside = place // piece, place % piece
    block = jnp.zeros_like(spot)
    for depth, stage in enumerate(stages):
        axis, bit = stage
        shift = bit * blk_count if axis == "page" else bit
        value = ((spot >> (len(stages) - 1 - depth)) & 1) ^ stage_flag(stage)
        block = block + value * shift
    column = block * piece + inside
    return (column[:, None] == jnp.arange(width, dtype=jnp.int32)[None, :]).astype(BF16)


def add_up(terms):
    total = terms[0].astype(F32)
    for term in terms[1:]:
        total = total + term.astype(F32)
    return total


def halve_kernel(kept_ref, received_ref, marker, next_ref, send_ref, after_ref):
    rows = next_ref.shape[0]
    size = rows if rows % 48 else 48
    for start in range(0, rows, size):
        for base, ref in ((rows, send_ref), (0, next_ref)):
            if base % 16 or size % 16:
                place = slice(base + start, base + start + size)
                value = kept_ref[...].astype(F32)[place] + received_ref[...].astype(F32)[place]
            else:
                place = slice(base + start, base + start + size)
                value = kept_ref[place, :].astype(F32) + received_ref[place, :].astype(F32)
            ref[start : start + size, :] = value.astype(ref.dtype)
    after_ref[...] = jnp.zeros(after_ref.shape, F32)


def halve(kept, received, marker, flops=1000):
    rows, width = received.shape[0] // 2, received.shape[1]
    if rows % 8:
        total = kept.astype(F32) + received.astype(F32)
        return total[:rows], total[rows:].astype(BF16), marker
    return pl.pallas_call(
        halve_kernel,
        out_shape=(
            jax.ShapeDtypeStruct((rows, width), F32),
            jax.ShapeDtypeStruct((rows, width), BF16),
            jax.ShapeDtypeStruct((8, 128), F32),
        ),
        in_specs=[vmem(), vmem(), anywhere()],
        out_specs=(vmem(),) * 3,
        compiler_params=params(8),
        cost_estimate=pl.CostEstimate(flops=flops, bytes_accessed=1000, transcendentals=0),
        name="halve",
    )(kept, received, marker)


class Chain:
    def __init__(self, keep, send, stages):
        self.kept, self.stages, self.done = keep, stages, 0
        self.received = swap(send, stages[0])

    def turn(self, marker, flops=1000):
        self.done += 1
        if self.done >= len(self.stages):
            return marker
        self.kept, send, marker = halve(self.kept, self.received, marker, flops)
        self.received = swap(send, self.stages[self.done])
        return marker


def total_kernel(
    up_kept, up_received, out_kept, out_received, down_kept, down_received, marker,
    up_ref, out_ref, down_ref, after_ref,
):
    wide = out_kept.shape[1] - out_ref.shape[1]
    value = out_kept[...] + out_received[...].astype(F32)
    up_ref[:, :wide] = value[:, :wide]
    out_ref[...] = value[:, wide:]
    up_ref[:, wide:] = up_kept[...] + up_received[...].astype(F32)
    down_ref[...] = down_kept[...] + down_received[...].astype(F32)
    after_ref[...] = jnp.zeros(after_ref.shape, F32)


def total(up, out, down, marker):
    rows, width = up.kept.shape[0], down.kept.shape[1]
    full = lambda *shape: jax.ShapeDtypeStruct(shape, F32)
    return pl.pallas_call(
        total_kernel,
        out_shape=(
            full(rows, up.kept.shape[1] + out.kept.shape[1] - width), full(rows, width),
            full(*down.kept.shape), full(8, 128),
        ),
        in_specs=[vmem()] * 6 + [anywhere()],
        out_specs=(vmem(),) * 4,
        compiler_params=params(8),
        cost_estimate=pl.CostEstimate(flops=LONG, bytes_accessed=1000, transcendentals=0),
        name="total",
    )(up.kept, up.received, out.kept, out.received, down.kept, down.received, marker)


def little_kernel(now_ref, received_ref, marker, next_ref, message_ref, after_ref, *, shared):
    rows = received_ref.shape[0] - shared
    half = message_ref.shape[0] - shared
    common = now_ref[2 * rows :, :] + received_ref[rows:, :]
    kept = now_ref[:rows, :] + received_ref[:rows, :]
    next_ref[:rows, :] = kept
    next_ref[rows:, :] = common
    message_ref[:half, :] = kept[half:]
    message_ref[half:, :] = common
    after_ref[...] = jnp.zeros(after_ref.shape, F32)


class Little:
    def __init__(self, now, shared, stages):
        self.now, self.shared, self.stages, self.done = now, shared, stages, 0
        rows = (now.shape[0] - shared) // 2
        self.received = swap(now[rows:], stages[0])

    def turn(self, marker):
        self.done += 1
        if self.done > len(self.stages):
            return marker
        rows = self.received.shape[0] - self.shared
        if self.done == len(self.stages):
            return marker
        half = rows // 2
        if half % 8:
            kept = self.now[:rows] + self.received[:rows]
            common = self.now[2 * rows :] + self.received[rows:]
            self.now = jnp.concatenate([kept, common], axis=0)
            message = self.now[half:]
        else:
            lanes = self.now.shape[1]
            self.now, message, marker = pl.pallas_call(
                functools.partial(little_kernel, shared=self.shared),
                out_shape=(
                    jax.ShapeDtypeStruct((rows + self.shared, lanes), F32),
                    jax.ShapeDtypeStruct((half + self.shared, lanes), F32),
                    jax.ShapeDtypeStruct((8, 128), F32),
                ),
                in_specs=[vmem(), vmem(), anywhere()],
                out_specs=(vmem(),) * 3,
                compiler_params=params(4),
                cost_estimate=pl.CostEstimate(flops=1000, bytes_accessed=1000, transcendentals=0),
                name="little",
            )(self.now, self.received, marker)
        self.received = swap(message, self.stages[self.done])
        return marker


def gather_kernel(
    scalars, order_hbm, owner_hbm, inside_hbm, fold_hbm, rank_hbm, box_hbm, taps_hbm, cells_hbm, dense_hbm,
    blocks_hbm, sums_a, sums_b, sums_c, marker, out_ref, after_ref,
    order, owner, inside, fold, rank, box, taps, cells, dense_sums, blocks, sums, copies,
):
    fetches = fetch(
        [order_hbm, owner_hbm, inside_hbm, fold_hbm, rank_hbm, box_hbm, taps_hbm, cells_hbm,
         dense_hbm, blocks_hbm, sums_a, sums_b, sums_c],
        [order, owner, inside, fold, rank, box, taps, cells, dense_sums, blocks]
        + [sums.at[pl.ds(2 * n, 2)] for n in range(3)],
        copies,
    )
    for copy in fetches:
        copy.wait()
    after_ref[...] = jnp.zeros(after_ref.shape, F32)
    width = order.shape[0]

    rows = jnp.concatenate([taps[...], cells[...], dense_sums[...]], axis=0)
    rows = jnp.concatenate([rows, jnp.zeros((128 - rows.shape[0], width), F32)], axis=0)
    spread = dot_nn(owner[...], blocks[...].astype(BF16)) * inside[...].astype(F32)
    bias = dot_nn(spread.astype(BF16), fold[...]).astype(BF16)
    out_ref[:width, :] = dot_nt(order[...], rows.astype(BF16)) + dot_nn(order[...], bias)
    out_ref[width:, :] = jnp.zeros((32, 128), F32)
    heads = sums.shape[0]
    mine = pl.multiple_of(width + scalars[0] * 16, 16)
    pad = lambda value: jnp.concatenate([value, jnp.zeros((8 - heads, value.shape[1]), F32)], axis=0)
    by_rank = pad(jnp.concatenate([sums[head, 0:1, :] for head in range(heads)], axis=0))
    table = sum(dot_nn(piece, rank[...]) for piece in halves_of(by_rank))
    out_ref[pl.ds(mine, 8), 0:NB1] = table
    for half in range(2):
        by_box = pad(
            jnp.concatenate([sums[head, half + 1 : half + 2, : 2 * SPAN] for head in range(heads)], axis=0)
        )
        table = sum(dot_nn(piece, box[...]) for piece in halves_of(by_box))
        if half == 0:
            out_ref[pl.ds(mine, 8), NB1 : NB1 + NB2] = table
        else:
            out_ref[pl.ds(mine + 8, 8), 0:NB2] = table


def gather_small(scalars, order, taps, cells, dense_sums, blocks, sums, deep, marker):
    width = order.shape[0]
    devices = blocks.shape[0]
    ratio = deep // width
    piece = width // devices
    rows, lanes = np.arange(width), np.arange(128)
    owner = jnp.asarray(rows[:, None] // piece == np.arange(devices)[None, :], BF16)
    inside = jnp.asarray(
        (lanes[None, :] // ratio == rows[:, None] % piece) & (lanes[None, :] < piece * ratio), BF16
    )
    fold = jnp.asarray(lanes[:, None] % ratio + 40 == lanes[None, :], BF16)
    rank = jnp.asarray(bucket_rows(np.arange(RANK_LANES) - (RANK_MID - 1), rank_marks, NB1), BF16)
    box = jnp.asarray(bucket_rows(np.arange(2 * SPAN) - (SPAN - 1), box_marks, NB2), BF16)
    operands = (order, owner, inside, fold, rank, box, taps, cells, dense_sums, blocks)
    return pl.pallas_call(
        gather_kernel,
        out_shape=(
            jax.ShapeDtypeStruct((width + 32, 128), F32), jax.ShapeDtypeStruct((8, 128), F32)
        ),
        in_specs=[smem(), anywhere()] + [parameter()] * 5 + [anywhere()] * 8,
        out_specs=(vmem(), vmem()),
        scratch_shapes=[pltpu.VMEM(value.shape, value.dtype) for value in operands]
        + [pltpu.VMEM((2 * len(sums), 8, RANK_LANES), F32), pltpu.SemaphoreType.DMA((13,))],
        compiler_params=params(10),
        cost_estimate=pl.CostEstimate(flops=1000, bytes_accessed=1000, transcendentals=0),
        name="gather_small",
    )(scalars, *operands, *sums, marker)


def per_device(
    tokens,
    patch_count,
    reading_rank,
    boxes,
    text_kernel,
    patch_kernel,
    qkv_weight,
    rank_table,
    box_tables,
    out_weight,
    norm_gains,
    norm_shifts,
    up_weight,
    up_bias,
    down_weight,
    down_bias,
    cotangent,
):
    side = lax.axis_index("blk")
    blk_count = lax.axis_size("blk")
    page_stages = [("page", 1 << n) for n in range(lax.axis_size("page").bit_length() - 1)]
    across = ("blk", 1)
    out_stages = page_stages[:1] + [across] + page_stages[1:]
    up_stages = page_stages[:1] + page_stages[2:] + [across] + page_stages[1:2]
    down_stages = page_stages[:2] + [across] + page_stages[2:]
    qkv_stages = page_stages[:1] + page_stages[2:] + page_stages[1:2] + [across]
    little_stages = page_stages[:2] + [across] + page_stages[2:]
    devices = lax.axis_size("page") * blk_count
    count = patch_count[0]
    ranks = reading_rank
    own = tokens[0]
    local, width = own.shape
    deep = up_bias.shape[0]
    seq = ranks.shape[1]
    heads = HEADS // blk_count
    scalars = jnp.stack(
        [side, TEXT + count, (count == GRID_HI * GRID_HI).astype(jnp.int32), jnp.int32(0)]
    ).astype(jnp.int32)
    other = swap(own, across)

    xy, xyt, vectors = onehots(scalars, ranks, boxes, rank_table, box_tables, heads)
    mixed, mixed_low, packed = mix_and_project(
        scalars, ranks, own, other, text_kernel, patch_kernel, qkv_weight
    )
    pack = jnp.concatenate([norm_gains, norm_shifts, down_bias[None], up_bias.reshape(-1, width)], axis=0)
    own_context, other_context, shares = [], [], []
    for first, pairs in ((0, 2), (2, 1)):
        share, mine, theirs = attend(scalars, ranks, packed, xy, vectors, local, first, pairs)
        shares += [(share, place) for place in range(pairs)]
        own_context.append(mine)
        other_context.append(swap(theirs, across))
    order_qkv = order_matrix(width, qkv_stages, blk_count)
    order_little = order_matrix(width, little_stages, blk_count)
    turned, marker = turn_rows(order_qkv, mixed_low, own_context[-1])
    (
        layer_output, context, hidden_low, act_low, branch_grad, pre_grad, attend_grad,
        resid_one_grad, own_part, their_part, dense_sums, bias_blocks,
    ) = dense(
        scalars, mixed, own_context, other_context, pack, cotangent[0], out_weight, up_weight,
        down_weight, devices, marker,
    )
    part = width // blk_count
    received_part = swap(their_part, across)

    order_out = order_matrix(width, out_stages, blk_count)
    order_up = order_matrix(width, up_stages, blk_count)
    piece = deep // devices
    blocks = jnp.arange(devices, dtype=jnp.int32)
    spots = spot_of(blocks, down_stages, blk_count) * piece
    act_rows = act_low
    if piece % 16:
        place = jnp.arange(deep, dtype=jnp.int32)
        target = spots[place // piece] + place % piece
        act_rows = jnp.zeros_like(act_low).at[:, target].set(act_low, unique_indices=True)
        piece = width // 8
        spots = jnp.arange(deep // piece, dtype=jnp.int32) * piece
    steps = deep // width
    split = steps // 2
    down_keep, down_send = down_weight_grad(spots, act_rows, branch_grad, piece)
    down = Chain(down_keep, down_send, down_stages)
    out_keep, out_send, up_keep, up_send = up_weight_grads_of(
        pre_grad, hidden_low, context, attend_grad, order_out, order_up, split, down_keep
    )
    out = Chain(out_keep, out_send, out_stages)
    up = Chain(up_keep, up_send, up_stages)
    marker = down.turn(up_send)

    grads, sums = None, []
    for pair, (share, place) in enumerate(shares):
        if pair == 1:
            marker = up.turn(out.turn(sums[0]))
        *grads, pair_sums = attend_back(
            scalars, ranks, own_part, received_part, share, packed, xy, xyt, pair, place, grads,
            marker if pair < 2 else None,
        )
        sums.append(pair_sums)
    dq, dk, dv = grads
    qkv_keep, qkv_send, marker = project_weight_grad(turned, dq, dk, dv, sums[-1])
    qkv = Chain(qkv_keep, qkv_send, qkv_stages)
    marker = down.turn(out.turn(up.turn(marker)), LONG)
    marker = qkv.turn(marker)
    grad, outgoing, taps, cells = mixed_back(
        scalars, ranks, dq, dk, dv, qkv_weight, resid_one_grad, own, other, marker
    )
    incoming = swap(outgoing, across)
    gathered, marker = gather_small(
        scalars, order_little, taps, cells, dense_sums, bias_blocks, sums, deep, taps
    )
    little = Little(gathered, 32, little_stages)
    for chain in (qkv, up, out, down, little, little):
        marker = chain.turn(marker)
    token_grad, marker = token_back(
        scalars, grad, incoming, text_kernel, patch_kernel, seq, marker
    )
    for _ in range(len(qkv_stages) - 4):
        for chain in (qkv, little, up, out, down):
            marker = chain.turn(marker)
    marker = little.turn(qkv.turn(marker))
    up_weight_grads, out_weight_grads, down_weight_grads, marker = total(up, out, down, marker)
    for _ in qkv_stages:
        marker = little.turn(qkv.turn(marker))
    qkv_weight_grad, marker = finish(scalars, qkv.kept, qkv.received, marker)
    taps, cells, gains, shifts, down_bias_grad, up_bias_grad, rank_grad, box_grad = finish_little(
        little.now, little.received, steps, 32, heads, marker
    )
    return (
        layer_output[None],
        token_grad[None],
        taps,
        cells,
        qkv_weight_grad,
        rank_grad,
        jnp.swapaxes(box_grad, 0, 1),
        out_weight_grads,
        gains,
        shifts,
        up_weight_grads,
        up_bias_grad[0],
        down_weight_grads,
        down_bias_grad[0],
    )


def solution(mesh):
    in_specs = (
        P("page", "blk", None),
        P("page"),
        P("page", None),
        P(None, "page", None),
        P(),
        P(),
        P(),
        P(),
        P(),
        P(),
        P(),
        P(),
        P(),
        P(),
        P(),
        P(),
        P("page", "blk", None),
    )
    out_specs = (
        P("page", "blk", None),
        P("page", "blk", None),
        P(None, ("page", "blk")),
        P(None, ("page", "blk")),
        P(("page", "blk"), None),
        P(),
        P(),
        P(("page", "blk"), None),
        P(None, ("page", "blk")),
        P(None, ("page", "blk")),
        P(("page", "blk"), None),
        P(("page", "blk")),
        P(("page", "blk"), None),
        P(("page", "blk")),
    )
    return jax.shard_map(
        per_device, mesh=mesh, in_specs=in_specs, out_specs=out_specs, check_vma=False
    )
```

```python
import functools

import jax
import jax.numpy as jnp
import numpy as np
from jax import lax
from jax.experimental import pallas as pl
from jax.experimental.pallas import tpu as pltpu
from jax.sharding import PartitionSpec as P

TEXT = 512
GRID_LO = 7
GRID_HI = 14
RUN = 16
HEADS = 12
HEAD_DIM = 64
NB1 = 32
NB2 = 64
SPAN = 256
RANK_LANES = 1536
RANK_MID = RANK_LANES // 2
ROWS = 128
F32 = jnp.float32
BF16 = jnp.bfloat16
MIB = 1 << 20
LONG = 10**11

rank_marks = (1, 2, 3, 4, 5, 6, 7, 8, 12, 16, 23, 32, 46, 64, 91)
box_marks = tuple(range(1, 17)) + (19, 23, 27, 32, 39, 46, 54, 64, 77, 91, 108, 128, 153, 182, 216)
neg_fill = -1000000000.0
norm_eps = 1e-05
root_half = 0.7071067811865476
inv_root_tau = 0.3989422804014327
tap_list = ((1, -1), (1, 0), (1, 1), (2, -1), (2, 0), (2, 1), (3, -1), (3, 0), (3, 1))
cell_list = ((-1, -1), (-1, 0), (-1, 1), (0, -1), (0, 0), (0, 1), (1, -1), (1, 0), (1, 1))


def bucket_rows(deltas, marks, bins):
    spread = np.abs(deltas)
    ids = np.sum(spread[:, None] >= np.asarray(marks)[None, :], axis=1) + (bins // 2) * (deltas > 0)
    return (ids[:, None] == np.arange(bins)[None, :]).astype(np.float32)


def dot_nn(left, right):
    return lax.dot_general(left, right, (((1,), (0,)), ((), ())), preferred_element_type=F32)


def dot_nt(left, right):
    return lax.dot_general(left, right, (((1,), (1,)), ((), ())), preferred_element_type=F32)


def dot_tn(left, right):
    return lax.dot_general(left, right, (((0,), (0,)), ((), ())), preferred_element_type=F32)


def row_chunks(total, size):
    return [(start, min(size, total - start)) for start in range(0, total, size)]


def vmem():
    return pl.BlockSpec(memory_space=pltpu.VMEM)


def smem():
    return pl.BlockSpec(memory_space=pltpu.SMEM)


def anywhere():
    return pl.BlockSpec(memory_space=pl.ANY)


def parameter():
    return pl.BlockSpec(memory_space=pltpu.HBM)


def stay(value):
    return pltpu.with_memory_space_constraint(value, pltpu.HBM)


def fetch(sources, targets, semaphores):
    copies = []
    for number, (source, target) in enumerate(zip(sources, targets)):
        copies.append(pltpu.make_async_copy(source, target, semaphores.at[number]))
        copies[-1].start()
    return copies


def params(mib):
    return pltpu.CompilerParams(vmem_limit_bytes=mib * MIB)


def onehot_kernel(
    scalars, rank_hbm, box_hbm, rank_table_hbm, box_tables_hbm, rank_rows_hbm, box_rows_hbm,
    xy_ref, xyt_ref, rank_bias, box_bias,
    rank_ref, box_ref, rank_table, box_tables, rank_rows, box_rows, vectors, copies,
):
    fetches = fetch(
        [rank_hbm, box_hbm, rank_table_hbm, box_tables_hbm, rank_rows_hbm, box_rows_hbm],
        [rank_ref, box_ref, rank_table, box_tables, rank_rows, box_rows],
        copies,
    )
    for copy in fetches:
        copy.wait()
    seq = rank_ref.shape[1]
    for start, size in row_chunks(seq, 240):
        spot = lax.broadcasted_iota(jnp.int32, (size, seq), 0) + start
        order = (spot == rank_ref[...]).astype(F32).astype(BF16)
        for half in range(2):
            level = lax.broadcasted_iota(jnp.int32, (SPAN, seq), 0)
            marks = (level == box_ref[half]).astype(F32).astype(BF16)
            xy_ref[start : start + size, half * SPAN : (half + 1) * SPAN] = dot_nt(
                order, marks
            ).astype(BF16)
    row = lax.broadcasted_iota(jnp.int32, (SPAN, SPAN), 0)
    col = lax.broadcasted_iota(jnp.int32, (SPAN, SPAN), 1)
    flip = (row + col == SPAN - 1).astype(F32).astype(BF16)
    for half in range(2):
        part = slice(half * SPAN, (half + 1) * SPAN)
        xyt_ref[part, :] = dot_nt(flip, xy_ref[:, part]).astype(BF16)
    heads = vectors.shape[0]
    tables = [(dot_nt(rank_table[...], rank_rows[...]), RANK_LANES)]
    tables += [(dot_nt(box_tables[half], box_rows[...]), 2 * SPAN) for half in range(2)]
    for place, (table, lanes) in enumerate(tables):
        own = jnp.where(scalars[0] == 0, table[:heads], table[table.shape[0] - heads :])
        for head in range(heads):
            vectors[head, place : place + 1, :lanes] = own[head : head + 1]

    def one_head(head, carry):
        rank_bias[head] = skewed(vectors[head, 0:1, :], ROWS, RANK_LANES, RANK_LANES - 128)
        for half in range(2):
            part = slice(half * SPAN, (half + 1) * SPAN)
            table = skewed(vectors[head, half + 1 : half + 2, : 2 * SPAN], SPAN, 2 * SPAN, SPAN + 1)
            box_bias[head, :, part] = dot_nn(xy_ref[:, part], table[:, :SPAN].astype(BF16)).astype(BF16)
        return carry

    lax.fori_loop(0, heads, one_head, 0)


def onehots(scalars, ranks, boxes, rank_table, box_tables, heads):
    seq = ranks.shape[1]
    rank_rows = jnp.asarray(bucket_rows(np.arange(RANK_LANES) - RANK_MID, rank_marks, NB1), BF16)
    box_rows = jnp.asarray(bucket_rows(SPAN - 1 - np.arange(2 * SPAN), box_marks, NB2), BF16)
    operands = tuple(map(stay, (ranks, boxes, rank_table, box_tables, rank_rows, box_rows)))
    return pl.pallas_call(
        onehot_kernel,
        out_shape=(
            jax.ShapeDtypeStruct((seq, 2 * SPAN), BF16),
            jax.ShapeDtypeStruct((2 * SPAN, seq), BF16),
            jax.ShapeDtypeStruct((heads, ROWS, RANK_LANES), F32),
            jax.ShapeDtypeStruct((heads, seq, 2 * SPAN), BF16),
        ),
        in_specs=[smem()] + [parameter()] * 6,
        out_specs=(vmem(),) * 4,
        scratch_shapes=[pltpu.VMEM(value.shape, value.dtype) for value in operands]
        + [pltpu.VMEM((heads, 8, RANK_LANES), F32), pltpu.SemaphoreType.DMA((6,))],
        compiler_params=params(14),
        cost_estimate=pl.CostEstimate(
            flops=4 * seq * seq * SPAN, bytes_accessed=4 * seq * 2 * SPAN, transcendentals=0
        ),
        name="onehots",
    )(scalars, *operands)


def place_slots(own_ref, other_ref, side, text, patch, patch_pad):
    local = own_ref.shape[0]
    head = TEXT - local
    groups = text.shape[0]

    def place(low_ref, high_ref):
        for lane in range(groups):
            cols = slice(128 * lane, 128 * lane + 128)
            text[lane, 8 : 8 + local, :] = low_ref[:, cols].astype(F32)
            high = high_ref[:, cols].astype(F32)
            text[lane, 8 + local : 8 + TEXT, :] = high[:head]
            patch[lane, patch_pad : patch_pad + local - head, :] = high[head:]

    pl.when(side == 0)(lambda: place(own_ref, other_ref))
    pl.when(side != 0)(lambda: place(other_ref, own_ref))


def clear_pads(text, patch, patch_pad):
    groups, rows = patch.shape[0], patch.shape[1]
    for lane in range(groups):
        text[lane, 0:8, :] = jnp.zeros((8, 128), F32)
        text[lane, 8 + TEXT : 16 + TEXT, :] = jnp.zeros((8, 128), F32)
        patch[lane, 0:patch_pad, :] = jnp.zeros((patch_pad, 128), F32)
        patch[lane, rows - patch_pad : rows, :] = jnp.zeros((patch_pad, 128), F32)


def cell_masks(grid, rows):
    slot = lax.broadcasted_iota(jnp.int32, (rows, 128), 0)
    row_of = jnp.zeros((rows, 128), jnp.int32)
    for line in range(1, grid):
        row_of = row_of + (slot >= line * grid).astype(jnp.int32)
    column = slot - row_of * grid
    alive = slot < grid * grid
    masks = []
    for down, across in cell_list:
        masks.append(
            alive
            & (row_of + down >= 0)
            & (row_of + down < grid)
            & (column + across >= 0)
            & (column + across < grid)
        )
    return masks


def store_masks(masks, fine, rows):
    for grid, chosen in ((GRID_HI, fine != 0), (GRID_LO, fine == 0)):

        def fill(grid=grid):
            for number, mask in enumerate(cell_masks(grid, rows)):
                masks[number] = mask.astype(F32)

        pl.when(chosen)(fill)


def mix_lane(text, patch, masks, out, lane, text_kernel, patch_kernel, fine, patch_pad, flip):
    cols = pl.ds(pl.multiple_of(lane * 128, 128), 128)
    taps = {}
    for number, (reach, side) in enumerate(tap_list):
        offset = -reach * side if flip else reach * side
        value = text_kernel[number : number + 1, cols]
        taps[offset] = taps[offset] + value if offset in taps else value
    for start, size in row_chunks(TEXT, ROWS):
        total = text[lane, pl.ds(8 + start, size), :] * (1.0 + taps[0])
        for offset, value in taps.items():
            if offset:
                total = total + text[lane, pl.ds(8 + start + offset, size), :] * value
        out[lane, pl.ds(start, size), :] = total
    rows = masks.shape[1]
    for grid, chosen in ((GRID_HI, fine != 0), (GRID_LO, fine == 0)):

        def cells(grid=grid):
            for start, size in row_chunks(rows, 104):
                total = patch[lane, pl.ds(patch_pad + start, size), :]
                for number, (down, across) in enumerate(cell_list):
                    tap = len(cell_list) - 1 - number if flip else number
                    moved = patch[lane, pl.ds(patch_pad + start + down * grid + across, size), :]
                    total = total + (
                        moved * masks[number, pl.ds(start, size), :]
                    ) * patch_kernel[tap : tap + 1, cols]
                out[lane, pl.ds(TEXT + start, size), :] = total

        pl.when(chosen)(cells)


def sort_rows(ranks_ref, source, target, seq, cast):
    for run in range(TEXT // RUN):
        spot = pl.multiple_of(ranks_ref[0, run * RUN], RUN)
        target[pl.ds(spot, RUN), :] = source[run * RUN : (run + 1) * RUN, :].astype(cast)
    target[TEXT:seq, :] = source[TEXT:seq, :].astype(cast)


def unsort_rows(ranks_ref, source, target, seq):
    for run in range(TEXT // RUN):
        spot = pl.multiple_of(ranks_ref[0, run * RUN], RUN)
        target[run * RUN : (run + 1) * RUN, :] = source[pl.ds(spot, RUN), :]
    target[TEXT:seq, :] = source[TEXT:seq, :]


def mix_kernel(
    scalars, ranks_ref, own_ref, other_ref, text_kernel, patch_kernel, weight_ref,
    mixed_ref, low_ref, packed_ref, text, patch, masks, lanes, whole, weights, copies,
):
    side, fine = scalars[0], scalars[2]
    local, width = own_ref.shape
    seq = low_ref.shape[0]
    groups = width // 128
    pad = GRID_HI + 2
    part = width // 2
    fetches = fetch(
        [
            weight_ref.at[:, pl.ds(pl.multiple_of(block * width + side * part, 128), part)]
            for block in range(3)
        ],
        [weights.at[block] for block in range(3)],
        copies,
    )
    place_slots(own_ref, other_ref, side, text, patch, pad)
    clear_pads(text, patch, pad)
    store_masks(masks, fine, seq - TEXT)

    def one_lane(lane, carry):
        mix_lane(text, patch, masks, lanes, lane, text_kernel, patch_kernel, fine, pad, False)
        return carry

    lax.fori_loop(0, groups, one_lane, 0)
    for lane in range(groups):
        whole[:, 128 * lane : 128 * lane + 128] = lanes[lane]
    mixed_ref[...] = whole[pl.ds(pl.multiple_of(side * local, 8), local), :]
    sort_rows(ranks_ref, whole, low_ref, seq, BF16)
    for block in range(3):
        fetches[block].wait()
        for start, size in row_chunks(seq, 240):
            value = dot_nn(low_ref[start : start + size, :], weights[block]).astype(BF16)
            if block == 0:
                value = value * (HEAD_DIM**-0.5)
            packed_ref[start : start + size, block * part : (block + 1) * part] = value


def mix_and_project(scalars, ranks, own, other, text_kernel, patch_kernel, qkv_weight):
    local, width = own.shape
    seq = ranks.shape[1]
    groups = width // 128
    return pl.pallas_call(
        mix_kernel,
        out_shape=(
            jax.ShapeDtypeStruct((local, width), F32),
            jax.ShapeDtypeStruct((seq, width), BF16),
            jax.ShapeDtypeStruct((seq, 3 * width // 2), BF16),
        ),
        in_specs=[smem(), smem()] + [vmem()] * 4 + [parameter()],
        out_specs=(vmem(),) * 3,
        scratch_shapes=[
            pltpu.VMEM((groups, TEXT + 16, 128), F32),
            pltpu.VMEM((groups, seq - TEXT + 2 * (GRID_HI + 2), 128), F32),
            pltpu.VMEM((9, seq - TEXT, 128), F32),
            pltpu.VMEM((groups, seq, 128), F32),
            pltpu.VMEM((seq, width), F32),
            pltpu.VMEM((3, width, width // 2), BF16),
            pltpu.SemaphoreType.DMA((3,)),
        ],
        compiler_params=params(16),
        cost_estimate=pl.CostEstimate(
            flops=2 * seq * width * 3 * width // 2, bytes_accessed=12 * MIB, transcendentals=0
        ),
        name="mix_and_project",
    )(scalars, ranks, own, other, text_kernel, patch_kernel, qkv_weight)


def head_lanes(shape, parity):
    return (lax.broadcasted_iota(jnp.int32, shape, 1) >= HEAD_DIM) == (parity != 0)


def skewed(vector, rows, lanes, shift):
    return pltpu.roll(jnp.broadcast_to(vector, (rows, lanes)), shift, 1, stride=1, stride_axis=0)


def attend_kernel(
    scalars, ranks_ref, queries, keys, values, xy_ref, rank_bias, box_bias,
    shares_ref, own_ref, other_ref, left, right, gathered, slots, scores_ref,
):
    side, live = scalars[0], scalars[1]
    seq = queries.shape[0]
    local = own_ref.shape[0]
    head = pl.program_id(0)
    parity = lax.rem(head, 2)

    @pl.when(head == 0)
    def _():
        left[:, 128:] = xy_ref[...]

    left[:, :128] = queries[...]
    mine = head_lanes((seq, 128), parity)
    right[:, :128] = jnp.where(mine, keys[...], jnp.zeros((), BF16))
    right[:, 128:] = box_bias[0]
    top = (seq // ROWS) * ROWS
    alive = lax.broadcasted_iota(jnp.int32, (16, seq), 1) < live
    chunks = row_chunks(seq, 240)

    def product(start, size):
        scores_ref[start : start + size, :] = dot_nt(left[start : start + size, :], right[...])

    def soften(start, size):
        for first in range(start, start + size, 16):
            base = first // ROWS * ROWS
            scores = scores_ref[first : first + 16, :]
            scores = scores + rank_bias[0, first - base : first - base + 16, top - base : top - base + seq]
            scores = jnp.where(alive, scores, neg_fill)
            powered = jnp.exp(scores - jnp.max(scores, axis=1, keepdims=True))
            shares = powered * (1.0 / jnp.sum(powered, axis=1, keepdims=True))
            shares_ref[0, first : first + 16, :] = shares.astype(BF16)

    def apply(start, size):
        context = dot_nn(shares_ref[0, start : start + size, :], values[...])
        gathered[start : start + size, :] = jnp.where(
            head_lanes((size, 128), parity), context, gathered[start : start + size, :]
        )

    product(*chunks[0])
    for n in range(len(chunks)):
        if n + 1 < len(chunks):
            product(*chunks[n + 1])
        if n:
            apply(*chunks[n - 1])
        soften(*chunks[n])
    apply(*chunks[-1])

    @pl.when(parity == 1)
    def _():
        unsort_rows(ranks_ref, gathered, slots, seq)
        own_ref[...] = slots[pl.ds(pl.multiple_of(side * local, 8), local), :].astype(BF16)
        other_ref[...] = slots[pl.ds(pl.multiple_of((1 - side) * local, 8), local), :].astype(BF16)


def attend(scalars, ranks, packed, xy, rank_bias, box_bias, local, first, count):
    seq = packed.shape[0]
    pairs = rank_bias.shape[0] // 2
    heads = 2 * count
    width = heads * HEAD_DIM
    whole = pl.BlockSpec((seq, 2 * SPAN), lambda h: (0, 0))
    slot_spec = pl.BlockSpec((local, 128), lambda h: (0, h // 2))
    return pl.pallas_call(
        attend_kernel,
        grid=(heads,),
        out_shape=(
            jax.ShapeDtypeStruct((heads, seq, seq), BF16),
            jax.ShapeDtypeStruct((local, width), BF16),
            jax.ShapeDtypeStruct((local, width), BF16),
        ),
        in_specs=[
            smem(),
            smem(),
            pl.BlockSpec((seq, 128), lambda h: (0, first + h // 2)),
            pl.BlockSpec((seq, 128), lambda h: (0, pairs + first + h // 2)),
            pl.BlockSpec((seq, 128), lambda h: (0, 2 * pairs + first + h // 2)),
            whole,
            pl.BlockSpec((1, ROWS, RANK_LANES), lambda h: (2 * first + h, 0, 0)),
            pl.BlockSpec((1, seq, 2 * SPAN), lambda h: (2 * first + h, 0, 0)),
        ],
        out_specs=(pl.BlockSpec((1, seq, seq), lambda h: (h, 0, 0)), slot_spec, slot_spec),
        scratch_shapes=[
            pltpu.VMEM((seq, 128 + 2 * SPAN), BF16),
            pltpu.VMEM((seq, 128 + 2 * SPAN), BF16),
            pltpu.VMEM((seq, 128), F32),
            pltpu.VMEM((seq, 128), F32),
            pltpu.VMEM((seq, seq), F32),
        ],
        compiler_params=params(13),
        cost_estimate=pl.CostEstimate(
            flops=heads * 2 * seq * seq * 1024, bytes_accessed=heads * seq * seq * 2,
            transcendentals=heads * seq * seq,
        ),
        name="attend",
    )(scalars, ranks, packed, packed, packed, xy, rank_bias, box_bias)


def attend_back_kernel(
    ranks_ref, own_ref, other_ref, side_ref, shares_ref, queries, keys, values, xy_ref, xyt_ref,
    dq_ref, dk_ref, dv_ref, sums_ref, right, score_grad, spread, rank_sum, slots, upstream, share_grads,
):
    seq = queries.shape[0]
    local = own_ref.shape[0]
    side = side_ref[0]
    head = pl.program_id(0)
    parity = lax.rem(head, 2)
    scale = HEAD_DIM**-0.5

    @pl.when(head == 0)
    def _():
        right[:, 128:] = xy_ref[...]

    @pl.when(parity == 0)
    def _():
        slots[pl.ds(pl.multiple_of(side * local, 8), local), :] = own_ref[...].astype(F32)
        slots[pl.ds(pl.multiple_of((1 - side) * local, 8), local), :] = other_ref[...].astype(F32)
        sort_rows(ranks_ref, slots, upstream, seq, BF16)

    right[:, :128] = keys[...]
    mine = head_lanes((seq, 128), parity)
    own_values = jnp.where(mine, values[...], jnp.zeros((), BF16))
    rank_sum[...] = jnp.zeros(rank_sum.shape, F32)
    top = (seq // ROWS) * ROWS
    chunks = row_chunks(seq, 240)

    def product(start, size):
        share_grads[start : start + size, :] = dot_nt(upstream[start : start + size, :], own_values)

    def soften(start, size):
        for first in range(start, start + size, 16):
            base = first // ROWS * ROWS
            rows = slice(first, first + 16)
            shares = shares_ref[0, rows, :].astype(F32)
            weighted = shares * share_grads[rows, :]
            low = (weighted - shares * jnp.sum(weighted, axis=1, keepdims=True)).astype(BF16)
            score_grad[rows, :] = low
            place = (slice(first - base, first - base + 16), slice(top - base, top - base + seq))
            rank_sum[place] = rank_sum[place] + low.astype(F32)

    def apply(start, size):
        rows = slice(start, start + size)
        product = dot_nn(score_grad[rows, :], right[...])
        spread[rows, :] = product[:, 128:].astype(BF16)
        dq_ref[rows, :] = jnp.where(
            head_lanes((size, 128), parity), (product[:, :128] * scale).astype(BF16), dq_ref[rows, :]
        )

    product(*chunks[0])
    for n in range(len(chunks)):
        if n + 1 < len(chunks):
            product(*chunks[n + 1])
        if n:
            apply(*chunks[n - 1])
        soften(*chunks[n])
    apply(*chunks[-1])
    dk = dot_tn(score_grad[...], queries[...]).astype(BF16)
    dk_ref[...] = jnp.where(mine, dk, dk_ref[...])
    dv = dot_tn(shares_ref[0], upstream[...]).astype(BF16)
    dv_ref[...] = jnp.where(mine, dv, dv_ref[...])
    row = lax.broadcasted_iota(jnp.int32, (ROWS, ROWS), 0)
    col = lax.broadcasted_iota(jnp.int32, (ROWS, ROWS), 1)
    flip = (row + col == ROWS - 1).astype(F32).astype(BF16)
    high = rank_sum[...].astype(BF16)
    rest = (rank_sum[...] - high.astype(F32)).astype(BF16)
    turned = dot_nn(flip, high) + dot_nn(flip, rest)
    turned = pltpu.roll(turned, 0, 1, stride=1, stride_axis=0)
    sums_ref[0, 0:1, :] = jnp.sum(turned, axis=0, keepdims=True)
    for half in range(2):
        part = slice(half * SPAN, (half + 1) * SPAN)
        table = dot_nn(xyt_ref[part, :], spread[:, part])
        table = jnp.concatenate([table, jnp.zeros((SPAN, SPAN), F32)], axis=1)
        table = pltpu.roll(table, 0, 1, stride=1, stride_axis=0)
        sums_ref[0, half + 1 : half + 2, : 2 * SPAN] = jnp.sum(table, axis=0, keepdims=True)


def attend_back(scalars, ranks, own, other, shares, packed, xy, xyt, pair, place, so_far, marker):
    seq = packed.shape[0]
    local = own.shape[0]
    width = packed.shape[1] // 3
    pairs = width // 128
    slot_spec = pl.BlockSpec((local, 128), lambda h: (0, pair))
    out_spec = pl.BlockSpec((seq, 128), lambda h: (0, pair))
    so_far = tuple(so_far) if so_far else ()
    extra = so_far + ((marker,) if marker is not None else ())

    def body(*refs):
        ins, rest = refs[:10], refs[10 + len(extra) :]
        attend_back_kernel(*ins, *rest)

    return pl.pallas_call(
        body,
        grid=(2,),
        out_shape=(jax.ShapeDtypeStruct((seq, width), BF16),) * 3
        + (jax.ShapeDtypeStruct((2, 8, RANK_LANES), F32),),
        in_specs=[
            smem(),
            slot_spec,
            slot_spec,
            smem(),
            pl.BlockSpec((1, seq, seq), lambda h: (2 * place + h, 0, 0)),
            pl.BlockSpec((seq, 128), lambda h: (0, pair)),
            pl.BlockSpec((seq, 128), lambda h: (0, pairs + pair)),
            pl.BlockSpec((seq, 128), lambda h: (0, 2 * pairs + pair)),
            pl.BlockSpec((seq, 2 * SPAN), lambda h: (0, 0)),
            pl.BlockSpec((2 * SPAN, seq), lambda h: (0, 0)),
        ]
        + [anywhere()] * len(extra),
        out_specs=(out_spec,) * 3 + (pl.BlockSpec((1, 8, RANK_LANES), lambda h: (h, 0, 0)),),
        scratch_shapes=[
            pltpu.VMEM((seq, 128 + 2 * SPAN), BF16),
            pltpu.VMEM((seq, seq), BF16),
            pltpu.VMEM((seq, 2 * SPAN), BF16),
            pltpu.VMEM((ROWS, RANK_LANES), F32),
            pltpu.VMEM((seq, 128), F32),
            pltpu.VMEM((seq, 128), BF16),
            pltpu.VMEM((seq, seq), F32),
        ],
        input_output_aliases={10 + n: n for n in range(len(so_far))},
        compiler_params=params(15),
        cost_estimate=pl.CostEstimate(
            flops=1000 if pair else LONG, bytes_accessed=1000, transcendentals=0
        ),
        name="attend_back",
    )(ranks, own, other, scalars, shares, packed, packed, packed, xy, xyt, *extra)


def fold_rows(value):
    total = value[0:8]
    for start in range(8, value.shape[0], 8):
        total = total + value[start : start + 8]
    return total


def row_mean(value):
    return jnp.sum(value, axis=1, keepdims=True) * (1.0 / value.shape[1])


def normalize(value):
    center = value - row_mean(value)
    inverse = lax.rsqrt(row_mean(center * center) + norm_eps)
    return center * inverse, inverse


def dense_kernel(
    scalars, mixed_ref, own_a, own_b, other_a, other_b, pack, cot_ref, out_hbm, up_hbm, down_hbm, marker,
    result_ref, context_ref, hidden_ref, act_ref, branch_ref, pre_ref, attend_ref, resid_ref,
    own_grad, other_grad, sums_ref, blocks_ref,
    out_w, up_w, down_w, slope, product, stash, hidden, normed, scale, bias_sums_ref, copies,
):
    side, live = scalars[0], scalars[1]
    local, width = mixed_ref.shape
    deep = act_ref.shape[1]
    part = own_grad.shape[1]
    step = width // 2
    blocks = deep // step
    gains, shifts, down_bias = pack.at[0:2], pack.at[2:4], pack.at[4:5]
    fetches = [pltpu.make_async_copy(out_hbm, out_w, copies.at[0])]
    fetches += [
        pltpu.make_async_copy(
            up_hbm.at[:, n * width : (n + 1) * width], up_w.at[:, n * width : (n + 1) * width],
            copies.at[1 + n],
        )
        for n in range(deep // width)
    ]
    fetches.append(pltpu.make_async_copy(down_hbm, down_w, copies.at[1 + deep // width]))
    for fetch in fetches:
        fetch.start()
    wide = own_a.shape[1]
    for base, (first, second) in ((side * part, (own_a, own_b)), ((1 - side) * part, (other_a, other_b))):
        context_ref[:, pl.ds(pl.multiple_of(base, 128), wide)] = first[...]
        context_ref[:, pl.ds(pl.multiple_of(base + wide, 128), part - wide)] = second[...]
    chunks = row_chunks(local, 24)
    fetches[0].wait()
    product[...] = dot_nn(context_ref[...], out_w[...])
    for start, size in chunks:
        rows = slice(start, start + size)
        value, inverse = normalize(mixed_ref[rows, :] + product[rows, :])
        normed[rows, :] = value
        scale[rows, :] = jnp.broadcast_to(inverse, (size, 128))
        value = value * gains[0:1, :] + shifts[0:1, :]
        hidden[rows, :] = value
        hidden_ref[rows, :] = value.astype(BF16)

    def lift(block):
        if block % 2 == 0:
            fetches[1 + block // 2].wait()
        cols = slice(block * step, (block + 1) * step)
        stash[block % 2] = dot_nn(hidden_ref[...], up_w[:, cols])

    def bend(block):
        cols = slice(block * step, (block + 1) * step)
        half_cols = slice(block % 2 * step, (block % 2 + 1) * step)
        for start, size in chunks:
            rows = slice(start, start + size)
            value = stash[block % 2, rows, :] + pack[5 + block // 2 : 6 + block // 2, half_cols]
            half = 0.5 + 0.5 * lax.erf(value * root_half)
            act_ref[rows, cols] = (value * half).astype(BF16)
            slope[rows, cols] = half + value * jnp.exp(-0.5 * value * value) * inv_root_tau

    lift(0)
    for block in range(blocks):
        if block + 1 < blocks:
            lift(block + 1)
        bend(block)
    fetches[-1].wait()
    product[...] = dot_nn(act_ref[...], down_w[...])
    zero = jnp.zeros((8, width), F32)
    gain_sum, shift_sum, bias_sum = zero, zero, zero
    for start, size in chunks:
        rows = slice(start, start + size)
        value, inverse = normalize(hidden[rows, :] + product[rows, :] + down_bias[...])
        slot = lax.broadcasted_iota(jnp.int32, (size, width), 0) + (side * local + start)
        alive = (slot < live).astype(F32)
        result_ref[rows, :] = (alive * (value * gains[1:2, :] + shifts[1:2, :])).astype(BF16)
        upstream = cot_ref[rows, :].astype(F32) * alive
        gain_sum = gain_sum + fold_rows(upstream * value)
        shift_sum = shift_sum + fold_rows(upstream)
        scaled = upstream * gains[1:2, :]
        grad = inverse * (scaled - row_mean(scaled) - value * row_mean(scaled * value))
        bias_sum = bias_sum + fold_rows(grad)
        hidden[rows, :] = grad
        branch_ref[rows, :] = grad.astype(BF16)
    sums_ref[1:2, :] = jnp.sum(gain_sum, axis=0, keepdims=True)
    sums_ref[3:4, :] = jnp.sum(shift_sum, axis=0, keepdims=True)
    sums_ref[4:5, :] = jnp.sum(bias_sum, axis=0, keepdims=True)
    sums_ref[5:8, :] = jnp.zeros((3, width), F32)

    def lower(block):
        cols = slice(block * step, (block + 1) * step)
        stash[block % 2] = dot_nt(branch_ref[...], down_w[cols, :])

    def unbend(block):
        cols = slice(block * step, (block + 1) * step)
        total = jnp.zeros((8, step), F32)
        for start, size in chunks:
            rows = slice(start, start + size)
            value = (stash[block % 2, rows, :] * slope[rows, cols]).astype(BF16)
            pre_ref[rows, cols] = value
            total = total + fold_rows(value.astype(F32))
        bias_sums_ref[:, cols] = jnp.sum(total, axis=0, keepdims=True)

    lower(0)
    for block in range(blocks):
        if block + 1 < blocks:
            lower(block + 1)
        unbend(block)
    product[...] = dot_nt(pre_ref[...], up_w[...])
    piece = deep // blocks_ref.shape[0]
    blocks_ref[...] = jnp.zeros(blocks_ref.shape, F32)
    for block in range(blocks_ref.shape[0]):
        blocks_ref[block : block + 1, :piece] = bias_sums_ref[:, block * piece : (block + 1) * piece]
    gain_sum, shift_sum = zero, zero
    for start, size in chunks:
        rows = slice(start, start + size)
        upstream = hidden[rows, :] + product[rows, :]
        value = normed[rows, :]
        gain_sum = gain_sum + fold_rows(upstream * value)
        shift_sum = shift_sum + fold_rows(upstream)
        scaled = upstream * gains[0:1, :]
        inverse = jnp.concatenate([scale[rows, :]] * (width // 128), axis=1)
        grad = inverse * (scaled - row_mean(scaled) - value * row_mean(scaled * value))
        resid_ref[rows, :] = grad
        attend_ref[rows, :] = grad.astype(BF16)
    sums_ref[0:1, :] = jnp.sum(gain_sum, axis=0, keepdims=True)
    sums_ref[2:3, :] = jnp.sum(shift_sum, axis=0, keepdims=True)
    for base, ref in (((1 - side) * part, other_grad), (side * part, own_grad)):
        weight = out_w[pl.ds(pl.multiple_of(base, 128), part), :]
        ref[...] = dot_nt(attend_ref[...], weight).astype(BF16)


def dense(
    scalars, mixed, own_context, other_context, pack, cotangent, out_weight, up_weight, down_weight, devices, marker,
):
    local, width = mixed.shape
    deep = up_weight.shape[1]
    part = width // 2
    low = lambda *shape: jax.ShapeDtypeStruct(shape, BF16)
    full = lambda *shape: jax.ShapeDtypeStruct(shape, F32)
    return pl.pallas_call(
        dense_kernel,
        out_shape=(
            low(local, width), low(local, width), low(local, width), low(local, deep),
            low(local, width), low(local, deep), low(local, width), full(local, width),
            low(local, part), low(local, part), full(8, width), full(devices, 128),
        ),
        in_specs=[smem()] + [vmem()] * 7 + [parameter()] * 3 + [anywhere()],
        out_specs=(vmem(),) * 12,
        scratch_shapes=[
            pltpu.VMEM((width, width), BF16),
            pltpu.VMEM((width, deep), BF16),
            pltpu.VMEM((deep, width), BF16),
            pltpu.VMEM((local, deep), F32),
            pltpu.VMEM((local, width), F32),
            pltpu.VMEM((2, local, width // 2), F32),
            pltpu.VMEM((local, width), F32),
            pltpu.VMEM((local, width), F32),
            pltpu.VMEM((local, 128), F32),
            pltpu.VMEM((1, deep), F32),
            pltpu.SemaphoreType.DMA((2 + deep // width,)),
        ],
        compiler_params=params(23),
        cost_estimate=pl.CostEstimate(
            flops=2 * local * width * (4 * deep + 2 * width), bytes_accessed=20 * MIB,
            transcendentals=2 * local * deep,
        ),
        name="dense",
    )(
        scalars, mixed, *own_context, *other_context, pack, cotangent, out_weight, up_weight, down_weight,
        marker,
    )


def halves_of(value):
    high = value.astype(BF16)
    return high, (value - high.astype(F32)).astype(BF16)


def turn_kernel(order_ref, low_ref, marker, turned_ref, after_ref):
    turned_ref[...] = dot_nt(order_ref[...], low_ref[...]).astype(BF16)
    after_ref[...] = jnp.zeros(after_ref.shape, F32)


def turn_rows(order, low, marker):
    return pl.pallas_call(
        turn_kernel,
        out_shape=(
            jax.ShapeDtypeStruct((order.shape[0], low.shape[0]), BF16),
            jax.ShapeDtypeStruct((8, 128), F32),
        ),
        in_specs=[vmem(), vmem(), anywhere()],
        out_specs=(vmem(), vmem()),
        compiler_params=params(8),
        cost_estimate=pl.CostEstimate(flops=10**9, bytes_accessed=1000, transcendentals=0),
        name="turn_rows",
    )(order, low, marker)


def project_back_kernel(
    turned_hbm, dq_hbm, dk_hbm, dv_hbm, marker, keep_ref, send_ref, after_ref, turned, grads, copies
):
    half, part = keep_ref.shape[0], dq_hbm.shape[1]
    fetches = fetch(
        [turned_hbm, dq_hbm, dk_hbm, dv_hbm], [turned] + [grads.at[block] for block in range(3)], copies
    )
    after_ref[...] = jnp.zeros(after_ref.shape, F32)
    fetches[0].wait()
    for block in range(3):
        fetches[1 + block].wait()
        cols = slice(block * part, (block + 1) * part)
        send_ref[:, cols] = dot_nn(turned[half:, :], grads[block]).astype(BF16)
        keep_ref[:, cols] = dot_nn(turned[:half, :], grads[block]).astype(BF16)


def project_weight_grad(turned, dq, dk, dv, marker):
    width, seq = turned.shape
    part = dq.shape[1]
    shape = jax.ShapeDtypeStruct((width // 2, 3 * part), BF16)
    return pl.pallas_call(
        project_back_kernel,
        out_shape=(shape, shape, jax.ShapeDtypeStruct((8, 128), F32)),
        in_specs=[anywhere()] * 5,
        out_specs=(vmem(),) * 3,
        scratch_shapes=[
            pltpu.VMEM((width, seq), BF16),
            pltpu.VMEM((3, seq, part), BF16),
            pltpu.SemaphoreType.DMA((4,)),
        ],
        compiler_params=params(12),
        cost_estimate=pl.CostEstimate(flops=1000, bytes_accessed=1000, transcendentals=0),
        name="project_weight_grad",
    )(turned, dq, dk, dv, marker)


def fill_block(turned, keep_ref, send_ref, place, right):
    width = right.shape[1]
    middle = turned.shape[0] // 2
    cols = slice(place * width, (place + 1) * width)
    send_ref[:, cols] = dot_nn(turned[middle:, :], right).astype(BF16)
    keep_ref[:, cols] = dot_nn(turned[:middle, :], right).astype(BF16)


def down_kernel(spots, act_ref, branch_ref, keep_ref, send_ref, whole, *, piece):
    width = branch_ref.shape[1]
    half = keep_ref.shape[0]
    for step in range(act_ref.shape[1] // width):
        whole[...] = dot_tn(act_ref[:, step * width : (step + 1) * width], branch_ref[...]).astype(BF16)
        for block in range(width // piece):
            spot = spots[step * (width // piece) + block]
            rows = slice(block * piece, (block + 1) * piece)

            def keep(spot=spot, rows=rows):
                keep_ref[pl.ds(pl.multiple_of(spot, 16), piece), :] = whole[rows, :]

            def send(spot=spot, rows=rows):
                send_ref[pl.ds(pl.multiple_of(spot - half, 16), piece), :] = whole[rows, :]

            pl.when(spot < half)(keep)
            pl.when(spot >= half)(send)


def down_weight_grad(spots, act, branch, piece):
    deep, width = act.shape[1], branch.shape[1]
    tall = jax.ShapeDtypeStruct((deep // 2, width), BF16)
    return pl.pallas_call(
        functools.partial(down_kernel, piece=piece),
        out_shape=(tall, tall),
        in_specs=[smem()] + [vmem()] * 2,
        out_specs=(vmem(),) * 2,
        scratch_shapes=[pltpu.VMEM((width, width), BF16)],
        compiler_params=params(12),
        cost_estimate=pl.CostEstimate(flops=1000, bytes_accessed=1000, transcendentals=0),
        name="down_weight_grad",
    )(spots, act, branch)


def up_kernel(
    pre_ref, hidden_ref, context_ref, attend_ref, first_ref, second_ref, marker,
    out_keep, out_send, up_keep, up_send, turned, *, split,
):
    width = hidden_ref.shape[1]
    block = lambda step: pre_ref[:, step * width : (step + 1) * width]
    turned[...] = dot_nt(first_ref[...], hidden_ref[...]).astype(BF16)
    for step in range(split):
        fill_block(turned, out_keep, out_send, step, block(step))
    turned[...] = dot_nt(first_ref[...], context_ref[...]).astype(BF16)
    fill_block(turned, out_keep, out_send, split, attend_ref[...])
    turned[...] = dot_nt(second_ref[...], hidden_ref[...]).astype(BF16)
    for step in range(split, pre_ref.shape[1] // width):
        fill_block(turned, up_keep, up_send, step - split, block(step))


def up_weight_grads_of(pre, hidden, context, attend, first, second, split, marker):
    local, width = hidden.shape
    steps = pre.shape[1] // width
    low = lambda blocks: jax.ShapeDtypeStruct((width // 2, blocks * width), BF16)
    return pl.pallas_call(
        functools.partial(up_kernel, split=split),
        out_shape=(low(split + 1), low(split + 1), low(steps - split), low(steps - split)),
        in_specs=[vmem()] * 6 + [anywhere()],
        out_specs=(vmem(),) * 4,
        scratch_shapes=[pltpu.VMEM((width, local), BF16)],
        compiler_params=params(14),
        cost_estimate=pl.CostEstimate(flops=LONG, bytes_accessed=1000, transcendentals=0),
        name="up_weight_grad",
    )(pre, hidden, context, attend, first, second, marker)


def mixed_back_kernel(
    scalars, ranks_ref, dq_hbm, dk_hbm, dv_hbm, weight_hbm, resid_hbm, own_hbm, other_hbm,
    marker, grad_ref, send_ref, taps_ref, cells_ref, sorted_grad, whole, text, patch, masks, edge,
    grads, weights, resid_ref, own_ref, other_ref, copies,
):
    side, fine = scalars[0], scalars[2]
    local, width = own_ref.shape
    seq, part = dq_hbm.shape
    groups = width // 128
    pad = GRID_HI + 2
    fetches = fetch(
        [own_hbm, other_hbm, dq_hbm, dk_hbm, dv_hbm]
        + [
            weight_hbm.at[:, pl.ds(pl.multiple_of(block * width + side * part, 128), part)]
            for block in range(3)
        ]
        + [resid_hbm],
        [own_ref, other_ref]
        + [grads.at[block] for block in range(3)]
        + [weights.at[block] for block in range(3)]
        + [resid_ref],
        copies,
    )
    fetches[0].wait()
    fetches[1].wait()
    place_slots(own_ref, other_ref, side, text, patch, pad)
    clear_pads(text, patch, pad)
    store_masks(masks, fine, seq - TEXT)
    for copy in fetches[2:]:
        copy.wait()
    for start, size in row_chunks(seq, 240):
        total = None
        for block in range(3):
            product = dot_nt(grads[block, start : start + size, :], weights[block])
            total = product if total is None else total + product
        sorted_grad[start : start + size, :] = total
    unsort_rows(ranks_ref, sorted_grad, whole, seq)
    mine = pl.ds(pl.multiple_of(side * local, 8), local)
    theirs = pl.ds(pl.multiple_of((1 - side) * local, 8), local)
    whole[mine, :] = whole[mine, :] + resid_ref[...]
    inner = pl.ds(pl.multiple_of(local - 8 + side * 8, 8), 8)
    outer = pl.ds(pl.multiple_of(local - side * 8, 8), 8)
    edge[0:local, :] = whole[theirs, :]
    edge[local : local + 8, :] = whole[inner, :]
    send_ref[...] = edge[...].astype(BF16)
    grad_ref[0:local, :] = whole[mine, :]
    grad_ref[local : local + 8, :] = whole[outer, :]
    taps_ref[...] = jnp.zeros(taps_ref.shape, F32)
    cells_ref[...] = jnp.zeros(cells_ref.shape, F32)
    for lane in range(groups):
        cols = slice(lane * 128, lane * 128 + 128)
        totals = {offset: jnp.zeros((8, 128), F32) for offset in range(-3, 4)}
        for start, size in row_chunks(TEXT, 64):
            value = whole[start : start + size, cols]
            for offset in totals:
                moved = text[lane, pl.ds(8 + start + offset, size), :]
                totals[offset] = totals[offset] + fold_rows(value * moved)
        for number, (reach, direction) in enumerate(tap_list):
            taps_ref[number : number + 1, cols] = jnp.sum(totals[reach * direction], axis=0, keepdims=True)
    for grid, chosen in ((GRID_HI, fine != 0), (GRID_LO, fine == 0)):

        def cells(grid=grid):
            for lane in range(groups):
                cols = slice(lane * 128, lane * 128 + 128)
                totals = [jnp.zeros((8, 128), F32)] * len(cell_list)
                for start, size in row_chunks(seq - TEXT, 104):
                    value = whole[TEXT + start : TEXT + start + size, cols]
                    for number, (down, across) in enumerate(cell_list):
                        moved = patch[lane, pl.ds(pad + start + down * grid + across, size), :]
                        moved = moved * masks[number, start : start + size, :]
                        totals[number] = totals[number] + fold_rows(value * moved)
                for number, value in enumerate(totals):
                    cells_ref[number : number + 1, cols] = jnp.sum(value, axis=0, keepdims=True)

        pl.when(chosen)(cells)


def mixed_back(scalars, ranks, dq, dk, dv, qkv_weight, resid_grad, own, other, marker):
    local, width = own.shape
    seq, part = dq.shape
    groups = width // 128
    return pl.pallas_call(
        mixed_back_kernel,
        out_shape=(
            jax.ShapeDtypeStruct((local + 8, width), F32),
            jax.ShapeDtypeStruct((local + 8, width), BF16),
            jax.ShapeDtypeStruct((16, width), F32),
            jax.ShapeDtypeStruct((16, width), F32),
        ),
        in_specs=[smem(), smem()] + [anywhere()] * 3 + [parameter()] + [anywhere()] * 4,
        out_specs=(vmem(),) * 4,
        scratch_shapes=[
            pltpu.VMEM((seq, width), F32),
            pltpu.VMEM((seq, width), F32),
            pltpu.VMEM((groups, TEXT + 16, 128), F32),
            pltpu.VMEM((groups, seq - TEXT + 2 * (GRID_HI + 2), 128), F32),
            pltpu.VMEM((9, seq - TEXT, 128), F32),
            pltpu.VMEM((local + 8, width), F32),
            pltpu.VMEM((3, seq, part), BF16),
            pltpu.VMEM((3, width, part), BF16),
            pltpu.VMEM((local, width), F32),
            pltpu.VMEM((local, width), BF16),
            pltpu.VMEM((local, width), BF16),
            pltpu.SemaphoreType.DMA((9,)),
        ],
        compiler_params=params(15),
        cost_estimate=pl.CostEstimate(flops=1000, bytes_accessed=1000, transcendentals=0),
        name="mixed_back",
    )(scalars, ranks, dq, dk, dv, qkv_weight, resid_grad, own, other, marker)


def token_kernel(
    scalars, grad_ref, received_ref, text_kernel, patch_kernel, marker, out_ref, after_ref,
    text, patch, masks, lanes,
):
    side, fine = scalars[0], scalars[2]
    local, width = out_ref.shape
    groups = width // 128
    pad = GRID_HI + 2
    after_ref[...] = jnp.zeros(after_ref.shape, F32)
    rows = masks.shape[1]
    head = TEXT - local
    clear_pads(text, patch, pad)
    store_masks(masks, fine, rows)

    def load(low):
        for lane in range(groups):
            cols = slice(lane * 128, lane * 128 + 128)
            total = grad_ref[:, cols] + received_ref[:, cols].astype(F32)
            if low:
                text[lane, 8 : 8 + local + 8, :] = total
                text[lane, 16 + local : 8 + TEXT, :] = jnp.zeros((head - 8, 128), F32)
                patch[lane, pad : pad + rows, :] = jnp.zeros((rows, 128), F32)
            else:
                text[lane, 8 : local, :] = jnp.zeros((local - 8, 128), F32)
                text[lane, local : local + 8, :] = total[local:]
                text[lane, 8 + local : 8 + TEXT, :] = total[:head]
                patch[lane, pad : pad + rows, :] = total[head:local]

    pl.when(side == 0)(lambda: load(True))
    pl.when(side != 0)(lambda: load(False))

    def one_lane(lane, carry):
        mix_lane(text, patch, masks, lanes, lane, text_kernel, patch_kernel, fine, pad, True)
        return carry

    lax.fori_loop(0, groups, one_lane, 0)
    mine = pl.ds(pl.multiple_of(side * local, 8), local)
    for lane in range(groups):
        out_ref[:, lane * 128 : lane * 128 + 128] = lanes[lane, mine, :]


def token_back(scalars, grad, received, text_kernel, patch_kernel, seq, marker):
    local, width = grad.shape[0] - 8, grad.shape[1]
    groups = width // 128
    return pl.pallas_call(
        token_kernel,
        out_shape=(jax.ShapeDtypeStruct((local, width), F32), jax.ShapeDtypeStruct((8, 128), F32)),
        in_specs=[smem()] + [vmem()] * 4 + [anywhere()],
        out_specs=(vmem(), vmem()),
        scratch_shapes=[
            pltpu.VMEM((groups, TEXT + 16, 128), F32),
            pltpu.VMEM((groups, seq - TEXT + 2 * (GRID_HI + 2), 128), F32),
            pltpu.VMEM((9, seq - TEXT, 128), F32),
            pltpu.VMEM((groups, seq, 128), F32),
        ],
        compiler_params=params(9),
        cost_estimate=pl.CostEstimate(flops=1000, bytes_accessed=1000, transcendentals=0),
        name="token_back",
    )(scalars, grad, received, text_kernel, patch_kernel, marker)


def finish_kernel(scalars, kept_ref, received_ref, marker, grad_ref, after_ref):
    side = scalars[0]
    part = kept_ref.shape[1] // 3
    after_ref[...] = jnp.zeros(after_ref.shape, F32)
    for block in range(3):
        cols = slice(block * part, (block + 1) * part)
        mine = pl.ds(pl.multiple_of((2 * block + side) * part, 128), part)
        theirs = pl.ds(pl.multiple_of((2 * block + 1 - side) * part, 128), part)
        grad_ref[:, mine] = kept_ref[:, cols]
        grad_ref[:, theirs] = received_ref[:, cols].astype(F32)


def finish(scalars, kept, received, marker):
    return pl.pallas_call(
        finish_kernel,
        out_shape=(
            jax.ShapeDtypeStruct((kept.shape[0], 2 * kept.shape[1]), F32),
            jax.ShapeDtypeStruct((8, 128), F32),
        ),
        in_specs=[smem(), vmem(), vmem(), anywhere()],
        out_specs=(vmem(), vmem()),
        compiler_params=params(8),
        cost_estimate=pl.CostEstimate(flops=1000, bytes_accessed=1000, transcendentals=0),
        name="finish",
    )(scalars, kept, received, marker)


def finish_little_kernel(
    kept_ref, received_ref, marker, taps_ref, cells_ref, gains_ref, shifts_ref, down_ref, up_ref,
    rank_ref, box_ref, *, ratio, shared, heads,
):
    rows = taps_ref.shape[1]
    small = kept_ref[:rows, :] + received_ref[:rows, :]
    padded = jnp.concatenate([small, jnp.zeros((128 - rows, 128), F32)], axis=0)
    turned = padded.T
    taps_ref[...] = turned[0:9, :rows]
    cells_ref[...] = turned[16:25, :rows]
    gains_ref[...] = turned[32:34, :rows]
    shifts_ref[...] = turned[34:36, :rows]
    down_ref[...] = turned[36:37, :rows]
    row = lax.broadcasted_iota(jnp.int32, (rows, 128), 0)
    lane = lax.broadcasted_iota(jnp.int32, (rows, 128), 1)
    total = jnp.zeros((rows, 128), F32)
    for column in range(ratio):
        value = jnp.broadcast_to(small[:, 40 + column : 41 + column], (rows, 128))
        total = total + jnp.where(lane == row * ratio + column, value, 0.0)
    up_ref[...] = jnp.sum(total, axis=0, keepdims=True)[:, : rows * ratio]
    tables = kept_ref[kept_ref.shape[0] - shared :, :] + received_ref[received_ref.shape[0] - shared :, :]
    for head in range(2 * heads):
        row = head // heads * 16 + head % heads
        rank_ref[head : head + 1, :] = tables[row : row + 1, :NB1]
        box_ref[head, 0:1, :] = tables[row : row + 1, NB1 : NB1 + NB2]
        box_ref[head, 1:2, :] = tables[row + 8 : row + 9, :NB2]


def finish_little(kept, received, ratio, shared, heads, marker):
    rows = received.shape[0] - shared
    full = lambda *shape: jax.ShapeDtypeStruct(shape, F32)
    return pl.pallas_call(
        functools.partial(finish_little_kernel, ratio=ratio, shared=shared, heads=heads),
        out_shape=(
            full(9, rows), full(9, rows), full(2, rows), full(2, rows), full(1, rows),
            full(1, rows * ratio), full(2 * heads, NB1), full(2 * heads, 2, NB2),
        ),
        in_specs=[vmem(), vmem(), anywhere()],
        out_specs=(vmem(),) * 8,
        compiler_params=params(4),
        cost_estimate=pl.CostEstimate(flops=1000, bytes_accessed=1000, transcendentals=0),
        name="finish_little",
    )(kept, received, marker)


def swap(value, stage):
    axis, bit = stage
    count = lax.axis_size(axis)
    return lax.ppermute(value, axis, [(i, i ^ bit) for i in range(count)])


def stage_flag(stage):
    axis, bit = stage
    return (lax.axis_index(axis) & bit) // bit


def block_bit(block, stage, blk_count):
    axis, bit = stage
    shift = bit * blk_count if axis == "page" else bit
    return (block // shift) & 1


def spot_of(block, stages, blk_count):
    spot = jnp.zeros_like(block)
    for stage in stages:
        spot = spot * 2 + (block_bit(block, stage, blk_count) ^ stage_flag(stage))
    return spot


def order_matrix(width, stages, blk_count):
    count = lax.axis_size("page") * blk_count
    piece = width // count
    place = jnp.arange(width, dtype=jnp.int32)
    spot, inside = place // piece, place % piece
    block = jnp.zeros_like(spot)
    for depth, stage in enumerate(stages):
        axis, bit = stage
        shift = bit * blk_count if axis == "page" else bit
        value = ((spot >> (len(stages) - 1 - depth)) & 1) ^ stage_flag(stage)
        block = block + value * shift
    column = block * piece + inside
    return (column[:, None] == jnp.arange(width, dtype=jnp.int32)[None, :]).astype(BF16)


def add_up(terms):
    total = terms[0].astype(F32)
    for term in terms[1:]:
        total = total + term.astype(F32)
    return total


def halve_kernel(kept_ref, received_ref, marker, next_ref, send_ref, after_ref):
    rows = next_ref.shape[0]
    size = rows if rows % 48 else 48
    for start in range(0, rows, size):
        for base, ref in ((rows, send_ref), (0, next_ref)):
            if base % 16 or size % 16:
                place = slice(base + start, base + start + size)
                value = kept_ref[...].astype(F32)[place] + received_ref[...].astype(F32)[place]
            else:
                place = slice(base + start, base + start + size)
                value = kept_ref[place, :].astype(F32) + received_ref[place, :].astype(F32)
            ref[start : start + size, :] = value.astype(ref.dtype)
    after_ref[...] = jnp.zeros(after_ref.shape, F32)


def halve(kept, received, marker, flops=1000):
    rows, width = received.shape[0] // 2, received.shape[1]
    if rows % 8:
        total = kept.astype(F32) + received.astype(F32)
        return total[:rows], total[rows:].astype(BF16), marker
    return pl.pallas_call(
        halve_kernel,
        out_shape=(
            jax.ShapeDtypeStruct((rows, width), F32),
            jax.ShapeDtypeStruct((rows, width), BF16),
            jax.ShapeDtypeStruct((8, 128), F32),
        ),
        in_specs=[vmem(), vmem(), anywhere()],
        out_specs=(vmem(),) * 3,
        compiler_params=params(8),
        cost_estimate=pl.CostEstimate(flops=flops, bytes_accessed=1000, transcendentals=0),
        name="halve",
    )(kept, received, marker)


class Chain:
    def __init__(self, keep, send, stages):
        self.kept, self.stages, self.done = keep, stages, 0
        self.rows = 2 * keep.shape[0]
        self.received = swap(send, stages[0])

    def turn(self, marker, flops=1000):
        self.done += 1
        if self.done >= len(self.stages):
            return marker
        self.kept, send, marker = halve(self.kept, self.received, marker, flops)
        self.received = swap(send, self.stages[self.done])
        return marker


def join_kernel(
    out_kept, out_received, down_kept, down_received, marker, next_ref, send_ref, after_ref, sums, message,
    *, piece, ratio,
):
    rows, width = next_ref.shape[0], down_kept.shape[1]
    wide = out_kept.shape[1]
    for start in range(0, 2 * rows, rows):
        part = slice(start, start + rows)
        value = out_kept[part, :] + out_received[part, :].astype(F32)
        (message if start else next_ref)[:, :wide] = value
    for start in range(0, sums.shape[0], 48):
        part = slice(start, start + 48)
        sums[part, :] = down_kept[part, :] + down_received[part, :].astype(F32)
    for start in range(0, 2 * rows, piece):
        target, place = (next_ref, start) if start < rows else (message, start - rows)
        for turn in range(ratio):
            cols = slice(wide + turn * width, wide + (turn + 1) * width)
            source = ratio * start + turn * piece
            target[place : place + piece, cols] = sums[source : source + piece, :]
    for start in range(0, wide + ratio * width, width):
        cols = slice(start, start + width)
        send_ref[:, cols] = message[:, cols].astype(BF16)
    after_ref[...] = jnp.zeros(after_ref.shape, F32)


def join(out, down, devices, marker):
    rows, wide = out.kept.shape
    tall, width = down.kept.shape
    ratio = tall // rows
    piece = out.rows // devices
    full = wide + ratio * width
    out.done += 1
    down.done += 1
    if piece % 8:
        total = down.kept + down.received.astype(F32)
        total = total.reshape(rows // piece, ratio, piece, width).swapaxes(1, 2).reshape(rows, ratio * width)
        total = jnp.concatenate([out.kept + out.received.astype(F32), total], axis=1)
        kept, send = total[: rows // 2], total[rows // 2 :].astype(BF16)
    else:
        kept, send, marker = pl.pallas_call(
            functools.partial(join_kernel, piece=piece, ratio=ratio),
            out_shape=(
                jax.ShapeDtypeStruct((rows // 2, full), F32),
                jax.ShapeDtypeStruct((rows // 2, full), BF16),
                jax.ShapeDtypeStruct((8, 128), F32),
            ),
            in_specs=[vmem()] * 4 + [anywhere()],
            out_specs=(vmem(),) * 3,
            scratch_shapes=[pltpu.VMEM((tall, width), F32), pltpu.VMEM((rows // 2, full), F32)],
            compiler_params=params(10),
            cost_estimate=pl.CostEstimate(flops=1000, bytes_accessed=1000, transcendentals=0),
            name="join",
        )(out.kept, out.received, down.kept, down.received, marker)
    return Chain(kept, send, out.stages[out.done :]), marker


def total_kernel(
    up_kept, up_received, kept_ref, received_ref, marker, up_ref, out_ref, down_ref, after_ref
):
    piece, width = out_ref.shape
    wide = up_ref.shape[1] - up_kept.shape[1]
    value = kept_ref[...] + received_ref[...].astype(F32)
    up_ref[:, :wide] = value[:, :wide]
    up_ref[:, wide:] = up_kept[...] + up_received[...].astype(F32)
    out_ref[...] = value[:, wide : wide + width]
    for turn in range(down_ref.shape[0] // piece):
        start = wide + (turn + 1) * width
        down_ref[turn * piece : (turn + 1) * piece, :] = value[:, start : start + width]
    after_ref[...] = jnp.zeros(after_ref.shape, F32)


def total(up, joint, width, deep, marker):
    rows = up.kept.shape[0]
    full = lambda *shape: jax.ShapeDtypeStruct(shape, F32)
    return pl.pallas_call(
        total_kernel,
        out_shape=(full(rows, deep), full(rows, width), full(rows * deep // width, width), full(8, 128)),
        in_specs=[vmem()] * 4 + [anywhere()],
        out_specs=(vmem(),) * 4,
        compiler_params=params(8),
        cost_estimate=pl.CostEstimate(flops=LONG, bytes_accessed=1000, transcendentals=0),
        name="total",
    )(up.kept, up.received, joint.kept, joint.received, marker)


def little_kernel(now_ref, received_ref, marker, next_ref, message_ref, after_ref, *, shared):
    rows = received_ref.shape[0] - shared
    half = message_ref.shape[0] - shared
    common = now_ref[2 * rows :, :] + received_ref[rows:, :]
    kept = now_ref[:rows, :] + received_ref[:rows, :]
    next_ref[:rows, :] = kept
    next_ref[rows:, :] = common
    message_ref[:half, :] = kept[half:]
    message_ref[half:, :] = common
    after_ref[...] = jnp.zeros(after_ref.shape, F32)


class Little:
    def __init__(self, now, shared, stages):
        self.now, self.shared, self.stages, self.done = now, shared, stages, 0
        rows = (now.shape[0] - shared) // 2
        self.received = swap(now[rows:], stages[0])

    def turn(self, marker):
        self.done += 1
        if self.done > len(self.stages):
            return marker
        rows = self.received.shape[0] - self.shared
        if self.done == len(self.stages):
            return marker
        half = rows // 2
        if half % 8:
            kept = self.now[:rows] + self.received[:rows]
            common = self.now[2 * rows :] + self.received[rows:]
            self.now = jnp.concatenate([kept, common], axis=0)
            message = self.now[half:]
        else:
            lanes = self.now.shape[1]
            self.now, message, marker = pl.pallas_call(
                functools.partial(little_kernel, shared=self.shared),
                out_shape=(
                    jax.ShapeDtypeStruct((rows + self.shared, lanes), F32),
                    jax.ShapeDtypeStruct((half + self.shared, lanes), F32),
                    jax.ShapeDtypeStruct((8, 128), F32),
                ),
                in_specs=[vmem(), vmem(), anywhere()],
                out_specs=(vmem(),) * 3,
                compiler_params=params(4),
                cost_estimate=pl.CostEstimate(flops=1000, bytes_accessed=1000, transcendentals=0),
                name="little",
            )(self.now, self.received, marker)
        self.received = swap(message, self.stages[self.done])
        return marker


def gather_kernel(
    scalars, order_hbm, owner_hbm, inside_hbm, fold_hbm, rank_hbm, box_hbm, taps_hbm, cells_hbm, dense_hbm,
    blocks_hbm, sums_a, sums_b, sums_c, marker, out_ref, after_ref,
    order, owner, inside, fold, rank, box, taps, cells, dense_sums, blocks, sums, copies,
):
    fetches = fetch(
        [order_hbm, owner_hbm, inside_hbm, fold_hbm, rank_hbm, box_hbm, taps_hbm, cells_hbm,
         dense_hbm, blocks_hbm, sums_a, sums_b, sums_c],
        [order, owner, inside, fold, rank, box, taps, cells, dense_sums, blocks]
        + [sums.at[pl.ds(2 * n, 2)] for n in range(3)],
        copies,
    )
    for copy in fetches:
        copy.wait()
    after_ref[...] = jnp.zeros(after_ref.shape, F32)
    width = order.shape[0]

    rows = jnp.concatenate([taps[...], cells[...], dense_sums[...]], axis=0)
    rows = jnp.concatenate([rows, jnp.zeros((128 - rows.shape[0], width), F32)], axis=0)
    spread = dot_nn(owner[...], blocks[...].astype(BF16)) * inside[...].astype(F32)
    bias = dot_nn(spread.astype(BF16), fold[...]).astype(BF16)
    out_ref[:width, :] = dot_nt(order[...], rows.astype(BF16)) + dot_nn(order[...], bias)
    out_ref[width:, :] = jnp.zeros((32, 128), F32)
    heads = sums.shape[0]
    mine = pl.multiple_of(width + scalars[0] * 16, 16)
    pad = lambda value: jnp.concatenate([value, jnp.zeros((8 - heads, value.shape[1]), F32)], axis=0)
    by_rank = pad(jnp.concatenate([sums[head, 0:1, :] for head in range(heads)], axis=0))
    table = sum(dot_nn(piece, rank[...]) for piece in halves_of(by_rank))
    out_ref[pl.ds(mine, 8), 0:NB1] = table
    for half in range(2):
        by_box = pad(
            jnp.concatenate([sums[head, half + 1 : half + 2, : 2 * SPAN] for head in range(heads)], axis=0)
        )
        table = sum(dot_nn(piece, box[...]) for piece in halves_of(by_box))
        if half == 0:
            out_ref[pl.ds(mine, 8), NB1 : NB1 + NB2] = table
        else:
            out_ref[pl.ds(mine + 8, 8), 0:NB2] = table


def gather_small(scalars, order, taps, cells, dense_sums, blocks, sums, deep, marker):
    width = order.shape[0]
    devices = blocks.shape[0]
    ratio = deep // width
    piece = width // devices
    rows, lanes = np.arange(width), np.arange(128)
    owner = jnp.asarray(rows[:, None] // piece == np.arange(devices)[None, :], BF16)
    inside = jnp.asarray(
        (lanes[None, :] // ratio == rows[:, None] % piece) & (lanes[None, :] < piece * ratio), BF16
    )
    fold = jnp.asarray(lanes[:, None] % ratio + 40 == lanes[None, :], BF16)
    rank = jnp.asarray(bucket_rows(np.arange(RANK_LANES) - (RANK_MID - 1), rank_marks, NB1), BF16)
    box = jnp.asarray(bucket_rows(np.arange(2 * SPAN) - (SPAN - 1), box_marks, NB2), BF16)
    constants = tuple(map(stay, (owner, inside, fold, rank, box)))
    operands = (order, *constants, taps, cells, dense_sums, blocks)
    return pl.pallas_call(
        gather_kernel,
        out_shape=(
            jax.ShapeDtypeStruct((width + 32, 128), F32), jax.ShapeDtypeStruct((8, 128), F32)
        ),
        in_specs=[smem(), anywhere()] + [parameter()] * 5 + [anywhere()] * 8,
        out_specs=(vmem(), vmem()),
        scratch_shapes=[pltpu.VMEM(value.shape, value.dtype) for value in operands]
        + [pltpu.VMEM((2 * len(sums), 8, RANK_LANES), F32), pltpu.SemaphoreType.DMA((13,))],
        compiler_params=params(10),
        cost_estimate=pl.CostEstimate(flops=1000, bytes_accessed=1000, transcendentals=0),
        name="gather_small",
    )(scalars, *operands, *sums, marker)


def per_device(
    tokens,
    patch_count,
    reading_rank,
    boxes,
    text_kernel,
    patch_kernel,
    qkv_weight,
    rank_table,
    box_tables,
    out_weight,
    norm_gains,
    norm_shifts,
    up_weight,
    up_bias,
    down_weight,
    down_bias,
    cotangent,
):
    qkv_weight, out_weight, up_weight, down_weight = map(
        stay, (qkv_weight, out_weight, up_weight, down_weight)
    )
    side = lax.axis_index("blk")
    blk_count = lax.axis_size("blk")
    page_stages = [("page", 1 << n) for n in range(lax.axis_size("page").bit_length() - 1)]
    across = ("blk", 1)
    out_stages = page_stages[:1] + [across] + page_stages[1:]
    up_stages = page_stages[:1] + page_stages[2:] + [across] + page_stages[1:2]
    down_stages = page_stages[:2] + [across] + page_stages[2:]
    qkv_stages = page_stages[:1] + page_stages[2:] + page_stages[1:2] + [across]
    little_stages = page_stages[:2] + [across] + page_stages[2:]
    devices = lax.axis_size("page") * blk_count
    count = patch_count[0]
    ranks = reading_rank
    own = tokens[0]
    local, width = own.shape
    deep = up_bias.shape[0]
    seq = ranks.shape[1]
    heads = HEADS // blk_count
    scalars = jnp.stack(
        [side, TEXT + count, (count == GRID_HI * GRID_HI).astype(jnp.int32), jnp.int32(0)]
    ).astype(jnp.int32)
    other = swap(own, across)

    xy, xyt, rank_bias, box_bias = onehots(scalars, ranks, boxes, rank_table, box_tables, heads)
    mixed, mixed_low, packed = mix_and_project(
        scalars, ranks, own, other, text_kernel, patch_kernel, qkv_weight
    )
    pack = jnp.concatenate([norm_gains, norm_shifts, down_bias[None], up_bias.reshape(-1, width)], axis=0)
    own_context, other_context, shares = [], [], []
    for first, pairs in ((0, 2), (2, 1)):
        share, mine, theirs = attend(
            scalars, ranks, packed, xy, rank_bias, box_bias, local, first, pairs
        )
        shares += [(share, place) for place in range(pairs)]
        own_context.append(mine)
        other_context.append(swap(theirs, across))
    order_qkv = order_matrix(width, qkv_stages, blk_count)
    order_little = order_matrix(width, little_stages, blk_count)
    turned, marker = turn_rows(order_qkv, mixed_low, own_context[-1])
    (
        layer_output, context, hidden_low, act_low, branch_grad, pre_grad, attend_grad,
        resid_one_grad, own_part, their_part, dense_sums, bias_blocks,
    ) = dense(
        scalars, mixed, own_context, other_context, pack, cotangent[0], out_weight, up_weight,
        down_weight, devices, marker,
    )
    part = width // blk_count
    received_part = swap(their_part, across)

    order_out = order_matrix(width, out_stages, blk_count)
    order_up = order_matrix(width, up_stages, blk_count)
    piece = deep // devices
    blocks = jnp.arange(devices, dtype=jnp.int32)
    spots = spot_of(blocks, down_stages, blk_count) * piece
    act_rows = act_low
    if piece % 16:
        place = jnp.arange(deep, dtype=jnp.int32)
        target = spots[place // piece] + place % piece
        act_rows = jnp.zeros_like(act_low).at[:, target].set(act_low, unique_indices=True)
        piece = width // 8
        spots = jnp.arange(deep // piece, dtype=jnp.int32) * piece
    steps = deep // width
    split = steps // 2
    down_keep, down_send = down_weight_grad(spots, act_rows, branch_grad, piece)
    down = Chain(down_keep, down_send, down_stages)
    out_keep, out_send, up_keep, up_send = up_weight_grads_of(
        pre_grad, hidden_low, context, attend_grad, order_out, order_up, split, down_keep
    )
    out = Chain(out_keep, out_send, out_stages)
    up = Chain(up_keep, up_send, up_stages)
    marker = down.turn(up_send)

    grads, sums = None, []
    for pair, (share, place) in enumerate(shares):
        if pair == 1:
            marker = up.turn(out.turn(sums[0]))
        *grads, pair_sums = attend_back(
            scalars, ranks, own_part, received_part, share, packed, xy, xyt, pair, place, grads,
            marker if pair < 2 else None,
        )
        sums.append(pair_sums)
    dq, dk, dv = grads
    qkv_keep, qkv_send, marker = project_weight_grad(turned, dq, dk, dv, sums[-1])
    qkv = Chain(qkv_keep, qkv_send, qkv_stages)
    marker = down.turn(out.turn(up.turn(marker)), LONG)
    marker = qkv.turn(marker)
    grad, outgoing, taps, cells = mixed_back(
        scalars, ranks, dq, dk, dv, qkv_weight, resid_one_grad, stay(own), other, marker
    )
    incoming = swap(outgoing, across)
    gathered, marker = gather_small(
        scalars, order_little, taps, cells, dense_sums, bias_blocks, sums, deep, taps
    )
    little = Little(gathered, 32, little_stages)
    marker = up.turn(qkv.turn(marker))
    joint, marker = join(out, down, devices, marker)
    marker = little.turn(little.turn(marker))
    token_grad, marker = token_back(
        scalars, grad, incoming, text_kernel, patch_kernel, seq, marker
    )
    for _ in range(len(qkv_stages) - 4):
        for chain in (qkv, little, up, joint):
            marker = chain.turn(marker)
    marker = little.turn(qkv.turn(marker))
    up_weight_grads, out_weight_grads, down_weight_grads, marker = total(up, joint, width, deep, marker)
    for _ in qkv_stages:
        marker = little.turn(qkv.turn(marker))
    qkv_weight_grad, marker = finish(scalars, qkv.kept, qkv.received, marker)
    taps, cells, gains, shifts, down_bias_grad, up_bias_grad, rank_grad, box_grad = finish_little(
        little.now, little.received, steps, 32, heads, marker
    )
    return (
        layer_output[None],
        token_grad[None],
        taps,
        cells,
        qkv_weight_grad,
        rank_grad,
        jnp.swapaxes(box_grad, 0, 1),
        out_weight_grads,
        gains,
        shifts,
        up_weight_grads,
        up_bias_grad[0],
        down_weight_grads,
        down_bias_grad[0],
    )


def solution(mesh):
    in_specs = (
        P("page", "blk", None),
        P("page"),
        P("page", None),
        P(None, "page", None),
        P(),
        P(),
        P(),
        P(),
        P(),
        P(),
        P(),
        P(),
        P(),
        P(),
        P(),
        P(),
        P("page", "blk", None),
    )
    out_specs = (
        P("page", "blk", None),
        P("page", "blk", None),
        P(None, ("page", "blk")),
        P(None, ("page", "blk")),
        P(("page", "blk"), None),
        P(),
        P(),
        P(("page", "blk"), None),
        P(None, ("page", "blk")),
        P(None, ("page", "blk")),
        P(("page", "blk"), None),
        P(("page", "blk")),
        P(("page", "blk"), None),
        P(("page", "blk")),
    )
    return jax.shard_map(
        per_device, mesh=mesh, in_specs=in_specs, out_specs=out_specs, check_vma=False
    )
```

```python
import functools

import jax
import jax.numpy as jnp
import numpy as np
from jax import lax
from jax.experimental import pallas as pl
from jax.experimental.pallas import tpu as pltpu
from jax.sharding import PartitionSpec as P

TEXT = 512
GRID_LO = 7
GRID_HI = 14
RUN = 16
HEADS = 12
HEAD_DIM = 64
NB1 = 32
NB2 = 64
SPAN = 256
RANK_LANES = 1536
RANK_MID = RANK_LANES // 2
ROWS = 128
F32 = jnp.float32
BF16 = jnp.bfloat16
MIB = 1 << 20
LONG = 10**11

rank_marks = (1, 2, 3, 4, 5, 6, 7, 8, 12, 16, 23, 32, 46, 64, 91)
box_marks = tuple(range(1, 17)) + (19, 23, 27, 32, 39, 46, 54, 64, 77, 91, 108, 128, 153, 182, 216)
neg_fill = -1000000000.0
norm_eps = 1e-05
root_half = 0.7071067811865476
inv_root_tau = 0.3989422804014327
tap_list = ((1, -1), (1, 0), (1, 1), (2, -1), (2, 0), (2, 1), (3, -1), (3, 0), (3, 1))
cell_list = ((-1, -1), (-1, 0), (-1, 1), (0, -1), (0, 0), (0, 1), (1, -1), (1, 0), (1, 1))


def bucket_rows(deltas, marks, bins):
    spread = np.abs(deltas)
    ids = np.sum(spread[:, None] >= np.asarray(marks)[None, :], axis=1) + (bins // 2) * (deltas > 0)
    return (ids[:, None] == np.arange(bins)[None, :]).astype(np.float32)


def dot_nn(left, right):
    return lax.dot_general(left, right, (((1,), (0,)), ((), ())), preferred_element_type=F32)


def dot_nt(left, right):
    return lax.dot_general(left, right, (((1,), (1,)), ((), ())), preferred_element_type=F32)


def dot_tn(left, right):
    return lax.dot_general(left, right, (((0,), (0,)), ((), ())), preferred_element_type=F32)


def row_chunks(total, size):
    return [(start, min(size, total - start)) for start in range(0, total, size)]


def vmem():
    return pl.BlockSpec(memory_space=pltpu.VMEM)


def smem():
    return pl.BlockSpec(memory_space=pltpu.SMEM)


def anywhere():
    return pl.BlockSpec(memory_space=pl.ANY)


def parameter():
    return pl.BlockSpec(memory_space=pltpu.HBM)


def stay(value):
    return pltpu.with_memory_space_constraint(value, pltpu.HBM)


def fetch(sources, targets, semaphores):
    copies = []
    for number, (source, target) in enumerate(zip(sources, targets)):
        copies.append(pltpu.make_async_copy(source, target, semaphores.at[number]))
        copies[-1].start()
    return copies


def params(mib):
    return pltpu.CompilerParams(vmem_limit_bytes=mib * MIB)


def onehot_kernel(
    scalars, rank_hbm, box_hbm, rank_table_hbm, box_tables_hbm, rank_rows_hbm, box_rows_hbm,
    xy_ref, xyt_ref, rank_bias, box_bias,
    rank_ref, box_ref, rank_table, box_tables, rank_rows, box_rows, vectors, copies,
):
    fetches = fetch(
        [rank_hbm, box_hbm, rank_table_hbm, box_tables_hbm, rank_rows_hbm, box_rows_hbm],
        [rank_ref, box_ref, rank_table, box_tables, rank_rows, box_rows],
        copies,
    )
    for copy in fetches:
        copy.wait()
    seq = rank_ref.shape[1]
    for start, size in row_chunks(seq, 240):
        spot = lax.broadcasted_iota(jnp.int32, (size, seq), 0) + start
        order = (spot == rank_ref[...]).astype(F32).astype(BF16)
        for half in range(2):
            level = lax.broadcasted_iota(jnp.int32, (SPAN, seq), 0)
            marks = (level == box_ref[half]).astype(F32).astype(BF16)
            xy_ref[start : start + size, half * SPAN : (half + 1) * SPAN] = dot_nt(
                order, marks
            ).astype(BF16)
    row = lax.broadcasted_iota(jnp.int32, (SPAN, SPAN), 0)
    col = lax.broadcasted_iota(jnp.int32, (SPAN, SPAN), 1)
    flip = (row + col == SPAN - 1).astype(F32).astype(BF16)
    for half in range(2):
        part = slice(half * SPAN, (half + 1) * SPAN)
        xyt_ref[part, :] = dot_nt(flip, xy_ref[:, part]).astype(BF16)
    heads = vectors.shape[0]
    tables = [(dot_nt(rank_table[...], rank_rows[...]), RANK_LANES)]
    tables += [(dot_nt(box_tables[half], box_rows[...]), 2 * SPAN) for half in range(2)]
    for place, (table, lanes) in enumerate(tables):
        own = jnp.where(scalars[0] == 0, table[:heads], table[table.shape[0] - heads :])
        for head in range(heads):
            vectors[head, place : place + 1, :lanes] = own[head : head + 1]

    def one_head(head, carry):
        rank_bias[head] = skewed(vectors[head, 0:1, :], ROWS, RANK_LANES, RANK_LANES - 128)
        for half in range(2):
            part = slice(half * SPAN, (half + 1) * SPAN)
            table = skewed(vectors[head, half + 1 : half + 2, : 2 * SPAN], SPAN, 2 * SPAN, SPAN + 1)
            box_bias[head, :, part] = dot_nn(xy_ref[:, part], table[:, :SPAN].astype(BF16)).astype(BF16)
        return carry

    lax.fori_loop(0, heads, one_head, 0)


def onehots(scalars, ranks, boxes, rank_table, box_tables, heads):
    seq = ranks.shape[1]
    rank_rows = jnp.asarray(bucket_rows(np.arange(RANK_LANES) - RANK_MID, rank_marks, NB1), BF16)
    box_rows = jnp.asarray(bucket_rows(SPAN - 1 - np.arange(2 * SPAN), box_marks, NB2), BF16)
    operands = tuple(map(stay, (ranks, boxes, rank_table, box_tables, rank_rows, box_rows)))
    return pl.pallas_call(
        onehot_kernel,
        out_shape=(
            jax.ShapeDtypeStruct((seq, 2 * SPAN), BF16),
            jax.ShapeDtypeStruct((2 * SPAN, seq), BF16),
            jax.ShapeDtypeStruct((heads, ROWS, RANK_LANES), F32),
            jax.ShapeDtypeStruct((heads, seq, 2 * SPAN), BF16),
        ),
        in_specs=[smem()] + [parameter()] * 6,
        out_specs=(vmem(),) * 4,
        scratch_shapes=[pltpu.VMEM(value.shape, value.dtype) for value in operands]
        + [pltpu.VMEM((heads, 8, RANK_LANES), F32), pltpu.SemaphoreType.DMA((6,))],
        compiler_params=params(14),
        cost_estimate=pl.CostEstimate(
            flops=4 * seq * seq * SPAN, bytes_accessed=4 * seq * 2 * SPAN, transcendentals=0
        ),
        name="onehots",
    )(scalars, *operands)


def place_slots(own_ref, other_ref, side, text, patch, patch_pad):
    local = own_ref.shape[0]
    head = TEXT - local
    groups = text.shape[0]

    def place(low_ref, high_ref):
        for lane in range(groups):
            cols = slice(128 * lane, 128 * lane + 128)
            text[lane, 8 : 8 + local, :] = low_ref[:, cols].astype(F32)
            high = high_ref[:, cols].astype(F32)
            text[lane, 8 + local : 8 + TEXT, :] = high[:head]
            patch[lane, patch_pad : patch_pad + local - head, :] = high[head:]

    pl.when(side == 0)(lambda: place(own_ref, other_ref))
    pl.when(side != 0)(lambda: place(other_ref, own_ref))


def clear_pads(text, patch, patch_pad):
    groups, rows = patch.shape[0], patch.shape[1]
    for lane in range(groups):
        text[lane, 0:8, :] = jnp.zeros((8, 128), F32)
        text[lane, 8 + TEXT : 16 + TEXT, :] = jnp.zeros((8, 128), F32)
        patch[lane, 0:patch_pad, :] = jnp.zeros((patch_pad, 128), F32)
        patch[lane, rows - patch_pad : rows, :] = jnp.zeros((patch_pad, 128), F32)


def cell_masks(grid, rows):
    slot = lax.broadcasted_iota(jnp.int32, (rows, 128), 0)
    row_of = jnp.zeros((rows, 128), jnp.int32)
    for line in range(1, grid):
        row_of = row_of + (slot >= line * grid).astype(jnp.int32)
    column = slot - row_of * grid
    alive = slot < grid * grid
    masks = []
    for down, across in cell_list:
        masks.append(
            alive
            & (row_of + down >= 0)
            & (row_of + down < grid)
            & (column + across >= 0)
            & (column + across < grid)
        )
    return masks


def store_masks(masks, fine, rows):
    for grid, chosen in ((GRID_HI, fine != 0), (GRID_LO, fine == 0)):

        def fill(grid=grid):
            for number, mask in enumerate(cell_masks(grid, rows)):
                masks[number] = mask.astype(F32)

        pl.when(chosen)(fill)


def mix_lane(text, patch, masks, out, lane, text_kernel, patch_kernel, fine, patch_pad, flip):
    cols = pl.ds(pl.multiple_of(lane * 128, 128), 128)
    taps = {}
    for number, (reach, side) in enumerate(tap_list):
        offset = -reach * side if flip else reach * side
        value = text_kernel[number : number + 1, cols]
        taps[offset] = taps[offset] + value if offset in taps else value
    for start, size in row_chunks(TEXT, ROWS):
        total = text[lane, pl.ds(8 + start, size), :] * (1.0 + taps[0])
        for offset, value in taps.items():
            if offset:
                total = total + text[lane, pl.ds(8 + start + offset, size), :] * value
        out[lane, pl.ds(start, size), :] = total
    rows = masks.shape[1]
    for grid, chosen in ((GRID_HI, fine != 0), (GRID_LO, fine == 0)):

        def cells(grid=grid):
            for start, size in row_chunks(rows, 104):
                total = patch[lane, pl.ds(patch_pad + start, size), :]
                for number, (down, across) in enumerate(cell_list):
                    tap = len(cell_list) - 1 - number if flip else number
                    moved = patch[lane, pl.ds(patch_pad + start + down * grid + across, size), :]
                    total = total + (
                        moved * masks[number, pl.ds(start, size), :]
                    ) * patch_kernel[tap : tap + 1, cols]
                out[lane, pl.ds(TEXT + start, size), :] = total

        pl.when(chosen)(cells)


def sort_rows(ranks_ref, source, target, seq, cast):
    for run in range(TEXT // RUN):
        spot = pl.multiple_of(ranks_ref[0, run * RUN], RUN)
        target[pl.ds(spot, RUN), :] = source[run * RUN : (run + 1) * RUN, :].astype(cast)
    target[TEXT:seq, :] = source[TEXT:seq, :].astype(cast)


def unsort_rows(ranks_ref, source, target, seq):
    for run in range(TEXT // RUN):
        spot = pl.multiple_of(ranks_ref[0, run * RUN], RUN)
        target[run * RUN : (run + 1) * RUN, :] = source[pl.ds(spot, RUN), :]
    target[TEXT:seq, :] = source[TEXT:seq, :]


def mix_kernel(
    scalars, ranks_ref, own_ref, other_ref, text_kernel, patch_kernel, weight_ref,
    mixed_ref, low_ref, packed_ref, text, patch, masks, lanes, whole, weights, copies,
):
    side, fine = scalars[0], scalars[2]
    local, width = own_ref.shape
    seq = low_ref.shape[0]
    groups = width // 128
    pad = GRID_HI + 2
    part = width // 2
    fetches = fetch(
        [
            weight_ref.at[:, pl.ds(pl.multiple_of(block * width + side * part, 128), part)]
            for block in range(3)
        ],
        [weights.at[:, block * part : (block + 1) * part] for block in range(3)],
        copies,
    )
    place_slots(own_ref, other_ref, side, text, patch, pad)
    clear_pads(text, patch, pad)
    store_masks(masks, fine, seq - TEXT)

    def one_lane(lane, carry):
        mix_lane(text, patch, masks, lanes, lane, text_kernel, patch_kernel, fine, pad, False)
        return carry

    lax.fori_loop(0, groups, one_lane, 0)
    for lane in range(groups):
        whole[:, 128 * lane : 128 * lane + 128] = lanes[lane]
    mixed_ref[...] = whole[pl.ds(pl.multiple_of(side * local, 8), local), :]
    sort_rows(ranks_ref, whole, low_ref, seq, BF16)
    for copy in fetches:
        copy.wait()
    for start, size in row_chunks(seq, 240):
        rows = slice(start, start + size)
        value = dot_nn(low_ref[rows, :], weights[...]).astype(BF16)
        packed_ref[rows, :part] = value[:, :part] * (HEAD_DIM**-0.5)
        packed_ref[rows, part:] = value[:, part:]


def mix_and_project(scalars, ranks, own, other, text_kernel, patch_kernel, qkv_weight):
    local, width = own.shape
    seq = ranks.shape[1]
    groups = width // 128
    return pl.pallas_call(
        mix_kernel,
        out_shape=(
            jax.ShapeDtypeStruct((local, width), F32),
            jax.ShapeDtypeStruct((seq, width), BF16),
            jax.ShapeDtypeStruct((seq, 3 * width // 2), BF16),
        ),
        in_specs=[smem(), smem()] + [vmem()] * 4 + [parameter()],
        out_specs=(vmem(),) * 3,
        scratch_shapes=[
            pltpu.VMEM((groups, TEXT + 16, 128), F32),
            pltpu.VMEM((groups, seq - TEXT + 2 * (GRID_HI + 2), 128), F32),
            pltpu.VMEM((9, seq - TEXT, 128), F32),
            pltpu.VMEM((groups, seq, 128), F32),
            pltpu.VMEM((seq, width), F32),
            pltpu.VMEM((width, 3 * width // 2), BF16),
            pltpu.SemaphoreType.DMA((3,)),
        ],
        compiler_params=params(16),
        cost_estimate=pl.CostEstimate(
            flops=2 * seq * width * 3 * width // 2, bytes_accessed=12 * MIB, transcendentals=0
        ),
        name="mix_and_project",
    )(scalars, ranks, own, other, text_kernel, patch_kernel, qkv_weight)


def head_lanes(shape, parity):
    return (lax.broadcasted_iota(jnp.int32, shape, 1) >= HEAD_DIM) == (parity != 0)


def skewed(vector, rows, lanes, shift):
    return pltpu.roll(jnp.broadcast_to(vector, (rows, lanes)), shift, 1, stride=1, stride_axis=0)


def attend_kernel(
    scalars, ranks_ref, queries, keys, values, xy_ref, rank_bias, box_bias,
    shares_ref, own_ref, other_ref, left, right, gathered, slots, scores_ref,
):
    side, live = scalars[0], scalars[1]
    seq = queries.shape[0]
    local = own_ref.shape[0]
    head = pl.program_id(0)
    parity = lax.rem(head, 2)

    @pl.when(head == 0)
    def _():
        left[:, 128:] = xy_ref[...]

    left[:, :128] = queries[...]
    mine = head_lanes((seq, 128), parity)
    right[:, :128] = jnp.where(mine, keys[...], jnp.zeros((), BF16))
    right[:, 128:] = box_bias[0]
    top = (seq // ROWS) * ROWS
    alive = lax.broadcasted_iota(jnp.int32, (16, seq), 1) < live
    chunks = row_chunks(seq, 240)

    def product(start, size):
        scores_ref[start : start + size, :] = dot_nt(left[start : start + size, :], right[...])

    def soften(start, size):
        for first in range(start, start + size, 16):
            base = first // ROWS * ROWS
            scores = scores_ref[first : first + 16, :]
            scores = scores + rank_bias[0, first - base : first - base + 16, top - base : top - base + seq]
            scores = jnp.where(alive, scores, neg_fill)
            powered = jnp.exp(scores - jnp.max(scores, axis=1, keepdims=True))
            shares = powered * (1.0 / jnp.sum(powered, axis=1, keepdims=True))
            shares_ref[0, first : first + 16, :] = shares.astype(BF16)

    def apply(start, size):
        context = dot_nn(shares_ref[0, start : start + size, :], values[...])
        gathered[start : start + size, :] = jnp.where(
            head_lanes((size, 128), parity), context, gathered[start : start + size, :]
        )

    product(*chunks[0])
    for n in range(len(chunks)):
        if n + 1 < len(chunks):
            product(*chunks[n + 1])
        if n:
            apply(*chunks[n - 1])
        soften(*chunks[n])
    apply(*chunks[-1])

    @pl.when(parity == 1)
    def _():
        unsort_rows(ranks_ref, gathered, slots, seq)
        own_ref[...] = slots[pl.ds(pl.multiple_of(side * local, 8), local), :].astype(BF16)
        other_ref[...] = slots[pl.ds(pl.multiple_of((1 - side) * local, 8), local), :].astype(BF16)


def attend(scalars, ranks, packed, xy, rank_bias, box_bias, local, first, count):
    seq = packed.shape[0]
    pairs = rank_bias.shape[0] // 2
    heads = 2 * count
    width = heads * HEAD_DIM
    whole = pl.BlockSpec((seq, 2 * SPAN), lambda h: (0, 0))
    slot_spec = pl.BlockSpec((local, 128), lambda h: (0, h // 2))
    return pl.pallas_call(
        attend_kernel,
        grid=(heads,),
        out_shape=(
            jax.ShapeDtypeStruct((heads, seq, seq), BF16),
            jax.ShapeDtypeStruct((local, width), BF16),
            jax.ShapeDtypeStruct((local, width), BF16),
        ),
        in_specs=[
            smem(),
            smem(),
            pl.BlockSpec((seq, 128), lambda h: (0, first + h // 2)),
            pl.BlockSpec((seq, 128), lambda h: (0, pairs + first + h // 2)),
            pl.BlockSpec((seq, 128), lambda h: (0, 2 * pairs + first + h // 2)),
            whole,
            pl.BlockSpec((1, ROWS, RANK_LANES), lambda h: (2 * first + h, 0, 0)),
            pl.BlockSpec((1, seq, 2 * SPAN), lambda h: (2 * first + h, 0, 0)),
        ],
        out_specs=(pl.BlockSpec((1, seq, seq), lambda h: (h, 0, 0)), slot_spec, slot_spec),
        scratch_shapes=[
            pltpu.VMEM((seq, 128 + 2 * SPAN), BF16),
            pltpu.VMEM((seq, 128 + 2 * SPAN), BF16),
            pltpu.VMEM((seq, 128), F32),
            pltpu.VMEM((seq, 128), F32),
            pltpu.VMEM((seq, seq), F32),
        ],
        compiler_params=params(13),
        cost_estimate=pl.CostEstimate(
            flops=heads * 2 * seq * seq * 1024, bytes_accessed=heads * seq * seq * 2,
            transcendentals=heads * seq * seq,
        ),
        name="attend",
    )(scalars, ranks, packed, packed, packed, xy, rank_bias, box_bias)


def attend_back_kernel(
    ranks_ref, own_ref, other_ref, side_ref, shares_ref, queries, keys, values, xy_ref, xyt_ref,
    dq_ref, dk_ref, dv_ref, sums_ref, right, score_grad, spread, rank_sum, slots, upstream, share_grads,
):
    seq = queries.shape[0]
    local = own_ref.shape[0]
    side = side_ref[0]
    head = pl.program_id(0)
    parity = lax.rem(head, 2)
    scale = HEAD_DIM**-0.5

    @pl.when(head == 0)
    def _():
        right[:, 128:] = xy_ref[...]

    @pl.when(parity == 0)
    def _():
        slots[pl.ds(pl.multiple_of(side * local, 8), local), :] = own_ref[...].astype(F32)
        slots[pl.ds(pl.multiple_of((1 - side) * local, 8), local), :] = other_ref[...].astype(F32)
        sort_rows(ranks_ref, slots, upstream, seq, BF16)

    right[:, :128] = keys[...]
    mine = head_lanes((seq, 128), parity)
    own_values = jnp.where(mine, values[...], jnp.zeros((), BF16))
    rank_sum[...] = jnp.zeros(rank_sum.shape, F32)
    top = (seq // ROWS) * ROWS
    chunks = row_chunks(seq, 240)

    def product(start, size):
        share_grads[start : start + size, :] = dot_nt(upstream[start : start + size, :], own_values)

    def soften(start, size):
        for first in range(start, start + size, 16):
            base = first // ROWS * ROWS
            rows = slice(first, first + 16)
            shares = shares_ref[0, rows, :].astype(F32)
            weighted = shares * share_grads[rows, :]
            low = (weighted - shares * jnp.sum(weighted, axis=1, keepdims=True)).astype(BF16)
            score_grad[rows, :] = low
            place = (slice(first - base, first - base + 16), slice(top - base, top - base + seq))
            rank_sum[place] = rank_sum[place] + low.astype(F32)

    def apply(start, size):
        rows = slice(start, start + size)
        product = dot_nn(score_grad[rows, :], right[...])
        spread[rows, :] = product[:, 128:].astype(BF16)
        dq_ref[rows, :] = jnp.where(
            head_lanes((size, 128), parity), (product[:, :128] * scale).astype(BF16), dq_ref[rows, :]
        )

    product(*chunks[0])
    for n in range(len(chunks)):
        if n + 1 < len(chunks):
            product(*chunks[n + 1])
        if n:
            apply(*chunks[n - 1])
        soften(*chunks[n])
    apply(*chunks[-1])
    dk = dot_tn(score_grad[...], queries[...]).astype(BF16)
    dk_ref[...] = jnp.where(mine, dk, dk_ref[...])
    dv = dot_tn(shares_ref[0], upstream[...]).astype(BF16)
    dv_ref[...] = jnp.where(mine, dv, dv_ref[...])
    row = lax.broadcasted_iota(jnp.int32, (ROWS, ROWS), 0)
    col = lax.broadcasted_iota(jnp.int32, (ROWS, ROWS), 1)
    flip = (row + col == ROWS - 1).astype(F32).astype(BF16)
    high = rank_sum[...].astype(BF16)
    rest = (rank_sum[...] - high.astype(F32)).astype(BF16)
    turned = dot_nn(flip, high) + dot_nn(flip, rest)
    turned = pltpu.roll(turned, 0, 1, stride=1, stride_axis=0)
    sums_ref[0, 0:1, :] = jnp.sum(turned, axis=0, keepdims=True)
    for half in range(2):
        part = slice(half * SPAN, (half + 1) * SPAN)
        table = dot_nn(xyt_ref[part, :], spread[:, part])
        table = jnp.concatenate([table, jnp.zeros((SPAN, SPAN), F32)], axis=1)
        table = pltpu.roll(table, 0, 1, stride=1, stride_axis=0)
        sums_ref[0, half + 1 : half + 2, : 2 * SPAN] = jnp.sum(table, axis=0, keepdims=True)


def attend_back(scalars, ranks, own, other, shares, packed, xy, xyt, pair, place, so_far, marker):
    seq = packed.shape[0]
    local = own.shape[0]
    width = packed.shape[1] // 3
    pairs = width // 128
    slot_spec = pl.BlockSpec((local, 128), lambda h: (0, pair))
    out_spec = pl.BlockSpec((seq, 128), lambda h: (0, pair))
    so_far = tuple(so_far) if so_far else ()
    extra = so_far + ((marker,) if marker is not None else ())

    def body(*refs):
        ins, rest = refs[:10], refs[10 + len(extra) :]
        attend_back_kernel(*ins, *rest)

    return pl.pallas_call(
        body,
        grid=(2,),
        out_shape=(jax.ShapeDtypeStruct((seq, width), BF16),) * 3
        + (jax.ShapeDtypeStruct((2, 8, RANK_LANES), F32),),
        in_specs=[
            smem(),
            slot_spec,
            slot_spec,
            smem(),
            pl.BlockSpec((1, seq, seq), lambda h: (2 * place + h, 0, 0)),
            pl.BlockSpec((seq, 128), lambda h: (0, pair)),
            pl.BlockSpec((seq, 128), lambda h: (0, pairs + pair)),
            pl.BlockSpec((seq, 128), lambda h: (0, 2 * pairs + pair)),
            pl.BlockSpec((seq, 2 * SPAN), lambda h: (0, 0)),
            pl.BlockSpec((2 * SPAN, seq), lambda h: (0, 0)),
        ]
        + [anywhere()] * len(extra),
        out_specs=(out_spec,) * 3 + (pl.BlockSpec((1, 8, RANK_LANES), lambda h: (h, 0, 0)),),
        scratch_shapes=[
            pltpu.VMEM((seq, 128 + 2 * SPAN), BF16),
            pltpu.VMEM((seq, seq), BF16),
            pltpu.VMEM((seq, 2 * SPAN), BF16),
            pltpu.VMEM((ROWS, RANK_LANES), F32),
            pltpu.VMEM((seq, 128), F32),
            pltpu.VMEM((seq, 128), BF16),
            pltpu.VMEM((seq, seq), F32),
        ],
        input_output_aliases={10 + n: n for n in range(len(so_far))},
        compiler_params=params(15),
        cost_estimate=pl.CostEstimate(
            flops=1000 if pair else LONG, bytes_accessed=1000, transcendentals=0
        ),
        name="attend_back",
    )(ranks, own, other, scalars, shares, packed, packed, packed, xy, xyt, *extra)


def fold_rows(value):
    total = value[0:8]
    for start in range(8, value.shape[0], 8):
        total = total + value[start : start + 8]
    return total


def row_mean(value):
    return jnp.sum(value, axis=1, keepdims=True) * (1.0 / value.shape[1])


def normalize(value):
    center = value - row_mean(value)
    inverse = lax.rsqrt(row_mean(center * center) + norm_eps)
    return center * inverse, inverse


def dense_kernel(
    scalars, mixed_ref, own_a, own_b, other_a, other_b, pack, cot_ref, out_hbm, up_hbm, down_hbm, marker,
    result_ref, context_ref, hidden_ref, act_ref, branch_ref, pre_ref, attend_ref, resid_ref,
    own_grad, other_grad, sums_ref, blocks_ref,
    out_w, up_w, down_w, slope, product, stash, hidden, normed, scale, bias_sums_ref, copies,
):
    side, live = scalars[0], scalars[1]
    local, width = mixed_ref.shape
    deep = act_ref.shape[1]
    part = own_grad.shape[1]
    step = width
    blocks = deep // step
    gains, shifts, down_bias = pack.at[0:2], pack.at[2:4], pack.at[4:5]
    fetches = [pltpu.make_async_copy(out_hbm, out_w, copies.at[0])]
    fetches += [
        pltpu.make_async_copy(
            up_hbm.at[:, n * width : (n + 1) * width], up_w.at[:, n * width : (n + 1) * width],
            copies.at[1 + n],
        )
        for n in range(deep // width)
    ]
    fetches.append(pltpu.make_async_copy(down_hbm, down_w, copies.at[1 + deep // width]))
    for fetch in fetches:
        fetch.start()
    wide = own_a.shape[1]
    for base, (first, second) in ((side * part, (own_a, own_b)), ((1 - side) * part, (other_a, other_b))):
        context_ref[:, pl.ds(pl.multiple_of(base, 128), wide)] = first[...]
        context_ref[:, pl.ds(pl.multiple_of(base + wide, 128), part - wide)] = second[...]
    chunks = row_chunks(local, 24)
    fetches[0].wait()
    product[...] = dot_nn(context_ref[...], out_w[...])
    for start, size in chunks:
        rows = slice(start, start + size)
        value, inverse = normalize(mixed_ref[rows, :] + product[rows, :])
        normed[rows, :] = value
        scale[rows, :] = jnp.broadcast_to(inverse, (size, 128))
        value = value * gains[0:1, :] + shifts[0:1, :]
        hidden[rows, :] = value
        hidden_ref[rows, :] = value.astype(BF16)

    def lift(block):
        fetches[1 + block].wait()
        cols = slice(block * step, (block + 1) * step)
        stash[block % 2] = dot_nn(hidden_ref[...], up_w[:, cols])

    def bend(block):
        cols = slice(block * step, (block + 1) * step)
        for start, size in chunks:
            rows = slice(start, start + size)
            value = stash[block % 2, rows, :] + pack[5 + block : 6 + block, :]
            half = 0.5 + 0.5 * lax.erf(value * root_half)
            act_ref[rows, cols] = (value * half).astype(BF16)
            slope[rows, cols] = half + value * jnp.exp(-0.5 * value * value) * inv_root_tau

    lift(0)
    for block in range(blocks):
        if block + 1 < blocks:
            lift(block + 1)
        bend(block)
    fetches[-1].wait()
    product[...] = dot_nn(act_ref[...], down_w[...])
    zero = jnp.zeros((8, width), F32)
    gain_sum, shift_sum, bias_sum = zero, zero, zero
    for start, size in chunks:
        rows = slice(start, start + size)
        value, inverse = normalize(hidden[rows, :] + product[rows, :] + down_bias[...])
        slot = lax.broadcasted_iota(jnp.int32, (size, width), 0) + (side * local + start)
        alive = (slot < live).astype(F32)
        result_ref[rows, :] = (alive * (value * gains[1:2, :] + shifts[1:2, :])).astype(BF16)
        upstream = cot_ref[rows, :].astype(F32) * alive
        gain_sum = gain_sum + fold_rows(upstream * value)
        shift_sum = shift_sum + fold_rows(upstream)
        scaled = upstream * gains[1:2, :]
        grad = inverse * (scaled - row_mean(scaled) - value * row_mean(scaled * value))
        bias_sum = bias_sum + fold_rows(grad)
        hidden[rows, :] = grad
        branch_ref[rows, :] = grad.astype(BF16)
    sums_ref[1:2, :] = jnp.sum(gain_sum, axis=0, keepdims=True)
    sums_ref[3:4, :] = jnp.sum(shift_sum, axis=0, keepdims=True)
    sums_ref[4:5, :] = jnp.sum(bias_sum, axis=0, keepdims=True)
    sums_ref[5:8, :] = jnp.zeros((3, width), F32)

    def lower(block):
        cols = slice(block * step, (block + 1) * step)
        stash[block % 2] = dot_nt(branch_ref[...], down_w[cols, :])

    def unbend(block):
        cols = slice(block * step, (block + 1) * step)
        total = jnp.zeros((8, step), F32)
        for start, size in chunks:
            rows = slice(start, start + size)
            value = (stash[block % 2, rows, :] * slope[rows, cols]).astype(BF16)
            pre_ref[rows, cols] = value
            total = total + fold_rows(value.astype(F32))
        bias_sums_ref[:, cols] = jnp.sum(total, axis=0, keepdims=True)

    lower(0)
    for block in range(blocks):
        if block + 1 < blocks:
            lower(block + 1)
        unbend(block)
    product[...] = dot_nt(pre_ref[...], up_w[...])
    piece = deep // blocks_ref.shape[0]
    blocks_ref[...] = jnp.zeros(blocks_ref.shape, F32)
    for block in range(blocks_ref.shape[0]):
        blocks_ref[block : block + 1, :piece] = bias_sums_ref[:, block * piece : (block + 1) * piece]
    gain_sum, shift_sum = zero, zero
    for start, size in chunks:
        rows = slice(start, start + size)
        upstream = hidden[rows, :] + product[rows, :]
        value = normed[rows, :]
        gain_sum = gain_sum + fold_rows(upstream * value)
        shift_sum = shift_sum + fold_rows(upstream)
        scaled = upstream * gains[0:1, :]
        inverse = jnp.concatenate([scale[rows, :]] * (width // 128), axis=1)
        grad = inverse * (scaled - row_mean(scaled) - value * row_mean(scaled * value))
        resid_ref[rows, :] = grad
        attend_ref[rows, :] = grad.astype(BF16)
    sums_ref[0:1, :] = jnp.sum(gain_sum, axis=0, keepdims=True)
    sums_ref[2:3, :] = jnp.sum(shift_sum, axis=0, keepdims=True)
    product[...] = dot_nt(attend_ref[...], out_w[...])
    for base, ref in (((1 - side) * part, other_grad), (side * part, own_grad)):
        ref[...] = product[:, pl.ds(pl.multiple_of(base, 128), part)].astype(BF16)


def dense(
    scalars, mixed, own_context, other_context, pack, cotangent, out_weight, up_weight, down_weight, devices, marker,
):
    local, width = mixed.shape
    deep = up_weight.shape[1]
    part = width // 2
    low = lambda *shape: jax.ShapeDtypeStruct(shape, BF16)
    full = lambda *shape: jax.ShapeDtypeStruct(shape, F32)
    return pl.pallas_call(
        dense_kernel,
        out_shape=(
            low(local, width), low(local, width), low(local, width), low(local, deep),
            low(local, width), low(local, deep), low(local, width), full(local, width),
            low(local, part), low(local, part), full(8, width), full(devices, 128),
        ),
        in_specs=[smem()] + [vmem()] * 7 + [parameter()] * 3 + [anywhere()],
        out_specs=(vmem(),) * 12,
        scratch_shapes=[
            pltpu.VMEM((width, width), BF16),
            pltpu.VMEM((width, deep), BF16),
            pltpu.VMEM((deep, width), BF16),
            pltpu.VMEM((local, deep), F32),
            pltpu.VMEM((local, width), F32),
            pltpu.VMEM((2, local, width), F32),
            pltpu.VMEM((local, width), F32),
            pltpu.VMEM((local, width), F32),
            pltpu.VMEM((local, 128), F32),
            pltpu.VMEM((1, deep), F32),
            pltpu.SemaphoreType.DMA((2 + deep // width,)),
        ],
        compiler_params=params(26),
        cost_estimate=pl.CostEstimate(
            flops=2 * local * width * (4 * deep + 2 * width), bytes_accessed=20 * MIB,
            transcendentals=2 * local * deep,
        ),
        name="dense",
    )(
        scalars, mixed, *own_context, *other_context, pack, cotangent, out_weight, up_weight, down_weight,
        marker,
    )


def halves_of(value):
    high = value.astype(BF16)
    return high, (value - high.astype(F32)).astype(BF16)


def turn_kernel(order_ref, low_ref, marker, turned_ref, after_ref):
    turned_ref[...] = dot_nt(order_ref[...], low_ref[...]).astype(BF16)
    after_ref[...] = jnp.zeros(after_ref.shape, F32)


def turn_rows(order, low, marker):
    return pl.pallas_call(
        turn_kernel,
        out_shape=(
            jax.ShapeDtypeStruct((order.shape[0], low.shape[0]), BF16),
            jax.ShapeDtypeStruct((8, 128), F32),
        ),
        in_specs=[vmem(), vmem(), anywhere()],
        out_specs=(vmem(), vmem()),
        compiler_params=params(8),
        cost_estimate=pl.CostEstimate(flops=10**9, bytes_accessed=1000, transcendentals=0),
        name="turn_rows",
    )(order, low, marker)


def project_back_kernel(
    turned_hbm, dq_hbm, dk_hbm, dv_hbm, marker, keep_ref, send_ref, after_ref, turned, grads, copies
):
    half, part = keep_ref.shape[0], dq_hbm.shape[1]
    fetches = fetch(
        [turned_hbm, dq_hbm, dk_hbm, dv_hbm],
        [turned] + [grads.at[:, block * part : (block + 1) * part] for block in range(3)],
        copies,
    )
    after_ref[...] = jnp.zeros(after_ref.shape, F32)
    for copy in fetches:
        copy.wait()
    send_ref[...] = dot_nn(turned[half:, :], grads[...]).astype(BF16)
    keep_ref[...] = dot_nn(turned[:half, :], grads[...]).astype(BF16)


def project_weight_grad(turned, dq, dk, dv, marker):
    width, seq = turned.shape
    part = dq.shape[1]
    shape = jax.ShapeDtypeStruct((width // 2, 3 * part), BF16)
    return pl.pallas_call(
        project_back_kernel,
        out_shape=(shape, shape, jax.ShapeDtypeStruct((8, 128), F32)),
        in_specs=[anywhere()] * 5,
        out_specs=(vmem(),) * 3,
        scratch_shapes=[
            pltpu.VMEM((width, seq), BF16),
            pltpu.VMEM((seq, 3 * part), BF16),
            pltpu.SemaphoreType.DMA((4,)),
        ],
        compiler_params=params(12),
        cost_estimate=pl.CostEstimate(flops=1000, bytes_accessed=1000, transcendentals=0),
        name="project_weight_grad",
    )(turned, dq, dk, dv, marker)


def fill_block(turned, keep_ref, send_ref, place, right):
    width = right.shape[1]
    middle = turned.shape[0] // 2
    cols = slice(place * width, (place + 1) * width)
    send_ref[:, cols] = dot_nn(turned[middle:, :], right).astype(BF16)
    keep_ref[:, cols] = dot_nn(turned[:middle, :], right).astype(BF16)


def down_kernel(spots, act_ref, branch_ref, keep_ref, send_ref, whole, *, piece):
    width = branch_ref.shape[1]
    half = keep_ref.shape[0]
    for step in range(act_ref.shape[1] // width):
        whole[...] = dot_tn(act_ref[:, step * width : (step + 1) * width], branch_ref[...]).astype(BF16)
        for block in range(width // piece):
            spot = spots[step * (width // piece) + block]
            rows = slice(block * piece, (block + 1) * piece)

            def keep(spot=spot, rows=rows):
                keep_ref[pl.ds(pl.multiple_of(spot, 16), piece), :] = whole[rows, :]

            def send(spot=spot, rows=rows):
                send_ref[pl.ds(pl.multiple_of(spot - half, 16), piece), :] = whole[rows, :]

            pl.when(spot < half)(keep)
            pl.when(spot >= half)(send)


def down_weight_grad(spots, act, branch, piece):
    deep, width = act.shape[1], branch.shape[1]
    tall = jax.ShapeDtypeStruct((deep // 2, width), BF16)
    return pl.pallas_call(
        functools.partial(down_kernel, piece=piece),
        out_shape=(tall, tall),
        in_specs=[smem()] + [vmem()] * 2,
        out_specs=(vmem(),) * 2,
        scratch_shapes=[pltpu.VMEM((width, width), BF16)],
        compiler_params=params(12),
        cost_estimate=pl.CostEstimate(flops=1000, bytes_accessed=1000, transcendentals=0),
        name="down_weight_grad",
    )(spots, act, branch)


def up_kernel(
    pre_ref, hidden_ref, context_ref, attend_ref, first_ref, second_ref, marker,
    out_keep, out_send, up_keep, up_send, turned, *, split,
):
    width = hidden_ref.shape[1]
    block = lambda step: pre_ref[:, step * width : (step + 1) * width]
    turned[...] = dot_nt(first_ref[...], hidden_ref[...]).astype(BF16)
    for step in range(split):
        fill_block(turned, out_keep, out_send, step, block(step))
    turned[...] = dot_nt(first_ref[...], context_ref[...]).astype(BF16)
    fill_block(turned, out_keep, out_send, split, attend_ref[...])
    turned[...] = dot_nt(second_ref[...], hidden_ref[...]).astype(BF16)
    for step in range(split, pre_ref.shape[1] // width):
        fill_block(turned, up_keep, up_send, step - split, block(step))


def up_weight_grads_of(pre, hidden, context, attend, first, second, split, marker):
    local, width = hidden.shape
    steps = pre.shape[1] // width
    low = lambda blocks: jax.ShapeDtypeStruct((width // 2, blocks * width), BF16)
    return pl.pallas_call(
        functools.partial(up_kernel, split=split),
        out_shape=(low(split + 1), low(split + 1), low(steps - split), low(steps - split)),
        in_specs=[vmem()] * 6 + [anywhere()],
        out_specs=(vmem(),) * 4,
        scratch_shapes=[pltpu.VMEM((width, local), BF16)],
        compiler_params=params(14),
        cost_estimate=pl.CostEstimate(flops=LONG, bytes_accessed=1000, transcendentals=0),
        name="up_weight_grad",
    )(pre, hidden, context, attend, first, second, marker)


def mixed_back_kernel(
    scalars, ranks_ref, dq_hbm, dk_hbm, dv_hbm, weight_hbm, resid_hbm, own_hbm, other_hbm,
    marker, grad_ref, send_ref, taps_ref, cells_ref, sorted_grad, whole, text, patch, masks, edge,
    grads, weights, resid_ref, own_ref, other_ref, copies,
):
    side, fine = scalars[0], scalars[2]
    local, width = own_ref.shape
    seq, part = dq_hbm.shape
    groups = width // 128
    pad = GRID_HI + 2
    fetches = fetch(
        [own_hbm, other_hbm, dq_hbm, dk_hbm, dv_hbm]
        + [
            weight_hbm.at[:, pl.ds(pl.multiple_of(block * width + side * part, 128), part)]
            for block in range(3)
        ]
        + [resid_hbm],
        [own_ref, other_ref]
        + [grads.at[:, block * part : (block + 1) * part] for block in range(3)]
        + [weights.at[:, block * part : (block + 1) * part] for block in range(3)]
        + [resid_ref],
        copies,
    )
    fetches[0].wait()
    fetches[1].wait()
    place_slots(own_ref, other_ref, side, text, patch, pad)
    clear_pads(text, patch, pad)
    store_masks(masks, fine, seq - TEXT)
    for copy in fetches[2:]:
        copy.wait()
    for start, size in row_chunks(seq, 240):
        sorted_grad[start : start + size, :] = dot_nt(grads[start : start + size, :], weights[...])
    unsort_rows(ranks_ref, sorted_grad, whole, seq)
    mine = pl.ds(pl.multiple_of(side * local, 8), local)
    theirs = pl.ds(pl.multiple_of((1 - side) * local, 8), local)
    whole[mine, :] = whole[mine, :] + resid_ref[...]
    inner = pl.ds(pl.multiple_of(local - 8 + side * 8, 8), 8)
    outer = pl.ds(pl.multiple_of(local - side * 8, 8), 8)
    edge[0:local, :] = whole[theirs, :]
    edge[local : local + 8, :] = whole[inner, :]
    send_ref[...] = edge[...].astype(BF16)
    grad_ref[0:local, :] = whole[mine, :]
    grad_ref[local : local + 8, :] = whole[outer, :]
    taps_ref[...] = jnp.zeros(taps_ref.shape, F32)
    cells_ref[...] = jnp.zeros(cells_ref.shape, F32)
    for lane in range(groups):
        cols = slice(lane * 128, lane * 128 + 128)
        totals = {offset: jnp.zeros((8, 128), F32) for offset in range(-3, 4)}
        for start, size in row_chunks(TEXT, 64):
            value = whole[start : start + size, cols]
            for offset in totals:
                moved = text[lane, pl.ds(8 + start + offset, size), :]
                totals[offset] = totals[offset] + fold_rows(value * moved)
        for number, (reach, direction) in enumerate(tap_list):
            taps_ref[number : number + 1, cols] = jnp.sum(totals[reach * direction], axis=0, keepdims=True)
    for grid, chosen in ((GRID_HI, fine != 0), (GRID_LO, fine == 0)):

        def cells(grid=grid):
            for lane in range(groups):
                cols = slice(lane * 128, lane * 128 + 128)
                totals = [jnp.zeros((8, 128), F32)] * len(cell_list)
                for start, size in row_chunks(seq - TEXT, 104):
                    value = whole[TEXT + start : TEXT + start + size, cols]
                    for number, (down, across) in enumerate(cell_list):
                        moved = patch[lane, pl.ds(pad + start + down * grid + across, size), :]
                        moved = moved * masks[number, start : start + size, :]
                        totals[number] = totals[number] + fold_rows(value * moved)
                for number, value in enumerate(totals):
                    cells_ref[number : number + 1, cols] = jnp.sum(value, axis=0, keepdims=True)

        pl.when(chosen)(cells)


def mixed_back(scalars, ranks, dq, dk, dv, qkv_weight, resid_grad, own, other, marker):
    local, width = own.shape
    seq, part = dq.shape
    groups = width // 128
    return pl.pallas_call(
        mixed_back_kernel,
        out_shape=(
            jax.ShapeDtypeStruct((local + 8, width), F32),
            jax.ShapeDtypeStruct((local + 8, width), BF16),
            jax.ShapeDtypeStruct((16, width), F32),
            jax.ShapeDtypeStruct((16, width), F32),
        ),
        in_specs=[smem(), smem()] + [anywhere()] * 3 + [parameter()] + [anywhere()] * 4,
        out_specs=(vmem(),) * 4,
        scratch_shapes=[
            pltpu.VMEM((seq, width), F32),
            pltpu.VMEM((seq, width), F32),
            pltpu.VMEM((groups, TEXT + 16, 128), F32),
            pltpu.VMEM((groups, seq - TEXT + 2 * (GRID_HI + 2), 128), F32),
            pltpu.VMEM((9, seq - TEXT, 128), F32),
            pltpu.VMEM((local + 8, width), F32),
            pltpu.VMEM((seq, 3 * part), BF16),
            pltpu.VMEM((width, 3 * part), BF16),
            pltpu.VMEM((local, width), F32),
            pltpu.VMEM((local, width), BF16),
            pltpu.VMEM((local, width), BF16),
            pltpu.SemaphoreType.DMA((9,)),
        ],
        compiler_params=params(15),
        cost_estimate=pl.CostEstimate(flops=1000, bytes_accessed=1000, transcendentals=0),
        name="mixed_back",
    )(scalars, ranks, dq, dk, dv, qkv_weight, resid_grad, own, other, marker)


def token_kernel(
    scalars, grad_ref, received_ref, text_kernel, patch_kernel, marker, out_ref, after_ref,
    text, patch, masks, lanes,
):
    side, fine = scalars[0], scalars[2]
    local, width = out_ref.shape
    groups = width // 128
    pad = GRID_HI + 2
    after_ref[...] = jnp.zeros(after_ref.shape, F32)
    rows = masks.shape[1]
    head = TEXT - local
    clear_pads(text, patch, pad)
    store_masks(masks, fine, rows)

    def load(low):
        for lane in range(groups):
            cols = slice(lane * 128, lane * 128 + 128)
            total = grad_ref[:, cols] + received_ref[:, cols].astype(F32)
            if low:
                text[lane, 8 : 8 + local + 8, :] = total
                text[lane, 16 + local : 8 + TEXT, :] = jnp.zeros((head - 8, 128), F32)
                patch[lane, pad : pad + rows, :] = jnp.zeros((rows, 128), F32)
            else:
                text[lane, 8 : local, :] = jnp.zeros((local - 8, 128), F32)
                text[lane, local : local + 8, :] = total[local:]
                text[lane, 8 + local : 8 + TEXT, :] = total[:head]
                patch[lane, pad : pad + rows, :] = total[head:local]

    pl.when(side == 0)(lambda: load(True))
    pl.when(side != 0)(lambda: load(False))

    def one_lane(lane, carry):
        mix_lane(text, patch, masks, lanes, lane, text_kernel, patch_kernel, fine, pad, True)
        return carry

    lax.fori_loop(0, groups, one_lane, 0)
    mine = pl.ds(pl.multiple_of(side * local, 8), local)
    for lane in range(groups):
        out_ref[:, lane * 128 : lane * 128 + 128] = lanes[lane, mine, :]


def token_back(scalars, grad, received, text_kernel, patch_kernel, seq, marker):
    local, width = grad.shape[0] - 8, grad.shape[1]
    groups = width // 128
    return pl.pallas_call(
        token_kernel,
        out_shape=(jax.ShapeDtypeStruct((local, width), F32), jax.ShapeDtypeStruct((8, 128), F32)),
        in_specs=[smem()] + [vmem()] * 4 + [anywhere()],
        out_specs=(vmem(), vmem()),
        scratch_shapes=[
            pltpu.VMEM((groups, TEXT + 16, 128), F32),
            pltpu.VMEM((groups, seq - TEXT + 2 * (GRID_HI + 2), 128), F32),
            pltpu.VMEM((9, seq - TEXT, 128), F32),
            pltpu.VMEM((groups, seq, 128), F32),
        ],
        compiler_params=params(9),
        cost_estimate=pl.CostEstimate(flops=1000, bytes_accessed=1000, transcendentals=0),
        name="token_back",
    )(scalars, grad, received, text_kernel, patch_kernel, marker)


def finish_kernel(scalars, kept_ref, received_ref, grad_ref):
    side = scalars[0]
    part = kept_ref.shape[1] // 3
    for block in range(3):
        cols = slice(block * part, (block + 1) * part)
        mine = pl.ds(pl.multiple_of((2 * block + side) * part, 128), part)
        theirs = pl.ds(pl.multiple_of((2 * block + 1 - side) * part, 128), part)
        grad_ref[:, mine] = kept_ref[:, cols]
        grad_ref[:, theirs] = received_ref[:, cols].astype(F32)


def finish_little_kernel(
    kept_ref, received_ref, taps_ref, cells_ref, gains_ref, shifts_ref, down_ref, up_ref,
    rank_ref, box_ref, *, ratio, shared, heads,
):
    rows = taps_ref.shape[1]
    small = kept_ref[:rows, :] + received_ref[:rows, :]
    padded = jnp.concatenate([small, jnp.zeros((128 - rows, 128), F32)], axis=0)
    turned = padded.T
    taps_ref[...] = turned[0:9, :rows]
    cells_ref[...] = turned[16:25, :rows]
    gains_ref[...] = turned[32:34, :rows]
    shifts_ref[...] = turned[34:36, :rows]
    down_ref[...] = turned[36:37, :rows]
    row = lax.broadcasted_iota(jnp.int32, (rows, 128), 0)
    lane = lax.broadcasted_iota(jnp.int32, (rows, 128), 1)
    total = jnp.zeros((rows, 128), F32)
    for column in range(ratio):
        value = jnp.broadcast_to(small[:, 40 + column : 41 + column], (rows, 128))
        total = total + jnp.where(lane == row * ratio + column, value, 0.0)
    up_ref[...] = jnp.sum(total, axis=0, keepdims=True)[:, : rows * ratio]
    tables = kept_ref[kept_ref.shape[0] - shared :, :] + received_ref[received_ref.shape[0] - shared :, :]
    for head in range(2 * heads):
        row = head // heads * 16 + head % heads
        rank_ref[head : head + 1, :] = tables[row : row + 1, :NB1]
        box_ref[head, 0:1, :] = tables[row : row + 1, NB1 : NB1 + NB2]
        box_ref[head, 1:2, :] = tables[row + 8 : row + 9, :NB2]


def finish_all_kernel(*refs, ratio, shared, heads):
    scalars = refs[0]
    up_in, joint_in, qkv_in, little_in = (refs[n : n + 2] for n in (1, 3, 5, 7))
    totals, qkv_out, little_out = refs[9:12], refs[12], refs[13:]
    total_kernel(*up_in, *joint_in, *totals)
    finish_kernel(scalars, *qkv_in, qkv_out)
    finish_little_kernel(*little_in, *little_out, ratio=ratio, shared=shared, heads=heads)


def finish_all(scalars, up, joint, qkv, little, width, deep, heads):
    rows, ratio = up.kept.shape[0], deep // width
    full = lambda *shape: jax.ShapeDtypeStruct(shape, F32)
    return pl.pallas_call(
        functools.partial(finish_all_kernel, ratio=ratio, shared=little.shared, heads=heads),
        out_shape=(
            full(rows, deep), full(rows, width), full(rows * ratio, width), full(rows, 3 * width),
            full(9, rows), full(9, rows), full(2, rows), full(2, rows), full(1, rows),
            full(1, rows * ratio), full(2 * heads, NB1), full(2 * heads, 2, NB2),
        ),
        in_specs=[smem()] + [vmem()] * 8,
        out_specs=(vmem(),) * 12,
        compiler_params=params(10),
        cost_estimate=pl.CostEstimate(flops=1000, bytes_accessed=1000, transcendentals=0),
        name="finish_all",
    )(
        scalars, up.kept, up.received, joint.kept, joint.received, qkv.kept, qkv.received,
        little.now, little.received,
    )


def swap(value, stage):
    axis, bit = stage
    count = lax.axis_size(axis)
    return lax.ppermute(value, axis, [(i, i ^ bit) for i in range(count)])


def stage_flag(stage):
    axis, bit = stage
    return (lax.axis_index(axis) & bit) // bit


def block_bit(block, stage, blk_count):
    axis, bit = stage
    shift = bit * blk_count if axis == "page" else bit
    return (block // shift) & 1


def spot_of(block, stages, blk_count):
    spot = jnp.zeros_like(block)
    for stage in stages:
        spot = spot * 2 + (block_bit(block, stage, blk_count) ^ stage_flag(stage))
    return spot


def order_matrix(width, stages, blk_count):
    count = lax.axis_size("page") * blk_count
    piece = width // count
    place = jnp.arange(width, dtype=jnp.int32)
    spot, inside = place // piece, place % piece
    block = jnp.zeros_like(spot)
    for depth, stage in enumerate(stages):
        axis, bit = stage
        shift = bit * blk_count if axis == "page" else bit
        value = ((spot >> (len(stages) - 1 - depth)) & 1) ^ stage_flag(stage)
        block = block + value * shift
    column = block * piece + inside
    return (column[:, None] == jnp.arange(width, dtype=jnp.int32)[None, :]).astype(BF16)


def add_up(terms):
    total = terms[0].astype(F32)
    for term in terms[1:]:
        total = total + term.astype(F32)
    return total


def halve_kernel(kept_ref, received_ref, marker, next_ref, send_ref, after_ref):
    rows = next_ref.shape[0]
    size = rows if rows % 48 else 48
    for start in range(0, rows, size):
        for base, ref in ((rows, send_ref), (0, next_ref)):
            if base % 16 or size % 16:
                place = slice(base + start, base + start + size)
                value = kept_ref[...].astype(F32)[place] + received_ref[...].astype(F32)[place]
            else:
                place = slice(base + start, base + start + size)
                value = kept_ref[place, :].astype(F32) + received_ref[place, :].astype(F32)
            ref[start : start + size, :] = value.astype(ref.dtype)
    after_ref[...] = jnp.zeros(after_ref.shape, F32)


def halve(kept, received, marker, flops=1000):
    rows, width = received.shape[0] // 2, received.shape[1]
    if rows % 8:
        total = kept.astype(F32) + received.astype(F32)
        return total[:rows], total[rows:].astype(BF16), marker
    return pl.pallas_call(
        halve_kernel,
        out_shape=(
            jax.ShapeDtypeStruct((rows, width), F32),
            jax.ShapeDtypeStruct((rows, width), BF16),
            jax.ShapeDtypeStruct((8, 128), F32),
        ),
        in_specs=[vmem(), vmem(), anywhere()],
        out_specs=(vmem(),) * 3,
        compiler_params=params(8),
        cost_estimate=pl.CostEstimate(flops=flops, bytes_accessed=1000, transcendentals=0),
        name="halve",
    )(kept, received, marker)


class Chain:
    def __init__(self, keep, send, stages):
        self.kept, self.stages, self.done = keep, stages, 0
        self.rows = 2 * keep.shape[0]
        self.received = swap(send, stages[0])

    def turn(self, marker, flops=1000):
        self.done += 1
        if self.done >= len(self.stages):
            return marker
        self.kept, send, marker = halve(self.kept, self.received, marker, flops)
        self.received = swap(send, self.stages[self.done])
        return marker


def join_kernel(
    out_kept, out_received, down_kept, down_received, marker, next_ref, send_ref, after_ref, sums, message,
    *, piece, ratio,
):
    rows, width = next_ref.shape[0], down_kept.shape[1]
    wide = out_kept.shape[1]
    for start in range(0, 2 * rows, rows):
        part = slice(start, start + rows)
        value = out_kept[part, :] + out_received[part, :].astype(F32)
        (message if start else next_ref)[:, :wide] = value
    for start in range(0, sums.shape[0], 48):
        part = slice(start, start + 48)
        sums[part, :] = down_kept[part, :] + down_received[part, :].astype(F32)
    for start in range(0, 2 * rows, piece):
        target, place = (next_ref, start) if start < rows else (message, start - rows)
        for turn in range(ratio):
            cols = slice(wide + turn * width, wide + (turn + 1) * width)
            source = ratio * start + turn * piece
            target[place : place + piece, cols] = sums[source : source + piece, :]
    for start in range(0, wide + ratio * width, width):
        cols = slice(start, start + width)
        send_ref[:, cols] = message[:, cols].astype(BF16)
    after_ref[...] = jnp.zeros(after_ref.shape, F32)


def join(out, down, devices, marker):
    rows, wide = out.kept.shape
    tall, width = down.kept.shape
    ratio = tall // rows
    piece = out.rows // devices
    full = wide + ratio * width
    out.done += 1
    down.done += 1
    if piece % 8:
        total = down.kept + down.received.astype(F32)
        total = total.reshape(rows // piece, ratio, piece, width).swapaxes(1, 2).reshape(rows, ratio * width)
        total = jnp.concatenate([out.kept + out.received.astype(F32), total], axis=1)
        kept, send = total[: rows // 2], total[rows // 2 :].astype(BF16)
    else:
        kept, send, marker = pl.pallas_call(
            functools.partial(join_kernel, piece=piece, ratio=ratio),
            out_shape=(
                jax.ShapeDtypeStruct((rows // 2, full), F32),
                jax.ShapeDtypeStruct((rows // 2, full), BF16),
                jax.ShapeDtypeStruct((8, 128), F32),
            ),
            in_specs=[vmem()] * 4 + [anywhere()],
            out_specs=(vmem(),) * 3,
            scratch_shapes=[pltpu.VMEM((tall, width), F32), pltpu.VMEM((rows // 2, full), F32)],
            compiler_params=params(10),
            cost_estimate=pl.CostEstimate(flops=1000, bytes_accessed=1000, transcendentals=0),
            name="join",
        )(out.kept, out.received, down.kept, down.received, marker)
    return Chain(kept, send, out.stages[out.done :]), marker


def total_kernel(
    up_kept, up_received, kept_ref, received_ref, up_ref, out_ref, down_ref
):
    piece, width = out_ref.shape
    wide = up_ref.shape[1] - up_kept.shape[1]
    value = kept_ref[...] + received_ref[...].astype(F32)
    up_ref[:, :wide] = value[:, :wide]
    up_ref[:, wide:] = up_kept[...] + up_received[...].astype(F32)
    out_ref[...] = value[:, wide : wide + width]
    for turn in range(down_ref.shape[0] // piece):
        start = wide + (turn + 1) * width
        down_ref[turn * piece : (turn + 1) * piece, :] = value[:, start : start + width]


def little_kernel(now_ref, received_ref, marker, next_ref, message_ref, after_ref, *, shared):
    rows = received_ref.shape[0] - shared
    half = message_ref.shape[0] - shared
    common = now_ref[2 * rows :, :] + received_ref[rows:, :]
    kept = now_ref[:rows, :] + received_ref[:rows, :]
    next_ref[:rows, :] = kept
    next_ref[rows:, :] = common
    message_ref[:half, :] = kept[half:]
    message_ref[half:, :] = common
    after_ref[...] = jnp.zeros(after_ref.shape, F32)


class Little:
    def __init__(self, now, shared, stages):
        self.now, self.shared, self.stages, self.done = now, shared, stages, 0
        rows = (now.shape[0] - shared) // 2
        self.received = swap(now[rows:], stages[0])

    def turn(self, marker):
        self.done += 1
        if self.done > len(self.stages):
            return marker
        rows = self.received.shape[0] - self.shared
        if self.done == len(self.stages):
            return marker
        half = rows // 2
        if half % 8:
            kept = self.now[:rows] + self.received[:rows]
            common = self.now[2 * rows :] + self.received[rows:]
            self.now = jnp.concatenate([kept, common], axis=0)
            message = self.now[half:]
        else:
            lanes = self.now.shape[1]
            self.now, message, marker = pl.pallas_call(
                functools.partial(little_kernel, shared=self.shared),
                out_shape=(
                    jax.ShapeDtypeStruct((rows + self.shared, lanes), F32),
                    jax.ShapeDtypeStruct((half + self.shared, lanes), F32),
                    jax.ShapeDtypeStruct((8, 128), F32),
                ),
                in_specs=[vmem(), vmem(), anywhere()],
                out_specs=(vmem(),) * 3,
                compiler_params=params(4),
                cost_estimate=pl.CostEstimate(flops=1000, bytes_accessed=1000, transcendentals=0),
                name="little",
            )(self.now, self.received, marker)
        self.received = swap(message, self.stages[self.done])
        return marker


def gather_kernel(
    scalars, order_hbm, owner_hbm, inside_hbm, fold_hbm, rank_hbm, box_hbm, taps_hbm, cells_hbm, dense_hbm,
    blocks_hbm, sums_a, sums_b, sums_c, marker, out_ref, after_ref,
    order, owner, inside, fold, rank, box, taps, cells, dense_sums, blocks, sums, copies,
):
    fetches = fetch(
        [order_hbm, owner_hbm, inside_hbm, fold_hbm, rank_hbm, box_hbm, taps_hbm, cells_hbm,
         dense_hbm, blocks_hbm, sums_a, sums_b, sums_c],
        [order, owner, inside, fold, rank, box, taps, cells, dense_sums, blocks]
        + [sums.at[pl.ds(2 * n, 2)] for n in range(3)],
        copies,
    )
    for copy in fetches:
        copy.wait()
    after_ref[...] = jnp.zeros(after_ref.shape, F32)
    width = order.shape[0]

    rows = jnp.concatenate([taps[...], cells[...], dense_sums[...]], axis=0)
    rows = jnp.concatenate([rows, jnp.zeros((128 - rows.shape[0], width), F32)], axis=0)
    spread = dot_nn(owner[...], blocks[...].astype(BF16)) * inside[...].astype(F32)
    bias = dot_nn(spread.astype(BF16), fold[...]).astype(BF16)
    out_ref[:width, :] = dot_nt(order[...], rows.astype(BF16)) + dot_nn(order[...], bias)
    out_ref[width:, :] = jnp.zeros((32, 128), F32)
    heads = sums.shape[0]
    mine = pl.multiple_of(width + scalars[0] * 16, 16)
    pad = lambda value: jnp.concatenate([value, jnp.zeros((8 - heads, value.shape[1]), F32)], axis=0)
    by_rank = pad(jnp.concatenate([sums[head, 0:1, :] for head in range(heads)], axis=0))
    table = sum(dot_nn(piece, rank[...]) for piece in halves_of(by_rank))
    out_ref[pl.ds(mine, 8), 0:NB1] = table
    for half in range(2):
        by_box = pad(
            jnp.concatenate([sums[head, half + 1 : half + 2, : 2 * SPAN] for head in range(heads)], axis=0)
        )
        table = sum(dot_nn(piece, box[...]) for piece in halves_of(by_box))
        if half == 0:
            out_ref[pl.ds(mine, 8), NB1 : NB1 + NB2] = table
        else:
            out_ref[pl.ds(mine + 8, 8), 0:NB2] = table


def gather_small(scalars, order, taps, cells, dense_sums, blocks, sums, deep, marker):
    width = order.shape[0]
    devices = blocks.shape[0]
    ratio = deep // width
    piece = width // devices
    rows, lanes = np.arange(width), np.arange(128)
    owner = jnp.asarray(rows[:, None] // piece == np.arange(devices)[None, :], BF16)
    inside = jnp.asarray(
        (lanes[None, :] // ratio == rows[:, None] % piece) & (lanes[None, :] < piece * ratio), BF16
    )
    fold = jnp.asarray(lanes[:, None] % ratio + 40 == lanes[None, :], BF16)
    rank = jnp.asarray(bucket_rows(np.arange(RANK_LANES) - (RANK_MID - 1), rank_marks, NB1), BF16)
    box = jnp.asarray(bucket_rows(np.arange(2 * SPAN) - (SPAN - 1), box_marks, NB2), BF16)
    constants = tuple(map(stay, (owner, inside, fold, rank, box)))
    operands = (order, *constants, taps, cells, dense_sums, blocks)
    return pl.pallas_call(
        gather_kernel,
        out_shape=(
            jax.ShapeDtypeStruct((width + 32, 128), F32), jax.ShapeDtypeStruct((8, 128), F32)
        ),
        in_specs=[smem(), anywhere()] + [parameter()] * 5 + [anywhere()] * 8,
        out_specs=(vmem(), vmem()),
        scratch_shapes=[pltpu.VMEM(value.shape, value.dtype) for value in operands]
        + [pltpu.VMEM((2 * len(sums), 8, RANK_LANES), F32), pltpu.SemaphoreType.DMA((13,))],
        compiler_params=params(10),
        cost_estimate=pl.CostEstimate(flops=1000, bytes_accessed=1000, transcendentals=0),
        name="gather_small",
    )(scalars, *operands, *sums, marker)


def per_device(
    tokens,
    patch_count,
    reading_rank,
    boxes,
    text_kernel,
    patch_kernel,
    qkv_weight,
    rank_table,
    box_tables,
    out_weight,
    norm_gains,
    norm_shifts,
    up_weight,
    up_bias,
    down_weight,
    down_bias,
    cotangent,
):
    qkv_weight, out_weight, up_weight, down_weight = map(
        stay, (qkv_weight, out_weight, up_weight, down_weight)
    )
    side = lax.axis_index("blk")
    blk_count = lax.axis_size("blk")
    page_stages = [("page", 1 << n) for n in range(lax.axis_size("page").bit_length() - 1)]
    across = ("blk", 1)
    out_stages = page_stages[:1] + [across] + page_stages[1:]
    up_stages = page_stages[:1] + page_stages[2:] + [across] + page_stages[1:2]
    down_stages = page_stages[:2] + [across] + page_stages[2:]
    qkv_stages = page_stages[:1] + page_stages[2:] + page_stages[1:2] + [across]
    little_stages = page_stages[:2] + [across] + page_stages[2:]
    devices = lax.axis_size("page") * blk_count
    count = patch_count[0]
    ranks = reading_rank
    own = tokens[0]
    local, width = own.shape
    deep = up_bias.shape[0]
    seq = ranks.shape[1]
    heads = HEADS // blk_count
    scalars = jnp.stack(
        [side, TEXT + count, (count == GRID_HI * GRID_HI).astype(jnp.int32), jnp.int32(0)]
    ).astype(jnp.int32)
    other = swap(own, across)

    xy, xyt, rank_bias, box_bias = onehots(scalars, ranks, boxes, rank_table, box_tables, heads)
    mixed, mixed_low, packed = mix_and_project(
        scalars, ranks, own, other, text_kernel, patch_kernel, qkv_weight
    )
    pack = jnp.concatenate([norm_gains, norm_shifts, down_bias[None], up_bias.reshape(-1, width)], axis=0)
    own_context, other_context, shares = [], [], []
    for first, pairs in ((0, 2), (2, 1)):
        share, mine, theirs = attend(
            scalars, ranks, packed, xy, rank_bias, box_bias, local, first, pairs
        )
        shares += [(share, place) for place in range(pairs)]
        own_context.append(mine)
        other_context.append(swap(theirs, across))
    order_qkv = order_matrix(width, qkv_stages, blk_count)
    order_little = order_matrix(width, little_stages, blk_count)
    turned, marker = turn_rows(order_qkv, mixed_low, own_context[-1])
    (
        layer_output, context, hidden_low, act_low, branch_grad, pre_grad, attend_grad,
        resid_one_grad, own_part, their_part, dense_sums, bias_blocks,
    ) = dense(
        scalars, mixed, own_context, other_context, pack, cotangent[0], out_weight, up_weight,
        down_weight, devices, marker,
    )
    part = width // blk_count
    received_part = swap(their_part, across)

    order_out = order_matrix(width, out_stages, blk_count)
    order_up = order_matrix(width, up_stages, blk_count)
    piece = deep // devices
    blocks = jnp.arange(devices, dtype=jnp.int32)
    spots = spot_of(blocks, down_stages, blk_count) * piece
    act_rows = act_low
    if piece % 16:
        place = jnp.arange(deep, dtype=jnp.int32)
        target = spots[place // piece] + place % piece
        act_rows = jnp.zeros_like(act_low).at[:, target].set(act_low, unique_indices=True)
        piece = width // 8
        spots = jnp.arange(deep // piece, dtype=jnp.int32) * piece
    steps = deep // width
    split = steps // 2
    down_keep, down_send = down_weight_grad(spots, act_rows, branch_grad, piece)
    down = Chain(down_keep, down_send, down_stages)
    out_keep, out_send, up_keep, up_send = up_weight_grads_of(
        pre_grad, hidden_low, context, attend_grad, order_out, order_up, split, down_keep
    )
    out = Chain(out_keep, out_send, out_stages)
    up = Chain(up_keep, up_send, up_stages)
    marker = down.turn(up_send)

    grads, sums = None, []
    for pair, (share, place) in enumerate(shares):
        if pair == 1:
            marker = up.turn(out.turn(sums[0]))
        *grads, pair_sums = attend_back(
            scalars, ranks, own_part, received_part, share, packed, xy, xyt, pair, place, grads,
            marker if pair < 2 else None,
        )
        sums.append(pair_sums)
    dq, dk, dv = grads
    qkv_keep, qkv_send, marker = project_weight_grad(turned, dq, dk, dv, sums[-1])
    qkv = Chain(qkv_keep, qkv_send, qkv_stages)
    marker = down.turn(out.turn(up.turn(marker)), LONG)
    marker = qkv.turn(marker)
    grad, outgoing, taps, cells = mixed_back(
        scalars, ranks, dq, dk, dv, qkv_weight, resid_one_grad, stay(own), other, marker
    )
    incoming = swap(outgoing, across)
    gathered, marker = gather_small(
        scalars, order_little, taps, cells, dense_sums, bias_blocks, sums, deep, taps
    )
    little = Little(gathered, 32, little_stages)
    marker = up.turn(qkv.turn(marker))
    joint, marker = join(out, down, devices, marker)
    marker = little.turn(little.turn(marker))
    token_grad, marker = token_back(
        scalars, grad, incoming, text_kernel, patch_kernel, seq, marker
    )
    for _ in range(len(qkv_stages) - 4):
        for chain in (qkv, little, up, joint):
            marker = chain.turn(marker)
    marker = little.turn(qkv.turn(marker))
    for _ in qkv_stages:
        marker = little.turn(qkv.turn(marker))
    (
        up_weight_grads, out_weight_grads, down_weight_grads, qkv_weight_grad, taps, cells, gains, shifts,
        down_bias_grad, up_bias_grad, rank_grad, box_grad,
    ) = finish_all(scalars, up, joint, qkv, little, width, deep, heads)
    return (
        layer_output[None],
        token_grad[None],
        taps,
        cells,
        qkv_weight_grad,
        rank_grad,
        jnp.swapaxes(box_grad, 0, 1),
        out_weight_grads,
        gains,
        shifts,
        up_weight_grads,
        up_bias_grad[0],
        down_weight_grads,
        down_bias_grad[0],
    )


def solution(mesh):
    in_specs = (
        P("page", "blk", None),
        P("page"),
        P("page", None),
        P(None, "page", None),
        P(),
        P(),
        P(),
        P(),
        P(),
        P(),
        P(),
        P(),
        P(),
        P(),
        P(),
        P(),
        P("page", "blk", None),
    )
    out_specs = (
        P("page", "blk", None),
        P("page", "blk", None),
        P(None, ("page", "blk")),
        P(None, ("page", "blk")),
        P(("page", "blk"), None),
        P(),
        P(),
        P(("page", "blk"), None),
        P(None, ("page", "blk")),
        P(None, ("page", "blk")),
        P(("page", "blk"), None),
        P(("page", "blk")),
        P(("page", "blk"), None),
        P(("page", "blk")),
    )
    return jax.shard_map(
        per_device, mesh=mesh, in_specs=in_specs, out_specs=out_specs, check_vma=False
    )
```

```python
import functools

import jax
import jax.numpy as jnp
import numpy as np
from jax import lax
from jax.experimental import pallas as pl
from jax.experimental.pallas import tpu as pltpu
from jax.sharding import PartitionSpec as P

TEXT = 512
GRID_LO = 7
GRID_HI = 14
RUN = 16
HEADS = 12
HEAD_DIM = 64
NB1 = 32
NB2 = 64
SPAN = 256
RANK_LANES = 1536
RANK_MID = RANK_LANES // 2
ROWS = 128
F32 = jnp.float32
BF16 = jnp.bfloat16
MIB = 1 << 20
LONG = 10**11

rank_marks = (1, 2, 3, 4, 5, 6, 7, 8, 12, 16, 23, 32, 46, 64, 91)
box_marks = tuple(range(1, 17)) + (19, 23, 27, 32, 39, 46, 54, 64, 77, 91, 108, 128, 153, 182, 216)
neg_fill = -1000000000.0
norm_eps = 1e-05
root_half = 0.7071067811865476
inv_root_tau = 0.3989422804014327
tap_list = ((1, -1), (1, 0), (1, 1), (2, -1), (2, 0), (2, 1), (3, -1), (3, 0), (3, 1))
cell_list = ((-1, -1), (-1, 0), (-1, 1), (0, -1), (0, 0), (0, 1), (1, -1), (1, 0), (1, 1))


def bucket_rows(deltas, marks, bins):
    spread = np.abs(deltas)
    ids = np.sum(spread[:, None] >= np.asarray(marks)[None, :], axis=1) + (bins // 2) * (deltas > 0)
    return (ids[:, None] == np.arange(bins)[None, :]).astype(np.float32)


def dot_nn(left, right):
    return lax.dot_general(left, right, (((1,), (0,)), ((), ())), preferred_element_type=F32)


def dot_nt(left, right):
    return lax.dot_general(left, right, (((1,), (1,)), ((), ())), preferred_element_type=F32)


def dot_tn(left, right):
    return lax.dot_general(left, right, (((0,), (0,)), ((), ())), preferred_element_type=F32)


def row_chunks(total, size):
    return [(start, min(size, total - start)) for start in range(0, total, size)]


def vmem():
    return pl.BlockSpec(memory_space=pltpu.VMEM)


def smem():
    return pl.BlockSpec(memory_space=pltpu.SMEM)


def anywhere():
    return pl.BlockSpec(memory_space=pl.ANY)


def parameter():
    return pl.BlockSpec(memory_space=pltpu.HBM)


def stay(value):
    return pltpu.with_memory_space_constraint(value, pltpu.HBM)


def fetch(sources, targets, semaphores):
    copies = []
    for number, (source, target) in enumerate(zip(sources, targets)):
        copies.append(pltpu.make_async_copy(source, target, semaphores.at[number]))
        copies[-1].start()
    return copies


def params(mib):
    return pltpu.CompilerParams(vmem_limit_bytes=mib * MIB)


def onehot_kernel(
    scalars, rank_hbm, box_hbm, rank_table_hbm, box_tables_hbm, rank_rows_hbm, box_rows_hbm,
    xy_ref, xyt_ref, rank_bias, box_bias,
    rank_ref, box_ref, rank_table, box_tables, rank_rows, box_rows, vectors, copies,
):
    fetches = fetch(
        [rank_hbm, box_hbm, rank_table_hbm, box_tables_hbm, rank_rows_hbm, box_rows_hbm],
        [rank_ref, box_ref, rank_table, box_tables, rank_rows, box_rows],
        copies,
    )
    for copy in fetches:
        copy.wait()
    seq = rank_ref.shape[1]
    for start, size in row_chunks(seq, 240):
        spot = lax.broadcasted_iota(jnp.int32, (size, seq), 0) + start
        order = (spot == rank_ref[...]).astype(F32).astype(BF16)
        for half in range(2):
            level = lax.broadcasted_iota(jnp.int32, (SPAN, seq), 0)
            marks = (level == box_ref[half]).astype(F32).astype(BF16)
            xy_ref[start : start + size, half * SPAN : (half + 1) * SPAN] = dot_nt(
                order, marks
            ).astype(BF16)
    row = lax.broadcasted_iota(jnp.int32, (SPAN, SPAN), 0)
    col = lax.broadcasted_iota(jnp.int32, (SPAN, SPAN), 1)
    flip = (row + col == SPAN - 1).astype(F32).astype(BF16)
    for half in range(2):
        part = slice(half * SPAN, (half + 1) * SPAN)
        xyt_ref[part, :] = dot_nt(flip, xy_ref[:, part]).astype(BF16)
    heads = vectors.shape[0]
    tables = [(dot_nt(rank_table[...], rank_rows[...]), RANK_LANES)]
    tables += [(dot_nt(box_tables[half], box_rows[...]), 2 * SPAN) for half in range(2)]
    for place, (table, lanes) in enumerate(tables):
        own = jnp.where(scalars[0] == 0, table[:heads], table[table.shape[0] - heads :])
        for head in range(heads):
            vectors[head, place : place + 1, :lanes] = own[head : head + 1]

    def one_head(head, carry):
        rank_bias[head] = skewed(vectors[head, 0:1, :], ROWS, RANK_LANES, RANK_LANES - 128)
        for half in range(2):
            part = slice(half * SPAN, (half + 1) * SPAN)
            table = skewed(vectors[head, half + 1 : half + 2, : 2 * SPAN], SPAN, 2 * SPAN, SPAN + 1)
            box_bias[head, :, part] = dot_nn(xy_ref[:, part], table[:, :SPAN].astype(BF16)).astype(BF16)
        return carry

    lax.fori_loop(0, heads, one_head, 0)


def onehots(scalars, ranks, boxes, rank_table, box_tables, heads):
    seq = ranks.shape[1]
    rank_rows = jnp.asarray(bucket_rows(np.arange(RANK_LANES) - RANK_MID, rank_marks, NB1), BF16)
    box_rows = jnp.asarray(bucket_rows(SPAN - 1 - np.arange(2 * SPAN), box_marks, NB2), BF16)
    operands = tuple(map(stay, (ranks, boxes, rank_table, box_tables, rank_rows, box_rows)))
    return pl.pallas_call(
        onehot_kernel,
        out_shape=(
            jax.ShapeDtypeStruct((seq, 2 * SPAN), BF16),
            jax.ShapeDtypeStruct((2 * SPAN, seq), BF16),
            jax.ShapeDtypeStruct((heads, ROWS, RANK_LANES), F32),
            jax.ShapeDtypeStruct((heads, seq, 2 * SPAN), BF16),
        ),
        in_specs=[smem()] + [parameter()] * 6,
        out_specs=(vmem(),) * 4,
        scratch_shapes=[pltpu.VMEM(value.shape, value.dtype) for value in operands]
        + [pltpu.VMEM((heads, 8, RANK_LANES), F32), pltpu.SemaphoreType.DMA((6,))],
        compiler_params=params(14),
        cost_estimate=pl.CostEstimate(
            flops=4 * seq * seq * SPAN, bytes_accessed=4 * seq * 2 * SPAN, transcendentals=0
        ),
        name="onehots",
    )(scalars, *operands)


def place_slots(own_ref, other_ref, side, text, patch, patch_pad):
    local = own_ref.shape[0]
    head = TEXT - local
    groups = text.shape[0]

    def place(low_ref, high_ref):
        for lane in range(groups):
            cols = slice(128 * lane, 128 * lane + 128)
            text[lane, 8 : 8 + local, :] = low_ref[:, cols].astype(F32)
            high = high_ref[:, cols].astype(F32)
            text[lane, 8 + local : 8 + TEXT, :] = high[:head]
            patch[lane, patch_pad : patch_pad + local - head, :] = high[head:]

    pl.when(side == 0)(lambda: place(own_ref, other_ref))
    pl.when(side != 0)(lambda: place(other_ref, own_ref))


def clear_pads(text, patch, patch_pad):
    groups, rows = patch.shape[0], patch.shape[1]
    for lane in range(groups):
        text[lane, 0:8, :] = jnp.zeros((8, 128), F32)
        text[lane, 8 + TEXT : 16 + TEXT, :] = jnp.zeros((8, 128), F32)
        patch[lane, 0:patch_pad, :] = jnp.zeros((patch_pad, 128), F32)
        patch[lane, rows - patch_pad : rows, :] = jnp.zeros((patch_pad, 128), F32)


def cell_masks(grid, rows):
    slot = lax.broadcasted_iota(jnp.int32, (rows, 128), 0)
    row_of = jnp.zeros((rows, 128), jnp.int32)
    for line in range(1, grid):
        row_of = row_of + (slot >= line * grid).astype(jnp.int32)
    column = slot - row_of * grid
    alive = slot < grid * grid
    masks = []
    for down, across in cell_list:
        masks.append(
            alive
            & (row_of + down >= 0)
            & (row_of + down < grid)
            & (column + across >= 0)
            & (column + across < grid)
        )
    return masks


def store_masks(masks, fine, rows):
    for grid, chosen in ((GRID_HI, fine != 0), (GRID_LO, fine == 0)):

        def fill(grid=grid):
            for number, mask in enumerate(cell_masks(grid, rows)):
                masks[number] = mask.astype(F32)

        pl.when(chosen)(fill)


def mix_lane(text, patch, masks, out, lane, text_kernel, patch_kernel, fine, patch_pad, flip):
    cols = pl.ds(pl.multiple_of(lane * 128, 128), 128)
    taps = {}
    for number, (reach, side) in enumerate(tap_list):
        offset = -reach * side if flip else reach * side
        value = text_kernel[number : number + 1, cols]
        taps[offset] = taps[offset] + value if offset in taps else value
    for start, size in row_chunks(TEXT, ROWS):
        total = text[lane, pl.ds(8 + start, size), :] * (1.0 + taps[0])
        for offset, value in taps.items():
            if offset:
                total = total + text[lane, pl.ds(8 + start + offset, size), :] * value
        out[lane, pl.ds(start, size), :] = total
    rows = masks.shape[1]
    for grid, chosen in ((GRID_HI, fine != 0), (GRID_LO, fine == 0)):

        def cells(grid=grid):
            for start, size in row_chunks(rows, 104):
                total = patch[lane, pl.ds(patch_pad + start, size), :]
                for number, (down, across) in enumerate(cell_list):
                    tap = len(cell_list) - 1 - number if flip else number
                    moved = patch[lane, pl.ds(patch_pad + start + down * grid + across, size), :]
                    total = total + (
                        moved * masks[number, pl.ds(start, size), :]
                    ) * patch_kernel[tap : tap + 1, cols]
                out[lane, pl.ds(TEXT + start, size), :] = total

        pl.when(chosen)(cells)


def sort_rows(ranks_ref, source, target, seq, cast):
    for run in range(TEXT // RUN):
        spot = pl.multiple_of(ranks_ref[0, run * RUN], RUN)
        target[pl.ds(spot, RUN), :] = source[run * RUN : (run + 1) * RUN, :].astype(cast)
    target[TEXT:seq, :] = source[TEXT:seq, :].astype(cast)


def unsort_rows(ranks_ref, source, target, seq):
    for run in range(TEXT // RUN):
        spot = pl.multiple_of(ranks_ref[0, run * RUN], RUN)
        target[run * RUN : (run + 1) * RUN, :] = source[pl.ds(spot, RUN), :]
    target[TEXT:seq, :] = source[TEXT:seq, :]


def mix_kernel(
    scalars, ranks_ref, own_ref, other_ref, text_kernel, patch_kernel, weight_ref,
    mixed_ref, low_ref, packed_ref, text, patch, masks, lanes, whole, weights, copies,
):
    side, fine = scalars[0], scalars[2]
    local, width = own_ref.shape
    seq = low_ref.shape[0]
    groups = width // 128
    pad = GRID_HI + 2
    part = width // 2
    fetches = fetch(
        [
            weight_ref.at[:, pl.ds(pl.multiple_of(block * width + side * part, 128), part)]
            for block in range(3)
        ],
        [weights.at[:, block * part : (block + 1) * part] for block in range(3)],
        copies,
    )
    place_slots(own_ref, other_ref, side, text, patch, pad)
    clear_pads(text, patch, pad)
    store_masks(masks, fine, seq - TEXT)

    def one_lane(lane, carry):
        mix_lane(text, patch, masks, lanes, lane, text_kernel, patch_kernel, fine, pad, False)
        return carry

    lax.fori_loop(0, groups, one_lane, 0)
    for lane in range(groups):
        whole[:, 128 * lane : 128 * lane + 128] = lanes[lane]
    mixed_ref[...] = whole[pl.ds(pl.multiple_of(side * local, 8), local), :]
    sort_rows(ranks_ref, whole, low_ref, seq, BF16)
    for copy in fetches:
        copy.wait()
    for start, size in row_chunks(seq, 240):
        rows = slice(start, start + size)
        value = dot_nn(low_ref[rows, :], weights[...]).astype(BF16)
        packed_ref[rows, :part] = value[:, :part] * (HEAD_DIM**-0.5)
        packed_ref[rows, part:] = value[:, part:]


def mix_and_project(scalars, ranks, own, other, text_kernel, patch_kernel, qkv_weight):
    local, width = own.shape
    seq = ranks.shape[1]
    groups = width // 128
    return pl.pallas_call(
        mix_kernel,
        out_shape=(
            jax.ShapeDtypeStruct((local, width), F32),
            jax.ShapeDtypeStruct((seq, width), BF16),
            jax.ShapeDtypeStruct((seq, 3 * width // 2), BF16),
        ),
        in_specs=[smem(), smem()] + [vmem()] * 4 + [parameter()],
        out_specs=(vmem(),) * 3,
        scratch_shapes=[
            pltpu.VMEM((groups, TEXT + 16, 128), F32),
            pltpu.VMEM((groups, seq - TEXT + 2 * (GRID_HI + 2), 128), F32),
            pltpu.VMEM((9, seq - TEXT, 128), F32),
            pltpu.VMEM((groups, seq, 128), F32),
            pltpu.VMEM((seq, width), F32),
            pltpu.VMEM((width, 3 * width // 2), BF16),
            pltpu.SemaphoreType.DMA((3,)),
        ],
        compiler_params=params(16),
        cost_estimate=pl.CostEstimate(
            flops=2 * seq * width * 3 * width // 2, bytes_accessed=12 * MIB, transcendentals=0
        ),
        name="mix_and_project",
    )(scalars, ranks, own, other, text_kernel, patch_kernel, qkv_weight)


def head_lanes(shape, parity):
    return (lax.broadcasted_iota(jnp.int32, shape, 1) >= HEAD_DIM) == (parity != 0)


def skewed(vector, rows, lanes, shift):
    return pltpu.roll(jnp.broadcast_to(vector, (rows, lanes)), shift, 1, stride=1, stride_axis=0)


def attend_kernel(
    scalars, ranks_ref, queries, keys, values, xy_ref, rank_bias, box_bias,
    shares_ref, own_ref, other_ref, left, right, gathered, slots, scores_ref,
):
    side, live = scalars[0], scalars[1]
    seq = queries.shape[0]
    local = own_ref.shape[0]
    head = pl.program_id(0)
    parity = lax.rem(head, 2)

    @pl.when(head == 0)
    def _():
        left[:, 128:] = xy_ref[...]

    left[:, :128] = queries[...]
    mine = head_lanes((seq, 128), parity)
    right[:, :128] = jnp.where(mine, keys[...], jnp.zeros((), BF16))
    right[:, 128:] = box_bias[0]
    top = (seq // ROWS) * ROWS
    alive = lax.broadcasted_iota(jnp.int32, (16, seq), 1) < live
    chunks = row_chunks(seq, 240)

    def product(start, size):
        scores_ref[start : start + size, :] = dot_nt(left[start : start + size, :], right[...])

    def soften(start, size):
        for first in range(start, start + size, 16):
            base = first // ROWS * ROWS
            scores = scores_ref[first : first + 16, :]
            scores = scores + rank_bias[0, first - base : first - base + 16, top - base : top - base + seq]
            scores = jnp.where(alive, scores, neg_fill)
            powered = jnp.exp(scores - jnp.max(scores, axis=1, keepdims=True))
            shares = powered * (1.0 / jnp.sum(powered, axis=1, keepdims=True))
            shares_ref[0, first : first + 16, :] = shares.astype(BF16)

    def apply(start, size):
        context = dot_nn(shares_ref[0, start : start + size, :], values[...])
        gathered[start : start + size, :] = jnp.where(
            head_lanes((size, 128), parity), context, gathered[start : start + size, :]
        )

    product(*chunks[0])
    for n in range(len(chunks)):
        if n + 1 < len(chunks):
            product(*chunks[n + 1])
        if n:
            apply(*chunks[n - 1])
        soften(*chunks[n])
    apply(*chunks[-1])

    @pl.when(parity == 1)
    def _():
        unsort_rows(ranks_ref, gathered, slots, seq)
        own_ref[...] = slots[pl.ds(pl.multiple_of(side * local, 8), local), :].astype(BF16)
        other_ref[...] = slots[pl.ds(pl.multiple_of((1 - side) * local, 8), local), :].astype(BF16)


def attend(scalars, ranks, packed, xy, rank_bias, box_bias, local, first, count):
    seq = packed.shape[0]
    pairs = rank_bias.shape[0] // 2
    heads = 2 * count
    width = heads * HEAD_DIM
    whole = pl.BlockSpec((seq, 2 * SPAN), lambda h: (0, 0))
    slot_spec = pl.BlockSpec((local, 128), lambda h: (0, h // 2))
    return pl.pallas_call(
        attend_kernel,
        grid=(heads,),
        out_shape=(
            jax.ShapeDtypeStruct((heads, seq, seq), BF16),
            jax.ShapeDtypeStruct((local, width), BF16),
            jax.ShapeDtypeStruct((local, width), BF16),
        ),
        in_specs=[
            smem(),
            smem(),
            pl.BlockSpec((seq, 128), lambda h: (0, first + h // 2)),
            pl.BlockSpec((seq, 128), lambda h: (0, pairs + first + h // 2)),
            pl.BlockSpec((seq, 128), lambda h: (0, 2 * pairs + first + h // 2)),
            whole,
            pl.BlockSpec((1, ROWS, RANK_LANES), lambda h: (2 * first + h, 0, 0)),
            pl.BlockSpec((1, seq, 2 * SPAN), lambda h: (2 * first + h, 0, 0)),
        ],
        out_specs=(pl.BlockSpec((1, seq, seq), lambda h: (h, 0, 0)), slot_spec, slot_spec),
        scratch_shapes=[
            pltpu.VMEM((seq, 128 + 2 * SPAN), BF16),
            pltpu.VMEM((seq, 128 + 2 * SPAN), BF16),
            pltpu.VMEM((seq, 128), F32),
            pltpu.VMEM((seq, 128), F32),
            pltpu.VMEM((seq, seq), F32),
        ],
        compiler_params=params(13),
        cost_estimate=pl.CostEstimate(
            flops=heads * 2 * seq * seq * 1024, bytes_accessed=heads * seq * seq * 2,
            transcendentals=heads * seq * seq,
        ),
        name="attend",
    )(scalars, ranks, packed, packed, packed, xy, rank_bias, box_bias)


def attend_back_kernel(
    ranks_ref, own_ref, other_ref, side_ref, shares_ref, queries, keys, values, xy_ref, xyt_ref,
    dq_ref, dk_ref, dv_ref, sums_ref, right, score_grad, spread, rank_sum, slots, upstream, share_grads,
):
    seq = queries.shape[0]
    local = own_ref.shape[0]
    side = side_ref[0]
    head = pl.program_id(0)
    parity = lax.rem(head, 2)
    scale = HEAD_DIM**-0.5

    @pl.when(head == 0)
    def _():
        right[:, 128:] = xy_ref[...]

    @pl.when(parity == 0)
    def _():
        slots[pl.ds(pl.multiple_of(side * local, 8), local), :] = own_ref[...].astype(F32)
        slots[pl.ds(pl.multiple_of((1 - side) * local, 8), local), :] = other_ref[...].astype(F32)
        sort_rows(ranks_ref, slots, upstream, seq, BF16)

    right[:, :128] = keys[...]
    mine = head_lanes((seq, 128), parity)
    own_values = jnp.where(mine, values[...], jnp.zeros((), BF16))
    rank_sum[:, (2 * (-(-seq // ROWS)) - 1) * 128 :] = jnp.zeros((ROWS, 128), F32)
    blocks = -(-seq // ROWS)
    chunks = row_chunks(seq, 240)
    for start, size in chunks:
        share_grads[start : start + size, :] = dot_nt(upstream[start : start + size, :], own_values)
    dv = dot_tn(shares_ref[0], upstream[...]).astype(BF16)
    dv_ref[...] = jnp.where(mine, dv, dv_ref[...])
    blank = jnp.zeros((16, blocks * 128 - seq), F32)
    for inner in range(0, ROWS, 16):
        totals = [None] * (2 * blocks - 1)
        for block in range(blocks):
            first = block * ROWS + inner
            if first >= seq:
                continue
            rows = slice(first, first + 16)
            shares = shares_ref[0, rows, :].astype(F32)
            weighted = shares * share_grads[rows, :]
            low = (weighted - shares * jnp.sum(weighted, axis=1, keepdims=True)).astype(BF16)
            score_grad[rows, :] = low
            padded = jnp.concatenate([low.astype(F32), blank], axis=1)
            for tile in range(blocks):
                value = padded[:, tile * 128 : tile * 128 + 128]
                place = blocks - 1 - block + tile
                totals[place] = value if totals[place] is None else totals[place] + value
        for place, value in enumerate(totals):
            rank_sum[inner : inner + 16, place * 128 : place * 128 + 128] = (
                jnp.zeros((16, 128), F32) if value is None else value
            )
    for start, size in chunks:
        rows = slice(start, start + size)
        product = dot_nn(score_grad[rows, :], right[...])
        spread[rows, :] = product[:, 128:].astype(BF16)
        dq_ref[rows, :] = jnp.where(
            head_lanes((size, 128), parity), (product[:, :128] * scale).astype(BF16), dq_ref[rows, :]
        )
    dk = dot_tn(score_grad[...], queries[...]).astype(BF16)
    dk_ref[...] = jnp.where(mine, dk, dk_ref[...])
    row = lax.broadcasted_iota(jnp.int32, (ROWS, ROWS), 0)
    col = lax.broadcasted_iota(jnp.int32, (ROWS, ROWS), 1)
    flip = (row + col == ROWS - 1).astype(F32).astype(BF16)
    turned = dot_nn(flip, rank_sum[...].astype(BF16))
    turned = pltpu.roll(turned, 0, 1, stride=1, stride_axis=0)
    sums_ref[0, 0:1, :] = jnp.sum(turned, axis=0, keepdims=True)
    for half in range(2):
        part = slice(half * SPAN, (half + 1) * SPAN)
        table = dot_nn(xyt_ref[part, :], spread[:, part])
        table = jnp.concatenate([table, jnp.zeros((SPAN, SPAN), F32)], axis=1)
        table = pltpu.roll(table, 0, 1, stride=1, stride_axis=0)
        sums_ref[0, half + 1 : half + 2, : 2 * SPAN] = jnp.sum(table, axis=0, keepdims=True)


def attend_back(scalars, ranks, own, other, shares, packed, xy, xyt, pair, place, so_far, marker):
    seq = packed.shape[0]
    local = own.shape[0]
    width = packed.shape[1] // 3
    pairs = width // 128
    slot_spec = pl.BlockSpec((local, 128), lambda h: (0, pair))
    out_spec = pl.BlockSpec((seq, 128), lambda h: (0, pair))
    so_far = tuple(so_far) if so_far else ()
    extra = so_far + ((marker,) if marker is not None else ())

    def body(*refs):
        ins, rest = refs[:10], refs[10 + len(extra) :]
        attend_back_kernel(*ins, *rest)

    return pl.pallas_call(
        body,
        grid=(2,),
        out_shape=(jax.ShapeDtypeStruct((seq, width), BF16),) * 3
        + (jax.ShapeDtypeStruct((2, 8, RANK_LANES), F32),),
        in_specs=[
            smem(),
            slot_spec,
            slot_spec,
            smem(),
            pl.BlockSpec((1, seq, seq), lambda h: (2 * place + h, 0, 0)),
            pl.BlockSpec((seq, 128), lambda h: (0, pair)),
            pl.BlockSpec((seq, 128), lambda h: (0, pairs + pair)),
            pl.BlockSpec((seq, 128), lambda h: (0, 2 * pairs + pair)),
            pl.BlockSpec((seq, 2 * SPAN), lambda h: (0, 0)),
            pl.BlockSpec((2 * SPAN, seq), lambda h: (0, 0)),
        ]
        + [anywhere()] * len(extra),
        out_specs=(out_spec,) * 3 + (pl.BlockSpec((1, 8, RANK_LANES), lambda h: (h, 0, 0)),),
        scratch_shapes=[
            pltpu.VMEM((seq, 128 + 2 * SPAN), BF16),
            pltpu.VMEM((seq, seq), BF16),
            pltpu.VMEM((seq, 2 * SPAN), BF16),
            pltpu.VMEM((ROWS, RANK_LANES), F32),
            pltpu.VMEM((seq, 128), F32),
            pltpu.VMEM((seq, 128), BF16),
            pltpu.VMEM((seq, seq), F32),
        ],
        input_output_aliases={10 + n: n for n in range(len(so_far))},
        compiler_params=params(15),
        cost_estimate=pl.CostEstimate(
            flops=1000 if pair else LONG, bytes_accessed=1000, transcendentals=0
        ),
        name="attend_back",
    )(ranks, own, other, scalars, shares, packed, packed, packed, xy, xyt, *extra)


def fold_rows(value):
    total = value[0:8]
    for start in range(8, value.shape[0], 8):
        total = total + value[start : start + 8]
    return total


def row_mean(value):
    return jnp.sum(value, axis=1, keepdims=True) * (1.0 / value.shape[1])


def normalize(value):
    center = value - row_mean(value)
    inverse = lax.rsqrt(row_mean(center * center) + norm_eps)
    return center * inverse, inverse


def dense_kernel(
    scalars, mixed_ref, own_a, own_b, other_a, other_b, pack, cot_ref, out_hbm, up_hbm, down_hbm, marker,
    result_ref, context_ref, hidden_ref, act_ref, branch_ref, pre_ref, attend_ref, resid_ref,
    own_grad, other_grad, sums_ref, blocks_ref,
    out_w, up_w, down_w, slope, product, stash, hidden, normed, scale, bias_sums_ref, copies,
):
    side, live = scalars[0], scalars[1]
    local, width = mixed_ref.shape
    deep = act_ref.shape[1]
    part = own_grad.shape[1]
    step = width
    blocks = deep // step
    gains, shifts, down_bias = pack.at[0:2], pack.at[2:4], pack.at[4:5]
    fetches = [pltpu.make_async_copy(out_hbm, out_w, copies.at[0])]
    fetches += [
        pltpu.make_async_copy(
            up_hbm.at[:, n * width : (n + 1) * width], up_w.at[:, n * width : (n + 1) * width],
            copies.at[1 + n],
        )
        for n in range(deep // width)
    ]
    fetches.append(pltpu.make_async_copy(down_hbm, down_w, copies.at[1 + deep // width]))
    for fetch in fetches:
        fetch.start()
    wide = own_a.shape[1]
    for base, (first, second) in ((side * part, (own_a, own_b)), ((1 - side) * part, (other_a, other_b))):
        context_ref[:, pl.ds(pl.multiple_of(base, 128), wide)] = first[...]
        context_ref[:, pl.ds(pl.multiple_of(base + wide, 128), part - wide)] = second[...]
    chunks = row_chunks(local, 24)
    fetches[0].wait()
    product[...] = dot_nn(context_ref[...], out_w[...])
    for start, size in chunks:
        rows = slice(start, start + size)
        value, inverse = normalize(mixed_ref[rows, :] + product[rows, :])
        normed[rows, :] = value
        scale[rows, :] = jnp.broadcast_to(inverse, (size, 128))
        value = value * gains[0:1, :] + shifts[0:1, :]
        hidden[rows, :] = value
        hidden_ref[rows, :] = value.astype(BF16)

    def lift(block):
        fetches[1 + block].wait()
        cols = slice(block * step, (block + 1) * step)
        stash[block % 2] = dot_nn(hidden_ref[...], up_w[:, cols])

    def bend(block):
        cols = slice(block * step, (block + 1) * step)
        for start, size in chunks:
            rows = slice(start, start + size)
            value = stash[block % 2, rows, :] + pack[5 + block : 6 + block, :]
            half = 0.5 + 0.5 * lax.erf(value * root_half)
            act_ref[rows, cols] = (value * half).astype(BF16)
            slope[rows, cols] = half + value * jnp.exp(-0.5 * value * value) * inv_root_tau

    lift(0)
    for block in range(blocks):
        if block + 1 < blocks:
            lift(block + 1)
        bend(block)
    fetches[-1].wait()
    product[...] = dot_nn(act_ref[...], down_w[...])
    zero = jnp.zeros((8, width), F32)
    gain_sum, shift_sum, bias_sum = zero, zero, zero
    for start, size in chunks:
        rows = slice(start, start + size)
        value, inverse = normalize(hidden[rows, :] + product[rows, :] + down_bias[...])
        slot = lax.broadcasted_iota(jnp.int32, (size, width), 0) + (side * local + start)
        alive = (slot < live).astype(F32)
        result_ref[rows, :] = (alive * (value * gains[1:2, :] + shifts[1:2, :])).astype(BF16)
        upstream = cot_ref[rows, :].astype(F32) * alive
        gain_sum = gain_sum + fold_rows(upstream * value)
        shift_sum = shift_sum + fold_rows(upstream)
        scaled = upstream * gains[1:2, :]
        grad = inverse * (scaled - row_mean(scaled) - value * row_mean(scaled * value))
        bias_sum = bias_sum + fold_rows(grad)
        hidden[rows, :] = grad
        branch_ref[rows, :] = grad.astype(BF16)
    sums_ref[1:2, :] = jnp.sum(gain_sum, axis=0, keepdims=True)
    sums_ref[3:4, :] = jnp.sum(shift_sum, axis=0, keepdims=True)
    sums_ref[4:5, :] = jnp.sum(bias_sum, axis=0, keepdims=True)
    sums_ref[5:8, :] = jnp.zeros((3, width), F32)

    def lower(block):
        cols = slice(block * step, (block + 1) * step)
        stash[block % 2] = dot_nt(branch_ref[...], down_w[cols, :])

    def unbend(block):
        cols = slice(block * step, (block + 1) * step)
        total = jnp.zeros((8, step), F32)
        for start, size in chunks:
            rows = slice(start, start + size)
            value = (stash[block % 2, rows, :] * slope[rows, cols]).astype(BF16)
            pre_ref[rows, cols] = value
            total = total + fold_rows(value.astype(F32))
        bias_sums_ref[:, cols] = jnp.sum(total, axis=0, keepdims=True)

    lower(0)
    for block in range(blocks):
        if block + 1 < blocks:
            lower(block + 1)
        unbend(block)
    product[...] = dot_nt(pre_ref[...], up_w[...])
    piece = deep // blocks_ref.shape[0]
    blocks_ref[...] = jnp.zeros(blocks_ref.shape, F32)
    for block in range(blocks_ref.shape[0]):
        blocks_ref[block : block + 1, :piece] = bias_sums_ref[:, block * piece : (block + 1) * piece]
    gain_sum, shift_sum = zero, zero
    for start, size in chunks:
        rows = slice(start, start + size)
        upstream = hidden[rows, :] + product[rows, :]
        value = normed[rows, :]
        gain_sum = gain_sum + fold_rows(upstream * value)
        shift_sum = shift_sum + fold_rows(upstream)
        scaled = upstream * gains[0:1, :]
        inverse = jnp.concatenate([scale[rows, :]] * (width // 128), axis=1)
        grad = inverse * (scaled - row_mean(scaled) - value * row_mean(scaled * value))
        resid_ref[rows, :] = grad
        attend_ref[rows, :] = grad.astype(BF16)
    sums_ref[0:1, :] = jnp.sum(gain_sum, axis=0, keepdims=True)
    sums_ref[2:3, :] = jnp.sum(shift_sum, axis=0, keepdims=True)
    product[...] = dot_nt(attend_ref[...], out_w[...])
    for base, ref in (((1 - side) * part, other_grad), (side * part, own_grad)):
        ref[...] = product[:, pl.ds(pl.multiple_of(base, 128), part)].astype(BF16)


def dense(
    scalars, mixed, own_context, other_context, pack, cotangent, out_weight, up_weight, down_weight, devices, marker,
):
    local, width = mixed.shape
    deep = up_weight.shape[1]
    part = width // 2
    low = lambda *shape: jax.ShapeDtypeStruct(shape, BF16)
    full = lambda *shape: jax.ShapeDtypeStruct(shape, F32)
    return pl.pallas_call(
        dense_kernel,
        out_shape=(
            low(local, width), low(local, width), low(local, width), low(local, deep),
            low(local, width), low(local, deep), low(local, width), full(local, width),
            low(local, part), low(local, part), full(8, width), full(devices, 128),
        ),
        in_specs=[smem()] + [vmem()] * 7 + [parameter()] * 3 + [anywhere()],
        out_specs=(vmem(),) * 12,
        scratch_shapes=[
            pltpu.VMEM((width, width), BF16),
            pltpu.VMEM((width, deep), BF16),
            pltpu.VMEM((deep, width), BF16),
            pltpu.VMEM((local, deep), F32),
            pltpu.VMEM((local, width), F32),
            pltpu.VMEM((2, local, width), F32),
            pltpu.VMEM((local, width), F32),
            pltpu.VMEM((local, width), F32),
            pltpu.VMEM((local, 128), F32),
            pltpu.VMEM((1, deep), F32),
            pltpu.SemaphoreType.DMA((2 + deep // width,)),
        ],
        compiler_params=params(26),
        cost_estimate=pl.CostEstimate(
            flops=2 * local * width * (4 * deep + 2 * width), bytes_accessed=20 * MIB,
            transcendentals=2 * local * deep,
        ),
        name="dense",
    )(
        scalars, mixed, *own_context, *other_context, pack, cotangent, out_weight, up_weight, down_weight,
        marker,
    )


def halves_of(value):
    high = value.astype(BF16)
    return high, (value - high.astype(F32)).astype(BF16)


def turn_kernel(order_ref, low_ref, marker, turned_ref, after_ref):
    turned_ref[...] = dot_nt(order_ref[...], low_ref[...]).astype(BF16)
    after_ref[...] = jnp.zeros(after_ref.shape, F32)


def turn_rows(order, low, marker):
    return pl.pallas_call(
        turn_kernel,
        out_shape=(
            jax.ShapeDtypeStruct((order.shape[0], low.shape[0]), BF16),
            jax.ShapeDtypeStruct((8, 128), F32),
        ),
        in_specs=[vmem(), vmem(), anywhere()],
        out_specs=(vmem(), vmem()),
        compiler_params=params(8),
        cost_estimate=pl.CostEstimate(flops=10**9, bytes_accessed=1000, transcendentals=0),
        name="turn_rows",
    )(order, low, marker)


def project_back_kernel(
    turned_hbm, dq_hbm, dk_hbm, dv_hbm, marker, keep_ref, send_ref, after_ref, turned, grads, copies
):
    half, part = keep_ref.shape[0], dq_hbm.shape[1]
    fetches = fetch(
        [turned_hbm, dq_hbm, dk_hbm, dv_hbm],
        [turned] + [grads.at[:, block * part : (block + 1) * part] for block in range(3)],
        copies,
    )
    after_ref[...] = jnp.zeros(after_ref.shape, F32)
    for copy in fetches:
        copy.wait()
    send_ref[...] = dot_nn(turned[half:, :], grads[...]).astype(BF16)
    keep_ref[...] = dot_nn(turned[:half, :], grads[...]).astype(BF16)


def project_weight_grad(turned, dq, dk, dv, marker):
    width, seq = turned.shape
    part = dq.shape[1]
    shape = jax.ShapeDtypeStruct((width // 2, 3 * part), BF16)
    return pl.pallas_call(
        project_back_kernel,
        out_shape=(shape, shape, jax.ShapeDtypeStruct((8, 128), F32)),
        in_specs=[anywhere()] * 5,
        out_specs=(vmem(),) * 3,
        scratch_shapes=[
            pltpu.VMEM((width, seq), BF16),
            pltpu.VMEM((seq, 3 * part), BF16),
            pltpu.SemaphoreType.DMA((4,)),
        ],
        compiler_params=params(12),
        cost_estimate=pl.CostEstimate(flops=1000, bytes_accessed=1000, transcendentals=0),
        name="project_weight_grad",
    )(turned, dq, dk, dv, marker)


def fill_block(turned, keep_ref, send_ref, start, right):
    middle = turned.shape[0] // 2
    cols = slice(start, start + right.shape[1])
    send_ref[:, cols] = dot_nn(turned[middle:, :], right).astype(BF16)
    keep_ref[:, cols] = dot_nn(turned[:middle, :], right).astype(BF16)


def down_kernel(spots, act_ref, branch_ref, keep_ref, send_ref, whole, *, piece):
    width = branch_ref.shape[1]
    half = keep_ref.shape[0]
    for step in range(act_ref.shape[1] // width):
        whole[...] = dot_tn(act_ref[:, step * width : (step + 1) * width], branch_ref[...]).astype(BF16)
        for block in range(width // piece):
            spot = spots[step * (width // piece) + block]
            rows = slice(block * piece, (block + 1) * piece)

            def keep(spot=spot, rows=rows):
                keep_ref[pl.ds(pl.multiple_of(spot, 16), piece), :] = whole[rows, :]

            def send(spot=spot, rows=rows):
                send_ref[pl.ds(pl.multiple_of(spot - half, 16), piece), :] = whole[rows, :]

            pl.when(spot < half)(keep)
            pl.when(spot >= half)(send)


def down_weight_grad(spots, act, branch, piece):
    deep, width = act.shape[1], branch.shape[1]
    tall = jax.ShapeDtypeStruct((deep // 2, width), BF16)
    return pl.pallas_call(
        functools.partial(down_kernel, piece=piece),
        out_shape=(tall, tall),
        in_specs=[smem()] + [vmem()] * 2,
        out_specs=(vmem(),) * 2,
        scratch_shapes=[pltpu.VMEM((width, width), BF16)],
        compiler_params=params(12),
        cost_estimate=pl.CostEstimate(flops=1000, bytes_accessed=1000, transcendentals=0),
        name="down_weight_grad",
    )(spots, act, branch)


def up_kernel(
    pre_ref, hidden_ref, context_ref, attend_ref, first_ref, second_ref, marker,
    out_keep, out_send, up_keep, up_send, turned, *, split,
):
    width, deep = hidden_ref.shape[1], pre_ref.shape[1]
    turned[...] = dot_nt(first_ref[...], hidden_ref[...]).astype(BF16)
    for start, size in row_chunks(split, width):
        fill_block(turned, out_keep, out_send, start, pre_ref[:, start : start + size])
    turned[...] = dot_nt(first_ref[...], context_ref[...]).astype(BF16)
    fill_block(turned, out_keep, out_send, split, attend_ref[...])
    turned[...] = dot_nt(second_ref[...], hidden_ref[...]).astype(BF16)
    for start, size in row_chunks(deep - split, width):
        fill_block(turned, up_keep, up_send, start, pre_ref[:, split + start : split + start + size])


def up_weight_grads_of(pre, hidden, context, attend, first, second, split, marker):
    local, width = hidden.shape
    deep = pre.shape[1]
    low = lambda columns: jax.ShapeDtypeStruct((width // 2, columns), BF16)
    return pl.pallas_call(
        functools.partial(up_kernel, split=split),
        out_shape=(low(split + width), low(split + width), low(deep - split), low(deep - split)),
        in_specs=[vmem()] * 6 + [anywhere()],
        out_specs=(vmem(),) * 4,
        scratch_shapes=[pltpu.VMEM((width, local), BF16)],
        compiler_params=params(14),
        cost_estimate=pl.CostEstimate(flops=LONG, bytes_accessed=1000, transcendentals=0),
        name="up_weight_grad",
    )(pre, hidden, context, attend, first, second, marker)


def mixed_back_kernel(
    scalars, ranks_ref, dq_hbm, dk_hbm, dv_hbm, weight_hbm, resid_hbm, own_hbm, other_hbm,
    marker, grad_ref, send_ref, taps_ref, cells_ref, sorted_grad, whole, text, patch, masks, edge,
    grads, weights, resid_ref, own_ref, other_ref, copies,
):
    side, fine = scalars[0], scalars[2]
    local, width = own_ref.shape
    seq, part = dq_hbm.shape
    groups = width // 128
    pad = GRID_HI + 2
    fetches = fetch(
        [own_hbm, other_hbm, dq_hbm, dk_hbm, dv_hbm]
        + [
            weight_hbm.at[:, pl.ds(pl.multiple_of(block * width + side * part, 128), part)]
            for block in range(3)
        ]
        + [resid_hbm],
        [own_ref, other_ref]
        + [grads.at[:, block * part : (block + 1) * part] for block in range(3)]
        + [weights.at[:, block * part : (block + 1) * part] for block in range(3)]
        + [resid_ref],
        copies,
    )
    fetches[0].wait()
    fetches[1].wait()
    place_slots(own_ref, other_ref, side, text, patch, pad)
    clear_pads(text, patch, pad)
    store_masks(masks, fine, seq - TEXT)
    for copy in fetches[2:]:
        copy.wait()
    for start, size in row_chunks(seq, 240):
        sorted_grad[start : start + size, :] = dot_nt(grads[start : start + size, :], weights[...])
    unsort_rows(ranks_ref, sorted_grad, whole, seq)
    mine = pl.ds(pl.multiple_of(side * local, 8), local)
    theirs = pl.ds(pl.multiple_of((1 - side) * local, 8), local)
    whole[mine, :] = whole[mine, :] + resid_ref[...]
    inner = pl.ds(pl.multiple_of(local - 8 + side * 8, 8), 8)
    outer = pl.ds(pl.multiple_of(local - side * 8, 8), 8)
    edge[0:local, :] = whole[theirs, :]
    edge[local : local + 8, :] = whole[inner, :]
    send_ref[...] = edge[...].astype(BF16)
    grad_ref[0:local, :] = whole[mine, :]
    grad_ref[local : local + 8, :] = whole[outer, :]
    taps_ref[...] = jnp.zeros(taps_ref.shape, F32)
    cells_ref[...] = jnp.zeros(cells_ref.shape, F32)
    for lane in range(groups):
        cols = slice(lane * 128, lane * 128 + 128)
        totals = {offset: jnp.zeros((8, 128), F32) for offset in range(-3, 4)}
        for start, size in row_chunks(TEXT, 64):
            value = whole[start : start + size, cols]
            for offset in totals:
                moved = text[lane, pl.ds(8 + start + offset, size), :]
                totals[offset] = totals[offset] + fold_rows(value * moved)
        for number, (reach, direction) in enumerate(tap_list):
            taps_ref[number : number + 1, cols] = jnp.sum(totals[reach * direction], axis=0, keepdims=True)
    for grid, chosen in ((GRID_HI, fine != 0), (GRID_LO, fine == 0)):

        def cells(grid=grid):
            for lane in range(groups):
                cols = slice(lane * 128, lane * 128 + 128)
                totals = [jnp.zeros((8, 128), F32)] * len(cell_list)
                for start, size in row_chunks(seq - TEXT, 104):
                    value = whole[TEXT + start : TEXT + start + size, cols]
                    for number, (down, across) in enumerate(cell_list):
                        moved = patch[lane, pl.ds(pad + start + down * grid + across, size), :]
                        moved = moved * masks[number, start : start + size, :]
                        totals[number] = totals[number] + fold_rows(value * moved)
                for number, value in enumerate(totals):
                    cells_ref[number : number + 1, cols] = jnp.sum(value, axis=0, keepdims=True)

        pl.when(chosen)(cells)


def mixed_back(scalars, ranks, dq, dk, dv, qkv_weight, resid_grad, own, other, marker):
    local, width = own.shape
    seq, part = dq.shape
    groups = width // 128
    return pl.pallas_call(
        mixed_back_kernel,
        out_shape=(
            jax.ShapeDtypeStruct((local + 8, width), F32),
            jax.ShapeDtypeStruct((local + 8, width), BF16),
            jax.ShapeDtypeStruct((16, width), F32),
            jax.ShapeDtypeStruct((16, width), F32),
        ),
        in_specs=[smem(), smem()] + [anywhere()] * 3 + [parameter()] + [anywhere()] * 4,
        out_specs=(vmem(),) * 4,
        scratch_shapes=[
            pltpu.VMEM((seq, width), F32),
            pltpu.VMEM((seq, width), F32),
            pltpu.VMEM((groups, TEXT + 16, 128), F32),
            pltpu.VMEM((groups, seq - TEXT + 2 * (GRID_HI + 2), 128), F32),
            pltpu.VMEM((9, seq - TEXT, 128), F32),
            pltpu.VMEM((local + 8, width), F32),
            pltpu.VMEM((seq, 3 * part), BF16),
            pltpu.VMEM((width, 3 * part), BF16),
            pltpu.VMEM((local, width), F32),
            pltpu.VMEM((local, width), BF16),
            pltpu.VMEM((local, width), BF16),
            pltpu.SemaphoreType.DMA((9,)),
        ],
        compiler_params=params(15),
        cost_estimate=pl.CostEstimate(flops=1000, bytes_accessed=1000, transcendentals=0),
        name="mixed_back",
    )(scalars, ranks, dq, dk, dv, qkv_weight, resid_grad, own, other, marker)


def token_kernel(
    scalars, grad_ref, received_ref, text_kernel, patch_kernel, marker, out_ref, after_ref,
    text, patch, masks, lanes,
):
    side, fine = scalars[0], scalars[2]
    local, width = out_ref.shape
    groups = width // 128
    pad = GRID_HI + 2
    after_ref[...] = jnp.zeros(after_ref.shape, F32)
    rows = masks.shape[1]
    head = TEXT - local
    clear_pads(text, patch, pad)
    store_masks(masks, fine, rows)

    def load(low):
        for lane in range(groups):
            cols = slice(lane * 128, lane * 128 + 128)
            total = grad_ref[:, cols] + received_ref[:, cols].astype(F32)
            if low:
                text[lane, 8 : 8 + local + 8, :] = total
                text[lane, 16 + local : 8 + TEXT, :] = jnp.zeros((head - 8, 128), F32)
                patch[lane, pad : pad + rows, :] = jnp.zeros((rows, 128), F32)
            else:
                text[lane, 8 : local, :] = jnp.zeros((local - 8, 128), F32)
                text[lane, local : local + 8, :] = total[local:]
                text[lane, 8 + local : 8 + TEXT, :] = total[:head]
                patch[lane, pad : pad + rows, :] = total[head:local]

    pl.when(side == 0)(lambda: load(True))
    pl.when(side != 0)(lambda: load(False))

    def one_lane(lane, carry):
        mix_lane(text, patch, masks, lanes, lane, text_kernel, patch_kernel, fine, pad, True)
        return carry

    lax.fori_loop(0, groups, one_lane, 0)
    mine = pl.ds(pl.multiple_of(side * local, 8), local)
    for lane in range(groups):
        out_ref[:, lane * 128 : lane * 128 + 128] = lanes[lane, mine, :]


def token_back(scalars, grad, received, text_kernel, patch_kernel, seq, marker):
    local, width = grad.shape[0] - 8, grad.shape[1]
    groups = width // 128
    return pl.pallas_call(
        token_kernel,
        out_shape=(jax.ShapeDtypeStruct((local, width), F32), jax.ShapeDtypeStruct((8, 128), F32)),
        in_specs=[smem()] + [vmem()] * 4 + [anywhere()],
        out_specs=(vmem(), vmem()),
        scratch_shapes=[
            pltpu.VMEM((groups, TEXT + 16, 128), F32),
            pltpu.VMEM((groups, seq - TEXT + 2 * (GRID_HI + 2), 128), F32),
            pltpu.VMEM((9, seq - TEXT, 128), F32),
            pltpu.VMEM((groups, seq, 128), F32),
        ],
        compiler_params=params(9),
        cost_estimate=pl.CostEstimate(flops=1000, bytes_accessed=1000, transcendentals=0),
        name="token_back",
    )(scalars, grad, received, text_kernel, patch_kernel, marker)


def finish_kernel(scalars, kept_ref, received_ref, grad_ref):
    side = scalars[0]
    part = kept_ref.shape[1] // 3
    for block in range(3):
        cols = slice(block * part, (block + 1) * part)
        mine = pl.ds(pl.multiple_of((2 * block + side) * part, 128), part)
        theirs = pl.ds(pl.multiple_of((2 * block + 1 - side) * part, 128), part)
        grad_ref[:, mine] = kept_ref[:, cols]
        grad_ref[:, theirs] = received_ref[:, cols].astype(F32)


def finish_little_kernel(
    kept_ref, received_ref, taps_ref, cells_ref, gains_ref, shifts_ref, down_ref, up_ref,
    rank_ref, box_ref, *, ratio, shared, heads,
):
    rows = taps_ref.shape[1]
    small = kept_ref[:rows, :] + received_ref[:rows, :]
    padded = jnp.concatenate([small, jnp.zeros((128 - rows, 128), F32)], axis=0)
    turned = padded.T
    taps_ref[...] = turned[0:9, :rows]
    cells_ref[...] = turned[16:25, :rows]
    gains_ref[...] = turned[32:34, :rows]
    shifts_ref[...] = turned[34:36, :rows]
    down_ref[...] = turned[36:37, :rows]
    row = lax.broadcasted_iota(jnp.int32, (rows, 128), 0)
    lane = lax.broadcasted_iota(jnp.int32, (rows, 128), 1)
    total = jnp.zeros((rows, 128), F32)
    for column in range(ratio):
        value = jnp.broadcast_to(small[:, 40 + column : 41 + column], (rows, 128))
        total = total + jnp.where(lane == row * ratio + column, value, 0.0)
    up_ref[...] = jnp.sum(total, axis=0, keepdims=True)[:, : rows * ratio]
    tables = kept_ref[kept_ref.shape[0] - shared :, :] + received_ref[received_ref.shape[0] - shared :, :]
    for head in range(2 * heads):
        row = head // heads * 16 + head % heads
        rank_ref[head : head + 1, :] = tables[row : row + 1, :NB1]
        box_ref[head, 0:1, :] = tables[row : row + 1, NB1 : NB1 + NB2]
        box_ref[head, 1:2, :] = tables[row + 8 : row + 9, :NB2]


def finish_all_kernel(*refs, ratio, shared, heads):
    scalars = refs[0]
    up_in, joint_in, qkv_in, little_in = (refs[n : n + 2] for n in (1, 3, 5, 7))
    totals, qkv_out, little_out = refs[9:12], refs[12], refs[13:]
    total_kernel(*up_in, *joint_in, *totals)
    finish_kernel(scalars, *qkv_in, qkv_out)
    finish_little_kernel(*little_in, *little_out, ratio=ratio, shared=shared, heads=heads)


def finish_all(scalars, up, joint, qkv, little, width, deep, heads):
    rows, ratio = up.kept.shape[0], deep // width
    full = lambda *shape: jax.ShapeDtypeStruct(shape, F32)
    return pl.pallas_call(
        functools.partial(finish_all_kernel, ratio=ratio, shared=little.shared, heads=heads),
        out_shape=(
            full(rows, deep), full(rows, width), full(rows * ratio, width), full(rows, 3 * width),
            full(9, rows), full(9, rows), full(2, rows), full(2, rows), full(1, rows),
            full(1, rows * ratio), full(2 * heads, NB1), full(2 * heads, 2, NB2),
        ),
        in_specs=[smem()] + [vmem()] * 8,
        out_specs=(vmem(),) * 12,
        compiler_params=params(10),
        cost_estimate=pl.CostEstimate(flops=1000, bytes_accessed=1000, transcendentals=0),
        name="finish_all",
    )(
        scalars, up.kept, up.received, joint.kept, joint.received, qkv.kept, qkv.received,
        little.now, little.received,
    )


def swap(value, stage):
    axis, bit = stage
    count = lax.axis_size(axis)
    return lax.ppermute(value, axis, [(i, i ^ bit) for i in range(count)])


def stage_flag(stage):
    axis, bit = stage
    return (lax.axis_index(axis) & bit) // bit


def block_bit(block, stage, blk_count):
    axis, bit = stage
    shift = bit * blk_count if axis == "page" else bit
    return (block // shift) & 1


def spot_of(block, stages, blk_count):
    spot = jnp.zeros_like(block)
    for stage in stages:
        spot = spot * 2 + (block_bit(block, stage, blk_count) ^ stage_flag(stage))
    return spot


def order_matrix(width, stages, blk_count):
    count = lax.axis_size("page") * blk_count
    piece = width // count
    place = jnp.arange(width, dtype=jnp.int32)
    spot, inside = place // piece, place % piece
    block = jnp.zeros_like(spot)
    for depth, stage in enumerate(stages):
        axis, bit = stage
        shift = bit * blk_count if axis == "page" else bit
        value = ((spot >> (len(stages) - 1 - depth)) & 1) ^ stage_flag(stage)
        block = block + value * shift
    column = block * piece + inside
    return (column[:, None] == jnp.arange(width, dtype=jnp.int32)[None, :]).astype(BF16)


def add_up(terms):
    total = terms[0].astype(F32)
    for term in terms[1:]:
        total = total + term.astype(F32)
    return total


def halve_kernel(kept_ref, received_ref, marker, next_ref, send_ref, after_ref):
    rows = next_ref.shape[0]
    size = rows if rows % 48 else 48
    for start in range(0, rows, size):
        for base, ref in ((rows, send_ref), (0, next_ref)):
            if base % 16 or size % 16:
                place = slice(base + start, base + start + size)
                value = kept_ref[...].astype(F32)[place] + received_ref[...].astype(F32)[place]
            else:
                place = slice(base + start, base + start + size)
                value = kept_ref[place, :].astype(F32) + received_ref[place, :].astype(F32)
            ref[start : start + size, :] = value.astype(ref.dtype)
    after_ref[...] = jnp.zeros(after_ref.shape, F32)


def halve(kept, received, marker, flops=1000):
    rows, width = received.shape[0] // 2, received.shape[1]
    if rows % 8:
        total = kept.astype(F32) + received.astype(F32)
        return total[:rows], total[rows:].astype(BF16), marker
    return pl.pallas_call(
        halve_kernel,
        out_shape=(
            jax.ShapeDtypeStruct((rows, width), F32),
            jax.ShapeDtypeStruct((rows, width), BF16),
            jax.ShapeDtypeStruct((8, 128), F32),
        ),
        in_specs=[vmem(), vmem(), anywhere()],
        out_specs=(vmem(),) * 3,
        compiler_params=params(8),
        cost_estimate=pl.CostEstimate(flops=flops, bytes_accessed=1000, transcendentals=0),
        name="halve",
    )(kept, received, marker)


class Chain:
    def __init__(self, keep, send, stages):
        self.kept, self.stages, self.done = keep, stages, 0
        self.rows = 2 * keep.shape[0]
        self.received = swap(send, stages[0])

    def turn(self, marker, flops=1000):
        self.done += 1
        if self.done >= len(self.stages):
            return marker
        self.kept, send, marker = halve(self.kept, self.received, marker, flops)
        self.received = swap(send, self.stages[self.done])
        return marker


def join_kernel(
    out_kept, out_received, down_kept, down_received, marker, next_ref, send_ref, after_ref, sums, message,
    *, piece, ratio,
):
    rows, width = next_ref.shape[0], down_kept.shape[1]
    wide = out_kept.shape[1]
    for start in range(0, 2 * rows, rows):
        part = slice(start, start + rows)
        value = out_kept[part, :] + out_received[part, :].astype(F32)
        (message if start else next_ref)[:, :wide] = value
    for start in range(0, sums.shape[0], 48):
        part = slice(start, start + 48)
        sums[part, :] = down_kept[part, :] + down_received[part, :].astype(F32)
    for start in range(0, 2 * rows, piece):
        target, place = (next_ref, start) if start < rows else (message, start - rows)
        for turn in range(ratio):
            cols = slice(wide + turn * width, wide + (turn + 1) * width)
            source = ratio * start + turn * piece
            target[place : place + piece, cols] = sums[source : source + piece, :]
    for start, size in row_chunks(wide + ratio * width, 512):
        cols = slice(start, start + size)
        send_ref[:, cols] = message[:, cols].astype(BF16)
    after_ref[...] = jnp.zeros(after_ref.shape, F32)


def join(out, down, devices, marker):
    rows, wide = out.kept.shape
    tall, width = down.kept.shape
    ratio = tall // rows
    piece = out.rows // devices
    full = wide + ratio * width
    out.done += 1
    down.done += 1
    if piece % 8:
        total = down.kept + down.received.astype(F32)
        total = total.reshape(rows // piece, ratio, piece, width).swapaxes(1, 2).reshape(rows, ratio * width)
        total = jnp.concatenate([out.kept + out.received.astype(F32), total], axis=1)
        kept, send = total[: rows // 2], total[rows // 2 :].astype(BF16)
    else:
        kept, send, marker = pl.pallas_call(
            functools.partial(join_kernel, piece=piece, ratio=ratio),
            out_shape=(
                jax.ShapeDtypeStruct((rows // 2, full), F32),
                jax.ShapeDtypeStruct((rows // 2, full), BF16),
                jax.ShapeDtypeStruct((8, 128), F32),
            ),
            in_specs=[vmem()] * 4 + [anywhere()],
            out_specs=(vmem(),) * 3,
            scratch_shapes=[pltpu.VMEM((tall, width), F32), pltpu.VMEM((rows // 2, full), F32)],
            compiler_params=params(10),
            cost_estimate=pl.CostEstimate(flops=1000, bytes_accessed=1000, transcendentals=0),
            name="join",
        )(out.kept, out.received, down.kept, down.received, marker)
    return Chain(kept, send, out.stages[out.done :]), marker


def total_kernel(
    up_kept, up_received, kept_ref, received_ref, up_ref, out_ref, down_ref
):
    piece, width = out_ref.shape
    wide = up_ref.shape[1] - up_kept.shape[1]
    value = kept_ref[...] + received_ref[...].astype(F32)
    up_ref[:, :wide] = value[:, :wide]
    up_ref[:, wide:] = up_kept[...] + up_received[...].astype(F32)
    out_ref[...] = value[:, wide : wide + width]
    for turn in range(down_ref.shape[0] // piece):
        start = wide + (turn + 1) * width
        down_ref[turn * piece : (turn + 1) * piece, :] = value[:, start : start + width]


def little_kernel(now_ref, received_ref, marker, next_ref, message_ref, after_ref, *, shared):
    rows = received_ref.shape[0] - shared
    half = message_ref.shape[0] - shared
    common = now_ref[2 * rows :, :] + received_ref[rows:, :]
    kept = now_ref[:rows, :] + received_ref[:rows, :]
    next_ref[:rows, :] = kept
    next_ref[rows:, :] = common
    message_ref[:half, :] = kept[half:]
    message_ref[half:, :] = common
    after_ref[...] = jnp.zeros(after_ref.shape, F32)


class Little:
    def __init__(self, now, shared, stages):
        self.now, self.shared, self.stages, self.done = now, shared, stages, 0
        rows = (now.shape[0] - shared) // 2
        self.received = swap(now[rows:], stages[0])

    def turn(self, marker):
        self.done += 1
        if self.done > len(self.stages):
            return marker
        rows = self.received.shape[0] - self.shared
        if self.done == len(self.stages):
            return marker
        half = rows // 2
        if half % 8:
            kept = self.now[:rows] + self.received[:rows]
            common = self.now[2 * rows :] + self.received[rows:]
            self.now = jnp.concatenate([kept, common], axis=0)
            message = self.now[half:]
        else:
            lanes = self.now.shape[1]
            self.now, message, marker = pl.pallas_call(
                functools.partial(little_kernel, shared=self.shared),
                out_shape=(
                    jax.ShapeDtypeStruct((rows + self.shared, lanes), F32),
                    jax.ShapeDtypeStruct((half + self.shared, lanes), F32),
                    jax.ShapeDtypeStruct((8, 128), F32),
                ),
                in_specs=[vmem(), vmem(), anywhere()],
                out_specs=(vmem(),) * 3,
                compiler_params=params(4),
                cost_estimate=pl.CostEstimate(flops=1000, bytes_accessed=1000, transcendentals=0),
                name="little",
            )(self.now, self.received, marker)
        self.received = swap(message, self.stages[self.done])
        return marker


def gather_kernel(
    scalars, order_hbm, owner_hbm, inside_hbm, fold_hbm, rank_hbm, box_hbm, taps_hbm, cells_hbm, dense_hbm,
    blocks_hbm, sums_a, sums_b, sums_c, marker, out_ref, after_ref,
    order, owner, inside, fold, rank, box, taps, cells, dense_sums, blocks, sums, copies,
):
    fetches = fetch(
        [order_hbm, owner_hbm, inside_hbm, fold_hbm, rank_hbm, box_hbm, taps_hbm, cells_hbm,
         dense_hbm, blocks_hbm, sums_a, sums_b, sums_c],
        [order, owner, inside, fold, rank, box, taps, cells, dense_sums, blocks]
        + [sums.at[pl.ds(2 * n, 2)] for n in range(3)],
        copies,
    )
    for copy in fetches:
        copy.wait()
    after_ref[...] = jnp.zeros(after_ref.shape, F32)
    width = order.shape[0]

    rows = jnp.concatenate([taps[...], cells[...], dense_sums[...]], axis=0)
    rows = jnp.concatenate([rows, jnp.zeros((128 - rows.shape[0], width), F32)], axis=0)
    spread = dot_nn(owner[...], blocks[...].astype(BF16)) * inside[...].astype(F32)
    bias = dot_nn(spread.astype(BF16), fold[...]).astype(BF16)
    out_ref[:width, :] = dot_nt(order[...], rows.astype(BF16)) + dot_nn(order[...], bias)
    out_ref[width:, :] = jnp.zeros((32, 128), F32)
    heads = sums.shape[0]
    mine = pl.multiple_of(width + scalars[0] * 16, 16)
    pad = lambda value: jnp.concatenate([value, jnp.zeros((8 - heads, value.shape[1]), F32)], axis=0)
    by_rank = pad(jnp.concatenate([sums[head, 0:1, :] for head in range(heads)], axis=0))
    table = sum(dot_nn(piece, rank[...]) for piece in halves_of(by_rank))
    out_ref[pl.ds(mine, 8), 0:NB1] = table
    for half in range(2):
        by_box = pad(
            jnp.concatenate([sums[head, half + 1 : half + 2, : 2 * SPAN] for head in range(heads)], axis=0)
        )
        table = sum(dot_nn(piece, box[...]) for piece in halves_of(by_box))
        if half == 0:
            out_ref[pl.ds(mine, 8), NB1 : NB1 + NB2] = table
        else:
            out_ref[pl.ds(mine + 8, 8), 0:NB2] = table


def gather_small(scalars, order, taps, cells, dense_sums, blocks, sums, deep, marker):
    width = order.shape[0]
    devices = blocks.shape[0]
    ratio = deep // width
    piece = width // devices
    rows, lanes = np.arange(width), np.arange(128)
    owner = jnp.asarray(rows[:, None] // piece == np.arange(devices)[None, :], BF16)
    inside = jnp.asarray(
        (lanes[None, :] // ratio == rows[:, None] % piece) & (lanes[None, :] < piece * ratio), BF16
    )
    fold = jnp.asarray(lanes[:, None] % ratio + 40 == lanes[None, :], BF16)
    rank = jnp.asarray(bucket_rows(np.arange(RANK_LANES) - (RANK_MID - 1), rank_marks, NB1), BF16)
    box = jnp.asarray(bucket_rows(np.arange(2 * SPAN) - (SPAN - 1), box_marks, NB2), BF16)
    constants = tuple(map(stay, (owner, inside, fold, rank, box)))
    operands = (order, *constants, taps, cells, dense_sums, blocks)
    return pl.pallas_call(
        gather_kernel,
        out_shape=(
            jax.ShapeDtypeStruct((width + 32, 128), F32), jax.ShapeDtypeStruct((8, 128), F32)
        ),
        in_specs=[smem(), anywhere()] + [parameter()] * 5 + [anywhere()] * 8,
        out_specs=(vmem(), vmem()),
        scratch_shapes=[pltpu.VMEM(value.shape, value.dtype) for value in operands]
        + [pltpu.VMEM((2 * len(sums), 8, RANK_LANES), F32), pltpu.SemaphoreType.DMA((13,))],
        compiler_params=params(10),
        cost_estimate=pl.CostEstimate(flops=1000, bytes_accessed=1000, transcendentals=0),
        name="gather_small",
    )(scalars, *operands, *sums, marker)


def per_device(
    tokens,
    patch_count,
    reading_rank,
    boxes,
    text_kernel,
    patch_kernel,
    qkv_weight,
    rank_table,
    box_tables,
    out_weight,
    norm_gains,
    norm_shifts,
    up_weight,
    up_bias,
    down_weight,
    down_bias,
    cotangent,
):
    qkv_weight, out_weight, up_weight, down_weight = map(
        stay, (qkv_weight, out_weight, up_weight, down_weight)
    )
    side = lax.axis_index("blk")
    blk_count = lax.axis_size("blk")
    page_stages = [("page", 1 << n) for n in range(lax.axis_size("page").bit_length() - 1)]
    across = ("blk", 1)
    out_stages = page_stages[:1] + [across] + page_stages[1:]
    up_stages = page_stages[:1] + page_stages[2:] + [across] + page_stages[1:2]
    down_stages = page_stages[:2] + [across] + page_stages[2:]
    qkv_stages = page_stages[:1] + page_stages[2:] + page_stages[1:2] + [across]
    little_stages = page_stages[:2] + [across] + page_stages[2:]
    devices = lax.axis_size("page") * blk_count
    count = patch_count[0]
    ranks = reading_rank
    own = tokens[0]
    local, width = own.shape
    deep = up_bias.shape[0]
    seq = ranks.shape[1]
    heads = HEADS // blk_count
    scalars = jnp.stack(
        [side, TEXT + count, (count == GRID_HI * GRID_HI).astype(jnp.int32), jnp.int32(0)]
    ).astype(jnp.int32)
    other = swap(own, across)

    xy, xyt, rank_bias, box_bias = onehots(scalars, ranks, boxes, rank_table, box_tables, heads)
    mixed, mixed_low, packed = mix_and_project(
        scalars, ranks, own, other, text_kernel, patch_kernel, qkv_weight
    )
    pack = jnp.concatenate([norm_gains, norm_shifts, down_bias[None], up_bias.reshape(-1, width)], axis=0)
    own_context, other_context, shares = [], [], []
    for first, pairs in ((0, 2), (2, 1)):
        share, mine, theirs = attend(
            scalars, ranks, packed, xy, rank_bias, box_bias, local, first, pairs
        )
        shares += [(share, place) for place in range(pairs)]
        own_context.append(mine)
        other_context.append(swap(theirs, across))
    order_qkv = order_matrix(width, qkv_stages, blk_count)
    order_little = order_matrix(width, little_stages, blk_count)
    turned, marker = turn_rows(order_qkv, mixed_low, own_context[-1])
    (
        layer_output, context, hidden_low, act_low, branch_grad, pre_grad, attend_grad,
        resid_one_grad, own_part, their_part, dense_sums, bias_blocks,
    ) = dense(
        scalars, mixed, own_context, other_context, pack, cotangent[0], out_weight, up_weight,
        down_weight, devices, marker,
    )
    part = width // blk_count
    received_part = swap(their_part, across)

    order_out = order_matrix(width, out_stages, blk_count)
    order_up = order_matrix(width, up_stages, blk_count)
    piece = deep // devices
    blocks = jnp.arange(devices, dtype=jnp.int32)
    spots = spot_of(blocks, down_stages, blk_count) * piece
    act_rows = act_low
    if piece % 16:
        place = jnp.arange(deep, dtype=jnp.int32)
        target = spots[place // piece] + place % piece
        act_rows = jnp.zeros_like(act_low).at[:, target].set(act_low, unique_indices=True)
        piece = width // 8
        spots = jnp.arange(deep // piece, dtype=jnp.int32) * piece
    steps = deep // width
    split = deep * 11 // 24
    down_keep, down_send = down_weight_grad(spots, act_rows, branch_grad, piece)
    down = Chain(down_keep, down_send, down_stages)
    out_keep, out_send, up_keep, up_send = up_weight_grads_of(
        pre_grad, hidden_low, context, attend_grad, order_out, order_up, split, down_keep
    )
    out = Chain(out_keep, out_send, out_stages)
    up = Chain(up_keep, up_send, up_stages)
    marker = down.turn(up_send)

    grads, sums = None, []
    for pair, (share, place) in enumerate(shares):
        if pair == 1:
            marker = up.turn(out.turn(sums[0]))
        *grads, pair_sums = attend_back(
            scalars, ranks, own_part, received_part, share, packed, xy, xyt, pair, place, grads,
            marker if pair < 2 else None,
        )
        sums.append(pair_sums)
    dq, dk, dv = grads
    qkv_keep, qkv_send, marker = project_weight_grad(turned, dq, dk, dv, sums[-1])
    qkv = Chain(qkv_keep, qkv_send, qkv_stages)
    marker = down.turn(out.turn(up.turn(marker)), LONG)
    marker = qkv.turn(marker)
    grad, outgoing, taps, cells = mixed_back(
        scalars, ranks, dq, dk, dv, qkv_weight, resid_one_grad, stay(own), other, marker
    )
    incoming = swap(outgoing, across)
    gathered, marker = gather_small(
        scalars, order_little, taps, cells, dense_sums, bias_blocks, sums, deep, taps
    )
    little = Little(gathered, 32, little_stages)
    marker = up.turn(qkv.turn(marker))
    joint, marker = join(out, down, devices, marker)
    marker = little.turn(little.turn(marker))
    token_grad, marker = token_back(
        scalars, grad, incoming, text_kernel, patch_kernel, seq, marker
    )
    for _ in range(len(qkv_stages) - 4):
        for chain in (qkv, little, up, joint):
            marker = chain.turn(marker)
    marker = little.turn(qkv.turn(marker))
    for _ in qkv_stages:
        marker = little.turn(qkv.turn(marker))
    (
        up_weight_grads, out_weight_grads, down_weight_grads, qkv_weight_grad, taps, cells, gains, shifts,
        down_bias_grad, up_bias_grad, rank_grad, box_grad,
    ) = finish_all(scalars, up, joint, qkv, little, width, deep, heads)
    return (
        layer_output[None],
        token_grad[None],
        taps,
        cells,
        qkv_weight_grad,
        rank_grad,
        jnp.swapaxes(box_grad, 0, 1),
        out_weight_grads,
        gains,
        shifts,
        up_weight_grads,
        up_bias_grad[0],
        down_weight_grads,
        down_bias_grad[0],
    )


def solution(mesh):
    in_specs = (
        P("page", "blk", None),
        P("page"),
        P("page", None),
        P(None, "page", None),
        P(),
        P(),
        P(),
        P(),
        P(),
        P(),
        P(),
        P(),
        P(),
        P(),
        P(),
        P(),
        P("page", "blk", None),
    )
    out_specs = (
        P("page", "blk", None),
        P("page", "blk", None),
        P(None, ("page", "blk")),
        P(None, ("page", "blk")),
        P(("page", "blk"), None),
        P(),
        P(),
        P(("page", "blk"), None),
        P(None, ("page", "blk")),
        P(None, ("page", "blk")),
        P(("page", "blk"), None),
        P(("page", "blk")),
        P(("page", "blk"), None),
        P(("page", "blk")),
    )
    return jax.shard_map(
        per_device, mesh=mesh, in_specs=in_specs, out_specs=out_specs, check_vma=False
    )
```

```python
import functools

import jax
import jax.numpy as jnp
import numpy as np
from jax import lax
from jax.experimental import pallas as pl
from jax.experimental.pallas import tpu as pltpu
from jax.sharding import PartitionSpec as P

TEXT = 512
GRID_LO = 7
GRID_HI = 14
RUN = 16
HEADS = 12
HEAD_DIM = 64
NB1 = 32
NB2 = 64
SPAN = 256
RANK_LANES = 1536
RANK_MID = RANK_LANES // 2
ROWS = 128
F32 = jnp.float32
BF16 = jnp.bfloat16
MIB = 1 << 20
LONG = 10**11

rank_marks = (1, 2, 3, 4, 5, 6, 7, 8, 12, 16, 23, 32, 46, 64, 91)
box_marks = tuple(range(1, 17)) + (19, 23, 27, 32, 39, 46, 54, 64, 77, 91, 108, 128, 153, 182, 216)
neg_fill = -1000000000.0
norm_eps = 1e-05
root_half = 0.7071067811865476
inv_root_tau = 0.3989422804014327
tap_list = ((1, -1), (1, 0), (1, 1), (2, -1), (2, 0), (2, 1), (3, -1), (3, 0), (3, 1))
cell_list = ((-1, -1), (-1, 0), (-1, 1), (0, -1), (0, 0), (0, 1), (1, -1), (1, 0), (1, 1))


def bucket_rows(deltas, marks, bins):
    spread = np.abs(deltas)
    ids = np.sum(spread[:, None] >= np.asarray(marks)[None, :], axis=1) + (bins // 2) * (deltas > 0)
    return (ids[:, None] == np.arange(bins)[None, :]).astype(np.float32)


def dot_nn(left, right):
    return lax.dot_general(left, right, (((1,), (0,)), ((), ())), preferred_element_type=F32)


def dot_nt(left, right):
    return lax.dot_general(left, right, (((1,), (1,)), ((), ())), preferred_element_type=F32)


def dot_tn(left, right):
    return lax.dot_general(left, right, (((0,), (0,)), ((), ())), preferred_element_type=F32)


def row_chunks(total, size):
    return [(start, min(size, total - start)) for start in range(0, total, size)]


def vmem():
    return pl.BlockSpec(memory_space=pltpu.VMEM)


def smem():
    return pl.BlockSpec(memory_space=pltpu.SMEM)


def anywhere():
    return pl.BlockSpec(memory_space=pl.ANY)


def parameter():
    return pl.BlockSpec(memory_space=pltpu.HBM)


def stay(value):
    return pltpu.with_memory_space_constraint(value, pltpu.HBM)


def fetch(sources, targets, semaphores):
    copies = []
    for number, (source, target) in enumerate(zip(sources, targets)):
        copies.append(pltpu.make_async_copy(source, target, semaphores.at[number]))
        copies[-1].start()
    return copies


def params(mib):
    return pltpu.CompilerParams(vmem_limit_bytes=mib * MIB)


def onehot_kernel(
    scalars, rank_hbm, box_hbm, rank_table_hbm, box_tables_hbm, rank_rows_hbm, box_rows_hbm,
    xy_ref, xyt_ref, rank_bias, box_bias,
    rank_ref, box_ref, rank_table, box_tables, rank_rows, box_rows, vectors, copies,
):
    fetches = fetch(
        [rank_hbm, box_hbm, rank_table_hbm, box_tables_hbm, rank_rows_hbm, box_rows_hbm],
        [rank_ref, box_ref, rank_table, box_tables, rank_rows, box_rows],
        copies,
    )
    for copy in fetches:
        copy.wait()
    seq = rank_ref.shape[1]
    for start, size in row_chunks(seq, 240):
        spot = lax.broadcasted_iota(jnp.int32, (size, seq), 0) + start
        order = (spot == rank_ref[...]).astype(F32).astype(BF16)
        for half in range(2):
            level = lax.broadcasted_iota(jnp.int32, (SPAN, seq), 0)
            marks = (level == box_ref[half]).astype(F32).astype(BF16)
            xy_ref[start : start + size, half * SPAN : (half + 1) * SPAN] = dot_nt(
                order, marks
            ).astype(BF16)
    row = lax.broadcasted_iota(jnp.int32, (SPAN, SPAN), 0)
    col = lax.broadcasted_iota(jnp.int32, (SPAN, SPAN), 1)
    flip = (row + col == SPAN - 1).astype(F32).astype(BF16)
    for half in range(2):
        part = slice(half * SPAN, (half + 1) * SPAN)
        xyt_ref[part, :] = dot_nt(flip, xy_ref[:, part]).astype(BF16)
    heads = vectors.shape[0]
    tables = [(dot_nt(rank_table[...], rank_rows[...]), RANK_LANES)]
    tables += [(dot_nt(box_tables[half], box_rows[...]), 2 * SPAN) for half in range(2)]
    for place, (table, lanes) in enumerate(tables):
        own = jnp.where(scalars[0] == 0, table[:heads], table[table.shape[0] - heads :])
        for head in range(heads):
            vectors[head, place : place + 1, :lanes] = own[head : head + 1]

    def one_head(head, carry):
        rank_bias[head] = skewed(vectors[head, 0:1, :], ROWS, RANK_LANES, RANK_LANES - 128)
        for half in range(2):
            part = slice(half * SPAN, (half + 1) * SPAN)
            table = skewed(vectors[head, half + 1 : half + 2, : 2 * SPAN], SPAN, 2 * SPAN, SPAN + 1)
            box_bias[head, :, part] = dot_nn(xy_ref[:, part], table[:, :SPAN].astype(BF16)).astype(BF16)
        return carry

    lax.fori_loop(0, heads, one_head, 0)


def onehots(scalars, ranks, boxes, rank_table, box_tables, heads):
    seq = ranks.shape[1]
    rank_rows = jnp.asarray(bucket_rows(np.arange(RANK_LANES) - RANK_MID, rank_marks, NB1), BF16)
    box_rows = jnp.asarray(bucket_rows(SPAN - 1 - np.arange(2 * SPAN), box_marks, NB2), BF16)
    operands = tuple(map(stay, (ranks, boxes, rank_table, box_tables, rank_rows, box_rows)))
    return pl.pallas_call(
        onehot_kernel,
        out_shape=(
            jax.ShapeDtypeStruct((seq, 2 * SPAN), BF16),
            jax.ShapeDtypeStruct((2 * SPAN, seq), BF16),
            jax.ShapeDtypeStruct((heads, ROWS, RANK_LANES), F32),
            jax.ShapeDtypeStruct((heads, seq, 2 * SPAN), BF16),
        ),
        in_specs=[smem()] + [parameter()] * 6,
        out_specs=(vmem(),) * 4,
        scratch_shapes=[pltpu.VMEM(value.shape, value.dtype) for value in operands]
        + [pltpu.VMEM((heads, 8, RANK_LANES), F32), pltpu.SemaphoreType.DMA((6,))],
        compiler_params=params(14),
        cost_estimate=pl.CostEstimate(
            flops=4 * seq * seq * SPAN, bytes_accessed=4 * seq * 2 * SPAN, transcendentals=0
        ),
        name="onehots",
    )(scalars, *operands)


def place_slots(own_ref, other_ref, side, text, patch, patch_pad):
    local = own_ref.shape[0]
    head = TEXT - local
    groups = text.shape[0]

    def place(low_ref, high_ref):
        for lane in range(groups):
            cols = slice(128 * lane, 128 * lane + 128)
            text[lane, 8 : 8 + local, :] = low_ref[:, cols].astype(F32)
            high = high_ref[:, cols].astype(F32)
            text[lane, 8 + local : 8 + TEXT, :] = high[:head]
            patch[lane, patch_pad : patch_pad + local - head, :] = high[head:]

    pl.when(side == 0)(lambda: place(own_ref, other_ref))
    pl.when(side != 0)(lambda: place(other_ref, own_ref))


def clear_pads(text, patch, patch_pad):
    groups, rows = patch.shape[0], patch.shape[1]
    for lane in range(groups):
        text[lane, 0:8, :] = jnp.zeros((8, 128), F32)
        text[lane, 8 + TEXT : 16 + TEXT, :] = jnp.zeros((8, 128), F32)
        patch[lane, 0:patch_pad, :] = jnp.zeros((patch_pad, 128), F32)
        patch[lane, rows - patch_pad : rows, :] = jnp.zeros((patch_pad, 128), F32)


def cell_masks(grid, rows):
    slot = lax.broadcasted_iota(jnp.int32, (rows, 128), 0)
    row_of = jnp.zeros((rows, 128), jnp.int32)
    for line in range(1, grid):
        row_of = row_of + (slot >= line * grid).astype(jnp.int32)
    column = slot - row_of * grid
    alive = slot < grid * grid
    masks = []
    for down, across in cell_list:
        masks.append(
            alive
            & (row_of + down >= 0)
            & (row_of + down < grid)
            & (column + across >= 0)
            & (column + across < grid)
        )
    return masks


def store_masks(masks, fine, rows):
    for grid, chosen in ((GRID_HI, fine != 0), (GRID_LO, fine == 0)):

        def fill(grid=grid):
            for number, mask in enumerate(cell_masks(grid, rows)):
                masks[number] = mask.astype(F32)

        pl.when(chosen)(fill)


def mix_lane(text, patch, masks, out, lane, text_kernel, patch_kernel, fine, patch_pad, flip):
    cols = pl.ds(pl.multiple_of(lane * 128, 128), 128)
    taps = {}
    for number, (reach, side) in enumerate(tap_list):
        offset = -reach * side if flip else reach * side
        value = text_kernel[number : number + 1, cols]
        taps[offset] = taps[offset] + value if offset in taps else value
    for start, size in row_chunks(TEXT, ROWS):
        total = text[lane, pl.ds(8 + start, size), :] * (1.0 + taps[0])
        for offset, value in taps.items():
            if offset:
                total = total + text[lane, pl.ds(8 + start + offset, size), :] * value
        out[lane, pl.ds(start, size), :] = total
    rows = masks.shape[1]
    for grid, chosen in ((GRID_HI, fine != 0), (GRID_LO, fine == 0)):

        def cells(grid=grid):
            for start, size in row_chunks(rows, 104):
                total = patch[lane, pl.ds(patch_pad + start, size), :]
                for number, (down, across) in enumerate(cell_list):
                    tap = len(cell_list) - 1 - number if flip else number
                    moved = patch[lane, pl.ds(patch_pad + start + down * grid + across, size), :]
                    total = total + (
                        moved * masks[number, pl.ds(start, size), :]
                    ) * patch_kernel[tap : tap + 1, cols]
                out[lane, pl.ds(TEXT + start, size), :] = total

        pl.when(chosen)(cells)


def sort_rows(ranks_ref, source, target, seq, cast):
    for run in range(TEXT // RUN):
        spot = pl.multiple_of(ranks_ref[0, run * RUN], RUN)
        target[pl.ds(spot, RUN), :] = source[run * RUN : (run + 1) * RUN, :].astype(cast)
    target[TEXT:seq, :] = source[TEXT:seq, :].astype(cast)


def unsort_rows(ranks_ref, source, target, seq):
    for run in range(TEXT // RUN):
        spot = pl.multiple_of(ranks_ref[0, run * RUN], RUN)
        target[run * RUN : (run + 1) * RUN, :] = source[pl.ds(spot, RUN), :]
    target[TEXT:seq, :] = source[TEXT:seq, :]


def mix_kernel(
    scalars, ranks_ref, own_ref, other_ref, text_kernel, patch_kernel, weight_ref,
    mixed_ref, low_ref, packed_ref, text, patch, masks, lanes, whole, weights, copies,
):
    side, fine = scalars[0], scalars[2]
    local, width = own_ref.shape
    seq = low_ref.shape[0]
    groups = width // 128
    pad = GRID_HI + 2
    part = width // 2
    fetches = fetch(
        [
            weight_ref.at[:, pl.ds(pl.multiple_of(block * width + side * part, 128), part)]
            for block in range(3)
        ],
        [weights.at[:, block * part : (block + 1) * part] for block in range(3)],
        copies,
    )
    place_slots(own_ref, other_ref, side, text, patch, pad)
    clear_pads(text, patch, pad)
    store_masks(masks, fine, seq - TEXT)

    def one_lane(lane, carry):
        mix_lane(text, patch, masks, lanes, lane, text_kernel, patch_kernel, fine, pad, False)
        return carry

    lax.fori_loop(0, groups, one_lane, 0, unroll=True)
    for lane in range(groups):
        whole[:, 128 * lane : 128 * lane + 128] = lanes[lane]
    mixed_ref[...] = whole[pl.ds(pl.multiple_of(side * local, 8), local), :]
    sort_rows(ranks_ref, whole, low_ref, seq, BF16)
    for copy in fetches:
        copy.wait()
    for start, size in row_chunks(seq, 240):
        rows = slice(start, start + size)
        value = dot_nn(low_ref[rows, :], weights[...]).astype(BF16)
        packed_ref[rows, :part] = value[:, :part] * (HEAD_DIM**-0.5)
        packed_ref[rows, part:] = value[:, part:]


def mix_and_project(scalars, ranks, own, other, text_kernel, patch_kernel, qkv_weight):
    local, width = own.shape
    seq = ranks.shape[1]
    groups = width // 128
    return pl.pallas_call(
        mix_kernel,
        out_shape=(
            jax.ShapeDtypeStruct((local, width), F32),
            jax.ShapeDtypeStruct((seq, width), BF16),
            jax.ShapeDtypeStruct((seq, 3 * width // 2), BF16),
        ),
        in_specs=[smem(), smem()] + [vmem()] * 4 + [parameter()],
        out_specs=(vmem(),) * 3,
        scratch_shapes=[
            pltpu.VMEM((groups, TEXT + 16, 128), F32),
            pltpu.VMEM((groups, seq - TEXT + 2 * (GRID_HI + 2), 128), F32),
            pltpu.VMEM((9, seq - TEXT, 128), F32),
            pltpu.VMEM((groups, seq, 128), F32),
            pltpu.VMEM((seq, width), F32),
            pltpu.VMEM((width, 3 * width // 2), BF16),
            pltpu.SemaphoreType.DMA((3,)),
        ],
        compiler_params=params(16),
        cost_estimate=pl.CostEstimate(
            flops=2 * seq * width * 3 * width // 2, bytes_accessed=12 * MIB, transcendentals=0
        ),
        name="mix_and_project",
    )(scalars, ranks, own, other, text_kernel, patch_kernel, qkv_weight)


def head_lanes(shape, parity):
    return (lax.broadcasted_iota(jnp.int32, shape, 1) >= HEAD_DIM) == (parity != 0)


def skewed(vector, rows, lanes, shift):
    return pltpu.roll(jnp.broadcast_to(vector, (rows, lanes)), shift, 1, stride=1, stride_axis=0)


def attend_kernel(
    scalars, ranks_ref, queries, keys, values, xy_ref, rank_bias, box_bias,
    shares_ref, own_ref, other_ref, left, right, gathered, slots, scores_ref,
):
    side, live = scalars[0], scalars[1]
    seq = queries.shape[0]
    local = own_ref.shape[0]
    head = pl.program_id(0)
    parity = lax.rem(head, 2)

    @pl.when(head == 0)
    def _():
        left[:, 128:] = xy_ref[...]

    left[:, :128] = queries[...]
    mine = head_lanes((seq, 128), parity)
    right[:, :128] = jnp.where(mine, keys[...], jnp.zeros((), BF16))
    right[:, 128:] = box_bias[0]
    top = (seq // ROWS) * ROWS
    alive = lax.broadcasted_iota(jnp.int32, (16, seq), 1) < live
    chunks = row_chunks(seq, 240)

    def product(start, size):
        scores_ref[start : start + size, :] = dot_nt(left[start : start + size, :], right[...])

    def soften(start, size):
        for first in range(start, start + size, 16):
            base = first // ROWS * ROWS
            scores = scores_ref[first : first + 16, :]
            scores = scores + rank_bias[0, first - base : first - base + 16, top - base : top - base + seq]
            scores = jnp.where(alive, scores, neg_fill)
            powered = jnp.exp(scores - jnp.max(scores, axis=1, keepdims=True))
            shares = powered * (1.0 / jnp.sum(powered, axis=1, keepdims=True))
            shares_ref[0, first : first + 16, :] = shares.astype(BF16)

    def apply(start, size):
        context = dot_nn(shares_ref[0, start : start + size, :], values[...])
        gathered[start : start + size, :] = jnp.where(
            head_lanes((size, 128), parity), context, gathered[start : start + size, :]
        )

    product(*chunks[0])
    for n in range(len(chunks)):
        if n + 1 < len(chunks):
            product(*chunks[n + 1])
        if n:
            apply(*chunks[n - 1])
        soften(*chunks[n])
    apply(*chunks[-1])

    @pl.when(parity == 1)
    def _():
        unsort_rows(ranks_ref, gathered, slots, seq)
        own_ref[...] = slots[pl.ds(pl.multiple_of(side * local, 8), local), :].astype(BF16)
        other_ref[...] = slots[pl.ds(pl.multiple_of((1 - side) * local, 8), local), :].astype(BF16)


def attend(scalars, ranks, packed, xy, rank_bias, box_bias, local, first, count):
    seq = packed.shape[0]
    pairs = rank_bias.shape[0] // 2
    heads = 2 * count
    width = heads * HEAD_DIM
    whole = pl.BlockSpec((seq, 2 * SPAN), lambda h: (0, 0))
    slot_spec = pl.BlockSpec((local, 128), lambda h: (0, h // 2))
    return pl.pallas_call(
        attend_kernel,
        grid=(heads,),
        out_shape=(
            jax.ShapeDtypeStruct((heads, seq, seq), BF16),
            jax.ShapeDtypeStruct((local, width), BF16),
            jax.ShapeDtypeStruct((local, width), BF16),
        ),
        in_specs=[
            smem(),
            smem(),
            pl.BlockSpec((seq, 128), lambda h: (0, first + h // 2)),
            pl.BlockSpec((seq, 128), lambda h: (0, pairs + first + h // 2)),
            pl.BlockSpec((seq, 128), lambda h: (0, 2 * pairs + first + h // 2)),
            whole,
            pl.BlockSpec((1, ROWS, RANK_LANES), lambda h: (2 * first + h, 0, 0)),
            pl.BlockSpec((1, seq, 2 * SPAN), lambda h: (2 * first + h, 0, 0)),
        ],
        out_specs=(pl.BlockSpec((1, seq, seq), lambda h: (h, 0, 0)), slot_spec, slot_spec),
        scratch_shapes=[
            pltpu.VMEM((seq, 128 + 2 * SPAN), BF16),
            pltpu.VMEM((seq, 128 + 2 * SPAN), BF16),
            pltpu.VMEM((seq, 128), F32),
            pltpu.VMEM((seq, 128), F32),
            pltpu.VMEM((seq, seq), F32),
        ],
        compiler_params=params(13),
        cost_estimate=pl.CostEstimate(
            flops=heads * 2 * seq * seq * 1024, bytes_accessed=heads * seq * seq * 2,
            transcendentals=heads * seq * seq,
        ),
        name="attend",
    )(scalars, ranks, packed, packed, packed, xy, rank_bias, box_bias)


def attend_back_kernel(
    ranks_ref, own_ref, other_ref, side_ref, shares_ref, queries, keys, values, xy_ref, xyt_ref,
    dq_ref, dk_ref, dv_ref, sums_ref, right, score_grad, spread, rank_sum, slots, upstream, share_grads,
):
    seq = queries.shape[0]
    local = own_ref.shape[0]
    side = side_ref[0]
    head = pl.program_id(0)
    parity = lax.rem(head, 2)
    scale = HEAD_DIM**-0.5

    @pl.when(head == 0)
    def _():
        right[:, 128:] = xy_ref[...]

    @pl.when(parity == 0)
    def _():
        slots[pl.ds(pl.multiple_of(side * local, 8), local), :] = own_ref[...].astype(F32)
        slots[pl.ds(pl.multiple_of((1 - side) * local, 8), local), :] = other_ref[...].astype(F32)
        sort_rows(ranks_ref, slots, upstream, seq, BF16)

    right[:, :128] = keys[...]
    mine = head_lanes((seq, 128), parity)
    own_values = jnp.where(mine, values[...], jnp.zeros((), BF16))
    rank_sum[:, (2 * (-(-seq // ROWS)) - 1) * 128 :] = jnp.zeros((ROWS, 128), F32)
    blocks = -(-seq // ROWS)
    chunks = row_chunks(seq, 240)
    for start, size in chunks:
        share_grads[start : start + size, :] = dot_nt(upstream[start : start + size, :], own_values)
    dv = dot_tn(shares_ref[0], upstream[...]).astype(BF16)
    dv_ref[...] = jnp.where(mine, dv, dv_ref[...])
    blank = jnp.zeros((16, blocks * 128 - seq), F32)
    for inner in range(0, ROWS, 16):
        totals = [None] * (2 * blocks - 1)
        for block in range(blocks):
            first = block * ROWS + inner
            if first >= seq:
                continue
            rows = slice(first, first + 16)
            shares = shares_ref[0, rows, :].astype(F32)
            weighted = shares * share_grads[rows, :]
            low = (weighted - shares * jnp.sum(weighted, axis=1, keepdims=True)).astype(BF16)
            score_grad[rows, :] = low
            padded = jnp.concatenate([low.astype(F32), blank], axis=1)
            for tile in range(blocks):
                value = padded[:, tile * 128 : tile * 128 + 128]
                place = blocks - 1 - block + tile
                totals[place] = value if totals[place] is None else totals[place] + value
        for place, value in enumerate(totals):
            rank_sum[inner : inner + 16, place * 128 : place * 128 + 128] = (
                jnp.zeros((16, 128), F32) if value is None else value
            )
    for start, size in chunks:
        rows = slice(start, start + size)
        product = dot_nn(score_grad[rows, :], right[...])
        spread[rows, :] = product[:, 128:].astype(BF16)
        dq_ref[rows, :] = jnp.where(
            head_lanes((size, 128), parity), (product[:, :128] * scale).astype(BF16), dq_ref[rows, :]
        )
    dk = dot_tn(score_grad[...], queries[...]).astype(BF16)
    dk_ref[...] = jnp.where(mine, dk, dk_ref[...])
    row = lax.broadcasted_iota(jnp.int32, (ROWS, ROWS), 0)
    col = lax.broadcasted_iota(jnp.int32, (ROWS, ROWS), 1)
    flip = (row + col == ROWS - 1).astype(F32).astype(BF16)
    turned = dot_nn(flip, rank_sum[...].astype(BF16))
    turned = pltpu.roll(turned, 0, 1, stride=1, stride_axis=0)
    sums_ref[0, 0:1, :] = jnp.sum(turned, axis=0, keepdims=True)
    for half in range(2):
        part = slice(half * SPAN, (half + 1) * SPAN)
        table = dot_nn(xyt_ref[part, :], spread[:, part])
        table = jnp.concatenate([table, jnp.zeros((SPAN, SPAN), F32)], axis=1)
        table = pltpu.roll(table, 0, 1, stride=1, stride_axis=0)
        sums_ref[0, half + 1 : half + 2, : 2 * SPAN] = jnp.sum(table, axis=0, keepdims=True)


def attend_back(scalars, ranks, own, other, shares, packed, xy, xyt, pair, place, so_far, marker):
    seq = packed.shape[0]
    local = own.shape[0]
    width = packed.shape[1] // 3
    pairs = width // 128
    slot_spec = pl.BlockSpec((local, 128), lambda h: (0, pair))
    out_spec = pl.BlockSpec((seq, 128), lambda h: (0, pair))
    so_far = tuple(so_far) if so_far else ()
    extra = so_far + ((marker,) if marker is not None else ())

    def body(*refs):
        ins, rest = refs[:10], refs[10 + len(extra) :]
        attend_back_kernel(*ins, *rest)

    return pl.pallas_call(
        body,
        grid=(2,),
        out_shape=(jax.ShapeDtypeStruct((seq, width), BF16),) * 3
        + (jax.ShapeDtypeStruct((2, 8, RANK_LANES), F32),),
        in_specs=[
            smem(),
            slot_spec,
            slot_spec,
            smem(),
            pl.BlockSpec((1, seq, seq), lambda h: (2 * place + h, 0, 0)),
            pl.BlockSpec((seq, 128), lambda h: (0, pair)),
            pl.BlockSpec((seq, 128), lambda h: (0, pairs + pair)),
            pl.BlockSpec((seq, 128), lambda h: (0, 2 * pairs + pair)),
            pl.BlockSpec((seq, 2 * SPAN), lambda h: (0, 0)),
            pl.BlockSpec((2 * SPAN, seq), lambda h: (0, 0)),
        ]
        + [anywhere()] * len(extra),
        out_specs=(out_spec,) * 3 + (pl.BlockSpec((1, 8, RANK_LANES), lambda h: (h, 0, 0)),),
        scratch_shapes=[
            pltpu.VMEM((seq, 128 + 2 * SPAN), BF16),
            pltpu.VMEM((seq, seq), BF16),
            pltpu.VMEM((seq, 2 * SPAN), BF16),
            pltpu.VMEM((ROWS, RANK_LANES), F32),
            pltpu.VMEM((seq, 128), F32),
            pltpu.VMEM((seq, 128), BF16),
            pltpu.VMEM((seq, seq), F32),
        ],
        input_output_aliases={10 + n: n for n in range(len(so_far))},
        compiler_params=params(15),
        cost_estimate=pl.CostEstimate(
            flops=1000 if pair else LONG, bytes_accessed=1000, transcendentals=0
        ),
        name="attend_back",
    )(ranks, own, other, scalars, shares, packed, packed, packed, xy, xyt, *extra)


def fold_rows(value):
    total = value[0:8]
    for start in range(8, value.shape[0], 8):
        total = total + value[start : start + 8]
    return total


def row_mean(value):
    return jnp.sum(value, axis=1, keepdims=True) * (1.0 / value.shape[1])


def normalize(value):
    center = value - row_mean(value)
    inverse = lax.rsqrt(row_mean(center * center) + norm_eps)
    return center * inverse, inverse


def dense_kernel(
    scalars, mixed_ref, own_a, own_b, other_a, other_b, pack, cot_ref, out_hbm, up_hbm, down_hbm, marker,
    result_ref, context_ref, hidden_ref, act_ref, branch_ref, pre_ref, attend_ref, resid_ref,
    own_grad, other_grad, sums_ref, blocks_ref,
    out_w, up_w, down_w, slope, product, stash, hidden, normed, scale, bias_sums_ref, copies,
):
    side, live = scalars[0], scalars[1]
    local, width = mixed_ref.shape
    deep = act_ref.shape[1]
    part = own_grad.shape[1]
    step = width
    blocks = deep // step
    gains, shifts, down_bias = pack.at[0:2], pack.at[2:4], pack.at[4:5]
    fetches = [pltpu.make_async_copy(out_hbm, out_w, copies.at[0])]
    fetches += [
        pltpu.make_async_copy(
            up_hbm.at[:, n * width : (n + 1) * width], up_w.at[:, n * width : (n + 1) * width],
            copies.at[1 + n],
        )
        for n in range(deep // width)
    ]
    fetches.append(pltpu.make_async_copy(down_hbm, down_w, copies.at[1 + deep // width]))
    for fetch in fetches:
        fetch.start()
    wide = own_a.shape[1]
    for base, (first, second) in ((side * part, (own_a, own_b)), ((1 - side) * part, (other_a, other_b))):
        context_ref[:, pl.ds(pl.multiple_of(base, 128), wide)] = first[...]
        context_ref[:, pl.ds(pl.multiple_of(base + wide, 128), part - wide)] = second[...]
    chunks = row_chunks(local, 24)
    fetches[0].wait()
    product[...] = dot_nn(context_ref[...], out_w[...])
    for start, size in chunks:
        rows = slice(start, start + size)
        value, inverse = normalize(mixed_ref[rows, :] + product[rows, :])
        normed[rows, :] = value
        scale[rows, :] = jnp.broadcast_to(inverse, (size, 128))
        value = value * gains[0:1, :] + shifts[0:1, :]
        hidden[rows, :] = value
        hidden_ref[rows, :] = value.astype(BF16)

    def lift(block):
        fetches[1 + block].wait()
        cols = slice(block * step, (block + 1) * step)
        stash[block % 2] = dot_nn(hidden_ref[...], up_w[:, cols])

    def bend(block):
        cols = slice(block * step, (block + 1) * step)
        for start, size in chunks:
            rows = slice(start, start + size)
            value = stash[block % 2, rows, :] + pack[5 + block : 6 + block, :]
            half = 0.5 + 0.5 * lax.erf(value * root_half)
            act_ref[rows, cols] = (value * half).astype(BF16)
            slope[rows, cols] = half + value * jnp.exp(-0.5 * value * value) * inv_root_tau

    lift(0)
    for block in range(blocks):
        if block + 1 < blocks:
            lift(block + 1)
        bend(block)
    fetches[-1].wait()
    product[...] = dot_nn(act_ref[...], down_w[...])
    zero = jnp.zeros((8, width), F32)
    gain_sum, shift_sum, bias_sum = zero, zero, zero
    for start, size in chunks:
        rows = slice(start, start + size)
        value, inverse = normalize(hidden[rows, :] + product[rows, :] + down_bias[...])
        slot = lax.broadcasted_iota(jnp.int32, (size, width), 0) + (side * local + start)
        alive = (slot < live).astype(F32)
        result_ref[rows, :] = (alive * (value * gains[1:2, :] + shifts[1:2, :])).astype(BF16)
        upstream = cot_ref[rows, :].astype(F32) * alive
        gain_sum = gain_sum + fold_rows(upstream * value)
        shift_sum = shift_sum + fold_rows(upstream)
        scaled = upstream * gains[1:2, :]
        grad = inverse * (scaled - row_mean(scaled) - value * row_mean(scaled * value))
        bias_sum = bias_sum + fold_rows(grad)
        hidden[rows, :] = grad
        branch_ref[rows, :] = grad.astype(BF16)
    sums_ref[1:2, :] = jnp.sum(gain_sum, axis=0, keepdims=True)
    sums_ref[3:4, :] = jnp.sum(shift_sum, axis=0, keepdims=True)
    sums_ref[4:5, :] = jnp.sum(bias_sum, axis=0, keepdims=True)
    sums_ref[5:8, :] = jnp.zeros((3, width), F32)

    def lower(block):
        cols = slice(block * step, (block + 1) * step)
        stash[block % 2] = dot_nt(branch_ref[...], down_w[cols, :])

    def unbend(block):
        cols = slice(block * step, (block + 1) * step)
        total = jnp.zeros((8, step), F32)
        for start, size in chunks:
            rows = slice(start, start + size)
            value = (stash[block % 2, rows, :] * slope[rows, cols]).astype(BF16)
            pre_ref[rows, cols] = value
            total = total + fold_rows(value.astype(F32))
        bias_sums_ref[:, cols] = jnp.sum(total, axis=0, keepdims=True)

    lower(0)
    for block in range(blocks):
        if block + 1 < blocks:
            lower(block + 1)
        unbend(block)
    product[...] = dot_nt(pre_ref[...], up_w[...])
    piece = deep // blocks_ref.shape[0]
    blocks_ref[...] = jnp.zeros(blocks_ref.shape, F32)
    for block in range(blocks_ref.shape[0]):
        blocks_ref[block : block + 1, :piece] = bias_sums_ref[:, block * piece : (block + 1) * piece]
    gain_sum, shift_sum = zero, zero
    for start, size in chunks:
        rows = slice(start, start + size)
        upstream = hidden[rows, :] + product[rows, :]
        value = normed[rows, :]
        gain_sum = gain_sum + fold_rows(upstream * value)
        shift_sum = shift_sum + fold_rows(upstream)
        scaled = upstream * gains[0:1, :]
        inverse = jnp.concatenate([scale[rows, :]] * (width // 128), axis=1)
        grad = inverse * (scaled - row_mean(scaled) - value * row_mean(scaled * value))
        resid_ref[rows, :] = grad
        attend_ref[rows, :] = grad.astype(BF16)
    sums_ref[0:1, :] = jnp.sum(gain_sum, axis=0, keepdims=True)
    sums_ref[2:3, :] = jnp.sum(shift_sum, axis=0, keepdims=True)
    product[...] = dot_nt(attend_ref[...], out_w[...])
    for base, ref in (((1 - side) * part, other_grad), (side * part, own_grad)):
        ref[...] = product[:, pl.ds(pl.multiple_of(base, 128), part)].astype(BF16)


def dense(
    scalars, mixed, own_context, other_context, pack, cotangent, out_weight, up_weight, down_weight, devices, marker,
):
    local, width = mixed.shape
    deep = up_weight.shape[1]
    part = width // 2
    low = lambda *shape: jax.ShapeDtypeStruct(shape, BF16)
    full = lambda *shape: jax.ShapeDtypeStruct(shape, F32)
    return pl.pallas_call(
        dense_kernel,
        out_shape=(
            low(local, width), low(local, width), low(local, width), low(local, deep),
            low(local, width), low(local, deep), low(local, width), full(local, width),
            low(local, part), low(local, part), full(8, width), full(devices, 128),
        ),
        in_specs=[smem()] + [vmem()] * 7 + [parameter()] * 3 + [anywhere()],
        out_specs=(vmem(),) * 12,
        scratch_shapes=[
            pltpu.VMEM((width, width), BF16),
            pltpu.VMEM((width, deep), BF16),
            pltpu.VMEM((deep, width), BF16),
            pltpu.VMEM((local, deep), F32),
            pltpu.VMEM((local, width), F32),
            pltpu.VMEM((2, local, width), F32),
            pltpu.VMEM((local, width), F32),
            pltpu.VMEM((local, width), F32),
            pltpu.VMEM((local, 128), F32),
            pltpu.VMEM((1, deep), F32),
            pltpu.SemaphoreType.DMA((2 + deep // width,)),
        ],
        compiler_params=params(26),
        cost_estimate=pl.CostEstimate(
            flops=2 * local * width * (4 * deep + 2 * width), bytes_accessed=20 * MIB,
            transcendentals=2 * local * deep,
        ),
        name="dense",
    )(
        scalars, mixed, *own_context, *other_context, pack, cotangent, out_weight, up_weight, down_weight,
        marker,
    )


def halves_of(value):
    high = value.astype(BF16)
    return high, (value - high.astype(F32)).astype(BF16)


def turn_kernel(order_ref, low_ref, marker, turned_ref, after_ref):
    turned_ref[...] = dot_nt(order_ref[...], low_ref[...]).astype(BF16)
    after_ref[...] = jnp.zeros(after_ref.shape, F32)


def turn_rows(order, low, marker):
    return pl.pallas_call(
        turn_kernel,
        out_shape=(
            jax.ShapeDtypeStruct((order.shape[0], low.shape[0]), BF16),
            jax.ShapeDtypeStruct((8, 128), F32),
        ),
        in_specs=[vmem(), vmem(), anywhere()],
        out_specs=(vmem(), vmem()),
        compiler_params=params(8),
        cost_estimate=pl.CostEstimate(flops=10**9, bytes_accessed=1000, transcendentals=0),
        name="turn_rows",
    )(order, low, marker)


def project_back_kernel(
    turned_hbm, dq_hbm, dk_hbm, dv_hbm, marker, keep_ref, send_ref, after_ref, turned, grads, copies
):
    half, part = keep_ref.shape[0], dq_hbm.shape[1]
    fetches = fetch(
        [turned_hbm, dq_hbm, dk_hbm, dv_hbm],
        [turned] + [grads.at[:, block * part : (block + 1) * part] for block in range(3)],
        copies,
    )
    after_ref[...] = jnp.zeros(after_ref.shape, F32)
    for copy in fetches:
        copy.wait()
    send_ref[...] = dot_nn(turned[half:, :], grads[...]).astype(BF16)
    keep_ref[...] = dot_nn(turned[:half, :], grads[...]).astype(BF16)


def project_weight_grad(turned, dq, dk, dv, marker):
    width, seq = turned.shape
    part = dq.shape[1]
    shape = jax.ShapeDtypeStruct((width // 2, 3 * part), BF16)
    return pl.pallas_call(
        project_back_kernel,
        out_shape=(shape, shape, jax.ShapeDtypeStruct((8, 128), F32)),
        in_specs=[anywhere()] * 5,
        out_specs=(vmem(),) * 3,
        scratch_shapes=[
            pltpu.VMEM((width, seq), BF16),
            pltpu.VMEM((seq, 3 * part), BF16),
            pltpu.SemaphoreType.DMA((4,)),
        ],
        compiler_params=params(12),
        cost_estimate=pl.CostEstimate(flops=1000, bytes_accessed=1000, transcendentals=0),
        name="project_weight_grad",
    )(turned, dq, dk, dv, marker)


def fill_block(turned, keep_ref, send_ref, start, right):
    middle = turned.shape[0] // 2
    cols = slice(start, start + right.shape[1])
    send_ref[:, cols] = dot_nn(turned[middle:, :], right).astype(BF16)
    keep_ref[:, cols] = dot_nn(turned[:middle, :], right).astype(BF16)


def down_kernel(spots, act_ref, branch_ref, keep_ref, send_ref, whole, *, piece):
    width = branch_ref.shape[1]
    half = keep_ref.shape[0]
    for step in range(act_ref.shape[1] // width):
        whole[...] = dot_tn(act_ref[:, step * width : (step + 1) * width], branch_ref[...]).astype(BF16)
        for block in range(width // piece):
            spot = spots[step * (width // piece) + block]
            rows = slice(block * piece, (block + 1) * piece)

            def keep(spot=spot, rows=rows):
                keep_ref[pl.ds(pl.multiple_of(spot, 16), piece), :] = whole[rows, :]

            def send(spot=spot, rows=rows):
                send_ref[pl.ds(pl.multiple_of(spot - half, 16), piece), :] = whole[rows, :]

            pl.when(spot < half)(keep)
            pl.when(spot >= half)(send)


def down_weight_grad(spots, act, branch, piece):
    deep, width = act.shape[1], branch.shape[1]
    tall = jax.ShapeDtypeStruct((deep // 2, width), BF16)
    return pl.pallas_call(
        functools.partial(down_kernel, piece=piece),
        out_shape=(tall, tall),
        in_specs=[smem()] + [vmem()] * 2,
        out_specs=(vmem(),) * 2,
        scratch_shapes=[pltpu.VMEM((width, width), BF16)],
        compiler_params=params(12),
        cost_estimate=pl.CostEstimate(flops=1000, bytes_accessed=1000, transcendentals=0),
        name="down_weight_grad",
    )(spots, act, branch)


def up_kernel(
    pre_ref, hidden_ref, context_ref, attend_ref, first_ref, second_ref, marker,
    out_keep, out_send, up_keep, up_send, turned, *, split,
):
    width, deep = hidden_ref.shape[1], pre_ref.shape[1]
    turned[...] = dot_nt(first_ref[...], hidden_ref[...]).astype(BF16)
    for start, size in row_chunks(split, width):
        fill_block(turned, out_keep, out_send, start, pre_ref[:, start : start + size])
    turned[...] = dot_nt(first_ref[...], context_ref[...]).astype(BF16)
    fill_block(turned, out_keep, out_send, split, attend_ref[...])
    turned[...] = dot_nt(second_ref[...], hidden_ref[...]).astype(BF16)
    for start, size in row_chunks(deep - split, width):
        fill_block(turned, up_keep, up_send, start, pre_ref[:, split + start : split + start + size])


def up_weight_grads_of(pre, hidden, context, attend, first, second, split, marker):
    local, width = hidden.shape
    deep = pre.shape[1]
    low = lambda columns: jax.ShapeDtypeStruct((width // 2, columns), BF16)
    return pl.pallas_call(
        functools.partial(up_kernel, split=split),
        out_shape=(low(split + width), low(split + width), low(deep - split), low(deep - split)),
        in_specs=[vmem()] * 6 + [anywhere()],
        out_specs=(vmem(),) * 4,
        scratch_shapes=[pltpu.VMEM((width, local), BF16)],
        compiler_params=params(14),
        cost_estimate=pl.CostEstimate(flops=LONG, bytes_accessed=1000, transcendentals=0),
        name="up_weight_grad",
    )(pre, hidden, context, attend, first, second, marker)


def mixed_back_kernel(
    scalars, ranks_ref, dq_hbm, dk_hbm, dv_hbm, weight_hbm, resid_hbm, own_hbm, other_hbm,
    marker, grad_ref, send_ref, taps_ref, cells_ref, sorted_grad, whole, text, patch, masks, edge,
    grads, weights, resid_ref, own_ref, other_ref, copies,
):
    side, fine = scalars[0], scalars[2]
    local, width = own_ref.shape
    seq, part = dq_hbm.shape
    groups = width // 128
    pad = GRID_HI + 2
    fetches = fetch(
        [own_hbm, other_hbm, dq_hbm, dk_hbm, dv_hbm]
        + [
            weight_hbm.at[:, pl.ds(pl.multiple_of(block * width + side * part, 128), part)]
            for block in range(3)
        ]
        + [resid_hbm],
        [own_ref, other_ref]
        + [grads.at[:, block * part : (block + 1) * part] for block in range(3)]
        + [weights.at[:, block * part : (block + 1) * part] for block in range(3)]
        + [resid_ref],
        copies,
    )
    fetches[0].wait()
    fetches[1].wait()
    place_slots(own_ref, other_ref, side, text, patch, pad)
    clear_pads(text, patch, pad)
    store_masks(masks, fine, seq - TEXT)
    for copy in fetches[2:]:
        copy.wait()
    for start, size in row_chunks(seq, 240):
        sorted_grad[start : start + size, :] = dot_nt(grads[start : start + size, :], weights[...])
    unsort_rows(ranks_ref, sorted_grad, whole, seq)
    mine = pl.ds(pl.multiple_of(side * local, 8), local)
    theirs = pl.ds(pl.multiple_of((1 - side) * local, 8), local)
    whole[mine, :] = whole[mine, :] + resid_ref[...]
    inner = pl.ds(pl.multiple_of(local - 8 + side * 8, 8), 8)
    outer = pl.ds(pl.multiple_of(local - side * 8, 8), 8)
    edge[0:local, :] = whole[theirs, :]
    edge[local : local + 8, :] = whole[inner, :]
    send_ref[...] = edge[...].astype(BF16)
    grad_ref[0:local, :] = whole[mine, :]
    grad_ref[local : local + 8, :] = whole[outer, :]
    taps_ref[...] = jnp.zeros(taps_ref.shape, F32)
    cells_ref[...] = jnp.zeros(cells_ref.shape, F32)
    for lane in range(groups):
        cols = slice(lane * 128, lane * 128 + 128)
        totals = {offset: jnp.zeros((8, 128), F32) for offset in range(-3, 4)}
        for start, size in row_chunks(TEXT, 64):
            value = whole[start : start + size, cols]
            for offset in totals:
                moved = text[lane, pl.ds(8 + start + offset, size), :]
                totals[offset] = totals[offset] + fold_rows(value * moved)
        for number, (reach, direction) in enumerate(tap_list):
            taps_ref[number : number + 1, cols] = jnp.sum(totals[reach * direction], axis=0, keepdims=True)
    for grid, chosen in ((GRID_HI, fine != 0), (GRID_LO, fine == 0)):

        def cells(grid=grid):
            for lane in range(groups):
                cols = slice(lane * 128, lane * 128 + 128)
                totals = [jnp.zeros((8, 128), F32)] * len(cell_list)
                for start, size in row_chunks(seq - TEXT, 104):
                    value = whole[TEXT + start : TEXT + start + size, cols]
                    for number, (down, across) in enumerate(cell_list):
                        moved = patch[lane, pl.ds(pad + start + down * grid + across, size), :]
                        moved = moved * masks[number, start : start + size, :]
                        totals[number] = totals[number] + fold_rows(value * moved)
                for number, value in enumerate(totals):
                    cells_ref[number : number + 1, cols] = jnp.sum(value, axis=0, keepdims=True)

        pl.when(chosen)(cells)


def mixed_back(scalars, ranks, dq, dk, dv, qkv_weight, resid_grad, own, other, marker):
    local, width = own.shape
    seq, part = dq.shape
    groups = width // 128
    return pl.pallas_call(
        mixed_back_kernel,
        out_shape=(
            jax.ShapeDtypeStruct((local + 8, width), F32),
            jax.ShapeDtypeStruct((local + 8, width), BF16),
            jax.ShapeDtypeStruct((16, width), F32),
            jax.ShapeDtypeStruct((16, width), F32),
        ),
        in_specs=[smem(), smem()] + [anywhere()] * 3 + [parameter()] + [anywhere()] * 4,
        out_specs=(vmem(),) * 4,
        scratch_shapes=[
            pltpu.VMEM((seq, width), F32),
            pltpu.VMEM((seq, width), F32),
            pltpu.VMEM((groups, TEXT + 16, 128), F32),
            pltpu.VMEM((groups, seq - TEXT + 2 * (GRID_HI + 2), 128), F32),
            pltpu.VMEM((9, seq - TEXT, 128), F32),
            pltpu.VMEM((local + 8, width), F32),
            pltpu.VMEM((seq, 3 * part), BF16),
            pltpu.VMEM((width, 3 * part), BF16),
            pltpu.VMEM((local, width), F32),
            pltpu.VMEM((local, width), BF16),
            pltpu.VMEM((local, width), BF16),
            pltpu.SemaphoreType.DMA((9,)),
        ],
        compiler_params=params(15),
        cost_estimate=pl.CostEstimate(flops=1000, bytes_accessed=1000, transcendentals=0),
        name="mixed_back",
    )(scalars, ranks, dq, dk, dv, qkv_weight, resid_grad, own, other, marker)


def token_kernel(
    scalars, grad_ref, received_ref, text_kernel, patch_kernel, marker, out_ref, after_ref,
    text, patch, masks, lanes,
):
    side, fine = scalars[0], scalars[2]
    local, width = out_ref.shape
    groups = width // 128
    pad = GRID_HI + 2
    after_ref[...] = jnp.zeros(after_ref.shape, F32)
    rows = masks.shape[1]
    head = TEXT - local
    clear_pads(text, patch, pad)
    store_masks(masks, fine, rows)

    def load(low):
        for lane in range(groups):
            cols = slice(lane * 128, lane * 128 + 128)
            total = grad_ref[:, cols] + received_ref[:, cols].astype(F32)
            if low:
                text[lane, 8 : 8 + local + 8, :] = total
                text[lane, 16 + local : 8 + TEXT, :] = jnp.zeros((head - 8, 128), F32)
                patch[lane, pad : pad + rows, :] = jnp.zeros((rows, 128), F32)
            else:
                text[lane, 8 : local, :] = jnp.zeros((local - 8, 128), F32)
                text[lane, local : local + 8, :] = total[local:]
                text[lane, 8 + local : 8 + TEXT, :] = total[:head]
                patch[lane, pad : pad + rows, :] = total[head:local]

    pl.when(side == 0)(lambda: load(True))
    pl.when(side != 0)(lambda: load(False))

    def one_lane(lane, carry):
        mix_lane(text, patch, masks, lanes, lane, text_kernel, patch_kernel, fine, pad, True)
        return carry

    lax.fori_loop(0, groups, one_lane, 0, unroll=True)
    mine = pl.ds(pl.multiple_of(side * local, 8), local)
    for lane in range(groups):
        out_ref[:, lane * 128 : lane * 128 + 128] = lanes[lane, mine, :]


def token_back(scalars, grad, received, text_kernel, patch_kernel, seq, marker):
    local, width = grad.shape[0] - 8, grad.shape[1]
    groups = width // 128
    return pl.pallas_call(
        token_kernel,
        out_shape=(jax.ShapeDtypeStruct((local, width), F32), jax.ShapeDtypeStruct((8, 128), F32)),
        in_specs=[smem()] + [vmem()] * 4 + [anywhere()],
        out_specs=(vmem(), vmem()),
        scratch_shapes=[
            pltpu.VMEM((groups, TEXT + 16, 128), F32),
            pltpu.VMEM((groups, seq - TEXT + 2 * (GRID_HI + 2), 128), F32),
            pltpu.VMEM((9, seq - TEXT, 128), F32),
            pltpu.VMEM((groups, seq, 128), F32),
        ],
        compiler_params=params(9),
        cost_estimate=pl.CostEstimate(flops=1000, bytes_accessed=1000, transcendentals=0),
        name="token_back",
    )(scalars, grad, received, text_kernel, patch_kernel, marker)


def finish_kernel(scalars, kept_ref, received_ref, grad_ref):
    side = scalars[0]
    part = kept_ref.shape[1] // 3
    for block in range(3):
        cols = slice(block * part, (block + 1) * part)
        mine = pl.ds(pl.multiple_of((2 * block + side) * part, 128), part)
        theirs = pl.ds(pl.multiple_of((2 * block + 1 - side) * part, 128), part)
        grad_ref[:, mine] = kept_ref[:, cols]
        grad_ref[:, theirs] = received_ref[:, cols].astype(F32)


def finish_little_kernel(
    kept_ref, received_ref, taps_ref, cells_ref, gains_ref, shifts_ref, down_ref, up_ref,
    rank_ref, box_ref, *, ratio, shared, heads,
):
    rows = taps_ref.shape[1]
    small = kept_ref[:rows, :] + received_ref[:rows, :]
    padded = jnp.concatenate([small, jnp.zeros((128 - rows, 128), F32)], axis=0)
    turned = padded.T
    taps_ref[...] = turned[0:9, :rows]
    cells_ref[...] = turned[16:25, :rows]
    gains_ref[...] = turned[32:34, :rows]
    shifts_ref[...] = turned[34:36, :rows]
    down_ref[...] = turned[36:37, :rows]
    row = lax.broadcasted_iota(jnp.int32, (rows, 128), 0)
    lane = lax.broadcasted_iota(jnp.int32, (rows, 128), 1)
    total = jnp.zeros((rows, 128), F32)
    for column in range(ratio):
        value = jnp.broadcast_to(small[:, 40 + column : 41 + column], (rows, 128))
        total = total + jnp.where(lane == row * ratio + column, value, 0.0)
    up_ref[...] = jnp.sum(total, axis=0, keepdims=True)[:, : rows * ratio]
    tables = kept_ref[kept_ref.shape[0] - shared :, :] + received_ref[received_ref.shape[0] - shared :, :]
    for head in range(2 * heads):
        row = head // heads * 16 + head % heads
        rank_ref[head : head + 1, :] = tables[row : row + 1, :NB1]
        box_ref[head, 0:1, :] = tables[row : row + 1, NB1 : NB1 + NB2]
        box_ref[head, 1:2, :] = tables[row + 8 : row + 9, :NB2]


def finish_all_kernel(*refs, ratio, shared, heads):
    scalars = refs[0]
    up_in, joint_in, qkv_in, little_in = (refs[n : n + 2] for n in (1, 3, 5, 7))
    totals, qkv_out, little_out = refs[9:12], refs[12], refs[13:]
    total_kernel(*up_in, *joint_in, *totals)
    finish_kernel(scalars, *qkv_in, qkv_out)
    finish_little_kernel(*little_in, *little_out, ratio=ratio, shared=shared, heads=heads)


def finish_all(scalars, up, joint, qkv, little, width, deep, heads):
    rows, ratio = up.kept.shape[0], deep // width
    full = lambda *shape: jax.ShapeDtypeStruct(shape, F32)
    return pl.pallas_call(
        functools.partial(finish_all_kernel, ratio=ratio, shared=little.shared, heads=heads),
        out_shape=(
            full(rows, deep), full(rows, width), full(rows * ratio, width), full(rows, 3 * width),
            full(9, rows), full(9, rows), full(2, rows), full(2, rows), full(1, rows),
            full(1, rows * ratio), full(2 * heads, NB1), full(2 * heads, 2, NB2),
        ),
        in_specs=[smem()] + [vmem()] * 8,
        out_specs=(vmem(),) * 12,
        compiler_params=params(10),
        cost_estimate=pl.CostEstimate(flops=1000, bytes_accessed=1000, transcendentals=0),
        name="finish_all",
    )(
        scalars, up.kept, up.received, joint.kept, joint.received, qkv.kept, qkv.received,
        little.now, little.received,
    )


def swap(value, stage):
    axis, bit = stage
    count = lax.axis_size(axis)
    return lax.ppermute(value, axis, [(i, i ^ bit) for i in range(count)])


def stage_flag(stage):
    axis, bit = stage
    return (lax.axis_index(axis) & bit) // bit


def block_bit(block, stage, blk_count):
    axis, bit = stage
    shift = bit * blk_count if axis == "page" else bit
    return (block // shift) & 1


def spot_of(block, stages, blk_count):
    spot = jnp.zeros_like(block)
    for stage in stages:
        spot = spot * 2 + (block_bit(block, stage, blk_count) ^ stage_flag(stage))
    return spot


def order_matrix(width, stages, blk_count):
    count = lax.axis_size("page") * blk_count
    piece = width // count
    place = jnp.arange(width, dtype=jnp.int32)
    spot, inside = place // piece, place % piece
    block = jnp.zeros_like(spot)
    for depth, stage in enumerate(stages):
        axis, bit = stage
        shift = bit * blk_count if axis == "page" else bit
        value = ((spot >> (len(stages) - 1 - depth)) & 1) ^ stage_flag(stage)
        block = block + value * shift
    column = block * piece + inside
    return (column[:, None] == jnp.arange(width, dtype=jnp.int32)[None, :]).astype(BF16)


def add_up(terms):
    total = terms[0].astype(F32)
    for term in terms[1:]:
        total = total + term.astype(F32)
    return total


def halve_kernel(kept_ref, received_ref, marker, next_ref, send_ref, after_ref):
    rows = next_ref.shape[0]
    size = rows if rows % 48 else 48
    for start in range(0, rows, size):
        for base, ref in ((rows, send_ref), (0, next_ref)):
            if base % 16 or size % 16:
                place = slice(base + start, base + start + size)
                value = kept_ref[...].astype(F32)[place] + received_ref[...].astype(F32)[place]
            else:
                place = slice(base + start, base + start + size)
                value = kept_ref[place, :].astype(F32) + received_ref[place, :].astype(F32)
            ref[start : start + size, :] = value.astype(ref.dtype)
    after_ref[...] = jnp.zeros(after_ref.shape, F32)


def halve(kept, received, marker, flops=1000):
    rows, width = received.shape[0] // 2, received.shape[1]
    if rows % 8:
        total = kept.astype(F32) + received.astype(F32)
        return total[:rows], total[rows:].astype(BF16), marker
    return pl.pallas_call(
        halve_kernel,
        out_shape=(
            jax.ShapeDtypeStruct((rows, width), F32),
            jax.ShapeDtypeStruct((rows, width), BF16),
            jax.ShapeDtypeStruct((8, 128), F32),
        ),
        in_specs=[vmem(), vmem(), anywhere()],
        out_specs=(vmem(),) * 3,
        compiler_params=params(8),
        cost_estimate=pl.CostEstimate(flops=flops, bytes_accessed=1000, transcendentals=0),
        name="halve",
    )(kept, received, marker)


class Chain:
    def __init__(self, keep, send, stages):
        self.kept, self.stages, self.done = keep, stages, 0
        self.rows = 2 * keep.shape[0]
        self.received = swap(send, stages[0])

    def turn(self, marker, flops=1000):
        self.done += 1
        if self.done >= len(self.stages):
            return marker
        self.kept, send, marker = halve(self.kept, self.received, marker, flops)
        self.received = swap(send, self.stages[self.done])
        return marker


def join_kernel(
    out_kept, out_received, down_kept, down_received, marker, next_ref, send_ref, after_ref, sums, message,
    *, piece, ratio,
):
    rows, width = next_ref.shape[0], down_kept.shape[1]
    wide = out_kept.shape[1]
    for start in range(0, 2 * rows, rows):
        part = slice(start, start + rows)
        value = out_kept[part, :] + out_received[part, :].astype(F32)
        (message if start else next_ref)[:, :wide] = value
    for start in range(0, sums.shape[0], 48):
        part = slice(start, start + 48)
        sums[part, :] = down_kept[part, :] + down_received[part, :].astype(F32)
    for start in range(0, 2 * rows, piece):
        target, place = (next_ref, start) if start < rows else (message, start - rows)
        for turn in range(ratio):
            cols = slice(wide + turn * width, wide + (turn + 1) * width)
            source = ratio * start + turn * piece
            target[place : place + piece, cols] = sums[source : source + piece, :]
    for start, size in row_chunks(wide + ratio * width, 512):
        cols = slice(start, start + size)
        send_ref[:, cols] = message[:, cols].astype(BF16)
    after_ref[...] = jnp.zeros(after_ref.shape, F32)


def join(out, down, devices, marker):
    rows, wide = out.kept.shape
    tall, width = down.kept.shape
    ratio = tall // rows
    piece = out.rows // devices
    full = wide + ratio * width
    out.done += 1
    down.done += 1
    if piece % 8:
        total = down.kept + down.received.astype(F32)
        total = total.reshape(rows // piece, ratio, piece, width).swapaxes(1, 2).reshape(rows, ratio * width)
        total = jnp.concatenate([out.kept + out.received.astype(F32), total], axis=1)
        kept, send = total[: rows // 2], total[rows // 2 :].astype(BF16)
    else:
        kept, send, marker = pl.pallas_call(
            functools.partial(join_kernel, piece=piece, ratio=ratio),
            out_shape=(
                jax.ShapeDtypeStruct((rows // 2, full), F32),
                jax.ShapeDtypeStruct((rows // 2, full), BF16),
                jax.ShapeDtypeStruct((8, 128), F32),
            ),
            in_specs=[vmem()] * 4 + [anywhere()],
            out_specs=(vmem(),) * 3,
            scratch_shapes=[pltpu.VMEM((tall, width), F32), pltpu.VMEM((rows // 2, full), F32)],
            compiler_params=params(10),
            cost_estimate=pl.CostEstimate(flops=1000, bytes_accessed=1000, transcendentals=0),
            name="join",
        )(out.kept, out.received, down.kept, down.received, marker)
    return Chain(kept, send, out.stages[out.done :]), marker


def total_kernel(
    up_kept, up_received, kept_ref, received_ref, up_ref, out_ref, down_ref
):
    piece, width = out_ref.shape
    wide = up_ref.shape[1] - up_kept.shape[1]
    value = kept_ref[...] + received_ref[...].astype(F32)
    up_ref[:, :wide] = value[:, :wide]
    up_ref[:, wide:] = up_kept[...] + up_received[...].astype(F32)
    out_ref[...] = value[:, wide : wide + width]
    for turn in range(down_ref.shape[0] // piece):
        start = wide + (turn + 1) * width
        down_ref[turn * piece : (turn + 1) * piece, :] = value[:, start : start + width]


def little_kernel(now_ref, received_ref, marker, next_ref, message_ref, after_ref, *, shared):
    rows = received_ref.shape[0] - shared
    half = message_ref.shape[0] - shared
    common = now_ref[2 * rows :, :] + received_ref[rows:, :]
    kept = now_ref[:rows, :] + received_ref[:rows, :]
    next_ref[:rows, :] = kept
    next_ref[rows:, :] = common
    message_ref[:half, :] = kept[half:]
    message_ref[half:, :] = common
    after_ref[...] = jnp.zeros(after_ref.shape, F32)


class Little:
    def __init__(self, now, shared, stages):
        self.now, self.shared, self.stages, self.done = now, shared, stages, 0
        rows = (now.shape[0] - shared) // 2
        self.received = swap(now[rows:], stages[0])

    def turn(self, marker):
        self.done += 1
        if self.done > len(self.stages):
            return marker
        rows = self.received.shape[0] - self.shared
        if self.done == len(self.stages):
            return marker
        half = rows // 2
        if half % 8:
            kept = self.now[:rows] + self.received[:rows]
            common = self.now[2 * rows :] + self.received[rows:]
            self.now = jnp.concatenate([kept, common], axis=0)
            message = self.now[half:]
        else:
            lanes = self.now.shape[1]
            self.now, message, marker = pl.pallas_call(
                functools.partial(little_kernel, shared=self.shared),
                out_shape=(
                    jax.ShapeDtypeStruct((rows + self.shared, lanes), F32),
                    jax.ShapeDtypeStruct((half + self.shared, lanes), F32),
                    jax.ShapeDtypeStruct((8, 128), F32),
                ),
                in_specs=[vmem(), vmem(), anywhere()],
                out_specs=(vmem(),) * 3,
                compiler_params=params(4),
                cost_estimate=pl.CostEstimate(flops=1000, bytes_accessed=1000, transcendentals=0),
                name="little",
            )(self.now, self.received, marker)
        self.received = swap(message, self.stages[self.done])
        return marker


def gather_kernel(
    scalars, order_hbm, owner_hbm, inside_hbm, fold_hbm, rank_hbm, box_hbm, taps_hbm, cells_hbm, dense_hbm,
    blocks_hbm, sums_a, sums_b, sums_c, marker, out_ref, after_ref,
    order, owner, inside, fold, rank, box, taps, cells, dense_sums, blocks, sums, copies,
):
    fetches = fetch(
        [order_hbm, owner_hbm, inside_hbm, fold_hbm, rank_hbm, box_hbm, taps_hbm, cells_hbm,
         dense_hbm, blocks_hbm, sums_a, sums_b, sums_c],
        [order, owner, inside, fold, rank, box, taps, cells, dense_sums, blocks]
        + [sums.at[pl.ds(2 * n, 2)] for n in range(3)],
        copies,
    )
    for copy in fetches:
        copy.wait()
    after_ref[...] = jnp.zeros(after_ref.shape, F32)
    width = order.shape[0]

    rows = jnp.concatenate([taps[...], cells[...], dense_sums[...]], axis=0)
    rows = jnp.concatenate([rows, jnp.zeros((128 - rows.shape[0], width), F32)], axis=0)
    spread = dot_nn(owner[...], blocks[...].astype(BF16)) * inside[...].astype(F32)
    bias = dot_nn(spread.astype(BF16), fold[...]).astype(BF16)
    out_ref[:width, :] = dot_nt(order[...], rows.astype(BF16)) + dot_nn(order[...], bias)
    out_ref[width:, :] = jnp.zeros((32, 128), F32)
    heads = sums.shape[0]
    mine = pl.multiple_of(width + scalars[0] * 16, 16)
    pad = lambda value: jnp.concatenate([value, jnp.zeros((8 - heads, value.shape[1]), F32)], axis=0)
    by_rank = pad(jnp.concatenate([sums[head, 0:1, :] for head in range(heads)], axis=0))
    table = sum(dot_nn(piece, rank[...]) for piece in halves_of(by_rank))
    out_ref[pl.ds(mine, 8), 0:NB1] = table
    for half in range(2):
        by_box = pad(
            jnp.concatenate([sums[head, half + 1 : half + 2, : 2 * SPAN] for head in range(heads)], axis=0)
        )
        table = sum(dot_nn(piece, box[...]) for piece in halves_of(by_box))
        if half == 0:
            out_ref[pl.ds(mine, 8), NB1 : NB1 + NB2] = table
        else:
            out_ref[pl.ds(mine + 8, 8), 0:NB2] = table


def gather_small(scalars, order, taps, cells, dense_sums, blocks, sums, deep, marker):
    width = order.shape[0]
    devices = blocks.shape[0]
    ratio = deep // width
    piece = width // devices
    rows, lanes = np.arange(width), np.arange(128)
    owner = jnp.asarray(rows[:, None] // piece == np.arange(devices)[None, :], BF16)
    inside = jnp.asarray(
        (lanes[None, :] // ratio == rows[:, None] % piece) & (lanes[None, :] < piece * ratio), BF16
    )
    fold = jnp.asarray(lanes[:, None] % ratio + 40 == lanes[None, :], BF16)
    rank = jnp.asarray(bucket_rows(np.arange(RANK_LANES) - (RANK_MID - 1), rank_marks, NB1), BF16)
    box = jnp.asarray(bucket_rows(np.arange(2 * SPAN) - (SPAN - 1), box_marks, NB2), BF16)
    constants = tuple(map(stay, (owner, inside, fold, rank, box)))
    operands = (order, *constants, taps, cells, dense_sums, blocks)
    return pl.pallas_call(
        gather_kernel,
        out_shape=(
            jax.ShapeDtypeStruct((width + 32, 128), F32), jax.ShapeDtypeStruct((8, 128), F32)
        ),
        in_specs=[smem(), anywhere()] + [parameter()] * 5 + [anywhere()] * 8,
        out_specs=(vmem(), vmem()),
        scratch_shapes=[pltpu.VMEM(value.shape, value.dtype) for value in operands]
        + [pltpu.VMEM((2 * len(sums), 8, RANK_LANES), F32), pltpu.SemaphoreType.DMA((13,))],
        compiler_params=params(10),
        cost_estimate=pl.CostEstimate(flops=1000, bytes_accessed=1000, transcendentals=0),
        name="gather_small",
    )(scalars, *operands, *sums, marker)


def per_device(
    tokens,
    patch_count,
    reading_rank,
    boxes,
    text_kernel,
    patch_kernel,
    qkv_weight,
    rank_table,
    box_tables,
    out_weight,
    norm_gains,
    norm_shifts,
    up_weight,
    up_bias,
    down_weight,
    down_bias,
    cotangent,
):
    qkv_weight, out_weight, up_weight, down_weight = map(
        stay, (qkv_weight, out_weight, up_weight, down_weight)
    )
    side = lax.axis_index("blk")
    blk_count = lax.axis_size("blk")
    page_stages = [("page", 1 << n) for n in range(lax.axis_size("page").bit_length() - 1)]
    across = ("blk", 1)
    out_stages = page_stages[:1] + [across] + page_stages[1:]
    up_stages = page_stages[:1] + page_stages[2:] + [across] + page_stages[1:2]
    down_stages = page_stages[:2] + [across] + page_stages[2:]
    qkv_stages = page_stages[:1] + page_stages[2:] + page_stages[1:2] + [across]
    little_stages = page_stages[:2] + [across] + page_stages[2:]
    devices = lax.axis_size("page") * blk_count
    count = patch_count[0]
    ranks = reading_rank
    own = tokens[0]
    local, width = own.shape
    deep = up_bias.shape[0]
    seq = ranks.shape[1]
    heads = HEADS // blk_count
    scalars = jnp.stack(
        [side, TEXT + count, (count == GRID_HI * GRID_HI).astype(jnp.int32), jnp.int32(0)]
    ).astype(jnp.int32)
    other = swap(own, across)

    xy, xyt, rank_bias, box_bias = onehots(scalars, ranks, boxes, rank_table, box_tables, heads)
    mixed, mixed_low, packed = mix_and_project(
        scalars, ranks, own, other, text_kernel, patch_kernel, qkv_weight
    )
    pack = jnp.concatenate([norm_gains, norm_shifts, down_bias[None], up_bias.reshape(-1, width)], axis=0)
    own_context, other_context, shares = [], [], []
    for first, pairs in ((0, 2), (2, 1)):
        share, mine, theirs = attend(
            scalars, ranks, packed, xy, rank_bias, box_bias, local, first, pairs
        )
        shares += [(share, place) for place in range(pairs)]
        own_context.append(mine)
        other_context.append(swap(theirs, across))
    order_qkv = order_matrix(width, qkv_stages, blk_count)
    order_little = order_matrix(width, little_stages, blk_count)
    turned, marker = turn_rows(order_qkv, mixed_low, own_context[-1])
    (
        layer_output, context, hidden_low, act_low, branch_grad, pre_grad, attend_grad,
        resid_one_grad, own_part, their_part, dense_sums, bias_blocks,
    ) = dense(
        scalars, mixed, own_context, other_context, pack, cotangent[0], out_weight, up_weight,
        down_weight, devices, marker,
    )
    part = width // blk_count
    received_part = swap(their_part, across)

    order_out = order_matrix(width, out_stages, blk_count)
    order_up = order_matrix(width, up_stages, blk_count)
    piece = deep // devices
    blocks = jnp.arange(devices, dtype=jnp.int32)
    spots = spot_of(blocks, down_stages, blk_count) * piece
    act_rows = act_low
    if piece % 16:
        place = jnp.arange(deep, dtype=jnp.int32)
        target = spots[place // piece] + place % piece
        act_rows = jnp.zeros_like(act_low).at[:, target].set(act_low, unique_indices=True)
        piece = width // 8
        spots = jnp.arange(deep // piece, dtype=jnp.int32) * piece
    steps = deep // width
    split = deep * 11 // 24
    down_keep, down_send = down_weight_grad(spots, act_rows, branch_grad, piece)
    down = Chain(down_keep, down_send, down_stages)
    out_keep, out_send, up_keep, up_send = up_weight_grads_of(
        pre_grad, hidden_low, context, attend_grad, order_out, order_up, split, down_keep
    )
    out = Chain(out_keep, out_send, out_stages)
    up = Chain(up_keep, up_send, up_stages)
    marker = down.turn(up_send)

    grads, sums = None, []
    for pair, (share, place) in enumerate(shares):
        if pair == 1:
            marker = up.turn(out.turn(sums[0]))
        *grads, pair_sums = attend_back(
            scalars, ranks, own_part, received_part, share, packed, xy, xyt, pair, place, grads,
            marker if pair < 2 else None,
        )
        sums.append(pair_sums)
    dq, dk, dv = grads
    qkv_keep, qkv_send, marker = project_weight_grad(turned, dq, dk, dv, sums[-1])
    qkv = Chain(qkv_keep, qkv_send, qkv_stages)
    marker = down.turn(out.turn(up.turn(marker)), LONG)
    marker = qkv.turn(marker)
    grad, outgoing, taps, cells = mixed_back(
        scalars, ranks, dq, dk, dv, qkv_weight, resid_one_grad, stay(own), other, marker
    )
    incoming = swap(outgoing, across)
    gathered, marker = gather_small(
        scalars, order_little, taps, cells, dense_sums, bias_blocks, sums, deep, taps
    )
    little = Little(gathered, 32, little_stages)
    marker = up.turn(qkv.turn(marker))
    joint, marker = join(out, down, devices, marker)
    marker = little.turn(little.turn(marker))
    token_grad, marker = token_back(
        scalars, grad, incoming, text_kernel, patch_kernel, seq, marker
    )
    for _ in range(len(qkv_stages) - 4):
        for chain in (qkv, little, up, joint):
            marker = chain.turn(marker)
    marker = little.turn(qkv.turn(marker))
    for _ in qkv_stages:
        marker = little.turn(qkv.turn(marker))
    (
        up_weight_grads, out_weight_grads, down_weight_grads, qkv_weight_grad, taps, cells, gains, shifts,
        down_bias_grad, up_bias_grad, rank_grad, box_grad,
    ) = finish_all(scalars, up, joint, qkv, little, width, deep, heads)
    return (
        layer_output[None],
        token_grad[None],
        taps,
        cells,
        qkv_weight_grad,
        rank_grad,
        jnp.swapaxes(box_grad, 0, 1),
        out_weight_grads,
        gains,
        shifts,
        up_weight_grads,
        up_bias_grad[0],
        down_weight_grads,
        down_bias_grad[0],
    )


def solution(mesh):
    in_specs = (
        P("page", "blk", None),
        P("page"),
        P("page", None),
        P(None, "page", None),
        P(),
        P(),
        P(),
        P(),
        P(),
        P(),
        P(),
        P(),
        P(),
        P(),
        P(),
        P(),
        P("page", "blk", None),
    )
    out_specs = (
        P("page", "blk", None),
        P("page", "blk", None),
        P(None, ("page", "blk")),
        P(None, ("page", "blk")),
        P(("page", "blk"), None),
        P(),
        P(),
        P(("page", "blk"), None),
        P(None, ("page", "blk")),
        P(None, ("page", "blk")),
        P(("page", "blk"), None),
        P(("page", "blk")),
        P(("page", "blk"), None),
        P(("page", "blk")),
    )
    return jax.shard_map(
        per_device, mesh=mesh, in_specs=in_specs, out_specs=out_specs, check_vma=False
    )
```
